32 devices in a mesh: dp: 8 (over y, x, core), fsdp: 4 (over z).
Axes of the slice: x: 2, y: 2, z: 4, core: 2. Of those that a mesh axis runs over, the one named last changes fastest.
Arguments:
- tokens: bfloat16 [8192, 2048], P(('dp', 'fsdp')), may hold values from -6 to 6
- cotangent: bfloat16 [8192, 2048], P(('dp', 'fsdp')), may hold values from -6 to 6
- group_ids: int32 [32], P(('dp', 'fsdp')), may hold values from 0 to 7
- norm_first: bfloat16 [2048], P(('dp', 'fsdp')), may hold values from 0.5 to 1.5
- input_weight: bfloat16 [2048, 12288], P(('dp', 'fsdp')), may hold values from -0.125 to 0.125
- decay_weight: bfloat16 [2048, 32], P(('dp', 'fsdp')), may hold values from -0.125 to 0.125
- conv_weight: bfloat16 [4, 8192], P(None, ('dp', 'fsdp')), may hold values from -2.5 to 2.5
- decay_scale: float32 [16], replicated, may hold values from -5 to -1
- decay_bias: float32 [16], replicated, may hold values from -1 to 1
- output_gain: float32 [256], replicated, may hold values from 0.5 to 1.5
- output_weight: bfloat16 [4096, 2048], P(('dp', 'fsdp')), may hold values from -0.09375 to 0.09375
- norm_second: bfloat16 [2048], P(('dp', 'fsdp')), may hold values from 0.5 to 1.5
- upgate_weight: bfloat16 [2048, 11264], P(('dp', 'fsdp')), may hold values from -0.125 to 0.125
- down_weight: bfloat16 [5632, 2048], P(('dp', 'fsdp')), may hold values from -0.078125 to 0.078125
Outputs:
- block_out: float32 [8192, 2048], P(('dp', 'fsdp'))
- tokens_grad: float32 [8192, 2048], P(('dp', 'fsdp'))
- norm_first_grad: float32 [2048], P(('dp', 'fsdp'))
- input_weight_grad: float32 [2048, 12288], P(('dp', 'fsdp'))
- decay_weight_grad: float32 [2048, 32], P(('dp', 'fsdp'))
- conv_weight_grad: float32 [4, 8192], P(None, ('dp', 'fsdp'))
- decay_scale_grad: float32 [16], replicated
- decay_bias_grad: float32 [16], replicated
- output_gain_grad: float32 [256], replicated
- output_weight_grad: float32 [4096, 2048], P(('dp', 'fsdp'))
- norm_second_grad: float32 [2048], P(('dp', 'fsdp'))
- upgate_weight_grad: float32 [2048, 11264], P(('dp', 'fsdp'))
- down_weight_grad: float32 [5632, 2048], P(('dp', 'fsdp'))
The draws below stay inside these ranges and needn't reach their ends.
All inputs are finite; a program needn't handle non-finite values.
Results may differ from the reference program's by a relative error of at most 0.015.
Values may be sent and summed in bfloat16 or wider, within the bound.
A program may use at most 576 MiB of HBM per device.

```python
import math
import jax
import jax.numpy as jnp
import numpy as np
from jax import lax

D = 2048
H = 16
DK = 128
DV = 256
FF = 5632
SPAN = 64
KCONV = 4
GROUPS = 8
SEQ = 256
HV = 4096
NCONV = 8192
NIN = 12288
SEQS = 32
TOKENS = 8192


def touch_ends(entries, rng, least, high):
    place = [jax.random.randint(jax.random.fold_in(rng, axis), (), 0, length) for axis, length in enumerate(entries.shape)]
    widest = entries.shape.index(max(entries.shape))
    next_to = place[:widest] + [(place[widest] + 1) % entries.shape[widest]] + place[widest + 1:]
    return entries.at[tuple(place)].set(least).at[tuple(next_to)].set(high)


def levels(own_key, dims, split, low, top_value):
    factor_of, own = 1.0, jax.random.fold_in(own_key, 6)
    for position, parts in split:
        draws = jnp.exp(jax.random.uniform(jax.random.fold_in(own, position), (parts,), jnp.float32, low / len(split), top_value / len(split)))
        factor_of = factor_of * jnp.repeat(draws, dims[position] // parts).reshape([-1 if axis == position else 1 for axis in range(len(dims))])
    return factor_of


def rank_bounds(number_of, skew):
    weights = [(1 << 20) // math.isqrt(standing ** skew) + 1 for standing in range(1, number_of + 1)]
    width = 1 + sum(weights) // (1 << 30)
    return np.cumsum(np.array([max(1, weight // width) for weight in weights]))


def ranked_ids(own_key, dims, count, skew):
    listing = rank_bounds(count, skew)
    pick = jax.random.randint(jax.random.fold_in(own_key, 1), dims, 0, int(listing[count - 1]))
    standing = jnp.searchsorted(jnp.asarray(listing, jnp.int32), pick, side="right")
    return jax.random.permutation(jax.random.fold_in(own_key, 2), count)[standing].astype(jnp.int32)


def noise(own_key, shape, scale, bound, shards=(), kind=jnp.bfloat16):
    array = jax.random.normal(own_key, shape, jnp.float32) * scale
    if len(shards) > 0:
        array = levels(own_key, shape, shards, -0.22, 0.18) * array
    return jnp.clip(array, min=-bound, max=bound).astype(kind)


def setup_inputs(seed: int = 0) -> dict:
    key_list = jax.random.split(jax.random.key(seed), 15)
    return {
        "tokens": noise(key_list[0], (TOKENS, D), 1.0, 6.0, ((0, 32),)),
        "cotangent": noise(key_list[1], (TOKENS, D), 1.0, 6.0, ((0, 32),)),
        "group_ids": touch_ends(ranked_ids(key_list[2], (SEQS,), GROUPS, 2), jax.random.fold_in(key_list[2], 3), 0, GROUPS - 1).astype(jnp.int32),
        "norm_first": jnp.clip(1.0 + 0.1 * jax.random.normal(key_list[3], (D,), jnp.float32), 0.5, 1.5).astype(jnp.bfloat16),
        "input_weight": noise(key_list[4], (D, NIN), D ** -0.5, 0.125, ((0, 32),)),
        "decay_weight": noise(key_list[5], (D, 2 * H), D ** -0.5, 0.125, ((0, 32),)),
        "conv_weight": noise(key_list[6], (KCONV, NCONV), 0.5, 2.5, ((1, 32),)),
        "decay_scale": jnp.clip(jax.random.uniform(key_list[7], (H,), jnp.float32, -5.0, -1.0), -5.0, -1.0),
        "decay_bias": jnp.clip(jax.random.uniform(key_list[8], (H,), jnp.float32, -1.0, 1.0), -1.0, 1.0),
        "output_gain": jnp.clip(1.0 + 0.1 * jax.random.normal(key_list[9], (DV,), jnp.float32), 0.5, 1.5),
        "output_weight": noise(key_list[10], (HV, D), HV ** -0.5, 0.09375, ((0, 32),)),
        "norm_second": jnp.clip(1.0 + 0.1 * jax.random.normal(key_list[11], (D,), jnp.float32), 0.5, 1.5).astype(jnp.bfloat16),
        "upgate_weight": noise(key_list[12], (D, 2 * FF), D ** -0.5, 0.125, ((0, 32),)),
        "down_weight": noise(key_list[13], (FF, D), FF ** -0.5, 0.078125, ((0, 32),)),
    }


EPSILON = 1e-06
EXACT_MATMUL = lax.Precision.HIGHEST

@jax.custom_vjp
def low(v):
    return lax.optimization_barrier(v.astype(jnp.bfloat16)).astype(jnp.float32)

@jax.custom_vjp
def low_back(v):
    return v

def low_keep(v):
    return (low(v), None)

def low_pass(kept, grad):
    return (grad,)

def back_keep(v):
    return (v, None)

def back_low(kept, grad):
    return (low(grad),)
low.defvjp(low_keep, low_pass)
low_back.defvjp(back_keep, back_low)

def rms_norm(values_in, gain):
    return values_in * lax.rsqrt(lax.optimization_barrier(jnp.mean(values_in * values_in, axis=-1, keepdims=True)) + EPSILON) * gain

def prepare(projected, decay_raw, conv_taps, decay_scale, decay_bias):
    length = projected.shape[0]
    tap_count = conv_taps.shape[0]
    mix_width = conv_taps.shape[1]
    conv_input = projected[:, :mix_width]
    padded = jnp.pad(conv_input, ((tap_count - 1, 0), (0, 0)))
    convolved = padded[0:length] * conv_taps[0]
    for offset in range(1, tap_count):
        convolved = convolved + padded[offset:offset + length] * conv_taps[offset]
    active = jax.nn.silu(convolved)
    key_width = H * DK
    queries = active[:, :key_width].reshape(length, H, DK)
    keys_all = active[:, key_width:2 * key_width].reshape(length, H, DK)
    values_all = active[:, 2 * key_width:].reshape(length, H, DV)
    queries = queries * lax.rsqrt(lax.optimization_barrier(jnp.sum(queries * queries, axis=-1, keepdims=True)) + EPSILON) * DK ** (-0.5)
    keys_all = keys_all * lax.rsqrt(lax.optimization_barrier(jnp.sum(keys_all * keys_all, axis=-1, keepdims=True)) + EPSILON)
    decay_rate = -jnp.exp(decay_scale) * jax.nn.softplus(decay_raw[:, :H] + decay_bias)
    strength = jax.nn.sigmoid(decay_raw[:, H:])
    gate_values = projected[:, mix_width:].reshape(length, H, DV)
    return (jnp.transpose(queries, (1, 0, 2)), jnp.transpose(keys_all, (1, 0, 2)), jnp.transpose(values_all, (1, 0, 2)), decay_rate.T, strength.T, gate_values)

def delta_rule(queries, keys_all, values_all, decay_rate, strength):
    head_count, length, key_dim = queries.shape
    value_dim = values_all.shape[2]
    block_count = length // SPAN

    def to_blocks(tensor):
        return jnp.moveaxis(tensor.reshape((head_count, block_count, SPAN) + tensor.shape[2:]), 1, 0)
    query_blocks = to_blocks(queries)
    key_blocks = to_blocks(keys_all)
    value_blocks = to_blocks(values_all)
    rate_blocks = to_blocks(decay_rate)
    beta_blocks = to_blocks(strength)
    cumulated = jnp.cumsum(rate_blocks, axis=-1)
    row_ids = jnp.arange(SPAN, dtype=jnp.int32)
    strict = row_ids[:, None] > row_ids[None, :]
    within = row_ids[:, None] >= row_ids[None, :]
    gaps_log = cumulated[..., :, None] - cumulated[..., None, :]
    key_gram = jnp.einsum('bhid,bhjd->bhij', key_blocks, key_blocks, precision=EXACT_MATMUL)
    lower_part = jnp.where(strict, jnp.exp(jnp.where(strict, gaps_log, 0.0)) * key_gram * beta_blocks[..., :, None], 0.0)
    growth = jnp.exp(cumulated)
    solved_values = jax.scipy.linalg.solve_triangular(lower_part, beta_blocks[..., None] * value_blocks, lower=True, unit_diagonal=True)
    solved_keys = jax.scipy.linalg.solve_triangular(lower_part, (beta_blocks * growth)[..., None] * key_blocks, lower=True, unit_diagonal=True)
    query_key = jnp.einsum('bhid,bhjd->bhij', query_blocks, key_blocks, precision=EXACT_MATMUL)
    weights_in = jnp.where(within, jnp.exp(jnp.where(within, gaps_log, 0.0)) * query_key, 0.0)
    query_grow = growth[..., None] * query_blocks
    key_tail = jnp.exp(cumulated[..., -1:] - cumulated)[..., None] * key_blocks
    final_decay = jnp.exp(cumulated[..., -1])[..., None, None]

    def advance(running_state, span_items):
        current_values, current_keys, weights_now, current_query, current_tail, current_decay = span_items
        written_state = current_values - jnp.einsum('ynr,yrg->yng', current_keys, running_state, precision=EXACT_MATMUL)
        current_output = jnp.einsum('ynr,yrg->yng', current_query, running_state, precision=EXACT_MATMUL)
        current_output = current_output + jnp.einsum('hij,hjv->hiv', weights_now, written_state, precision=EXACT_MATMUL)
        running_state = current_decay * running_state + jnp.einsum('izu,izx->iux', current_tail, written_state, precision=EXACT_MATMUL)
        return (running_state, current_output)
    initial = jnp.zeros((head_count, key_dim, value_dim), queries.dtype)
    _, outputs = lax.scan(jax.checkpoint(advance), initial, (solved_values, solved_keys, weights_in, query_grow, key_tail, final_decay))
    return jnp.moveaxis(outputs, 0, 1).reshape(head_count, length, value_dim)

def finish(core_out, gate_values, output_gain):
    length = gate_values.shape[0]
    ordered = jnp.transpose(core_out, (1, 0, 2))
    normed = rms_norm(ordered, output_gain) * jax.nn.silu(gate_values)
    return normed.reshape(length, -1)

def token_mixer(projected, decay_raw, conv_taps, decay_scale, decay_bias, output_gain):
    queries, keys_all, values_all, decay_rate, strength, gate_values = prepare(projected, decay_raw, conv_taps, decay_scale, decay_bias)
    core_out = delta_rule(low(queries), low(keys_all), low(values_all), decay_rate, strength)
    return finish(core_out, gate_values, output_gain)

def block_layer(weights_all, inputs):
    norm_first, input_weight, decay_weight, conv_weight, decay_scale, decay_bias, output_gain, output_weight, norm_second, upgate_weight, down_weight = weights_all
    normed_one = low(rms_norm(inputs, norm_first))
    projected = low_back(jnp.dot(normed_one, input_weight, precision=EXACT_MATMUL))
    decay_raw = low_back(jnp.dot(normed_one, decay_weight, precision=EXACT_MATMUL))
    mixed_out = jax.vmap(token_mixer, in_axes=(0, 0, None, None, None, None))(projected, decay_raw, conv_weight, decay_scale, decay_bias, output_gain)
    branch = low_back(jnp.dot(low(mixed_out), output_weight, precision=EXACT_MATMUL))
    middle = inputs + branch
    normed_two = low(rms_norm(middle, norm_second))
    upgate = low_back(jnp.dot(normed_two, upgate_weight, precision=EXACT_MATMUL))
    hidden = low(jax.nn.silu(upgate[..., :FF]) * upgate[..., FF:])
    return middle + low_back(jnp.dot(hidden, down_weight, precision=EXACT_MATMUL))

def reference(tokens, cotangent, group_ids, norm_first, input_weight, decay_weight, conv_weight, decay_scale, decay_bias, output_gain, output_weight, norm_second, upgate_weight, down_weight):
    weights_all = tuple((source.astype(jnp.float32) for source in (norm_first, input_weight, decay_weight, conv_weight, decay_scale, decay_bias, output_gain, output_weight, norm_second, upgate_weight, down_weight)))
    labels = jnp.arange(GROUPS, dtype=jnp.int32)
    onehot = (group_ids[:, None] == labels[None, :]).astype(jnp.float32)
    counts = lax.optimization_barrier(jnp.sum(onehot, axis=0))
    scales = 1.0 / lax.optimization_barrier(jnp.sum(onehot * counts[None, :], axis=1))
    block_size = 4
    block_count = SEQS // block_size
    inputs = tokens.astype(jnp.float32).reshape(block_count, block_size, SEQ, D)
    scaled_cotangent = (cotangent.astype(jnp.float32).reshape(SEQS, SEQ, D) * scales[:, None, None]).reshape(block_count, block_size, SEQ, D)

    def advance(totals, seq_pair):
        outputs, pullback = jax.vjp(block_layer, weights_all, seq_pair[0])
        weight_grads, input_grads = pullback(seq_pair[1])
        totals = jax.tree.map(lambda earlier, latest: earlier + latest, totals, weight_grads)
        return (totals, (outputs, input_grads))
    zero_totals = jax.tree.map(jnp.zeros_like, weights_all)
    totals, (outputs, input_grads) = lax.scan(advance, zero_totals, (inputs, scaled_cotangent))
    return (outputs.reshape(TOKENS, D), input_grads.reshape(TOKENS, D), totals[0], totals[1], totals[2], totals[3], totals[4], totals[5], totals[6], totals[7], totals[8], totals[9], totals[10])
```

```python
import functools

import jax
import jax.numpy as jnp
from jax import lax
from jax.experimental import pallas as pl
from jax.experimental.pallas import tpu as pltpu
from jax.sharding import PartitionSpec as P

MESH = pl.DeviceIdType.MESH
F32 = jnp.float32
BF16 = jnp.bfloat16
EPSILON = 1e-06
DK = 128
DV = 256
NN = (((1,), (0,)), ((), ()))
NT = (((1,), (1,)), ((), ()))
TN = (((0,), (0,)), ((), ()))


def dot1(a, b, dims=NN):
    return lax.dot_general(a.astype(BF16), b.astype(BF16), dims, preferred_element_type=F32)


def halves(a):
    if a.dtype == BF16:
        return (a,)
    high = a.astype(BF16)
    return (high, (a - high.astype(F32)).astype(BF16))


def dot3(a, b, dims=NN):
    a, b = halves(a), halves(b)
    total = lax.dot_general(a[0], b[0], dims, preferred_element_type=F32)
    if len(a) > 1:
        total = total + lax.dot_general(a[1], b[0], dims, preferred_element_type=F32)
    if len(b) > 1:
        total = total + lax.dot_general(a[0], b[1], dims, preferred_element_type=F32)
    return total


def dot6(a, b, dims=NN):
    return lax.dot_general(a, b, dims, precision=lax.Precision.HIGHEST, preferred_element_type=F32)


def shift_down(v, n, rows):
    if n == 0:
        return v
    return jnp.where(rows >= n, pltpu.roll(v, n, 0), 0.0)


def shift_up(v, n, rows):
    if n == 0:
        return v
    length = v.shape[0]
    return jnp.where(rows < length - n, pltpu.roll(v, length - n, 0), 0.0)


def conv(c, taps, rows):
    count = taps.shape[0]
    total = c * taps[count - 1 : count]
    for j in range(count - 1):
        total = total + shift_down(c, count - 1 - j, rows) * taps[j : j + 1]
    return total


def sigmoid(v):
    return 1.0 / (1.0 + jnp.exp(-v))


def softplus(v):
    return jnp.maximum(v, 0.0) + jnp.log1p(jnp.exp(-jnp.abs(v)))


def unit_inverse(lower, row_ids, col_ids):
    length = lower.shape[0]
    eye = jnp.where(row_ids == col_ids, 1.0, 0.0)
    size = 8
    base = jnp.where(row_ids // size == col_ids // size, lower, 0.0)
    square = dot6(base, base)
    inverse = dot6(eye - base, eye + square)
    inverse = inverse + dot6(inverse, dot6(square, square))
    while size < length:
        wide = 2 * size
        off = jnp.where(
            (row_ids // wide == col_ids // wide) & (row_ids // size != col_ids // size), lower, 0.0
        )
        inverse = inverse - dot3(inverse, dot3(off, inverse))
        size = wide
    return inverse


def common(proj, taps, decay, heads, length):
    rows = lax.broadcasted_iota(jnp.int32, (length, 1), 0)
    row_ids = lax.broadcasted_iota(jnp.int32, (length, length), 0)
    col_ids = lax.broadcasted_iota(jnp.int32, (length, length), 1)
    raw = proj[:, heads * 768 :]
    lanes = lax.broadcasted_iota(jnp.int32, raw.shape, 1)
    shifted = raw + decay[1:2]
    rate = jnp.where(lanes < heads, -jnp.exp(decay[0:1]) * softplus(shifted), 0.0)
    beta = sigmoid(raw)
    cumulated = dot6(jnp.where(row_ids >= col_ids, 1.0, 0.0), rate)
    return rows, row_ids, col_ids, raw, lanes, shifted, rate, beta, cumulated, cumulated.T


def head_parts(h, proj, taps, heads, rows):
    key = slice(h * DK, (h + 1) * DK)
    keyk = slice((heads + h) * DK, (heads + h + 1) * DK)
    val = slice(heads * DV + h * DV, heads * DV + (h + 1) * DV)
    gat = slice(2 * heads * DV + h * DV, 2 * heads * DV + (h + 1) * DV)
    return key, keyk, val, gat


def mixer_forward_kernel(heads, proj_ref, taps_ref, decay_ref, gain_ref, mixed_ref, inv_ref, solved_ref, core_ref):
    length = proj_ref.shape[0]
    taps_all = taps_ref[...]
    decay = decay_ref[...]
    gain = gain_ref[...]
    rows, row_ids, col_ids, raw, lanes, shifted, rate, beta, cumulated, cum_t = common(
        proj_ref[...], taps_all, decay, heads, length
    )
    for h in range(heads):
        qs, ks, vs, gs = head_parts(h, None, None, heads, rows)

        def active(cols):
            y = conv(proj_ref[:, cols], taps_ref[:, cols], rows)
            return y * sigmoid(y)

        q = active(qs)
        q = (q * lax.rsqrt(jnp.sum(q * q, axis=-1, keepdims=True) + EPSILON) * DK ** (-0.5)).astype(BF16)
        k = active(ks)
        k = (k * lax.rsqrt(jnp.sum(k * k, axis=-1, keepdims=True) + EPSILON)).astype(BF16)
        v = active(vs).astype(BF16)
        beta_h = beta[:, heads + h : heads + h + 1]
        gap = cumulated[:, h : h + 1] - cum_t[h : h + 1, :]
        growth = jnp.where(row_ids >= col_ids, jnp.exp(jnp.where(row_ids >= col_ids, gap, 0.0)), 0.0)
        gram = dot1(k, k, NT)
        lower = jnp.where(row_ids > col_ids, growth * gram * beta_h, 0.0)
        inverse = unit_inverse(lower, row_ids, col_ids)
        solved = dot3(inverse, beta_h * v.astype(F32))
        weights = growth * dot1(q, k, NT)
        core = dot3(weights, solved)
        inv_ref[h] = inverse
        solved_ref[:, h * DV : (h + 1) * DV] = solved
        core_ref[:, h * DV : (h + 1) * DV] = core
        gate = proj_ref[:, gs]
        normed = core * lax.rsqrt(jnp.mean(core * core, axis=-1, keepdims=True) + EPSILON) * gain
        mixed_ref[:, h * DV : (h + 1) * DV] = (normed * (gate * sigmoid(gate))).astype(BF16)


def mixer_forward(proj, taps, decay, gain, heads, length):
    tokens, width = proj.shape
    seqs = tokens // length
    hv = heads * DV
    row = lambda cols: pl.BlockSpec((length, cols), lambda s: (s, 0))
    whole = lambda a: pl.BlockSpec(a.shape, lambda s: (0,) * a.ndim)
    return pl.pallas_call(
        functools.partial(mixer_forward_kernel, heads),
        grid=(seqs,),
        in_specs=[row(width), whole(taps), whole(decay), whole(gain)],
        out_specs=[row(hv), pl.BlockSpec((None, heads, length, length), lambda s: (s, 0, 0, 0)), row(hv), row(hv)],
        out_shape=[
            jax.ShapeDtypeStruct((tokens, hv), BF16),
            jax.ShapeDtypeStruct((seqs, heads, length, length), F32),
            jax.ShapeDtypeStruct((tokens, hv), F32),
            jax.ShapeDtypeStruct((tokens, hv), F32),
        ],
        compiler_params=pltpu.CompilerParams(vmem_limit_bytes=48 << 20),
    )(proj, taps, decay, gain)


def mixer_backward_kernel(
    heads, proj_ref, taps_ref, decay_ref, gain_ref, inv_ref, solved_ref, core_ref, grad_ref,
    low_ref, conv_ref, gain_grad_ref, decay_grad_ref,
):
    length = proj_ref.shape[0]
    count = taps_ref.shape[0]
    decay = decay_ref[...]
    gain = gain_ref[...]
    rows, row_ids, col_ids, raw, lanes, shifted, rate, beta, cumulated, cum_t = common(
        proj_ref[...], None, decay, heads, length
    )
    within = row_ids >= col_ids
    strict = row_ids > col_ids

    @pl.when(pl.program_id(0) == 0)
    def _():
        conv_ref[...] = jnp.zeros_like(conv_ref)
        gain_grad_ref[...] = jnp.zeros_like(gain_grad_ref)
        decay_grad_ref[...] = jnp.zeros_like(decay_grad_ref)

    cum_grad = jnp.zeros(raw.shape, F32)
    beta_grad = jnp.zeros(raw.shape, F32)
    for h in range(heads):
        qs, ks, vs, gs = head_parts(h, None, None, heads, rows)
        hs = slice(h * DV, (h + 1) * DV)

        def active(cols):
            y = conv(proj_ref[:, cols], taps_ref[:, cols], rows)
            s = sigmoid(y)
            return y * s, s * (1.0 + y * (1.0 - s))

        def conv_back(cols, grad):
            c = proj_ref[:, cols]
            total = grad * taps_ref[count - 1 : count, cols]
            conv_ref[count - 1 : count, cols] += jnp.sum(grad * c, axis=0, keepdims=True)
            for j in range(count - 1):
                n = count - 1 - j
                total = total + shift_up(grad, n, rows) * taps_ref[j : j + 1, cols]
                conv_ref[j : j + 1, cols] += jnp.sum(grad * shift_down(c, n, rows), axis=0, keepdims=True)
            low_ref[:, cols] = total.astype(BF16)

        core = core_ref[:, hs]
        gate = proj_ref[:, gs]
        gate_sig = sigmoid(gate)
        grad = grad_ref[:, hs]
        root = lax.rsqrt(jnp.mean(core * core, axis=-1, keepdims=True) + EPSILON)
        normed = core * root
        silu_gate = gate * gate_sig
        gain_grad_ref[...] += jnp.sum(grad * normed * silu_gate, axis=0, keepdims=True)
        low_ref[:, gs] = (grad * normed * gain * gate_sig * (1.0 + gate * (1.0 - gate_sig))).astype(BF16)
        normed_grad = grad * gain * silu_gate
        core_grad = root * (normed_grad - normed * jnp.mean(normed_grad * normed, axis=-1, keepdims=True))

        q_act, q_slope = active(qs)
        q_root = lax.rsqrt(jnp.sum(q_act * q_act, axis=-1, keepdims=True) + EPSILON)
        q_unit = q_act * q_root
        q = (q_unit * DK ** (-0.5)).astype(BF16)
        k_act, k_slope = active(ks)
        k_root = lax.rsqrt(jnp.sum(k_act * k_act, axis=-1, keepdims=True) + EPSILON)
        k_unit = k_act * k_root
        k = k_unit.astype(BF16)
        v_act, v_slope = active(vs)
        v = v_act.astype(BF16).astype(F32)
        beta_h = beta[:, heads + h : heads + h + 1]
        gap = cumulated[:, h : h + 1] - cum_t[h : h + 1, :]
        growth = jnp.where(within, jnp.exp(jnp.where(within, gap, 0.0)), 0.0)
        decayed_gram = jnp.where(strict, growth * dot1(k, k, NT), 0.0)
        weights = growth * dot1(q, k, NT)
        inverse = inv_ref[h]
        solved = solved_ref[:, hs]
        solved_grad = dot3(weights, core_grad, TN)
        weights_grad = dot3(core_grad, solved, NT)
        value_grad = dot3(inverse, solved_grad, TN)
        lower_grad = jnp.where(strict, -dot3(value_grad, solved, NT), 0.0)
        gap_part = lower_grad * decayed_gram
        beta_col = jnp.sum(gap_part, axis=-1, keepdims=True) + jnp.sum(value_grad * v, axis=-1, keepdims=True)
        gap_grad = gap_part * beta_h + weights_grad * weights
        cum_col = jnp.sum(gap_grad, axis=-1, keepdims=True)
        cum_row = jnp.sum(gap_grad, axis=0, keepdims=True)
        cum_col = cum_col - jnp.broadcast_to(cum_row, (8, length)).T[:, 0:1]
        gram_grad = lower_grad * growth * beta_h
        score_grad = weights_grad * growth
        k_grad = dot3(gram_grad, k) + dot3(gram_grad, k, TN) + dot3(score_grad, q, TN)
        q_grad = dot3(score_grad, k)
        cum_grad = jnp.where(lanes == h, cum_col, cum_grad)
        beta_grad = jnp.where(lanes == heads + h, beta_col, beta_grad)

        q_grad = q_grad * DK ** (-0.5)
        q_grad = q_root * (q_grad - q_unit * jnp.sum(q_grad * q_unit, axis=-1, keepdims=True))
        conv_back(qs, q_grad * q_slope)
        k_grad = k_root * (k_grad - k_unit * jnp.sum(k_grad * k_unit, axis=-1, keepdims=True))
        conv_back(ks, k_grad * k_slope)
        conv_back(vs, value_grad * beta_h * v_slope)

    rate_grad = dot6(jnp.where(col_ids >= row_ids, 1.0, 0.0), cum_grad)
    bias_part = rate_grad * -jnp.exp(decay[0:1]) * sigmoid(shifted)
    raw_grad = jnp.where(lanes < heads, bias_part, beta_grad * beta * (1.0 - beta))
    low_ref[:, heads * 768 :] = raw_grad.astype(BF16)
    decay_grad_ref[0:1] += jnp.sum(jnp.where(lanes < heads, rate_grad * rate, 0.0), axis=0, keepdims=True)
    decay_grad_ref[1:2] += jnp.sum(jnp.where(lanes < heads, bias_part, 0.0), axis=0, keepdims=True)


def mixer_backward(proj, taps, decay, gain, inverse, solved, core, grad, heads, length):
    tokens, width = proj.shape
    seqs = tokens // length
    hv = heads * DV
    row = lambda cols: pl.BlockSpec((length, cols), lambda s: (s, 0))
    whole = lambda a: pl.BlockSpec(a.shape, lambda s: (0,) * a.ndim)
    return pl.pallas_call(
        functools.partial(mixer_backward_kernel, heads),
        grid=(seqs,),
        in_specs=[row(width), whole(taps), whole(decay), whole(gain),
                  pl.BlockSpec((None, heads, length, length), lambda s: (s, 0, 0, 0)), row(hv), row(hv), row(hv)],
        out_specs=[row(width), whole(taps), whole(gain), whole(decay)],
        out_shape=[
            jax.ShapeDtypeStruct((tokens, width), BF16),
            jax.ShapeDtypeStruct(taps.shape, F32),
            jax.ShapeDtypeStruct(gain.shape, F32),
            jax.ShapeDtypeStruct(decay.shape, F32),
        ],
        compiler_params=pltpu.CompilerParams(vmem_limit_bytes=56 << 20),
    )(proj, taps, decay, gain, inverse, solved, core, grad)


def _place(n_dp):
    me = lax.axis_index("dp")
    z = lax.axis_index("fsdp")
    core = lax.rem(me, 2)
    chip = me // 2
    return me, z, core, lax.rem(chip, 2), chip // 2

def ag_square(x, cid, chunks=4):
    rows, cols = x.shape
    r = rows // chunks
    def kernel(x_ref, o_ref, lsem, ssem, rsem, dssem, drsem, fs, fr):
        me, z, core, cx, cy = _place(8)
        dev = lambda dx, dy, c: 2*(2*lax.rem(cy+dy,2)+lax.rem(cx+dx,2))+c
        nx, ny, nd = dev(1,0,core), dev(0,1,core), dev(1,1,core)
        src = dev(1-core, core, core)
        tgt = dev(core, 1-core, core)
        sib = dev(0,0,1-core)
        bar = pltpu.get_barrier_semaphore()
        for d in (sib,nx,ny):
            pl.semaphore_signal(bar, inc=1, device_id=(d,z), device_id_type=MESH)
        pl.semaphore_wait(bar, 3)
        lc = pltpu.make_async_copy(x_ref, o_ref.at[me], lsem); lc.start()
        def rc(a, b, s, q, d):
            return pltpu.make_async_remote_copy(a, b, s, q, device_id=(d,z), device_id_type=MESH)
        own = []
        for c in range(chunks):
            sl = pl.ds(c*r, r)
            for i, d in ((0,nx),(1,ny)):
                cp = rc(x_ref.at[sl], o_ref.at[me,sl], ssem.at[i,c], rsem.at[i,c], d); cp.start(); own.append(cp)
        sibs=[]
        for c in range(chunks):
            sl = pl.ds(c*r, r)
            cp = rc(x_ref.at[sl], o_ref.at[me,sl], fs.at[0,c], fr.at[0,c], sib); cp.start(); sibs.append(cp)
        other = dev(core, 1-core, core)
        for c in range(chunks):
            sl = pl.ds(c*r, r)
            rc(x_ref.at[sl], o_ref.at[src,sl], ssem.at[core,c], rsem.at[core,c], sib).wait_recv()
            cp = rc(o_ref.at[src,sl], o_ref.at[src,sl], dssem.at[c], drsem.at[c], tgt); cp.start(); sibs.append((cp,))
            cp = rc(o_ref.at[src,sl], o_ref.at[src,sl], fs.at[1,c], fr.at[1,c], sib); cp.start(); sibs.append(cp)
            rc(x_ref.at[sl], o_ref.at[other,sl], ssem.at[1-core,c], rsem.at[1-core,c], sib).wait_recv()
            cp = rc(o_ref.at[other,sl], o_ref.at[other,sl], fs.at[2,c], fr.at[2,c], sib); cp.start(); sibs.append(cp)
        for c in range(chunks):
            sl = pl.ds(c*r, r)
            rc(x_ref.at[sl], o_ref.at[nd,sl], dssem.at[c], drsem.at[c], sib).wait_recv()
            cp = rc(o_ref.at[nd,sl], o_ref.at[nd,sl], fs.at[3,c], fr.at[3,c], sib); cp.start(); sibs.append(cp)
        for cp in own: cp.wait_send()
        for cp in sibs:
            if isinstance(cp, tuple): cp[0].wait_send()
            else: cp.wait()
        lc.wait()
    D=pltpu.SemaphoreType.DMA
    return pl.pallas_call(kernel, out_shape=jax.ShapeDtypeStruct((8,rows,cols),x.dtype),
        in_specs=[pl.BlockSpec(memory_space=pl.ANY)], out_specs=pl.BlockSpec(memory_space=pl.ANY),
        scratch_shapes=[D, D((2,chunks)), D((2,chunks)), D((chunks,)), D((chunks,)), D((4,chunks)), D((4,chunks))],
        compiler_params=pltpu.CompilerParams(collective_id=cid, has_side_effects=True))(x)

def rs_square(x, cid, chunks=4):
    _, rows, cols = x.shape
    r = rows // chunks
    def kernel(x_ref, o_ref, X, A, B, R, lsem, sa, ra, sb, rb):
        me, z, core, cx, cy = _place(8)
        dev = lambda dx, dy, c: 2*(2*lax.rem(cy+dy,2)+lax.rem(cx+dx,2))+c
        fdx, fdy = 1-core, core
        nf, ng = dev(fdx,fdy,core), dev(fdy,fdx,core)
        sib = dev(0,0,1-core)
        bar = pltpu.get_barrier_semaphore()
        for d in (sib,nf,ng):
            pl.semaphore_signal(bar, inc=1, device_id=(d,z), device_id_type=MESH)
        mine = [dev(1,1,core), ng, nf, me]
        s_f, s_g = dev(core,1-core,1-core), dev(1-core,core,1-core)
        theirs = [dev(1,1,1-core), s_g, s_f, sib]
        loads=[]
        for k in range(4):
            for c in range(chunks):
                sl=pl.ds(c*r,r)
                cp=pltpu.make_async_copy(x_ref.at[mine[k],sl], X.at[k,sl], lsem.at[k,c]); cp.start(); loads.append(cp)
        pl.semaphore_wait(bar, 3)
        def rc(a, b, s, q, d):
            return pltpu.make_async_remote_copy(a, b, s, q, device_id=(d,z), device_id_type=MESH)
        sends=[]; ga={}
        for k in range(4):
            for c in range(chunks):
                sl=pl.ds(c*r,r)
                cp=rc(x_ref.at[theirs[k],sl], A.at[k,sl], sa.at[k,c], ra.at[k,c], sib); cp.start(); sends.append(cp); ga[k,c]=cp
        def pair(k,c):
            sl=pl.ds(c*r,r)
            loads[k*chunks+c].wait(); ga[k,c].wait_recv()
            return X[k,sl].astype(F32)+A[k,sl].astype(F32)
        gb={}
        def ship(slot, c, d):
            sl=pl.ds(c*r,r)
            cp=rc(B.at[slot,sl], R.at[slot,sl], sb.at[slot,c], rb.at[slot,c], d); cp.start(); sends.append(cp); gb[slot,c]=cp
        for c in range(chunks):
            sl=pl.ds(c*r,r)
            B[0,sl]=pair(0,c).astype(BF16); ship(0,c,nf)
        for c in range(chunks):
            sl=pl.ds(c*r,r)
            B[2,sl]=pair(2,c).astype(BF16); ship(2,c,nf)
        for c in range(chunks):
            sl=pl.ds(c*r,r)
            v=pair(1,c)
            gb[0,c].wait_recv()
            B[1,sl]=(v+R[0,sl].astype(F32)).astype(BF16); ship(1,c,ng)
        for c in range(chunks):
            sl=pl.ds(c*r,r)
            v=pair(3,c)
            gb[2,c].wait_recv()
            o_ref[sl]=v+R[2,sl].astype(F32)
        for c in range(chunks):
            sl=pl.ds(c*r,r)
            gb[1,c].wait_recv()
            o_ref[sl]=o_ref[sl]+R[1,sl].astype(F32)
        for cp in sends: cp.wait_send()
    D=pltpu.SemaphoreType.DMA
    V=lambda n: pltpu.VMEM((n,rows,cols),x.dtype)
    return pl.pallas_call(kernel, out_shape=jax.ShapeDtypeStruct((rows,cols),F32),
        in_specs=[pl.BlockSpec(memory_space=pl.ANY)], out_specs=pl.BlockSpec(memory_space=pltpu.VMEM),
        scratch_shapes=[V(4),V(4),V(3),V(3), D((4,chunks)), D((4,chunks)), D((4,chunks)), D((3,chunks)), D((3,chunks))],
        compiler_params=pltpu.CompilerParams(collective_id=cid, has_side_effects=True, vmem_limit_bytes=40<<20))(x)

def gather_small(x, n_dp, n_z, cid):
    rows, cols = x.shape
    count = n_dp * n_z

    def kernel(x_ref, o_ref, lsem, ssem, rsem):
        flat = lax.axis_index("dp") * n_z + lax.axis_index("fsdp")
        bar = pltpu.get_barrier_semaphore()

        def device(o):
            other = lax.rem(flat + o, count)
            return (other // n_z, lax.rem(other, n_z))

        def copy(o):
            return pltpu.make_async_remote_copy(
                x_ref, o_ref.at[flat], ssem.at[o - 1], rsem.at[o - 1], device_id=device(o), device_id_type=MESH
            )

        def greet(o, _):
            pl.semaphore_signal(bar, inc=1, device_id=device(o), device_id_type=MESH)
            return 0

        def send(o, _):
            copy(o).start()
            return 0

        def wait(o, _):
            copy(o).wait()
            return 0

        lax.fori_loop(1, count, greet, 0)
        local = pltpu.make_async_copy(x_ref, o_ref.at[flat], lsem)
        local.start()
        pl.semaphore_wait(bar, count - 1)
        lax.fori_loop(1, count, send, 0)
        lax.fori_loop(1, count, wait, 0)
        local.wait()

    dma = pltpu.SemaphoreType.DMA
    return pl.pallas_call(
        kernel,
        out_shape=jax.ShapeDtypeStruct((count, rows, cols), x.dtype),
        in_specs=[pl.BlockSpec(memory_space=pl.ANY)],
        out_specs=pl.BlockSpec(memory_space=pl.ANY),
        scratch_shapes=[dma, dma((count - 1,)), dma((count - 1,))],
        compiler_params=pltpu.CompilerParams(collective_id=cid, has_side_effects=True),
    )(x)


def pack(parts, unit):
    flat = jnp.concatenate([part.reshape(-1) for part in parts])
    size = flat.shape[0]
    full = -(-size // (128 * unit)) * 128 * unit
    return jnp.pad(flat, (0, full - size)).reshape(-1, 128)


def dot(a, b, dims=NN, out=F32):
    return lax.dot_general(a, b, dims, preferred_element_type=F32).astype(out)


def local(
    n_dp,
    n_z,
    tokens,
    cotangent,
    group_ids,
    norm_first,
    input_weight,
    decay_weight,
    conv_weight,
    decay_scale,
    decay_bias,
    output_gain,
    output_weight,
    norm_second,
    upgate_weight,
    down_weight,
):
    count = n_dp * n_z
    rows, width = tokens.shape
    all_heads = decay_scale.shape[0]
    heads = all_heads // n_dp
    taps = conv_weight.shape[0]
    own_conv = conv_weight.shape[1]
    own_d = norm_first.shape[0]
    units = upgate_weight.shape[1] // (2 * n_dp)
    key, value = heads * DK, heads * DV
    cols = 2 * key + 2 * value + 128
    square = n_dp == 8
    here = lax.axis_index("dp")
    flat = here * n_z + lax.axis_index("fsdp")

    def spread(x, cid):
        if square:
            return ag_square(x, cid).reshape(n_dp * rows, width)
        return lax.all_gather(x, "dp", axis=0, tiled=True)

    def total(x, cid):
        if square:
            return rs_square(x.reshape(n_dp, rows, width), cid)
        return lax.psum_scatter(x, "dp", scatter_dimension=0, tiled=True).astype(F32)

    def by_dp(a, parts):
        return a.reshape(a.shape[0], n_dp, parts)

    pieces = (
        by_dp(input_weight[:, : n_dp * key], key),
        by_dp(input_weight[:, n_dp * key : 2 * n_dp * key], key),
        by_dp(input_weight[:, 2 * n_dp * key : 2 * n_dp * key + n_dp * value], value),
        by_dp(input_weight[:, 2 * n_dp * key + n_dp * value :], value),
        by_dp(decay_weight[:, :all_heads], heads),
        by_dp(decay_weight[:, all_heads:], heads),
        jnp.zeros((own_d, n_dp, 128 - 2 * heads), BF16),
    )
    in_mine = jnp.concatenate(pieces, axis=2).transpose(1, 0, 2)
    gate_mine = by_dp(upgate_weight[:, : n_dp * units], units).transpose(1, 0, 2)
    up_mine = by_dp(upgate_weight[:, n_dp * units :], units).transpose(1, 0, 2)

    def whole_rows(a):
        a = lax.all_to_all(a, "dp", 0, 0, tiled=True)
        a = lax.all_gather(a[:, None], "fsdp", axis=1, tiled=True)
        return a.reshape(width, a.shape[-1])

    in_full = whole_rows(in_mine)
    out_full = lax.all_gather(output_weight, "fsdp", axis=0, tiled=True)
    gate_full = whole_rows(gate_mine)
    up_full = whole_rows(up_mine)
    down_full = lax.all_gather(down_weight, "fsdp", axis=0, tiled=True)

    small = gather_small(
        pack((conv_weight, norm_first, norm_second, group_ids.astype(BF16)), 16), n_dp, n_z, 1
    ).reshape(count, -1)
    conv_size = taps * own_conv
    conv_full = small[:, :conv_size].reshape(count, taps, own_conv).transpose(1, 0, 2).reshape(taps, -1)
    first_full = small[:, conv_size : conv_size + own_d].reshape(1, width).astype(F32)
    second_full = small[:, conv_size + own_d : conv_size + 2 * own_d].reshape(1, width).astype(F32)
    every_id = small[:, conv_size + 2 * own_d].astype(jnp.int32)
    scale = 1.0 / jnp.sum((every_id == group_ids[0]).astype(F32))

    def conv_columns(start, size):
        return lax.dynamic_slice_in_dim(conv_full, start + here * size, size, axis=1)

    conv_mine = jnp.concatenate(
        [conv_columns(0, key), conv_columns(n_dp * key, key), conv_columns(2 * n_dp * key, value)], axis=1
    ).astype(F32)
    decay_mine = jnp.pad(
        jnp.stack(
            [
                lax.dynamic_slice_in_dim(decay_scale, here * heads, heads),
                lax.dynamic_slice_in_dim(decay_bias, here * heads, heads),
            ]
        ),
        ((0, 0), (0, 128 - heads)),
    )
    gain = output_gain[None, :]

    inputs = tokens.astype(F32)
    first_root = lax.rsqrt(jnp.mean(inputs * inputs, axis=-1, keepdims=True) + EPSILON)
    normed_all = spread((inputs * first_root * first_full).astype(BF16), 2)
    seed = cotangent.astype(F32) * scale
    seed_all = spread(seed.astype(BF16), 3)
    projected = dot(normed_all, in_full)
    mixed, inverse, solved, core = mixer_forward(projected, conv_mine, decay_mine, gain, heads, rows)
    middle = inputs + total(dot(mixed, out_full, out=BF16), 4)
    second_root = lax.rsqrt(jnp.mean(middle * middle, axis=-1, keepdims=True) + EPSILON)
    second_all = spread((middle * second_root * second_full).astype(BF16), 5)
    gate_part = dot(second_all, gate_full)
    up_part = dot(second_all, up_full)
    gate_sig = jax.nn.sigmoid(gate_part)
    hidden = (gate_part * gate_sig * up_part).astype(BF16)
    hidden_grad = dot(seed_all, down_full, NT)
    gate_low = (hidden_grad * up_part * gate_sig * (1.0 + gate_part * (1.0 - gate_sig))).astype(BF16)
    up_low = (hidden_grad * gate_part * gate_sig).astype(BF16)

    back_two = (dot(gate_low, gate_full, NT) + dot(up_low, up_full, NT)).astype(BF16)
    normed_two_grad = total(back_two, 6)
    result = middle + total(dot(hidden, down_full, out=BF16), 7)

    def norm_back(v, root, gain_row, grad):
        hat = v * root
        scaled = grad * gain_row
        gain_grad = jnp.sum(grad * hat, axis=0)
        return root * (scaled - hat * jnp.mean(scaled * hat, axis=-1, keepdims=True)), gain_grad

    middle_part, second_grad = norm_back(middle, second_root, second_full, normed_two_grad)
    middle_grad = seed + middle_part
    middle_all = spread(middle_grad.astype(BF16), 8)
    mixed_grad = dot(middle_all, out_full, NT)
    projected_low, conv_grad, gain_grad, decay_grad = mixer_backward(
        projected, conv_mine, decay_mine, gain, inverse, solved, core, mixed_grad, heads, rows
    )
    normed_one_grad = total(dot(projected_low, in_full, NT, out=BF16), 9)
    input_part, first_grad = norm_back(inputs, first_root, first_full, normed_one_grad)
    tokens_grad = middle_grad + input_part

    def owned_rows(a):
        return lax.psum_scatter(a, "fsdp", scatter_dimension=0, tiled=True)

    def owned_parts(a):
        a = a.reshape(n_dp, n_z, own_d, a.shape[-1]).transpose(1, 0, 2, 3)
        a = lax.psum_scatter(a.reshape(width, -1), "fsdp", scatter_dimension=0, tiled=True)
        a = lax.all_to_all(a.reshape(n_dp, own_d, -1), "dp", 0, 0, tiled=True)
        return a.transpose(1, 0, 2).astype(F32)

    down_total = owned_rows(dot(hidden, seed_all, TN, out=BF16)).astype(F32)
    gate_total = owned_parts(dot(second_all, gate_low, TN, out=BF16))
    up_total = owned_parts(dot(second_all, up_low, TN, out=BF16))
    upgate_total = jnp.concatenate([gate_total.reshape(own_d, -1), up_total.reshape(own_d, -1)], axis=1)
    output_total = owned_rows(dot(mixed, middle_all, TN, out=BF16)).astype(F32)
    in_total = owned_parts(dot(normed_all, projected_low, TN, out=BF16))
    bounds = (0, key, 2 * key, 2 * key + value, 2 * key + 2 * value)
    input_total = jnp.concatenate(
        [in_total[:, :, a:b].reshape(own_d, -1) for a, b in zip(bounds[:-1], bounds[1:])], axis=1
    )
    start = bounds[-1]
    decay_total = jnp.concatenate(
        [
            in_total[:, :, start : start + heads].reshape(own_d, -1),
            in_total[:, :, start + heads : start + 2 * heads].reshape(own_d, -1),
        ],
        axis=1,
    )

    sizes = (first_grad.size, second_grad.size, gain_grad.size, conv_grad.size, 2 * heads)
    shared = gather_small(
        pack((first_grad, second_grad, gain_grad, conv_grad, decay_grad[:, :heads]), 8), n_dp, n_z, 10
    ).reshape(count, -1)
    edges = [0]
    for size in sizes:
        edges.append(edges[-1] + size)
    summed = jnp.sum(shared[:, : edges[3]], axis=0)
    first_total = lax.dynamic_slice_in_dim(summed, flat * own_d, own_d)
    second_total = lax.dynamic_slice_in_dim(summed, edges[1] + flat * own_d, own_d)
    gain_total = summed[edges[2] : edges[3]]
    by_plane = jnp.sum(shared[:, edges[3] : edges[5]].reshape(n_dp, n_z, -1), axis=1)
    conv_all = by_plane[:, : sizes[3]].reshape(n_dp, taps, 2 * key + value)
    conv_row = jnp.concatenate(
        [
            conv_all[:, :, a:b].transpose(1, 0, 2).reshape(taps, -1)
            for a, b in ((0, key), (key, 2 * key), (2 * key, 2 * key + value))
        ],
        axis=1,
    )
    conv_total = lax.dynamic_slice_in_dim(conv_row, flat * own_conv, own_conv, axis=1)
    scale_bias = by_plane[:, sizes[3] :].reshape(n_dp, 2, heads)
    scale_total = scale_bias[:, 0].reshape(-1)
    bias_total = scale_bias[:, 1].reshape(-1)
    return (
        result,
        tokens_grad,
        first_total,
        input_total,
        decay_total,
        conv_total,
        scale_total,
        bias_total,
        gain_total,
        output_total,
        second_total,
        upgate_total,
        down_total,
    )


def solution(mesh):
    both = ("dp", "fsdp")
    rows, vector = P(both, None), P(both)
    return jax.shard_map(
        functools.partial(local, mesh.shape["dp"], mesh.shape["fsdp"]),
        mesh=mesh,
        in_specs=(
            rows, rows, vector, vector, rows, rows, P(None, both), P(), P(), P(), rows, vector, rows, rows,
        ),
        out_specs=(
            rows, rows, vector, rows, rows, P(None, both), P(), P(), P(), rows, vector, rows, rows,
        ),
        check_vma=False,
    )
```

```python
import functools

import jax
import jax.numpy as jnp
from jax import lax
from jax.experimental import pallas as pl
from jax.experimental.pallas import tpu as pltpu
from jax.sharding import PartitionSpec as P

MESH = pl.DeviceIdType.MESH
F32 = jnp.float32
BF16 = jnp.bfloat16
EPSILON = 1e-06
DK = 128
DV = 256
BASE = 8
NN = (((1,), (0,)), ((), ()))
NT = (((1,), (1,)), ((), ()))
TN = (((0,), (0,)), ((), ()))


def dot1(a, b, dims=NN):
    return lax.dot_general(a.astype(BF16), b.astype(BF16), dims, preferred_element_type=F32)


def halves(a):
    if a.dtype == BF16:
        return (a,)
    high = a.astype(BF16)
    return (high, (a - high.astype(F32)).astype(BF16))


def dot3(a, b, dims=NN):
    a, b = halves(a), halves(b)
    total = lax.dot_general(a[0], b[0], dims, preferred_element_type=F32)
    if len(a) > 1:
        total = total + lax.dot_general(a[1], b[0], dims, preferred_element_type=F32)
    if len(b) > 1:
        total = total + lax.dot_general(a[0], b[1], dims, preferred_element_type=F32)
    return total


def dot6(a, b, dims=NN):
    return lax.dot_general(a, b, dims, precision=lax.Precision.HIGHEST, preferred_element_type=F32)


def shift_down(v, n, rows):
    if n == 0:
        return v
    return jnp.where(rows >= n, pltpu.roll(v, n, 0), 0.0)


def shift_up(v, n, rows):
    if n == 0:
        return v
    length = v.shape[0]
    return jnp.where(rows < length - n, pltpu.roll(v, length - n, 0), 0.0)


def conv(c, taps, rows):
    count = taps.shape[0]
    total = c * taps[count - 1 : count]
    for j in range(count - 1):
        total = total + shift_down(c, count - 1 - j, rows) * taps[j : j + 1]
    return total


def sigmoid(v):
    return 1.0 / (1.0 + jnp.exp(-v))


def softplus(v):
    return jnp.maximum(v, 0.0) + jnp.log1p(jnp.exp(-jnp.abs(v)))


def unit_inverses(lowers, row_ids, col_ids):
    length = lowers[0].shape[0]
    size = BASE
    same = row_ids // size == col_ids // size
    pick = jnp.where(col_ids[:, :128] == lax.rem(row_ids[:, :128], size), 1.0, 0.0).astype(BF16)
    lanes = lax.broadcasted_iota(jnp.int32, (length // size, size, 128), 2)
    places = lax.broadcasted_iota(jnp.int32, (length // size, size, 128), 1)
    compact = [dot3(jnp.where(same, lower, 0.0), pick).reshape(length // size, size, 128) for lower in lowers]
    solved = [jnp.where(lanes == places, 1.0, 0.0) for _ in lowers]
    for j in range(size - 1):
        solved = [x - a[:, :, j : j + 1] * x[:, j : j + 1, :] for a, x in zip(compact, solved)]
    inverses = [jnp.where(same, dot3(x.reshape(length, 128), pick, NT), 0.0) for x in solved]
    while size < length:
        wide = 2 * size
        off = (row_ids // wide == col_ids // wide) & (row_ids // size != col_ids // size)
        inner = [dot3(jnp.where(off, lower, 0.0), inverse) for lower, inverse in zip(lowers, inverses)]
        inverses = [inverse - dot3(inverse, x) for inverse, x in zip(inverses, inner)]
        size = wide
    return inverses


def common(proj, decay, heads, length):
    rows = lax.broadcasted_iota(jnp.int32, (length, 1), 0)
    row_ids = lax.broadcasted_iota(jnp.int32, (length, length), 0)
    col_ids = lax.broadcasted_iota(jnp.int32, (length, length), 1)
    raw = proj[:, heads * 768 :]
    lanes = lax.broadcasted_iota(jnp.int32, raw.shape, 1)
    shifted = raw + decay[1:2]
    rate = jnp.where(lanes < heads, -jnp.exp(decay[0:1]) * softplus(shifted), 0.0)
    beta = sigmoid(raw)
    cumulated = dot6(jnp.where(row_ids >= col_ids, 1.0, 0.0), rate)
    return rows, row_ids, col_ids, raw, lanes, shifted, rate, beta, cumulated, cumulated.T


def head_parts(h, heads):
    key = slice(h * DK, (h + 1) * DK)
    keyk = slice((heads + h) * DK, (heads + h + 1) * DK)
    val = slice(heads * DV + h * DV, heads * DV + (h + 1) * DV)
    gat = slice(2 * heads * DV + h * DV, 2 * heads * DV + (h + 1) * DV)
    return key, keyk, val, gat


def mixer_forward_kernel(heads, proj_ref, taps_ref, decay_ref, gain_ref, mixed_ref, inv_ref, solved_ref, core_ref):
    length = proj_ref.shape[0]
    decay = decay_ref[...]
    gain = gain_ref[...]
    rows, row_ids, col_ids, raw, lanes, shifted, rate, beta, cumulated, cum_t = common(
        proj_ref[...], decay, heads, length
    )
    def active(cols):
        y = conv(proj_ref[:, cols], taps_ref[:, cols], rows)
        return y * sigmoid(y)

    parts = [head_parts(h, heads) for h in range(heads)]
    queries, keys, values, growths, betas, lowers = [], [], [], [], [], []
    for h, (qs, ks, vs, gs) in enumerate(parts):
        k = active(ks)
        k = (k * lax.rsqrt(jnp.sum(k * k, axis=-1, keepdims=True) + EPSILON)).astype(BF16)
        beta_h = beta[:, heads + h : heads + h + 1]
        gap = cumulated[:, h : h + 1] - cum_t[h : h + 1, :]
        growth = jnp.where(row_ids >= col_ids, jnp.exp(jnp.where(row_ids >= col_ids, gap, 0.0)), 0.0)
        keys.append(k)
        growths.append(growth)
        betas.append(beta_h)
        lowers.append(jnp.where(row_ids > col_ids, growth * dot1(k, k, NT) * beta_h, 0.0))
    inverses = unit_inverses(lowers, row_ids, col_ids)
    for h, (qs, ks, vs, gs) in enumerate(parts):
        q = active(qs)
        q = (q * lax.rsqrt(jnp.sum(q * q, axis=-1, keepdims=True) + EPSILON) * DK ** (-0.5)).astype(BF16)
        v = active(vs).astype(BF16)
        inv_ref[h] = inverses[h]
        solved = dot3(inverses[h], betas[h] * v.astype(F32))
        core = dot3(growths[h] * dot1(q, keys[h], NT), solved)
        solved_ref[:, h * DV : (h + 1) * DV] = solved
        core_ref[:, h * DV : (h + 1) * DV] = core
        gate = proj_ref[:, gs]
        normed = core * lax.rsqrt(jnp.mean(core * core, axis=-1, keepdims=True) + EPSILON) * gain
        mixed_ref[:, h * DV : (h + 1) * DV] = (normed * (gate * sigmoid(gate))).astype(BF16)


def mixer_forward(proj, taps, decay, gain, heads, length):
    tokens, width = proj.shape
    seqs = tokens // length
    hv = heads * DV
    row = lambda cols: pl.BlockSpec((length, cols), lambda s: (s, 0))
    whole = lambda a: pl.BlockSpec(a.shape, lambda s: (0,) * a.ndim)
    return pl.pallas_call(
        functools.partial(mixer_forward_kernel, heads),
        grid=(seqs,),
        in_specs=[row(width), whole(taps), whole(decay), whole(gain)],
        out_specs=[row(hv), pl.BlockSpec((None, heads, length, length), lambda s: (s, 0, 0, 0)), row(hv), row(hv)],
        out_shape=[
            jax.ShapeDtypeStruct((tokens, hv), BF16),
            jax.ShapeDtypeStruct((seqs, heads, length, length), F32),
            jax.ShapeDtypeStruct((tokens, hv), F32),
            jax.ShapeDtypeStruct((tokens, hv), F32),
        ],
        cost_estimate=busy(55), compiler_params=pltpu.CompilerParams(vmem_limit_bytes=48 << 20),
    )(proj, taps, decay, gain)


def mixer_backward_kernel(
    heads, proj_ref, taps_ref, decay_ref, gain_ref, inv_ref, solved_ref, core_ref, grad_ref,
    low_ref, conv_ref, gain_grad_ref, decay_grad_ref,
):
    length = proj_ref.shape[0]
    count = taps_ref.shape[0]
    decay = decay_ref[...]
    gain = gain_ref[...]
    rows, row_ids, col_ids, raw, lanes, shifted, rate, beta, cumulated, cum_t = common(
        proj_ref[...], decay, heads, length
    )
    within = row_ids >= col_ids
    strict = row_ids > col_ids

    @pl.when(pl.program_id(0) == 0)
    def _():
        conv_ref[...] = jnp.zeros_like(conv_ref)
        gain_grad_ref[...] = jnp.zeros_like(gain_grad_ref)
        decay_grad_ref[...] = jnp.zeros_like(decay_grad_ref)

    cum_grad = jnp.zeros(raw.shape, F32)
    beta_grad = jnp.zeros(raw.shape, F32)
    for h in range(heads):
        qs, ks, vs, gs = head_parts(h, heads)
        hs = slice(h * DV, (h + 1) * DV)

        def active(cols):
            y = conv(proj_ref[:, cols], taps_ref[:, cols], rows)
            s = sigmoid(y)
            return y * s, s * (1.0 + y * (1.0 - s))

        def conv_back(cols, grad):
            c = proj_ref[:, cols]
            total = grad * taps_ref[count - 1 : count, cols]
            conv_ref[count - 1 : count, cols] += jnp.sum(grad * c, axis=0, keepdims=True)
            for j in range(count - 1):
                n = count - 1 - j
                total = total + shift_up(grad, n, rows) * taps_ref[j : j + 1, cols]
                conv_ref[j : j + 1, cols] += jnp.sum(grad * shift_down(c, n, rows), axis=0, keepdims=True)
            low_ref[:, cols] = total.astype(BF16)

        core = core_ref[:, hs]
        gate = proj_ref[:, gs]
        gate_sig = sigmoid(gate)
        grad = grad_ref[:, hs]
        root = lax.rsqrt(jnp.mean(core * core, axis=-1, keepdims=True) + EPSILON)
        normed = core * root
        silu_gate = gate * gate_sig
        gain_grad_ref[...] += jnp.sum(grad * normed * silu_gate, axis=0, keepdims=True)
        low_ref[:, gs] = (grad * normed * gain * gate_sig * (1.0 + gate * (1.0 - gate_sig))).astype(BF16)
        normed_grad = grad * gain * silu_gate
        core_grad = root * (normed_grad - normed * jnp.mean(normed_grad * normed, axis=-1, keepdims=True))

        q_act, q_slope = active(qs)
        q_root = lax.rsqrt(jnp.sum(q_act * q_act, axis=-1, keepdims=True) + EPSILON)
        q_unit = q_act * q_root
        q = (q_unit * DK ** (-0.5)).astype(BF16)
        k_act, k_slope = active(ks)
        k_root = lax.rsqrt(jnp.sum(k_act * k_act, axis=-1, keepdims=True) + EPSILON)
        k_unit = k_act * k_root
        k = k_unit.astype(BF16)
        v_act, v_slope = active(vs)
        v = v_act.astype(BF16).astype(F32)
        beta_h = beta[:, heads + h : heads + h + 1]
        gap = cumulated[:, h : h + 1] - cum_t[h : h + 1, :]
        growth = jnp.where(within, jnp.exp(jnp.where(within, gap, 0.0)), 0.0)
        decayed_gram = jnp.where(strict, growth * dot1(k, k, NT), 0.0)
        weights = growth * dot1(q, k, NT)
        inverse = inv_ref[h]
        solved = solved_ref[:, hs]
        solved_grad = dot3(weights, core_grad, TN)
        weights_grad = dot3(core_grad, solved, NT)
        value_grad = dot3(inverse, solved_grad, TN)
        lower_grad = jnp.where(strict, -dot3(value_grad, solved, NT), 0.0)
        gap_part = lower_grad * decayed_gram
        beta_col = jnp.sum(gap_part, axis=-1, keepdims=True) + jnp.sum(value_grad * v, axis=-1, keepdims=True)
        gap_grad = gap_part * beta_h + weights_grad * weights
        cum_col = jnp.sum(gap_grad, axis=-1, keepdims=True)
        cum_row = jnp.sum(gap_grad, axis=0, keepdims=True)
        cum_col = cum_col - jnp.broadcast_to(cum_row, (8, length)).T[:, 0:1]
        gram_grad = lower_grad * growth * beta_h
        score_grad = weights_grad * growth
        k_grad = dot3(gram_grad, k) + dot3(gram_grad, k, TN) + dot3(score_grad, q, TN)
        q_grad = dot3(score_grad, k)
        cum_grad = jnp.where(lanes == h, cum_col, cum_grad)
        beta_grad = jnp.where(lanes == heads + h, beta_col, beta_grad)

        q_grad = q_grad * DK ** (-0.5)
        q_grad = q_root * (q_grad - q_unit * jnp.sum(q_grad * q_unit, axis=-1, keepdims=True))
        conv_back(qs, q_grad * q_slope)
        k_grad = k_root * (k_grad - k_unit * jnp.sum(k_grad * k_unit, axis=-1, keepdims=True))
        conv_back(ks, k_grad * k_slope)
        conv_back(vs, value_grad * beta_h * v_slope)

    rate_grad = dot6(jnp.where(col_ids >= row_ids, 1.0, 0.0), cum_grad)
    bias_part = rate_grad * -jnp.exp(decay[0:1]) * sigmoid(shifted)
    raw_grad = jnp.where(lanes < heads, bias_part, beta_grad * beta * (1.0 - beta))
    low_ref[:, heads * 768 :] = raw_grad.astype(BF16)
    decay_grad_ref[0:1] += jnp.sum(jnp.where(lanes < heads, rate_grad * rate, 0.0), axis=0, keepdims=True)
    decay_grad_ref[1:2] += jnp.sum(jnp.where(lanes < heads, bias_part, 0.0), axis=0, keepdims=True)


def mixer_backward(proj, taps, decay, gain, inverse, solved, core, grad, heads, length):
    tokens, width = proj.shape
    seqs = tokens // length
    hv = heads * DV
    row = lambda cols: pl.BlockSpec((length, cols), lambda s: (s, 0))
    whole = lambda a: pl.BlockSpec(a.shape, lambda s: (0,) * a.ndim)
    return pl.pallas_call(
        functools.partial(mixer_backward_kernel, heads),
        grid=(seqs,),
        in_specs=[row(width), whole(taps), whole(decay), whole(gain),
                  pl.BlockSpec((None, heads, length, length), lambda s: (s, 0, 0, 0)), row(hv), row(hv), row(hv)],
        out_specs=[row(width), whole(taps), whole(gain), whole(decay)],
        out_shape=[
            jax.ShapeDtypeStruct((tokens, width), BF16),
            jax.ShapeDtypeStruct(taps.shape, F32),
            jax.ShapeDtypeStruct(gain.shape, F32),
            jax.ShapeDtypeStruct(decay.shape, F32),
        ],
        cost_estimate=busy(50), compiler_params=pltpu.CompilerParams(vmem_limit_bytes=56 << 20),
    )(proj, taps, decay, gain, inverse, solved, core, grad)


def busy(us):
    return pl.CostEstimate(flops=us * 1_000_000_000, bytes_accessed=0, transcendentals=0)


def _place(n_dp):
    me = lax.axis_index("dp")
    z = lax.axis_index("fsdp")
    core = lax.rem(me, 2)
    chip = me // 2
    return me, z, core, lax.rem(chip, 2), chip // 2

def ag_square(x, cid, chunks=4):
    rows, cols = x.shape
    r = rows // chunks
    def kernel(x_ref, o_ref, lsem, ssem, rsem, dssem, drsem, fs, fr):
        me, z, core, cx, cy = _place(8)
        dev = lambda dx, dy, c: 2*(2*lax.rem(cy+dy,2)+lax.rem(cx+dx,2))+c
        nx, ny, nd = dev(1,0,core), dev(0,1,core), dev(1,1,core)
        src = dev(1-core, core, core)
        tgt = dev(core, 1-core, core)
        sib = dev(0,0,1-core)
        bar = pltpu.get_barrier_semaphore()
        for d in (sib,nx,ny):
            pl.semaphore_signal(bar, inc=1, device_id=(d,z), device_id_type=MESH)
        pl.semaphore_wait(bar, 3)
        lc = pltpu.make_async_copy(x_ref, o_ref.at[me], lsem); lc.start()
        def rc(a, b, s, q, d):
            return pltpu.make_async_remote_copy(a, b, s, q, device_id=(d,z), device_id_type=MESH)
        own = []
        for c in range(chunks):
            sl = pl.ds(c*r, r)
            for i, d in ((0,nx),(1,ny)):
                cp = rc(x_ref.at[sl], o_ref.at[me,sl], ssem.at[i,c], rsem.at[i,c], d); cp.start(); own.append(cp)
        sibs=[]
        for c in range(chunks):
            sl = pl.ds(c*r, r)
            cp = rc(x_ref.at[sl], o_ref.at[me,sl], fs.at[0,c], fr.at[0,c], sib); cp.start(); sibs.append(cp)
        other = dev(core, 1-core, core)
        for c in range(chunks):
            sl = pl.ds(c*r, r)
            rc(x_ref.at[sl], o_ref.at[src,sl], ssem.at[core,c], rsem.at[core,c], sib).wait_recv()
            cp = rc(o_ref.at[src,sl], o_ref.at[src,sl], dssem.at[c], drsem.at[c], tgt); cp.start(); sibs.append((cp,))
            cp = rc(o_ref.at[src,sl], o_ref.at[src,sl], fs.at[1,c], fr.at[1,c], sib); cp.start(); sibs.append(cp)
            rc(x_ref.at[sl], o_ref.at[other,sl], ssem.at[1-core,c], rsem.at[1-core,c], sib).wait_recv()
            cp = rc(o_ref.at[other,sl], o_ref.at[other,sl], fs.at[2,c], fr.at[2,c], sib); cp.start(); sibs.append(cp)
        for c in range(chunks):
            sl = pl.ds(c*r, r)
            rc(x_ref.at[sl], o_ref.at[nd,sl], dssem.at[c], drsem.at[c], sib).wait_recv()
            cp = rc(o_ref.at[nd,sl], o_ref.at[nd,sl], fs.at[3,c], fr.at[3,c], sib); cp.start(); sibs.append(cp)
        for cp in own: cp.wait_send()
        for cp in sibs:
            if isinstance(cp, tuple): cp[0].wait_send()
            else: cp.wait()
        lc.wait()
    D=pltpu.SemaphoreType.DMA
    return pl.pallas_call(kernel, out_shape=jax.ShapeDtypeStruct((8,rows,cols),x.dtype),
        in_specs=[pl.BlockSpec(memory_space=pl.ANY)], out_specs=pl.BlockSpec(memory_space=pl.ANY),
        scratch_shapes=[D, D((2,chunks)), D((2,chunks)), D((chunks,)), D((chunks,)), D((4,chunks)), D((4,chunks))],
        cost_estimate=busy(40), compiler_params=pltpu.CompilerParams(collective_id=cid, has_side_effects=True))(x)

def rs_square(x, cid, chunks=4):
    _, rows, cols = x.shape
    r = rows // chunks
    def kernel(x_ref, o_ref, X, A, B, R, lsem, sa, ra, sb, rb):
        me, z, core, cx, cy = _place(8)
        dev = lambda dx, dy, c: 2*(2*lax.rem(cy+dy,2)+lax.rem(cx+dx,2))+c
        fdx, fdy = 1-core, core
        nf, ng = dev(fdx,fdy,core), dev(fdy,fdx,core)
        sib = dev(0,0,1-core)
        bar = pltpu.get_barrier_semaphore()
        for d in (sib,nf,ng):
            pl.semaphore_signal(bar, inc=1, device_id=(d,z), device_id_type=MESH)
        mine = [dev(1,1,core), ng, nf, me]
        s_f, s_g = dev(core,1-core,1-core), dev(1-core,core,1-core)
        theirs = [dev(1,1,1-core), s_g, s_f, sib]
        loads=[]
        for k in range(4):
            for c in range(chunks):
                sl=pl.ds(c*r,r)
                cp=pltpu.make_async_copy(x_ref.at[mine[k],sl], X.at[k,sl], lsem.at[k,c]); cp.start(); loads.append(cp)
        pl.semaphore_wait(bar, 3)
        def rc(a, b, s, q, d):
            return pltpu.make_async_remote_copy(a, b, s, q, device_id=(d,z), device_id_type=MESH)
        sends=[]; ga={}
        for k in range(4):
            for c in range(chunks):
                sl=pl.ds(c*r,r)
                cp=rc(x_ref.at[theirs[k],sl], A.at[k,sl], sa.at[k,c], ra.at[k,c], sib); cp.start(); sends.append(cp); ga[k,c]=cp
        def pair(k,c):
            sl=pl.ds(c*r,r)
            loads[k*chunks+c].wait(); ga[k,c].wait_recv()
            return X[k,sl].astype(F32)+A[k,sl].astype(F32)
        gb={}
        def ship(slot, c, d):
            sl=pl.ds(c*r,r)
            cp=rc(B.at[slot,sl], R.at[slot,sl], sb.at[slot,c], rb.at[slot,c], d); cp.start(); sends.append(cp); gb[slot,c]=cp
        for c in range(chunks):
            sl=pl.ds(c*r,r)
            B[0,sl]=pair(0,c).astype(BF16); ship(0,c,nf)
        for c in range(chunks):
            sl=pl.ds(c*r,r)
            B[2,sl]=pair(2,c).astype(BF16); ship(2,c,nf)
        for c in range(chunks):
            sl=pl.ds(c*r,r)
            v=pair(1,c)
            gb[0,c].wait_recv()
            B[1,sl]=(v+R[0,sl].astype(F32)).astype(BF16); ship(1,c,ng)
        for c in range(chunks):
            sl=pl.ds(c*r,r)
            v=pair(3,c)
            gb[2,c].wait_recv()
            o_ref[sl]=v+R[2,sl].astype(F32)
        for c in range(chunks):
            sl=pl.ds(c*r,r)
            gb[1,c].wait_recv()
            o_ref[sl]=o_ref[sl]+R[1,sl].astype(F32)
        for cp in sends: cp.wait_send()
    D=pltpu.SemaphoreType.DMA
    V=lambda n: pltpu.VMEM((n,rows,cols),x.dtype)
    return pl.pallas_call(kernel, out_shape=jax.ShapeDtypeStruct((rows,cols),F32),
        in_specs=[pl.BlockSpec(memory_space=pl.ANY)], out_specs=pl.BlockSpec(memory_space=pltpu.VMEM),
        scratch_shapes=[V(4),V(4),V(3),V(3), D((4,chunks)), D((4,chunks)), D((4,chunks)), D((3,chunks)), D((3,chunks))],
        cost_estimate=busy(40), compiler_params=pltpu.CompilerParams(collective_id=cid, has_side_effects=True, vmem_limit_bytes=40<<20))(x)

def begin(weight, decays, ups, tokens, cotangent, small, bounds, n_z, cid):
    own = weight.shape[0]
    cols = bounds[-1] + 128
    units = ups.shape[2]
    rows, width = tokens.shape
    count = 8 * n_z
    chunks = 2
    part = rows // chunks

    def kernel(
        w_ref, dec_ref, u_ref, t_ref, c_ref, small_ref, w_out, u_out, n_out, c_out, small_out,
        toks, lsem, a_send, a_recv, g_send, g_recv, up_send, up_recv, down_send, down_recv,
        small_send, small_recv, x_send, x_recv, d_send, d_recv, f_send, f_recv,
    ):
        me, z, core, cx, cy = _place(8)
        flat = me * n_z + z
        bar = pltpu.get_barrier_semaphore()

        def dev(dx, dy, c):
            return 2 * (2 * lax.rem(cy + dy, 2) + lax.rem(cx + dx, 2)) + c

        sib = dev(0, 0, 1 - core)

        def partner(o):
            return dev(o // 4, lax.rem(o // 2, 2), lax.rem(core + o, 2))

        def anyone(o):
            other = lax.rem(flat + o, count)
            return (other // n_z, lax.rem(other, n_z))

        def remote(src, dst, send, recv, device):
            return pltpu.make_async_remote_copy(src, dst, send, recv, device_id=device, device_id_type=MESH)

        def loop(first, last, body):
            def step(o, _):
                body(o)
                return 0

            lax.fori_loop(first, last, step, 0)

        def sections(q):
            for first, last in zip(bounds[:-1], bounds[1:]):
                size = last - first
                at = pl.multiple_of(8 * first + q * size, 128)
                yield w_ref.at[:, pl.ds(at, size)], w_out.at[me, z, :, pl.ds(first, size)]
            yield dec_ref.at[q], w_out.at[me, z, :, pl.ds(bounds[-1], 128)]

        def send_piece(o):
            q = partner(o)
            for src, dst in sections(q):
                remote(src, dst, a_send.at[o - 1], a_recv.at[o - 1], (q, z)).start()

        def landed(o):
            at = w_out.at[partner(o), z]
            return remote(at, at, a_send.at[o - 1], a_recv.at[o - 1], (sib, z))

        def up(t, o):
            at = w_out.at[partner(o), z - t]
            return remote(at, at, up_send.at[t, o], up_recv.at[t, o], (me, z + 1))

        def down(t, o):
            at = w_out.at[partner(o), z + t]
            return remote(at, at, down_send.at[t, o], down_recv.at[t, o], (me, z - 1))

        def pass_on(t, o):
            if t > 0:

                @pl.when(z >= t)
                def _():
                    at = w_out.at[partner(o), z - t]
                    remote(at, at, up_send.at[t - 1, o], up_recv.at[t - 1, o], (sib, z)).wait_recv()

                @pl.when(z + t < n_z)
                def _():
                    at = w_out.at[partner(o), z + t]
                    remote(at, at, down_send.at[t - 1, o], down_recv.at[t - 1, o], (sib, z)).wait_recv()

            if t < n_z - 1:

                @pl.when((z >= t) & (z < n_z - 1))
                def _():
                    up(t, o).start()

                @pl.when((z + t < n_z) & (z > 0))
                def _():
                    down(t, o).start()

        def sent(t, o):
            @pl.when((z >= t) & (z < n_z - 1))
            def _():
                up(t, o).wait_send()

            @pl.when((z + t < n_z) & (z > 0))
            def _():
                down(t, o).wait_send()

        def unit_piece(o):
            q = partner(o)
            return remote(u_ref.at[q], u_out.at[me], g_send.at[o - 1], g_recv.at[o - 1], (q, z))

        def tiny(o):
            return remote(small_ref, small_out.at[flat], small_send.at[o - 1], small_recv.at[o - 1], anyone(o))

        near = (dev(1, 0, core), dev(0, 1, core))
        source, other, across = dev(1 - core, core, core), dev(core, 1 - core, core), dev(1, 1, core)

        def gather(i, ref, out):
            def at(q, c):
                return out.at[q, pl.ds(c * part, part)]

            def mine(c):
                return ref.at[pl.ds(c * part, part)]

            def first(k, c):
                return remote(mine(c), at(me, c), x_send.at[i, k, c], x_recv.at[i, k, c], (near[k], z))

            def twin(k, q, c):
                src = mine(c) if k == 0 else at(q, c)
                return remote(src, at(q, c), f_send.at[i, k, c], f_recv.at[i, k, c], (sib, z))

            def second(c):
                return remote(at(source, c), at(source, c), d_send.at[i, c], d_recv.at[i, c], (other, z))

            def keep():
                return pltpu.make_async_copy(ref, out.at[me], lsem.at[i])

            def begin_():
                keep().start()
                for c in range(chunks):
                    for k in range(2):
                        first(k, c).start()
                for c in range(chunks):
                    twin(0, me, c).start()

            def forward():
                for c in range(chunks):
                    remote(mine(c), at(source, c), x_send.at[i, core, c], x_recv.at[i, core, c], (sib, z)).wait_recv()
                    second(c).start()
                    twin(1, source, c).start()
                    remote(
                        mine(c), at(other, c), x_send.at[i, 1 - core, c], x_recv.at[i, 1 - core, c], (sib, z)
                    ).wait_recv()
                    twin(2, other, c).start()

            def last():
                for c in range(chunks):
                    remote(at(across, c), at(across, c), d_send.at[i, c], d_recv.at[i, c], (other, z)).wait_recv()
                    twin(3, across, c).start()

            def finish():
                keep().wait()
                theirs = (sib, dev(core, 1 - core, 1 - core), dev(1 - core, core, 1 - core), dev(1, 1, 1 - core))
                for c in range(chunks):
                    for k in range(4):
                        remote(
                            at(theirs[k], c), at(theirs[k], c), f_send.at[i, k, c], f_recv.at[i, k, c], (sib, z)
                        ).wait_recv()

            def close():
                for c in range(chunks):
                    for k in range(2):
                        first(k, c).wait_send()
                    second(c).wait_send()
                    for k, q in enumerate((me, source, other, across)):
                        twin(k, q, c).wait_send()

            return begin_, forward, last, finish, close

        tok_begin, tok_forward, tok_last, tok_finish, tok_close = gather(0, t_ref, toks)
        cot_begin, cot_forward, cot_last, cot_finish, cot_close = gather(1, c_ref, c_out)

        loop(1, count, lambda o: pl.semaphore_signal(bar, inc=1, device_id=anyone(o), device_id_type=MESH))
        for src, dst in sections(me):
            pltpu.make_async_copy(src, dst, lsem.at[2]).start()
        keep_u = pltpu.make_async_copy(u_ref.at[me], u_out.at[me], lsem.at[3])
        keep_s = pltpu.make_async_copy(small_ref, small_out.at[flat], lsem.at[4])
        keep_u.start()
        keep_s.start()
        pl.semaphore_wait(bar, count - 1)

        loop(1, 8, send_piece)
        pltpu.make_async_copy(w_out.at[me, z], w_out.at[me, z], lsem.at[2]).wait()
        pass_on(0, 0)
        loop(1, count, lambda o: tiny(o).start())

        def first_leg(o):
            landed(o).wait_recv()
            pass_on(0, o)

        tok_begin()
        loop(1, 8, first_leg)
        loop(0, 8, lambda o: pass_on(1, o))
        tok_forward()
        cot_begin()
        loop(1, 8, lambda o: unit_piece(o).start())
        loop(0, 4, lambda o: pass_on(2, o))
        tok_last()
        tok_finish()
        keep_s.wait()
        loop(1, count, lambda o: tiny(o).wait_recv())

        lanes = lax.broadcasted_iota(jnp.int32, (1, 128), 1)
        per = 128 // own
        blocks = []
        for m in range(width // 128):
            block = small_out[m * per, 0:1, :].astype(F32)
            for i in range(1, per):
                block = jnp.where(lanes >= i * own, small_out[m * per + i, 0:1, :].astype(F32), block)
            blocks.append(block)
        gain = jnp.concatenate(blocks, axis=1)
        step = 32

        def norm_rows(o):
            def some(r, _):
                sl = pl.ds(r * step, step)
                v = toks[o, sl].astype(F32)
                n_out[o, sl] = (
                    v * lax.rsqrt(jnp.mean(v * v, axis=-1, keepdims=True) + EPSILON) * gain
                ).astype(BF16)
                return 0

            lax.fori_loop(0, rows // step, some, 0)

        def third_leg(o):
            pass_on(2, o)
            norm_rows(o - 4)
            norm_rows(o)

        loop(4, 8, third_leg)
        cot_forward()
        loop(0, 4, lambda o: pass_on(3, o))
        cot_last()
        loop(4, 8, lambda o: pass_on(3, o))
        cot_finish()
        for t in range(n_z - 1):
            loop(0, 8, functools.partial(sent, t))
        loop(1, 8, lambda o: landed(o).wait_send())
        loop(1, 8, lambda o: unit_piece(o).wait())
        loop(1, count, lambda o: tiny(o).wait_send())
        keep_u.wait()
        tok_close()
        cot_close()

    dma = pltpu.SemaphoreType.DMA
    anywhere, vmem = pl.BlockSpec(memory_space=pl.ANY), pl.BlockSpec(memory_space=pltpu.VMEM)
    plane = jax.ShapeDtypeStruct((8, rows, width), BF16)
    legs = n_z - 1
    return pl.pallas_call(
        kernel,
        out_shape=[
            jax.ShapeDtypeStruct((8, n_z, own, cols), BF16),
            jax.ShapeDtypeStruct((8, own, units), BF16),
            plane,
            plane,
            jax.ShapeDtypeStruct((count,) + small.shape, BF16),
        ],
        in_specs=[anywhere] * 6,
        out_specs=[anywhere, anywhere, vmem, anywhere, vmem],
        scratch_shapes=[
            pltpu.VMEM((8, rows, width), BF16),
            dma((5,)),
            dma((7,)),
            dma((7,)),
            dma((7,)),
            dma((7,)),
            dma((legs, 8)),
            dma((legs, 8)),
            dma((legs, 8)),
            dma((legs, 8)),
            dma((count - 1,)),
            dma((count - 1,)),
            dma((2, 2, chunks)),
            dma((2, 2, chunks)),
            dma((2, chunks)),
            dma((2, chunks)),
            dma((2, 4, chunks)),
            dma((2, 4, chunks)),
        ],
        cost_estimate=busy(150),
        compiler_params=pltpu.CompilerParams(
            collective_id=cid, has_side_effects=True, vmem_limit_bytes=32 << 20
        ),
    )(weight, decays, ups, tokens, cotangent, small)


def gather_small(x, n_dp, n_z, cid):
    rows, cols = x.shape
    count = n_dp * n_z

    def kernel(x_ref, o_ref, lsem, ssem, rsem):
        flat = lax.axis_index("dp") * n_z + lax.axis_index("fsdp")
        bar = pltpu.get_barrier_semaphore()

        def device(o):
            other = lax.rem(flat + o, count)
            return (other // n_z, lax.rem(other, n_z))

        def copy(o):
            return pltpu.make_async_remote_copy(
                x_ref, o_ref.at[flat], ssem.at[o - 1], rsem.at[o - 1], device_id=device(o), device_id_type=MESH
            )

        def greet(o, _):
            pl.semaphore_signal(bar, inc=1, device_id=device(o), device_id_type=MESH)
            return 0

        def send(o, _):
            copy(o).start()
            return 0

        def wait(o, _):
            copy(o).wait()
            return 0

        lax.fori_loop(1, count, greet, 0)
        local = pltpu.make_async_copy(x_ref, o_ref.at[flat], lsem)
        local.start()
        pl.semaphore_wait(bar, count - 1)
        lax.fori_loop(1, count, send, 0)
        lax.fori_loop(1, count, wait, 0)
        local.wait()

    dma = pltpu.SemaphoreType.DMA
    return pl.pallas_call(
        kernel,
        out_shape=jax.ShapeDtypeStruct((count, rows, cols), x.dtype),
        in_specs=[pl.BlockSpec(memory_space=pl.ANY)],
        out_specs=pl.BlockSpec(memory_space=pl.ANY),
        scratch_shapes=[dma, dma((count - 1,)), dma((count - 1,))],
        cost_estimate=busy(15),
        compiler_params=pltpu.CompilerParams(collective_id=cid, has_side_effects=True),
    )(x)


def pack(parts, unit):
    flat = jnp.concatenate([part.reshape(-1) for part in parts])
    size = flat.shape[0]
    full = -(-size // (128 * unit)) * 128 * unit
    return jnp.pad(flat, (0, full - size)).reshape(-1, 128)


def dot(a, b, dims=NN, out=F32):
    return lax.dot_general(a, b, dims, preferred_element_type=F32).astype(out)


def local(
    n_dp,
    n_z,
    tokens,
    cotangent,
    group_ids,
    norm_first,
    input_weight,
    decay_weight,
    conv_weight,
    decay_scale,
    decay_bias,
    output_gain,
    output_weight,
    norm_second,
    upgate_weight,
    down_weight,
):
    count = n_dp * n_z
    rows, width = tokens.shape
    all_heads = decay_scale.shape[0]
    heads = all_heads // n_dp
    taps = conv_weight.shape[0]
    own_conv = conv_weight.shape[1]
    own_d = norm_first.shape[0]
    units = upgate_weight.shape[1] // (2 * n_dp)
    key, value = heads * DK, heads * DV
    cols = 2 * key + 2 * value + 128
    square = n_dp == 8 and n_z == 4
    here = lax.axis_index("dp")
    flat = here * n_z + lax.axis_index("fsdp")

    def spread(x, cid):
        if square:
            return ag_square(x, cid).reshape(n_dp * rows, width)
        return lax.all_gather(x, "dp", axis=0, tiled=True)

    def total(x, cid):
        if square:
            return rs_square(x.reshape(n_dp, rows, width), cid)
        return lax.psum_scatter(x, "dp", scatter_dimension=0, tiled=True).astype(F32)

    def by_dp(a, parts):
        return a.reshape(a.shape[0], n_dp, parts)

    main = units // 128 * 128
    bounds = (0, key, 2 * key, 2 * key + value, 2 * key + 2 * value)
    gates = by_dp(upgate_weight[:, : n_dp * units], units)
    ups = by_dp(upgate_weight[:, n_dp * units :], units)
    up_mine = jnp.concatenate(
        [gates[:, :, :main], ups[:, :, :main], gates[:, :, main:], ups[:, :, main:]], axis=2
    ).transpose(1, 0, 2)
    decay_cols = jnp.concatenate(
        [
            by_dp(decay_weight[:, :all_heads], heads),
            by_dp(decay_weight[:, all_heads:], heads),
            jnp.zeros((own_d, n_dp, 128 - 2 * heads), BF16),
        ],
        axis=2,
    ).transpose(1, 0, 2)

    def whole_rows(a):
        a = lax.all_gather(a[:, None], "fsdp", axis=1, tiled=True)
        return a.reshape(width, a.shape[-1])

    conv_size = taps * own_conv
    inputs = tokens.astype(F32)
    first_root = lax.rsqrt(jnp.mean(inputs * inputs, axis=-1, keepdims=True) + EPSILON)
    if square:
        small = jnp.concatenate(
            [
                jnp.tile(norm_first, 128 // own_d)[None],
                jnp.tile(norm_second, 128 // own_d)[None],
                jnp.broadcast_to(group_ids.astype(BF16)[:, None], (1, 128)),
                jnp.zeros((5, 128), BF16),
                conv_weight.reshape(8, 128),
            ],
            axis=0,
        )
        in_full, up_plane, normed_all, cot_all, small = begin(
            input_weight, decay_cols, up_mine, tokens, cotangent, small, bounds, n_z, 1
        )
        in_full = in_full.reshape(width, cols)
        normed_all = normed_all.reshape(n_dp * rows, width)
        cot_all = cot_all.reshape(n_dp * rows, width)
        conv_full = small[:, 8:].reshape(count, taps, own_conv)
        first_full = small[:, 0, :own_d]
        second_full = small[:, 1, :own_d]
        every_id = small[:, 2, 0]
        output_weight, down_weight, up_plane = lax.optimization_barrier(
            (output_weight, down_weight, up_plane, small)
        )[:3]
    else:
        in_mine = [
            by_dp(input_weight[:, n_dp * a : n_dp * b], b - a).transpose(1, 0, 2)
            for a, b in zip(bounds[:-1], bounds[1:])
        ]
        in_mine = jnp.concatenate(in_mine + [decay_cols], axis=2)
        in_full = whole_rows(lax.all_to_all(in_mine, "dp", 0, 0, tiled=True))
        up_plane = lax.all_to_all(up_mine, "dp", 0, 0, tiled=True)
        small = gather_small(
            pack((conv_weight, norm_first, norm_second, group_ids.astype(BF16)), 16), n_dp, n_z, 1
        ).reshape(count, -1)
        conv_full = small[:, :conv_size].reshape(count, taps, own_conv)
        first_full = small[:, conv_size : conv_size + own_d]
        second_full = small[:, conv_size + own_d : conv_size + 2 * own_d]
        every_id = small[:, conv_size + 2 * own_d]
    out_full = lax.all_gather(output_weight, "fsdp", axis=0, tiled=True)
    up_full = whole_rows(up_plane)
    down_full = lax.all_gather(down_weight, "fsdp", axis=0, tiled=True)
    conv_full = conv_full.transpose(1, 0, 2).reshape(taps, -1)
    first_full = first_full.reshape(1, width).astype(F32)
    second_full = second_full.reshape(1, width).astype(F32)
    every_id = every_id.astype(jnp.int32)
    scales = 1.0 / jnp.sum((every_id[:, None] == every_id[None, :]).astype(F32), axis=0).reshape(n_dp, n_z)
    scales = lax.dynamic_index_in_dim(scales, lax.axis_index("fsdp"), axis=1, keepdims=False)
    seed = cotangent.astype(F32) * lax.dynamic_index_in_dim(scales, here, axis=0, keepdims=False)
    scales = jnp.broadcast_to(scales[:, None, None], (n_dp, rows, 1)).reshape(n_dp * rows, 1)
    if not square:
        normed_all = spread((inputs * first_root * first_full).astype(BF16), 2)
        cot_all = spread(cotangent, 3)

    def conv_columns(start, size):
        return lax.dynamic_slice_in_dim(conv_full, start + here * size, size, axis=1)

    conv_mine = jnp.concatenate(
        [conv_columns(0, key), conv_columns(n_dp * key, key), conv_columns(2 * n_dp * key, value)], axis=1
    ).astype(F32)
    decay_mine = jnp.pad(
        jnp.stack(
            [
                lax.dynamic_slice_in_dim(decay_scale, here * heads, heads),
                lax.dynamic_slice_in_dim(decay_bias, here * heads, heads),
            ]
        ),
        ((0, 0), (0, 128 - heads)),
    )
    gain = output_gain[None, :]

    projected = dot(normed_all, in_full)
    mixed, inverse, solved, core = mixer_forward(projected, conv_mine, decay_mine, gain, heads, rows)
    middle = inputs + total(dot(mixed, out_full, out=BF16), 4)
    second_root = lax.rsqrt(jnp.mean(middle * middle, axis=-1, keepdims=True) + EPSILON)
    second_all = spread((middle * second_root * second_full).astype(BF16), 5)
    upgate = dot(second_all, up_full)

    def halves_of(a):
        return (a[:, :main], a[:, main : 2 * main]), (a[:, 2 * main : main + units], a[:, main + units :])

    acts = [(g, u, jax.nn.sigmoid(g)) for g, u in halves_of(upgate)]
    hidden = jnp.concatenate([g * s * u for g, u, s in acts], axis=1)
    hidden_seed = (hidden * scales).astype(BF16)
    hidden = hidden.astype(BF16)

    down_grad = dot(hidden_seed, cot_all, TN, out=BF16)
    down_grad, cot_all = lax.optimization_barrier((down_grad, cot_all))
    hidden_grad = dot(cot_all, down_full, NT) * scales
    parts = list(zip(acts, (hidden_grad[:, :main], hidden_grad[:, main:])))
    upgate_low = jnp.concatenate(
        [x for (g, u, s), grad in parts for x in (grad * u * s * (1.0 + g * (1.0 - s)), grad * g * s)], axis=1
    ).astype(BF16)
    back_two = dot(upgate_low, up_full, NT, out=BF16)
    upgate_grad = dot(second_all, upgate_low, TN, out=BF16)
    back_two, down_grad, upgate_grad = lax.optimization_barrier((back_two, down_grad, upgate_grad))
    normed_two_grad = total(back_two, 6)

    def norm_back(v, root, gain_row, grad):
        hat = v * root
        scaled = grad * gain_row
        gain_grad = jnp.sum(grad * hat, axis=0)
        return root * (scaled - hat * jnp.mean(scaled * hat, axis=-1, keepdims=True)), gain_grad

    middle_part, second_grad = norm_back(middle, second_root, second_full, normed_two_grad)
    middle_grad = seed + middle_part

    def owned_rows(a):
        return lax.psum_scatter(a, "fsdp", scatter_dimension=0, tiled=True)

    def owned_parts(a):
        a = a.reshape(n_dp, n_z, own_d, a.shape[-1]).transpose(1, 0, 2, 3)
        return lax.psum_scatter(a.reshape(width, -1), "fsdp", scatter_dimension=0, tiled=True)

    def to_owners(a):
        a = lax.all_to_all(a.reshape(n_dp, own_d, -1), "dp", 0, 0, tiled=True)
        return a.transpose(1, 0, 2).astype(F32)

    down_total = owned_rows(down_grad)
    middle_low, down_total = lax.optimization_barrier((middle_grad.astype(BF16), down_total))
    middle_all = spread(middle_low, 8)
    upgate_sum = owned_parts(upgate_grad)
    mixed_grad = dot(middle_all, out_full, NT)
    output_grad = dot(mixed, middle_all, TN, out=BF16)
    mixed_grad, output_grad = lax.optimization_barrier((mixed_grad, output_grad))
    projected_low, conv_grad, gain_grad, decay_grad = mixer_backward(
        projected, conv_mine, decay_mine, gain, inverse, solved, core, mixed_grad, heads, rows
    )
    projected_low, upgate_sum = lax.optimization_barrier((projected_low, upgate_sum))
    output_total = owned_rows(output_grad)
    in_grad = dot(normed_all, projected_low, TN, out=BF16)
    projected_low, in_grad = lax.optimization_barrier((projected_low, in_grad))
    back_one = dot(projected_low, in_full, NT, out=BF16)
    back_one, output_total = lax.optimization_barrier((back_one, output_total))
    in_sum = owned_parts(in_grad)
    normed_one_grad = total(back_one, 9)
    hidden, normed_one_grad = lax.optimization_barrier((hidden, normed_one_grad))
    result = middle + total(dot(hidden, down_full, out=BF16), 7)
    input_part, first_grad = norm_back(inputs, first_root, first_full, normed_one_grad)
    tokens_grad = middle_grad + input_part

    down_total = down_total.astype(F32)
    output_total = output_total.astype(F32)
    up_total = to_owners(upgate_sum)
    upgate_total = jnp.concatenate(
        [
            jnp.concatenate([a, b], axis=2).reshape(own_d, -1)
            for a, b in (
                (up_total[:, :, :main], up_total[:, :, 2 * main : main + units]),
                (up_total[:, :, main : 2 * main], up_total[:, :, main + units :]),
            )
        ],
        axis=1,
    )
    in_total = to_owners(in_sum)
    input_total = jnp.concatenate(
        [in_total[:, :, a:b].reshape(own_d, -1) for a, b in zip(bounds[:-1], bounds[1:])], axis=1
    )
    start = bounds[-1]
    decay_total = jnp.concatenate(
        [
            in_total[:, :, start : start + heads].reshape(own_d, -1),
            in_total[:, :, start + heads : start + 2 * heads].reshape(own_d, -1),
        ],
        axis=1,
    )

    sizes = (first_grad.size, second_grad.size, gain_grad.size, conv_grad.size, 2 * heads)
    shared = gather_small(
        pack((first_grad, second_grad, gain_grad, conv_grad, decay_grad[:, :heads]), 8), n_dp, n_z, 10
    ).reshape(count, -1)
    edges = [0]
    for size in sizes:
        edges.append(edges[-1] + size)
    summed = jnp.sum(shared[:, : edges[3]], axis=0)
    first_total = lax.dynamic_slice_in_dim(summed, flat * own_d, own_d)
    second_total = lax.dynamic_slice_in_dim(summed, edges[1] + flat * own_d, own_d)
    gain_total = summed[edges[2] : edges[3]]
    by_plane = jnp.sum(shared[:, edges[3] : edges[5]].reshape(n_dp, n_z, -1), axis=1)
    conv_all = by_plane[:, : sizes[3]].reshape(n_dp, taps, 2 * key + value)
    conv_row = jnp.concatenate(
        [
            conv_all[:, :, a:b].transpose(1, 0, 2).reshape(taps, -1)
            for a, b in ((0, key), (key, 2 * key), (2 * key, 2 * key + value))
        ],
        axis=1,
    )
    conv_total = lax.dynamic_slice_in_dim(conv_row, flat * own_conv, own_conv, axis=1)
    scale_bias = by_plane[:, sizes[3] :].reshape(n_dp, 2, heads)
    scale_total = scale_bias[:, 0].reshape(-1)
    bias_total = scale_bias[:, 1].reshape(-1)
    return (
        result,
        tokens_grad,
        first_total,
        input_total,
        decay_total,
        conv_total,
        scale_total,
        bias_total,
        gain_total,
        output_total,
        second_total,
        upgate_total,
        down_total,
    )


def solution(mesh):
    both = ("dp", "fsdp")
    rows, vector = P(both, None), P(both)
    return jax.shard_map(
        functools.partial(local, mesh.shape["dp"], mesh.shape["fsdp"]),
        mesh=mesh,
        in_specs=(
            rows, rows, vector, vector, rows, rows, P(None, both), P(), P(), P(), rows, vector, rows, rows,
        ),
        out_specs=(
            rows, rows, vector, rows, rows, P(None, both), P(), P(), P(), rows, vector, rows, rows,
        ),
        check_vma=False,
    )
```

```python
import functools

import jax
import jax.numpy as jnp
from jax import lax
from jax.experimental import pallas as pl
from jax.experimental.pallas import tpu as pltpu
from jax.sharding import PartitionSpec as P

MESH = pl.DeviceIdType.MESH
F32 = jnp.float32
BF16 = jnp.bfloat16
EPSILON = 1e-06
DK = 128
DV = 256
BASE = 8
NN = (((1,), (0,)), ((), ()))
NT = (((1,), (1,)), ((), ()))
TN = (((0,), (0,)), ((), ()))


def dot1(a, b, dims=NN):
    return lax.dot_general(a.astype(BF16), b.astype(BF16), dims, preferred_element_type=F32)


def halves(a):
    if a.dtype == BF16:
        return (a,)
    high = a.astype(BF16)
    return (high, (a - high.astype(F32)).astype(BF16))


def dot3(a, b, dims=NN):
    a, b = halves(a), halves(b)
    total = lax.dot_general(a[0], b[0], dims, preferred_element_type=F32)
    if len(a) > 1:
        total = total + lax.dot_general(a[1], b[0], dims, preferred_element_type=F32)
    if len(b) > 1:
        total = total + lax.dot_general(a[0], b[1], dims, preferred_element_type=F32)
    return total


def dot6(a, b, dims=NN):
    return lax.dot_general(a, b, dims, precision=lax.Precision.HIGHEST, preferred_element_type=F32)


def shift_down(v, n, rows):
    if n == 0:
        return v
    return jnp.where(rows >= n, pltpu.roll(v, n, 0), 0.0)


def shift_up(v, n, rows):
    if n == 0:
        return v
    length = v.shape[0]
    return jnp.where(rows < length - n, pltpu.roll(v, length - n, 0), 0.0)


def conv(c, taps, rows):
    count = taps.shape[0]
    total = c * taps[count - 1 : count]
    for j in range(count - 1):
        total = total + shift_down(c, count - 1 - j, rows) * taps[j : j + 1]
    return total


def sigmoid(v):
    return 1.0 / (1.0 + jnp.exp(-v))


def softplus(v):
    return jnp.maximum(v, 0.0) + jnp.log1p(jnp.exp(-jnp.abs(v)))


def unit_inverses(lowers, row_ids, col_ids):
    length = lowers[0].shape[0]
    size = BASE
    same = row_ids // size == col_ids // size
    pick = jnp.where(col_ids[:, :128] == lax.rem(row_ids[:, :128], size), 1.0, 0.0).astype(BF16)
    lanes = lax.broadcasted_iota(jnp.int32, (length // size, size, 128), 2)
    places = lax.broadcasted_iota(jnp.int32, (length // size, size, 128), 1)
    compact = [dot3(jnp.where(same, lower, 0.0), pick).reshape(length // size, size, 128) for lower in lowers]
    solved = [jnp.where(lanes == places, 1.0, 0.0) for _ in lowers]
    for j in range(size - 1):
        solved = [x - a[:, :, j : j + 1] * x[:, j : j + 1, :] for a, x in zip(compact, solved)]
    inverses = [jnp.where(same, dot3(x.reshape(length, 128), pick, NT), 0.0) for x in solved]
    while size < length:
        wide = 2 * size
        off = (row_ids // wide == col_ids // wide) & (row_ids // size != col_ids // size)
        inner = [dot3(jnp.where(off, lower, 0.0), inverse) for lower, inverse in zip(lowers, inverses)]
        inverses = [inverse - dot3(inverse, x) for inverse, x in zip(inverses, inner)]
        size = wide
    return inverses


def common(proj, decay, heads, length):
    rows = lax.broadcasted_iota(jnp.int32, (length, 1), 0)
    row_ids = lax.broadcasted_iota(jnp.int32, (length, length), 0)
    col_ids = lax.broadcasted_iota(jnp.int32, (length, length), 1)
    raw = proj[:, heads * 768 :]
    lanes = lax.broadcasted_iota(jnp.int32, raw.shape, 1)
    shifted = raw + decay[1:2]
    rate = jnp.where(lanes < heads, -jnp.exp(decay[0:1]) * softplus(shifted), 0.0)
    beta = sigmoid(raw)
    cumulated = dot6(jnp.where(row_ids >= col_ids, 1.0, 0.0), rate)
    return rows, row_ids, col_ids, raw, lanes, shifted, rate, beta, cumulated, cumulated.T


def head_parts(h, heads):
    key = slice(h * DK, (h + 1) * DK)
    keyk = slice((heads + h) * DK, (heads + h + 1) * DK)
    val = slice(heads * DV + h * DV, heads * DV + (h + 1) * DV)
    gat = slice(2 * heads * DV + h * DV, 2 * heads * DV + (h + 1) * DV)
    return key, keyk, val, gat


def mixer_forward_kernel(heads, proj_ref, taps_ref, decay_ref, gain_ref, mixed_ref, inv_ref, solved_ref, core_ref):
    length = proj_ref.shape[0]
    decay = decay_ref[...]
    gain = gain_ref[...]
    rows, row_ids, col_ids, raw, lanes, shifted, rate, beta, cumulated, cum_t = common(
        proj_ref[...], decay, heads, length
    )
    def active(cols):
        y = conv(proj_ref[:, cols], taps_ref[:, cols], rows)
        return y * sigmoid(y)

    parts = [head_parts(h, heads) for h in range(heads)]
    queries, keys, values, growths, betas, lowers = [], [], [], [], [], []
    for h, (qs, ks, vs, gs) in enumerate(parts):
        k = active(ks)
        k = (k * lax.rsqrt(jnp.sum(k * k, axis=-1, keepdims=True) + EPSILON)).astype(BF16)
        beta_h = beta[:, heads + h : heads + h + 1]
        gap = cumulated[:, h : h + 1] - cum_t[h : h + 1, :]
        growth = jnp.where(row_ids >= col_ids, jnp.exp(jnp.where(row_ids >= col_ids, gap, 0.0)), 0.0)
        keys.append(k)
        growths.append(growth)
        betas.append(beta_h)
        lowers.append(jnp.where(row_ids > col_ids, growth * dot1(k, k, NT) * beta_h, 0.0))
    inverses = unit_inverses(lowers, row_ids, col_ids)
    for h, (qs, ks, vs, gs) in enumerate(parts):
        q = active(qs)
        q = (q * lax.rsqrt(jnp.sum(q * q, axis=-1, keepdims=True) + EPSILON) * DK ** (-0.5)).astype(BF16)
        v = active(vs).astype(BF16)
        inv_ref[h] = inverses[h]
        solved = dot3(inverses[h], betas[h] * v.astype(F32))
        core = dot3(growths[h] * dot1(q, keys[h], NT), solved)
        solved_ref[:, h * DV : (h + 1) * DV] = solved
        core_ref[:, h * DV : (h + 1) * DV] = core
        gate = proj_ref[:, gs]
        normed = core * lax.rsqrt(jnp.mean(core * core, axis=-1, keepdims=True) + EPSILON) * gain
        mixed_ref[:, h * DV : (h + 1) * DV] = (normed * (gate * sigmoid(gate))).astype(BF16)


def mixer_forward(proj, taps, decay, gain, heads, length):
    tokens, width = proj.shape
    seqs = tokens // length
    hv = heads * DV
    row = lambda cols: pl.BlockSpec((length, cols), lambda s: (s, 0))
    whole = lambda a: pl.BlockSpec(a.shape, lambda s: (0,) * a.ndim)
    return pl.pallas_call(
        functools.partial(mixer_forward_kernel, heads),
        grid=(seqs,),
        in_specs=[row(width), whole(taps), whole(decay), whole(gain)],
        out_specs=[row(hv), pl.BlockSpec((None, heads, length, length), lambda s: (s, 0, 0, 0)), row(hv), row(hv)],
        out_shape=[
            jax.ShapeDtypeStruct((tokens, hv), BF16),
            jax.ShapeDtypeStruct((seqs, heads, length, length), F32),
            jax.ShapeDtypeStruct((tokens, hv), F32),
            jax.ShapeDtypeStruct((tokens, hv), F32),
        ],
        cost_estimate=busy(55), compiler_params=pltpu.CompilerParams(vmem_limit_bytes=48 << 20),
    )(proj, taps, decay, gain)


def mixer_backward_kernel(
    heads, proj_ref, taps_ref, decay_ref, gain_ref, inv_ref, solved_ref, core_ref, grad_ref,
    low_ref, conv_ref, gain_grad_ref, decay_grad_ref,
):
    length = proj_ref.shape[0]
    count = taps_ref.shape[0]
    decay = decay_ref[...]
    gain = gain_ref[...]
    rows, row_ids, col_ids, raw, lanes, shifted, rate, beta, cumulated, cum_t = common(
        proj_ref[...], decay, heads, length
    )
    within = row_ids >= col_ids
    strict = row_ids > col_ids

    @pl.when(pl.program_id(0) == 0)
    def _():
        conv_ref[...] = jnp.zeros_like(conv_ref)
        gain_grad_ref[...] = jnp.zeros_like(gain_grad_ref)
        decay_grad_ref[...] = jnp.zeros_like(decay_grad_ref)

    cum_grad = jnp.zeros(raw.shape, F32)
    beta_grad = jnp.zeros(raw.shape, F32)
    for h in range(heads):
        qs, ks, vs, gs = head_parts(h, heads)
        hs = slice(h * DV, (h + 1) * DV)

        def active(cols):
            y = conv(proj_ref[:, cols], taps_ref[:, cols], rows)
            s = sigmoid(y)
            return y * s, s * (1.0 + y * (1.0 - s))

        def conv_back(cols, grad):
            c = proj_ref[:, cols]
            total = grad * taps_ref[count - 1 : count, cols]
            conv_ref[count - 1 : count, cols] += jnp.sum(grad * c, axis=0, keepdims=True)
            for j in range(count - 1):
                n = count - 1 - j
                total = total + shift_up(grad, n, rows) * taps_ref[j : j + 1, cols]
                conv_ref[j : j + 1, cols] += jnp.sum(grad * shift_down(c, n, rows), axis=0, keepdims=True)
            low_ref[:, cols] = total.astype(BF16)

        core = core_ref[:, hs]
        gate = proj_ref[:, gs]
        gate_sig = sigmoid(gate)
        grad = grad_ref[:, hs]
        root = lax.rsqrt(jnp.mean(core * core, axis=-1, keepdims=True) + EPSILON)
        normed = core * root
        silu_gate = gate * gate_sig
        gain_grad_ref[...] += jnp.sum(grad * normed * silu_gate, axis=0, keepdims=True)
        low_ref[:, gs] = (grad * normed * gain * gate_sig * (1.0 + gate * (1.0 - gate_sig))).astype(BF16)
        normed_grad = grad * gain * silu_gate
        core_grad = root * (normed_grad - normed * jnp.mean(normed_grad * normed, axis=-1, keepdims=True))

        q_act, q_slope = active(qs)
        q_root = lax.rsqrt(jnp.sum(q_act * q_act, axis=-1, keepdims=True) + EPSILON)
        q_unit = q_act * q_root
        q = (q_unit * DK ** (-0.5)).astype(BF16)
        k_act, k_slope = active(ks)
        k_root = lax.rsqrt(jnp.sum(k_act * k_act, axis=-1, keepdims=True) + EPSILON)
        k_unit = k_act * k_root
        k = k_unit.astype(BF16)
        v_act, v_slope = active(vs)
        v = v_act.astype(BF16).astype(F32)
        beta_h = beta[:, heads + h : heads + h + 1]
        gap = cumulated[:, h : h + 1] - cum_t[h : h + 1, :]
        growth = jnp.where(within, jnp.exp(jnp.where(within, gap, 0.0)), 0.0)
        decayed_gram = jnp.where(strict, growth * dot1(k, k, NT), 0.0)
        weights = growth * dot1(q, k, NT)
        inverse = inv_ref[h]
        solved = solved_ref[:, hs]
        solved_grad = dot3(weights, core_grad, TN)
        weights_grad = dot3(core_grad, solved, NT)
        value_grad = dot3(inverse, solved_grad, TN)
        lower_grad = jnp.where(strict, -dot3(value_grad, solved, NT), 0.0)
        gap_part = lower_grad * decayed_gram
        beta_col = jnp.sum(gap_part, axis=-1, keepdims=True) + jnp.sum(value_grad * v, axis=-1, keepdims=True)
        gap_grad = gap_part * beta_h + weights_grad * weights
        cum_col = jnp.sum(gap_grad, axis=-1, keepdims=True)
        cum_row = jnp.sum(gap_grad, axis=0, keepdims=True)
        cum_col = cum_col - jnp.broadcast_to(cum_row, (8, length)).T[:, 0:1]
        gram_grad = lower_grad * growth * beta_h
        score_grad = weights_grad * growth
        k_grad = dot3(gram_grad, k) + dot3(gram_grad, k, TN) + dot3(score_grad, q, TN)
        q_grad = dot3(score_grad, k)
        cum_grad = jnp.where(lanes == h, cum_col, cum_grad)
        beta_grad = jnp.where(lanes == heads + h, beta_col, beta_grad)

        q_grad = q_grad * DK ** (-0.5)
        q_grad = q_root * (q_grad - q_unit * jnp.sum(q_grad * q_unit, axis=-1, keepdims=True))
        conv_back(qs, q_grad * q_slope)
        k_grad = k_root * (k_grad - k_unit * jnp.sum(k_grad * k_unit, axis=-1, keepdims=True))
        conv_back(ks, k_grad * k_slope)
        conv_back(vs, value_grad * beta_h * v_slope)

    rate_grad = dot6(jnp.where(col_ids >= row_ids, 1.0, 0.0), cum_grad)
    bias_part = rate_grad * -jnp.exp(decay[0:1]) * sigmoid(shifted)
    raw_grad = jnp.where(lanes < heads, bias_part, beta_grad * beta * (1.0 - beta))
    low_ref[:, heads * 768 :] = raw_grad.astype(BF16)
    decay_grad_ref[0:1] += jnp.sum(jnp.where(lanes < heads, rate_grad * rate, 0.0), axis=0, keepdims=True)
    decay_grad_ref[1:2] += jnp.sum(jnp.where(lanes < heads, bias_part, 0.0), axis=0, keepdims=True)


def mixer_backward(proj, taps, decay, gain, inverse, solved, core, grad, heads, length):
    tokens, width = proj.shape
    seqs = tokens // length
    hv = heads * DV
    row = lambda cols: pl.BlockSpec((length, cols), lambda s: (s, 0))
    whole = lambda a: pl.BlockSpec(a.shape, lambda s: (0,) * a.ndim)
    return pl.pallas_call(
        functools.partial(mixer_backward_kernel, heads),
        grid=(seqs,),
        in_specs=[row(width), whole(taps), whole(decay), whole(gain),
                  pl.BlockSpec((None, heads, length, length), lambda s: (s, 0, 0, 0)), row(hv), row(hv), row(hv)],
        out_specs=[row(width), whole(taps), whole(gain), whole(decay)],
        out_shape=[
            jax.ShapeDtypeStruct((tokens, width), BF16),
            jax.ShapeDtypeStruct(taps.shape, F32),
            jax.ShapeDtypeStruct(gain.shape, F32),
            jax.ShapeDtypeStruct(decay.shape, F32),
        ],
        cost_estimate=busy(50), compiler_params=pltpu.CompilerParams(vmem_limit_bytes=56 << 20),
    )(proj, taps, decay, gain, inverse, solved, core, grad)


def busy(us):
    return pl.CostEstimate(flops=us * 1_000_000_000, bytes_accessed=0, transcendentals=0)


def _place(n_dp):
    me = lax.axis_index("dp")
    z = lax.axis_index("fsdp")
    core = lax.rem(me, 2)
    chip = me // 2
    return me, z, core, lax.rem(chip, 2), chip // 2

def ag_square(x, cid, chunks=4):
    rows, cols = x.shape
    r = rows // chunks
    def kernel(x_ref, o_ref, lsem, ssem, rsem, dssem, drsem, fs, fr):
        me, z, core, cx, cy = _place(8)
        dev = lambda dx, dy, c: 2*(2*lax.rem(cy+dy,2)+lax.rem(cx+dx,2))+c
        nx, ny, nd = dev(1,0,core), dev(0,1,core), dev(1,1,core)
        src = dev(1-core, core, core)
        tgt = dev(core, 1-core, core)
        sib = dev(0,0,1-core)
        bar = pltpu.get_barrier_semaphore()
        for d in (sib,nx,ny):
            pl.semaphore_signal(bar, inc=1, device_id=(d,z), device_id_type=MESH)
        pl.semaphore_wait(bar, 3)
        lc = pltpu.make_async_copy(x_ref, o_ref.at[me], lsem); lc.start()
        def rc(a, b, s, q, d):
            return pltpu.make_async_remote_copy(a, b, s, q, device_id=(d,z), device_id_type=MESH)
        own = []
        for c in range(chunks):
            sl = pl.ds(c*r, r)
            for i, d in ((0,nx),(1,ny)):
                cp = rc(x_ref.at[sl], o_ref.at[me,sl], ssem.at[i,c], rsem.at[i,c], d); cp.start(); own.append(cp)
        sibs=[]
        for c in range(chunks):
            sl = pl.ds(c*r, r)
            cp = rc(x_ref.at[sl], o_ref.at[me,sl], fs.at[0,c], fr.at[0,c], sib); cp.start(); sibs.append(cp)
        other = dev(core, 1-core, core)
        for c in range(chunks):
            sl = pl.ds(c*r, r)
            rc(x_ref.at[sl], o_ref.at[src,sl], ssem.at[core,c], rsem.at[core,c], sib).wait_recv()
            cp = rc(o_ref.at[src,sl], o_ref.at[src,sl], dssem.at[c], drsem.at[c], tgt); cp.start(); sibs.append((cp,))
            cp = rc(o_ref.at[src,sl], o_ref.at[src,sl], fs.at[1,c], fr.at[1,c], sib); cp.start(); sibs.append(cp)
            rc(x_ref.at[sl], o_ref.at[other,sl], ssem.at[1-core,c], rsem.at[1-core,c], sib).wait_recv()
            cp = rc(o_ref.at[other,sl], o_ref.at[other,sl], fs.at[2,c], fr.at[2,c], sib); cp.start(); sibs.append(cp)
        for c in range(chunks):
            sl = pl.ds(c*r, r)
            rc(x_ref.at[sl], o_ref.at[nd,sl], dssem.at[c], drsem.at[c], sib).wait_recv()
            cp = rc(o_ref.at[nd,sl], o_ref.at[nd,sl], fs.at[3,c], fr.at[3,c], sib); cp.start(); sibs.append(cp)
        for cp in own: cp.wait_send()
        for cp in sibs:
            if isinstance(cp, tuple): cp[0].wait_send()
            else: cp.wait()
        lc.wait()
    D=pltpu.SemaphoreType.DMA
    return pl.pallas_call(kernel, out_shape=jax.ShapeDtypeStruct((8,rows,cols),x.dtype),
        in_specs=[pl.BlockSpec(memory_space=pl.ANY)], out_specs=pl.BlockSpec(memory_space=pl.ANY),
        scratch_shapes=[D, D((2,chunks)), D((2,chunks)), D((chunks,)), D((chunks,)), D((4,chunks)), D((4,chunks))],
        cost_estimate=busy(40), compiler_params=pltpu.CompilerParams(collective_id=cid, has_side_effects=True))(x)

def rs_square(x, cid, chunks=4):
    _, rows, cols = x.shape
    r = rows // chunks
    def kernel(x_ref, o_ref, X, A, B, R, lsem, sa, ra, sb, rb):
        me, z, core, cx, cy = _place(8)
        dev = lambda dx, dy, c: 2*(2*lax.rem(cy+dy,2)+lax.rem(cx+dx,2))+c
        fdx, fdy = 1-core, core
        nf, ng = dev(fdx,fdy,core), dev(fdy,fdx,core)
        sib = dev(0,0,1-core)
        bar = pltpu.get_barrier_semaphore()
        for d in (sib,nf,ng):
            pl.semaphore_signal(bar, inc=1, device_id=(d,z), device_id_type=MESH)
        mine = [dev(1,1,core), ng, nf, me]
        s_f, s_g = dev(core,1-core,1-core), dev(1-core,core,1-core)
        theirs = [dev(1,1,1-core), s_g, s_f, sib]
        loads=[]
        for k in range(4):
            for c in range(chunks):
                sl=pl.ds(c*r,r)
                cp=pltpu.make_async_copy(x_ref.at[mine[k],sl], X.at[k,sl], lsem.at[k,c]); cp.start(); loads.append(cp)
        pl.semaphore_wait(bar, 3)
        def rc(a, b, s, q, d):
            return pltpu.make_async_remote_copy(a, b, s, q, device_id=(d,z), device_id_type=MESH)
        sends=[]; ga={}
        for k in range(4):
            for c in range(chunks):
                sl=pl.ds(c*r,r)
                cp=rc(x_ref.at[theirs[k],sl], A.at[k,sl], sa.at[k,c], ra.at[k,c], sib); cp.start(); sends.append(cp); ga[k,c]=cp
        def pair(k,c):
            sl=pl.ds(c*r,r)
            loads[k*chunks+c].wait(); ga[k,c].wait_recv()
            return X[k,sl].astype(F32)+A[k,sl].astype(F32)
        gb={}
        def ship(slot, c, d):
            sl=pl.ds(c*r,r)
            cp=rc(B.at[slot,sl], R.at[slot,sl], sb.at[slot,c], rb.at[slot,c], d); cp.start(); sends.append(cp); gb[slot,c]=cp
        for c in range(chunks):
            sl=pl.ds(c*r,r)
            B[0,sl]=pair(0,c).astype(BF16); ship(0,c,nf)
        for c in range(chunks):
            sl=pl.ds(c*r,r)
            B[2,sl]=pair(2,c).astype(BF16); ship(2,c,nf)
        for c in range(chunks):
            sl=pl.ds(c*r,r)
            v=pair(1,c)
            gb[0,c].wait_recv()
            B[1,sl]=(v+R[0,sl].astype(F32)).astype(BF16); ship(1,c,ng)
        for c in range(chunks):
            sl=pl.ds(c*r,r)
            v=pair(3,c)
            gb[2,c].wait_recv()
            o_ref[sl]=v+R[2,sl].astype(F32)
        for c in range(chunks):
            sl=pl.ds(c*r,r)
            gb[1,c].wait_recv()
            o_ref[sl]=o_ref[sl]+R[1,sl].astype(F32)
        for cp in sends: cp.wait_send()
    D=pltpu.SemaphoreType.DMA
    V=lambda n: pltpu.VMEM((n,rows,cols),x.dtype)
    return pl.pallas_call(kernel, out_shape=jax.ShapeDtypeStruct((rows,cols),F32),
        in_specs=[pl.BlockSpec(memory_space=pl.ANY)], out_specs=pl.BlockSpec(memory_space=pltpu.VMEM),
        scratch_shapes=[V(4),V(4),V(3),V(3), D((4,chunks)), D((4,chunks)), D((4,chunks)), D((3,chunks)), D((3,chunks))],
        cost_estimate=busy(40), compiler_params=pltpu.CompilerParams(collective_id=cid, has_side_effects=True, vmem_limit_bytes=40<<20))(x)

def begin(weight, decays, ups, tokens, cotangent, small, bounds, n_z, cid):
    own = weight.shape[0]
    cols = bounds[-1] + 128
    units = ups.shape[2]
    rows, width = tokens.shape
    count = 8 * n_z
    chunks = 2
    part = rows // chunks

    def kernel(
        w_ref, dec_ref, u_ref, t_ref, c_ref, small_ref, w_out, u_out, n_out, c_out, small_out,
        toks, lsem, a_send, a_recv, g_send, g_recv, up_send, up_recv, down_send, down_recv,
        small_send, small_recv, x_send, x_recv, d_send, d_recv, f_send, f_recv,
    ):
        me, z, core, cx, cy = _place(8)
        flat = me * n_z + z
        bar = pltpu.get_barrier_semaphore()

        def dev(dx, dy, c):
            return 2 * (2 * lax.rem(cy + dy, 2) + lax.rem(cx + dx, 2)) + c

        sib = dev(0, 0, 1 - core)

        def partner(o):
            return dev(o // 4, lax.rem(o // 2, 2), lax.rem(core + o, 2))

        def anyone(o):
            other = lax.rem(flat + o, count)
            return (other // n_z, lax.rem(other, n_z))

        def remote(src, dst, send, recv, device):
            return pltpu.make_async_remote_copy(src, dst, send, recv, device_id=device, device_id_type=MESH)

        def loop(first, last, body):
            def step(o, _):
                body(o)
                return 0

            lax.fori_loop(first, last, step, 0)

        def sections(q):
            for first, last in zip(bounds[:-1], bounds[1:]):
                size = last - first
                at = pl.multiple_of(8 * first + q * size, 128)
                yield w_ref.at[:, pl.ds(at, size)], w_out.at[me, z, :, pl.ds(first, size)]
            yield dec_ref.at[q], w_out.at[me, z, :, pl.ds(bounds[-1], 128)]

        def send_piece(o):
            q = partner(o)
            for src, dst in sections(q):
                remote(src, dst, a_send.at[o - 1], a_recv.at[o - 1], (q, z)).start()

        def landed(o):
            at = w_out.at[partner(o), z]
            return remote(at, at, a_send.at[o - 1], a_recv.at[o - 1], (sib, z))

        def up(t, o):
            at = w_out.at[partner(o), z - t]
            return remote(at, at, up_send.at[t, o], up_recv.at[t, o], (me, z + 1))

        def down(t, o):
            at = w_out.at[partner(o), z + t]
            return remote(at, at, down_send.at[t, o], down_recv.at[t, o], (me, z - 1))

        def pass_on(t, o):
            if t > 0:

                @pl.when(z >= t)
                def _():
                    at = w_out.at[partner(o), z - t]
                    remote(at, at, up_send.at[t - 1, o], up_recv.at[t - 1, o], (sib, z)).wait_recv()

                @pl.when(z + t < n_z)
                def _():
                    at = w_out.at[partner(o), z + t]
                    remote(at, at, down_send.at[t - 1, o], down_recv.at[t - 1, o], (sib, z)).wait_recv()

            if t < n_z - 1:

                @pl.when((z >= t) & (z < n_z - 1))
                def _():
                    up(t, o).start()

                @pl.when((z + t < n_z) & (z > 0))
                def _():
                    down(t, o).start()

        def sent(t, o):
            @pl.when((z >= t) & (z < n_z - 1))
            def _():
                up(t, o).wait_send()

            @pl.when((z + t < n_z) & (z > 0))
            def _():
                down(t, o).wait_send()

        def unit_piece(o):
            q = partner(o)
            return remote(u_ref.at[q], u_out.at[me], g_send.at[o - 1], g_recv.at[o - 1], (q, z))

        def tiny(o):
            return remote(small_ref, small_out.at[flat], small_send.at[o - 1], small_recv.at[o - 1], anyone(o))

        near = (dev(1, 0, core), dev(0, 1, core))
        source, other, across = dev(1 - core, core, core), dev(core, 1 - core, core), dev(1, 1, core)

        def gather(i, ref, out):
            def at(q, c):
                return out.at[q, pl.ds(c * part, part)]

            def mine(c):
                return ref.at[pl.ds(c * part, part)]

            def first(k, c):
                return remote(mine(c), at(me, c), x_send.at[i, k, c], x_recv.at[i, k, c], (near[k], z))

            def twin(k, q, c):
                src = mine(c) if k == 0 else at(q, c)
                return remote(src, at(q, c), f_send.at[i, k, c], f_recv.at[i, k, c], (sib, z))

            def second(c):
                return remote(at(source, c), at(source, c), d_send.at[i, c], d_recv.at[i, c], (other, z))

            def keep():
                return pltpu.make_async_copy(ref, out.at[me], lsem.at[i])

            def begin_():
                keep().start()
                for c in range(chunks):
                    for k in range(2):
                        first(k, c).start()
                for c in range(chunks):
                    twin(0, me, c).start()

            def forward():
                for c in range(chunks):
                    remote(mine(c), at(source, c), x_send.at[i, core, c], x_recv.at[i, core, c], (sib, z)).wait_recv()
                    second(c).start()
                    twin(1, source, c).start()
                    remote(
                        mine(c), at(other, c), x_send.at[i, 1 - core, c], x_recv.at[i, 1 - core, c], (sib, z)
                    ).wait_recv()
                    twin(2, other, c).start()

            def last():
                for c in range(chunks):
                    remote(at(across, c), at(across, c), d_send.at[i, c], d_recv.at[i, c], (other, z)).wait_recv()
                    twin(3, across, c).start()

            def finish():
                keep().wait()
                theirs = (sib, dev(core, 1 - core, 1 - core), dev(1 - core, core, 1 - core), dev(1, 1, 1 - core))
                for c in range(chunks):
                    for k in range(4):
                        remote(
                            at(theirs[k], c), at(theirs[k], c), f_send.at[i, k, c], f_recv.at[i, k, c], (sib, z)
                        ).wait_recv()

            def close():
                for c in range(chunks):
                    for k in range(2):
                        first(k, c).wait_send()
                    second(c).wait_send()
                    for k, q in enumerate((me, source, other, across)):
                        twin(k, q, c).wait_send()

            return begin_, forward, last, finish, close

        tok_begin, tok_forward, tok_last, tok_finish, tok_close = gather(0, t_ref, toks)
        cot_begin, cot_forward, cot_last, cot_finish, cot_close = gather(1, c_ref, c_out)

        loop(1, count, lambda o: pl.semaphore_signal(bar, inc=1, device_id=anyone(o), device_id_type=MESH))
        for src, dst in sections(me):
            pltpu.make_async_copy(src, dst, lsem.at[2]).start()
        keep_u = pltpu.make_async_copy(u_ref.at[me], u_out.at[me], lsem.at[3])
        keep_s = pltpu.make_async_copy(small_ref, small_out.at[flat], lsem.at[4])
        keep_u.start()
        keep_s.start()
        pl.semaphore_wait(bar, count - 1)

        loop(1, 8, send_piece)
        pltpu.make_async_copy(w_out.at[me, z], w_out.at[me, z], lsem.at[2]).wait()
        pass_on(0, 0)
        loop(1, count, lambda o: tiny(o).start())

        def first_leg(o):
            landed(o).wait_recv()
            pass_on(0, o)

        tok_begin()
        loop(1, 8, first_leg)
        loop(0, 8, lambda o: pass_on(1, o))
        tok_forward()
        cot_begin()
        loop(1, 8, lambda o: unit_piece(o).start())
        loop(0, 4, lambda o: pass_on(2, o))
        tok_last()
        tok_finish()
        keep_s.wait()
        loop(1, count, lambda o: tiny(o).wait_recv())

        lanes = lax.broadcasted_iota(jnp.int32, (1, 128), 1)
        per = 128 // own
        blocks = []
        for m in range(width // 128):
            block = small_out[m * per, 0:1, :].astype(F32)
            for i in range(1, per):
                block = jnp.where(lanes >= i * own, small_out[m * per + i, 0:1, :].astype(F32), block)
            blocks.append(block)
        gain = jnp.concatenate(blocks, axis=1)
        step = 32

        def norm_rows(o):
            def some(r, _):
                sl = pl.ds(r * step, step)
                v = toks[o, sl].astype(F32)
                n_out[o, sl] = (
                    v * lax.rsqrt(jnp.mean(v * v, axis=-1, keepdims=True) + EPSILON) * gain
                ).astype(BF16)
                return 0

            lax.fori_loop(0, rows // step, some, 0)

        def third_leg(o):
            pass_on(2, o)
            norm_rows(o - 4)
            norm_rows(o)

        loop(4, 8, third_leg)
        cot_forward()
        loop(0, 4, lambda o: pass_on(3, o))
        cot_last()
        loop(4, 8, lambda o: pass_on(3, o))
        cot_finish()
        for t in range(n_z - 1):
            loop(0, 8, functools.partial(sent, t))
        loop(1, 8, lambda o: landed(o).wait_send())
        loop(1, 8, lambda o: unit_piece(o).wait())
        loop(1, count, lambda o: tiny(o).wait_send())
        keep_u.wait()
        tok_close()
        cot_close()

    dma = pltpu.SemaphoreType.DMA
    anywhere, vmem = pl.BlockSpec(memory_space=pl.ANY), pl.BlockSpec(memory_space=pltpu.VMEM)
    plane = jax.ShapeDtypeStruct((8, rows, width), BF16)
    legs = n_z - 1
    return pl.pallas_call(
        kernel,
        out_shape=[
            jax.ShapeDtypeStruct((8, n_z, own, cols), BF16),
            jax.ShapeDtypeStruct((8, own, units), BF16),
            plane,
            plane,
            jax.ShapeDtypeStruct((count,) + small.shape, BF16),
        ],
        in_specs=[anywhere] * 6,
        out_specs=[anywhere, anywhere, vmem, anywhere, vmem],
        scratch_shapes=[
            pltpu.VMEM((8, rows, width), BF16),
            dma((5,)),
            dma((7,)),
            dma((7,)),
            dma((7,)),
            dma((7,)),
            dma((legs, 8)),
            dma((legs, 8)),
            dma((legs, 8)),
            dma((legs, 8)),
            dma((count - 1,)),
            dma((count - 1,)),
            dma((2, 2, chunks)),
            dma((2, 2, chunks)),
            dma((2, chunks)),
            dma((2, chunks)),
            dma((2, 4, chunks)),
            dma((2, 4, chunks)),
        ],
        cost_estimate=busy(150),
        compiler_params=pltpu.CompilerParams(
            collective_id=cid, has_side_effects=True, vmem_limit_bytes=32 << 20
        ),
    )(weight, decays, ups, tokens, cotangent, small)


def relay(left, first, second, first_dims, second_dims, gain, extras, norm_back, cid):
    _, rows, depth = left.shape
    width = gain.shape[1]
    multiply = second is not None
    out_cols = 0 if not multiply else second.shape[1] if second_dims == NN else second.shape[0]
    chunks = 4
    part = rows // chunks
    tile = 512
    out_tiles = [(a, min(a + tile, out_cols)) for a in range(0, out_cols, tile)]

    def kernel(left_ref, first_ref, gain_ref, *refs):
        extra_refs, refs = refs[: len(extras)], refs[len(extras) :]
        if multiply:
            second_ref, *refs = refs
        rows_out, all_out, *refs = refs
        if multiply:
            prod_out, *refs = refs
        if norm_back:
            gain_grad, *refs = refs
        if multiply:
            *refs, w2, stage = refs
        (T, A, B, R, S, lsem, sa, ra, sb, rb, x_send, x_recv, d_send, d_recv, f_send, f_recv) = refs
        me, z, core, cx, cy = _place(8)

        def dev(dx, dy, c):
            return 2 * (2 * lax.rem(cy + dy, 2) + lax.rem(cx + dx, 2)) + c

        def remote(src, dst, send, recv, device):
            return pltpu.make_async_remote_copy(src, dst, send, recv, device_id=(device, z), device_id_type=MESH)

        sib = dev(0, 0, 1 - core)
        nf, ng, across = dev(1 - core, core, core), dev(core, 1 - core, core), dev(1, 1, core)
        bar = pltpu.get_barrier_semaphore()
        for d in (sib, nf, ng):
            pl.semaphore_signal(bar, inc=1, device_id=(d, z), device_id_type=MESH)
        if multiply:
            load = pltpu.make_async_copy(second_ref, w2, lsem.at[2])
            load.start()

        mine = (across, ng, nf, me)
        theirs = (dev(1, 1, 1 - core), dev(1 - core, core, 1 - core), dev(core, 1 - core, 1 - core), sib)

        def partial(q, write):
            def some(n, _):
                cols = pl.ds(pl.multiple_of(n * tile, tile), tile)
                w = first_ref[:, cols] if first_dims == NN else first_ref[cols, :]
                write(cols, lax.dot_general(left_ref[q], w, first_dims, preferred_element_type=F32))
                return 0

            lax.fori_loop(0, width // tile, some, 0)

        def give(k):
            def write(cols, v):
                T[k, :, cols] = v.astype(BF16)

            partial(theirs[k], write)
            remote(T.at[k], A.at[k], sa.at[k], ra.at[k], sib).start()

        def got(k):
            remote(T.at[k], A.at[k], sa.at[k], ra.at[k], sib).wait_recv()

        def cut(c):
            return pl.ds(c * part, part)

        def ship(k, c, d):
            return remote(B.at[k, cut(c)], R.at[k, cut(c)], sb.at[k, c], rb.at[k, c], d)

        def send_sum(k):
            got(k)

            def write(cols, v):
                B[k, :, cols] = (v + A[k, :, cols].astype(F32)).astype(BF16)

            partial(mine[k], write)
            for c in range(chunks):
                ship(k, c, nf).start()

        def keep_sum(k, out):
            got(k)

            def write(cols, v):
                out[:, cols] = v + A[k, :, cols].astype(F32)

            partial(mine[k], write)

        pl.semaphore_wait(bar, 3)
        give(0)
        give(2)
        send_sum(0)
        give(1)
        send_sum(2)
        give(3)
        keep_sum(1, S)
        for c in range(chunks):
            ship(0, c, nf).wait_recv()
            B[1, cut(c)] = (S[cut(c)] + R[0, cut(c)].astype(F32)).astype(BF16)
            ship(1, c, ng).start()
        keep_sum(3, S)

        source, other = nf, ng

        def at(q, c):
            return all_out.at[q, cut(c)]

        def step(k, c):
            return remote(at(me, c), at(me, c), x_send.at[k, c], x_recv.at[k, c], (dev(1, 0, core), dev(0, 1, core))[k])

        def twin(k, q, c):
            return remote(at(q, c), at(q, c), f_send.at[k, c], f_recv.at[k, c], sib)

        def second_step(c):
            return remote(at(source, c), at(source, c), d_send.at[c], d_recv.at[c], other)

        gains = gain_ref[...]
        if norm_back:
            gain_grad[...] = jnp.zeros_like(gain_grad)
        for c in range(chunks):
            ship(2, c, nf).wait_recv()
            ship(1, c, ng).wait_recv()
            for h in range(2):
                sl = pl.ds(c * part + h * (part // 2), part // 2)
                total = S[sl] + R[2, sl].astype(F32) + R[1, sl].astype(F32)
                if norm_back:
                    v = extra_refs[0][sl]
                    root = lax.rsqrt(jnp.mean(v * v, axis=-1, keepdims=True) + EPSILON)
                    hat = v * root
                    scaled = total * gains
                    gain_grad[...] += jnp.sum(total * hat, axis=0, keepdims=True)
                    done = extra_refs[1][sl] + root * (scaled - hat * jnp.mean(scaled * hat, axis=-1, keepdims=True))
                    low = done
                else:
                    done = extra_refs[0][sl].astype(F32) + total
                    low = done * lax.rsqrt(jnp.mean(done * done, axis=-1, keepdims=True) + EPSILON) * gains
                rows_out[sl] = done
                all_out[me, sl] = low.astype(BF16)
            for k in range(2):
                step(k, c).start()
            twin(0, me, c).start()
        if multiply:
            load.wait()

        flushes = []

        def product(q):
            if not multiply:
                return
            slot = len(flushes) % 2
            if len(flushes) > 1:
                flushes[-2].wait()
            for a, b in out_tiles:
                w = w2[:, a:b] if second_dims == NN else w2[a:b, :]
                stage[slot, :, a:b] = lax.dot_general(all_out[q], w, second_dims, preferred_element_type=F32)
            flush = pltpu.make_async_copy(stage.at[slot], prod_out.at[q], lsem.at[slot])
            flush.start()
            flushes.append(flush)

        def twin_got(k):
            for c in range(chunks):
                twin(k, theirs_at[k], c).wait_recv()

        theirs_at = (sib, dev(core, 1 - core, 1 - core), dev(1 - core, core, 1 - core), dev(1, 1, 1 - core))
        product(me)
        for c in range(chunks):
            remote(at(source, c), at(source, c), x_send.at[core, c], x_recv.at[core, c], sib).wait_recv()
            second_step(c).start()
            twin(1, source, c).start()
            remote(at(other, c), at(other, c), x_send.at[1 - core, c], x_recv.at[1 - core, c], sib).wait_recv()
            twin(2, other, c).start()
            if c == 0:
                twin_got(0)
                product(sib)
        product(source)
        product(other)
        for c in range(chunks):
            remote(at(across, c), at(across, c), d_send.at[c], d_recv.at[c], sib).wait_recv()
            twin(3, across, c).start()
            if c == 0:
                twin_got(1)
                product(theirs_at[1])
            if c == 1:
                twin_got(2)
                product(theirs_at[2])
        product(across)
        twin_got(3)
        product(theirs_at[3])

        for k in range(4):
            remote(T.at[k], A.at[k], sa.at[k], ra.at[k], sib).wait_send()
        for c in range(chunks):
            for k in range(3):
                ship(k, c, nf).wait_send()
            for k in range(2):
                step(k, c).wait_send()
            second_step(c).wait_send()
            for k, q in enumerate((me, source, other, across)):
                twin(k, q, c).wait_send()
        for flush in flushes[-2:]:
            flush.wait()

    dma = pltpu.SemaphoreType.DMA
    anywhere, vmem = pl.BlockSpec(memory_space=pl.ANY), pl.BlockSpec(memory_space=pltpu.VMEM)
    block = lambda n: pltpu.VMEM((n, rows, width), BF16)
    out_shape = [
        jax.ShapeDtypeStruct((rows, width), F32),
        jax.ShapeDtypeStruct((8, rows, width), BF16),
    ]
    out_specs = [vmem, vmem]
    operands = [left, first, gain, *extras]
    in_specs = [vmem] * len(operands)
    later = []
    if multiply:
        out_shape.append(jax.ShapeDtypeStruct((8, rows, out_cols), F32))
        out_specs.append(anywhere)
        operands.append(second)
        in_specs.append(anywhere)
        later = [pltpu.VMEM(second.shape, BF16), pltpu.VMEM((2, rows, out_cols), F32)]
    if norm_back:
        out_shape.append(jax.ShapeDtypeStruct((1, width), F32))
        out_specs.append(vmem)
    return pl.pallas_call(
        kernel,
        out_shape=out_shape,
        in_specs=in_specs,
        out_specs=out_specs,
        scratch_shapes=[
            block(4),
            block(4),
            block(3),
            block(3),
            pltpu.VMEM((rows, width), F32),
            dma((3,)),
            dma((4,)),
            dma((4,)),
            dma((3, chunks)),
            dma((3, chunks)),
            dma((2, chunks)),
            dma((2, chunks)),
            dma((chunks,)),
            dma((chunks,)),
            dma((4, chunks)),
            dma((4, chunks)),
            *later,
        ],
        cost_estimate=busy(80),
        compiler_params=pltpu.CompilerParams(
            collective_id=cid, has_side_effects=True, vmem_limit_bytes=58 << 20
        ),
    )(*operands)


def unit_pairs(a, main):
    tail = a[:, 2 * main :]
    size = tail.shape[1]
    turned = pltpu.roll(tail, size // 2, 1)
    left = lax.broadcasted_iota(jnp.int32, tail.shape, 1) < size // 2
    return (a[:, :main], a[:, main : 2 * main]), (jnp.where(left, tail, turned), jnp.where(left, turned, tail)), left


def units_forward(x, weight, scales, units, main):
    blocks, rows, width = x.shape
    cols = weight.shape[1]

    def kernel(x_ref, w_ref, s_ref, up_ref, hidden_ref, scaled_ref):
        scale = s_ref[pl.ds(pl.program_id(0), 1), :][:, 0:1]
        for a in range(0, cols, 512):
            b = min(a + 512, cols)
            up_ref[:, a:b] = jnp.dot(x_ref[...], w_ref[:, a:b], preferred_element_type=F32)
        (g, u), (g_tail, u_tail), _ = unit_pairs(up_ref[...], main)
        hidden = g * sigmoid(g) * u
        tail = (g_tail * sigmoid(g_tail) * u_tail)[:, : units - main]
        hidden_ref[:, :main] = hidden.astype(BF16)
        hidden_ref[:, main:] = tail.astype(BF16)
        scaled_ref[:, :main] = (hidden * scale).astype(BF16)
        scaled_ref[:, main:] = (tail * scale).astype(BF16)

    row = lambda n: pl.BlockSpec((rows, n), lambda i: (i, 0))
    whole = lambda a: pl.BlockSpec(a.shape, lambda i: (0, 0))
    tokens = blocks * rows
    return pl.pallas_call(
        kernel,
        grid=(blocks,),
        in_specs=[row(width), whole(weight), whole(scales)],
        out_specs=[row(cols), row(units), row(units)],
        out_shape=[
            jax.ShapeDtypeStruct((tokens, cols), F32),
            jax.ShapeDtypeStruct((tokens, units), BF16),
            jax.ShapeDtypeStruct((tokens, units), BF16),
        ],
        cost_estimate=busy(20),
        compiler_params=pltpu.CompilerParams(vmem_limit_bytes=48 << 20),
    )(x.reshape(tokens, width), weight, scales)


def units_backward(cot, weight, upgate, scales, units, main):
    blocks, rows, width = cot.shape
    cols = upgate.shape[1]

    def kernel(c_ref, w_ref, up_ref, s_ref, low_ref):
        scale = s_ref[pl.ds(pl.program_id(0), 1), :][:, 0:1]
        pair, pair_tail, left = unit_pairs(up_ref[...], main)
        tail_rows = w_ref[main:, :]
        grad = dot(c_ref[...], w_ref[:main, :], NT) * scale
        grad_tail = dot(c_ref[...], jnp.concatenate([tail_rows, tail_rows], axis=0), NT) * scale

        def both(g, u, grad):
            s = sigmoid(g)
            return grad * u * s * (1.0 + g * (1.0 - s)), grad * g * s

        gate_grad, up_grad = both(*pair, grad)
        low_ref[:, :main] = gate_grad.astype(BF16)
        low_ref[:, main : 2 * main] = up_grad.astype(BF16)
        gate_grad, up_grad = both(*pair_tail, grad_tail)
        low_ref[:, 2 * main :] = jnp.where(left, gate_grad, up_grad).astype(BF16)

    row = lambda n: pl.BlockSpec((rows, n), lambda i: (i, 0))
    whole = lambda a: pl.BlockSpec(a.shape, lambda i: (0, 0))
    tokens = blocks * rows
    return pl.pallas_call(
        kernel,
        grid=(blocks,),
        in_specs=[row(width), whole(weight), row(cols), whole(scales)],
        out_specs=row(cols),
        out_shape=jax.ShapeDtypeStruct((tokens, cols), BF16),
        cost_estimate=busy(12),
        compiler_params=pltpu.CompilerParams(vmem_limit_bytes=48 << 20),
    )(cot.reshape(tokens, width), weight, upgate, scales)


def gather_small(x, n_dp, n_z, cid):
    rows, cols = x.shape
    count = n_dp * n_z

    def kernel(x_ref, o_ref, lsem, ssem, rsem):
        flat = lax.axis_index("dp") * n_z + lax.axis_index("fsdp")
        bar = pltpu.get_barrier_semaphore()

        def device(o):
            other = lax.rem(flat + o, count)
            return (other // n_z, lax.rem(other, n_z))

        def copy(o):
            return pltpu.make_async_remote_copy(
                x_ref, o_ref.at[flat], ssem.at[o - 1], rsem.at[o - 1], device_id=device(o), device_id_type=MESH
            )

        def greet(o, _):
            pl.semaphore_signal(bar, inc=1, device_id=device(o), device_id_type=MESH)
            return 0

        def send(o, _):
            copy(o).start()
            return 0

        def wait(o, _):
            copy(o).wait()
            return 0

        lax.fori_loop(1, count, greet, 0)
        local = pltpu.make_async_copy(x_ref, o_ref.at[flat], lsem)
        local.start()
        pl.semaphore_wait(bar, count - 1)
        lax.fori_loop(1, count, send, 0)
        lax.fori_loop(1, count, wait, 0)
        local.wait()

    dma = pltpu.SemaphoreType.DMA
    return pl.pallas_call(
        kernel,
        out_shape=jax.ShapeDtypeStruct((count, rows, cols), x.dtype),
        in_specs=[pl.BlockSpec(memory_space=pl.ANY)],
        out_specs=pl.BlockSpec(memory_space=pl.ANY),
        scratch_shapes=[dma, dma((count - 1,)), dma((count - 1,))],
        cost_estimate=busy(15),
        compiler_params=pltpu.CompilerParams(collective_id=cid, has_side_effects=True),
    )(x)


def scatter_small(x, n_dp, n_z, cid):
    count, rows, cols = x.shape

    def kernel(x_ref, o_ref, lsem, ssem, rsem):
        flat = lax.axis_index("dp") * n_z + lax.axis_index("fsdp")
        bar = pltpu.get_barrier_semaphore()

        def device(o):
            other = lax.rem(flat + o, count)
            return (other // n_z, lax.rem(other, n_z))

        def copy(o):
            return pltpu.make_async_remote_copy(
                x_ref.at[lax.rem(flat + o, count)], o_ref.at[flat], ssem.at[o - 1], rsem.at[o - 1], device_id=device(o), device_id_type=MESH
            )

        def greet(o, _):
            pl.semaphore_signal(bar, inc=1, device_id=device(o), device_id_type=MESH)
            return 0

        def send(o, _):
            copy(o).start()
            return 0

        def wait(o, _):
            copy(o).wait()
            return 0

        lax.fori_loop(1, count, greet, 0)
        local = pltpu.make_async_copy(x_ref.at[flat], o_ref.at[flat], lsem)
        local.start()
        pl.semaphore_wait(bar, count - 1)
        lax.fori_loop(1, count, send, 0)
        lax.fori_loop(1, count, wait, 0)
        local.wait()

    dma = pltpu.SemaphoreType.DMA
    return pl.pallas_call(
        kernel,
        out_shape=jax.ShapeDtypeStruct((count, rows, cols), x.dtype),
        in_specs=[pl.BlockSpec(memory_space=pl.ANY)],
        out_specs=pl.BlockSpec(memory_space=pl.ANY),
        scratch_shapes=[dma, dma((count - 1,)), dma((count - 1,))],
        cost_estimate=busy(15),
        compiler_params=pltpu.CompilerParams(collective_id=cid, has_side_effects=True),
    )(x)


def pack(parts, unit):
    flat = jnp.concatenate([part.reshape(-1) for part in parts])
    size = flat.shape[0]
    full = -(-size // (128 * unit)) * 128 * unit
    return jnp.pad(flat, (0, full - size)).reshape(-1, 128)


def dot(a, b, dims=NN, out=F32):
    return lax.dot_general(a, b, dims, preferred_element_type=F32).astype(out)


def local(
    n_dp,
    n_z,
    tokens,
    cotangent,
    group_ids,
    norm_first,
    input_weight,
    decay_weight,
    conv_weight,
    decay_scale,
    decay_bias,
    output_gain,
    output_weight,
    norm_second,
    upgate_weight,
    down_weight,
):
    count = n_dp * n_z
    rows, width = tokens.shape
    all_heads = decay_scale.shape[0]
    heads = all_heads // n_dp
    taps = conv_weight.shape[0]
    own_conv = conv_weight.shape[1]
    own_d = norm_first.shape[0]
    units = upgate_weight.shape[1] // (2 * n_dp)
    key, value = heads * DK, heads * DV
    cols = 2 * key + 2 * value + 128
    square = n_dp == 8 and n_z == 4
    here = lax.axis_index("dp")
    flat = here * n_z + lax.axis_index("fsdp")

    def spread(x, cid):
        if square:
            return ag_square(x, cid).reshape(n_dp * rows, width)
        return lax.all_gather(x, "dp", axis=0, tiled=True)

    def total(x, cid):
        if square:
            return rs_square(x.reshape(n_dp, rows, width), cid)
        return lax.psum_scatter(x, "dp", scatter_dimension=0, tiled=True).astype(F32)

    def by_dp(a, parts):
        return a.reshape(a.shape[0], n_dp, parts)

    main = units // 128 * 128
    bounds = (0, key, 2 * key, 2 * key + value, 2 * key + 2 * value)
    gates = by_dp(upgate_weight[:, : n_dp * units], units)
    ups = by_dp(upgate_weight[:, n_dp * units :], units)
    up_mine = jnp.concatenate(
        [gates[:, :, :main], ups[:, :, :main], gates[:, :, main:], ups[:, :, main:]], axis=2
    ).transpose(1, 0, 2)
    decay_cols = jnp.concatenate(
        [
            by_dp(decay_weight[:, :all_heads], heads),
            by_dp(decay_weight[:, all_heads:], heads),
            jnp.zeros((own_d, n_dp, 128 - 2 * heads), BF16),
        ],
        axis=2,
    ).transpose(1, 0, 2)

    def whole_rows(a):
        a = lax.all_gather(a[:, None], "fsdp", axis=1, tiled=True)
        return a.reshape(width, a.shape[-1])

    conv_size = taps * own_conv
    inputs = tokens.astype(F32)
    first_root = lax.rsqrt(jnp.mean(inputs * inputs, axis=-1, keepdims=True) + EPSILON)
    if square:
        small = jnp.concatenate(
            [norm_first] * (128 // own_d)
            + [norm_second] * (128 // own_d)
            + [jnp.broadcast_to(group_ids.astype(BF16), (128,)), jnp.zeros((640,), BF16), conv_weight.reshape(-1)]
        ).reshape(16, 128)
        in_full, up_plane, normed_all, cot_all, small = begin(
            input_weight, decay_cols, up_mine, tokens, cotangent, small, bounds, n_z, 1
        )
        in_full = in_full.reshape(width, cols)
        normed_all = normed_all.reshape(n_dp * rows, width)
        cot_all = cot_all.reshape(n_dp * rows, width)
        conv_full = small[:, 8:].reshape(count, taps, own_conv)
        first_full = small[:, 0, :own_d]
        second_full = small[:, 1, :own_d]
        every_id = small[:, 2, 0]
        output_weight, down_weight, up_plane = lax.optimization_barrier(
            (output_weight, down_weight, up_plane, small)
        )[:3]
    else:
        in_mine = [
            by_dp(input_weight[:, n_dp * a : n_dp * b], b - a).transpose(1, 0, 2)
            for a, b in zip(bounds[:-1], bounds[1:])
        ]
        in_mine = jnp.concatenate(in_mine + [decay_cols], axis=2)
        in_full = whole_rows(lax.all_to_all(in_mine, "dp", 0, 0, tiled=True))
        up_plane = lax.all_to_all(up_mine, "dp", 0, 0, tiled=True)
        small = gather_small(
            pack((conv_weight, norm_first, norm_second, group_ids.astype(BF16)), 16), n_dp, n_z, 1
        ).reshape(count, -1)
        conv_full = small[:, :conv_size].reshape(count, taps, own_conv)
        first_full = small[:, conv_size : conv_size + own_d]
        second_full = small[:, conv_size + own_d : conv_size + 2 * own_d]
        every_id = small[:, conv_size + 2 * own_d]
    out_full = lax.all_gather(output_weight, "fsdp", axis=0, tiled=True)
    up_full = whole_rows(up_plane)
    down_full = lax.all_gather(down_weight, "fsdp", axis=0, tiled=True)
    conv_full = conv_full.transpose(1, 0, 2).reshape(taps, -1)
    first_full = first_full.reshape(1, width).astype(F32)
    second_full = second_full.reshape(1, width).astype(F32)
    every_id = every_id.astype(jnp.int32)
    scales = 1.0 / jnp.sum((every_id[:, None] == every_id[None, :]).astype(F32), axis=0).reshape(n_dp, n_z)
    scales = lax.dynamic_index_in_dim(scales, lax.axis_index("fsdp"), axis=1, keepdims=False)
    seed = cotangent.astype(F32) * lax.dynamic_index_in_dim(scales, here, axis=0, keepdims=False)
    lanes_of_scales = jnp.broadcast_to(scales[:, None], (n_dp, 128))
    scales = jnp.broadcast_to(scales[:, None, None], (n_dp, rows, 1)).reshape(n_dp * rows, 1)
    if not square:
        normed_all = spread((inputs * first_root * first_full).astype(BF16), 2)
        cot_all = spread(cotangent, 3)

    def conv_columns(start, size):
        return lax.dynamic_slice_in_dim(conv_full, start + here * size, size, axis=1)

    conv_mine = jnp.concatenate(
        [conv_columns(0, key), conv_columns(n_dp * key, key), conv_columns(2 * n_dp * key, value)], axis=1
    ).astype(F32)
    decay_mine = jnp.pad(
        jnp.stack(
            [
                lax.dynamic_slice_in_dim(decay_scale, here * heads, heads),
                lax.dynamic_slice_in_dim(decay_bias, here * heads, heads),
            ]
        ),
        ((0, 0), (0, 128 - heads)),
    )
    gain = output_gain[None, :]

    projected = dot(normed_all, in_full)
    mixed, inverse, solved, core = mixer_forward(projected, conv_mine, decay_mine, gain, heads, rows)
    if square:
        middle, second_all = relay(
            mixed.reshape(n_dp, rows, value), out_full, None, NN, NN, second_full, (tokens,), False, 4
        )
        upgate, hidden, hidden_seed = units_forward(second_all, up_full, lanes_of_scales, units, main)
        second_all = second_all.reshape(n_dp * rows, width)
    else:
        middle = inputs + total(dot(mixed, out_full, out=BF16), 4)
        second_root = lax.rsqrt(jnp.mean(middle * middle, axis=-1, keepdims=True) + EPSILON)
        second_all = spread((middle * second_root * second_full).astype(BF16), 5)
        upgate = dot(second_all, up_full)

        def halves_of(a):
            return (a[:, :main], a[:, main : 2 * main]), (a[:, 2 * main : main + units], a[:, main + units :])

        acts = [(g, u, jax.nn.sigmoid(g)) for g, u in halves_of(upgate)]
        hidden = jnp.concatenate([g * s * u for g, u, s in acts], axis=1)
        hidden_seed = (hidden * scales).astype(BF16)
        hidden = hidden.astype(BF16)

    down_grad = dot(hidden_seed, cot_all, TN, out=BF16)
    down_grad, cot_all = lax.optimization_barrier((down_grad, cot_all))
    if square:
        upgate_low = units_backward(
            cot_all.reshape(n_dp, rows, width), down_full, upgate, lanes_of_scales, units, main
        )
    else:
        hidden_grad = dot(cot_all, down_full, NT) * scales
        parts = list(zip(acts, (hidden_grad[:, :main], hidden_grad[:, main:])))
        upgate_low = jnp.concatenate(
            [x for (g, u, s), grad in parts for x in (grad * u * s * (1.0 + g * (1.0 - s)), grad * g * s)], axis=1
        ).astype(BF16)
    upgate_grad = dot(second_all, upgate_low, TN, out=BF16)
    upgate_low, upgate_grad = lax.optimization_barrier((upgate_low, upgate_grad))

    def norm_back(v, root, gain_row, grad):
        hat = v * root
        scaled = grad * gain_row
        gain_grad = jnp.sum(grad * hat, axis=0)
        return root * (scaled - hat * jnp.mean(scaled * hat, axis=-1, keepdims=True)), gain_grad

    def owned_rows(a):
        return lax.psum_scatter(a, "fsdp", scatter_dimension=0, tiled=True)

    def owned_parts(a):
        a = a.reshape(n_dp, n_z, own_d, a.shape[-1]).transpose(1, 0, 2, 3)
        return lax.psum_scatter(a.reshape(width, -1), "fsdp", scatter_dimension=0, tiled=True)

    def to_owners(a):
        a = lax.all_to_all(a.reshape(n_dp, own_d, -1), "dp", 0, 0, tiled=True)
        return a.transpose(1, 0, 2).astype(F32)

    down_total = owned_rows(down_grad)
    upgate_low, upgate_grad, down_total = lax.optimization_barrier((upgate_low, upgate_grad, down_total))
    upgate_sum = owned_parts(upgate_grad)
    if square:
        middle_grad, middle_all, mixed_grad, second_grad = relay(
            upgate_low.reshape(n_dp, rows, 2 * units), up_full, out_full, NT, NT, second_full, (middle, seed), True, 6
        )
        middle_all = middle_all.reshape(n_dp * rows, width)
        mixed_grad = mixed_grad.reshape(n_dp * rows, value)
    else:
        normed_two_grad = total(dot(upgate_low, up_full, NT, out=BF16), 6)
        middle_part, second_grad = norm_back(middle, second_root, second_full, normed_two_grad)
        middle_grad = seed + middle_part
        middle_all = spread(middle_grad.astype(BF16), 8)
        mixed_grad = dot(middle_all, out_full, NT)
    output_grad = dot(mixed, middle_all, TN, out=BF16)
    mixed_grad, output_grad, upgate_sum = lax.optimization_barrier((mixed_grad, output_grad, upgate_sum))
    output_total = owned_rows(output_grad)
    projected_low, conv_grad, gain_grad, decay_grad = mixer_backward(
        projected, conv_mine, decay_mine, gain, inverse, solved, core, mixed_grad, heads, rows
    )
    projected_low, output_total = lax.optimization_barrier((projected_low, output_total))
    in_grad = dot(normed_all, projected_low, TN, out=BF16)
    projected_low, in_grad = lax.optimization_barrier((projected_low, in_grad))
    back_one = dot(projected_low, in_full, NT, out=BF16)
    in_sum = owned_parts(in_grad)
    normed_one_grad = total(back_one, 9)
    hidden, normed_one_grad = lax.optimization_barrier((hidden, normed_one_grad))
    result = middle + total(dot(hidden, down_full, out=BF16), 7)
    input_part, first_grad = norm_back(inputs, first_root, first_full, normed_one_grad)
    tokens_grad = middle_grad + input_part

    down_total = down_total.astype(F32)
    output_total = output_total.astype(F32)
    up_total = to_owners(upgate_sum)
    upgate_total = jnp.concatenate(
        [
            jnp.concatenate([a, b], axis=2).reshape(own_d, -1)
            for a, b in (
                (up_total[:, :, :main], up_total[:, :, 2 * main : main + units]),
                (up_total[:, :, main : 2 * main], up_total[:, :, main + units :]),
            )
        ],
        axis=1,
    )
    in_total = to_owners(in_sum)
    input_total = jnp.concatenate(
        [in_total[:, :, a:b].reshape(own_d, -1) for a, b in zip(bounds[:-1], bounds[1:])], axis=1
    )
    start = bounds[-1]
    decay_total = jnp.concatenate(
        [
            in_total[:, :, start : start + heads].reshape(own_d, -1),
            in_total[:, :, start + heads : start + 2 * heads].reshape(own_d, -1),
        ],
        axis=1,
    )

    share = key // own_conv, value // own_conv
    owner = jnp.concatenate(
        [
            here * share[0] + jnp.arange(share[0]),
            (n_dp + here) * share[0] + jnp.arange(share[0]),
            2 * n_dp * share[0] + here * share[1] + jnp.arange(share[1]),
        ]
    )
    blocks = conv_grad.reshape(taps, -1, own_conv).transpose(1, 0, 2).reshape(-1, taps * own_conv)
    for_owner = owner[None, :] == jnp.arange(count)[:, None]
    everyone = jnp.concatenate([gain_grad.reshape(-1), decay_grad[:, :heads].reshape(-1)])
    packets = jnp.concatenate(
        [
            first_grad.reshape(count, own_d),
            second_grad.reshape(count, own_d),
            jnp.sum(jnp.where(for_owner[:, :, None], blocks[None], 0.0), axis=1),
            jnp.broadcast_to(everyone[None], (count, everyone.size)),
        ],
        axis=1,
    )
    size = packets.shape[1]
    lines = -(-size // 1024) * 8
    packets = jnp.pad(packets, ((0, 0), (0, lines * 128 - size))).reshape(count, lines, 128)
    shared = scatter_small(packets, n_dp, n_z, 10).reshape(count, -1)
    summed = jnp.sum(shared, axis=0)
    first_total = summed[:own_d]
    second_total = summed[own_d : 2 * own_d]
    start = 2 * own_d + taps * own_conv
    conv_total = summed[2 * own_d : start].reshape(taps, own_conv)
    gain_total = summed[start : start + gain_grad.size]
    start += gain_grad.size
    scale_bias = jnp.sum(shared[:, start : start + 2 * heads].reshape(n_dp, n_z, 2, heads), axis=1)
    scale_total = scale_bias[:, 0].reshape(-1)
    bias_total = scale_bias[:, 1].reshape(-1)
    return (
        result,
        tokens_grad,
        first_total,
        input_total,
        decay_total,
        conv_total,
        scale_total,
        bias_total,
        gain_total,
        output_total,
        second_total,
        upgate_total,
        down_total,
    )


def solution(mesh):
    both = ("dp", "fsdp")
    rows, vector = P(both, None), P(both)
    return jax.shard_map(
        functools.partial(local, mesh.shape["dp"], mesh.shape["fsdp"]),
        mesh=mesh,
        in_specs=(
            rows, rows, vector, vector, rows, rows, P(None, both), P(), P(), P(), rows, vector, rows, rows,
        ),
        out_specs=(
            rows, rows, vector, rows, rows, P(None, both), P(), P(), P(), rows, vector, rows, rows,
        ),
        check_vma=False,
    )
```

```python
import functools

import jax
import jax.numpy as jnp
from jax import lax
from jax.experimental import pallas as pl
from jax.experimental.pallas import tpu as pltpu
from jax.sharding import PartitionSpec as P

MESH = pl.DeviceIdType.MESH
F32 = jnp.float32
BF16 = jnp.bfloat16
EPSILON = 1e-06
DK = 128
DV = 256
BASE = 8
NN = (((1,), (0,)), ((), ()))
NT = (((1,), (1,)), ((), ()))
TN = (((0,), (0,)), ((), ()))


def dot1(a, b, dims=NN):
    return lax.dot_general(a.astype(BF16), b.astype(BF16), dims, preferred_element_type=F32)


def halves(a):
    if a.dtype == BF16:
        return (a,)
    high = a.astype(BF16)
    return (high, (a - high.astype(F32)).astype(BF16))


def dot3(a, b, dims=NN):
    a, b = halves(a), halves(b)
    total = lax.dot_general(a[0], b[0], dims, preferred_element_type=F32)
    if len(a) > 1:
        total = total + lax.dot_general(a[1], b[0], dims, preferred_element_type=F32)
    if len(b) > 1:
        total = total + lax.dot_general(a[0], b[1], dims, preferred_element_type=F32)
    return total


def dot6(a, b, dims=NN):
    return lax.dot_general(a, b, dims, precision=lax.Precision.HIGHEST, preferred_element_type=F32)


def shift_down(v, n, rows):
    if n == 0:
        return v
    return jnp.where(rows >= n, pltpu.roll(v, n, 0), 0.0)


def shift_up(v, n, rows):
    if n == 0:
        return v
    length = v.shape[0]
    return jnp.where(rows < length - n, pltpu.roll(v, length - n, 0), 0.0)


def conv(c, taps, rows):
    count = taps.shape[0]
    total = c * taps[count - 1 : count]
    for j in range(count - 1):
        total = total + shift_down(c, count - 1 - j, rows) * taps[j : j + 1]
    return total


def sigmoid(v):
    return 1.0 / (1.0 + jnp.exp(-v))


def softplus(v):
    return jnp.maximum(v, 0.0) + jnp.log1p(jnp.exp(-jnp.abs(v)))


def unit_inverses(lowers, row_ids, col_ids):
    length = lowers[0].shape[0]
    size = BASE
    same = row_ids // size == col_ids // size
    pick = jnp.where(col_ids[:, :128] == lax.rem(row_ids[:, :128], size), 1.0, 0.0).astype(BF16)
    lanes = lax.broadcasted_iota(jnp.int32, (length // size, size, 128), 2)
    places = lax.broadcasted_iota(jnp.int32, (length // size, size, 128), 1)
    compact = [dot3(jnp.where(same, lower, 0.0), pick).reshape(length // size, size, 128) for lower in lowers]
    solved = [jnp.where(lanes == places, 1.0, 0.0) for _ in lowers]
    for j in range(size - 1):
        solved = [x - a[:, :, j : j + 1] * x[:, j : j + 1, :] for a, x in zip(compact, solved)]
    inverses = [jnp.where(same, dot3(x.reshape(length, 128), pick, NT), 0.0) for x in solved]
    while size < length:
        wide = 2 * size
        off = (row_ids // wide == col_ids // wide) & (row_ids // size != col_ids // size)
        inner = [dot3(jnp.where(off, lower, 0.0), inverse) for lower, inverse in zip(lowers, inverses)]
        inverses = [inverse - dot3(inverse, x) for inverse, x in zip(inverses, inner)]
        size = wide
    return inverses


def common(proj, decay, heads, length):
    rows = lax.broadcasted_iota(jnp.int32, (length, 1), 0)
    row_ids = lax.broadcasted_iota(jnp.int32, (length, length), 0)
    col_ids = lax.broadcasted_iota(jnp.int32, (length, length), 1)
    raw = proj[:, heads * 768 :]
    lanes = lax.broadcasted_iota(jnp.int32, raw.shape, 1)
    shifted = raw + decay[1:2]
    rate = jnp.where(lanes < heads, -jnp.exp(decay[0:1]) * softplus(shifted), 0.0)
    beta = sigmoid(raw)
    cumulated = dot6(jnp.where(row_ids >= col_ids, 1.0, 0.0), rate)
    return rows, row_ids, col_ids, raw, lanes, shifted, rate, beta, cumulated, cumulated.T


def head_parts(h, heads):
    key = slice(h * DK, (h + 1) * DK)
    keyk = slice((heads + h) * DK, (heads + h + 1) * DK)
    val = slice(heads * DV + h * DV, heads * DV + (h + 1) * DV)
    gat = slice(2 * heads * DV + h * DV, 2 * heads * DV + (h + 1) * DV)
    return key, keyk, val, gat


def mixer_forward_kernel(heads, proj_ref, taps_ref, decay_ref, gain_ref, mixed_ref, inv_ref, solved_ref, core_ref):
    length = proj_ref.shape[0]
    decay = decay_ref[...]
    gain = gain_ref[...]
    rows, row_ids, col_ids, raw, lanes, shifted, rate, beta, cumulated, cum_t = common(
        proj_ref[...], decay, heads, length
    )
    def active(cols):
        y = conv(proj_ref[:, cols], taps_ref[:, cols], rows)
        return y * sigmoid(y)

    parts = [head_parts(h, heads) for h in range(heads)]
    queries, keys, values, growths, betas, lowers = [], [], [], [], [], []
    for h, (qs, ks, vs, gs) in enumerate(parts):
        k = active(ks)
        k = (k * lax.rsqrt(jnp.sum(k * k, axis=-1, keepdims=True) + EPSILON)).astype(BF16)
        beta_h = beta[:, heads + h : heads + h + 1]
        gap = cumulated[:, h : h + 1] - cum_t[h : h + 1, :]
        growth = jnp.where(row_ids >= col_ids, jnp.exp(jnp.where(row_ids >= col_ids, gap, 0.0)), 0.0)
        keys.append(k)
        growths.append(growth)
        betas.append(beta_h)
        lowers.append(jnp.where(row_ids > col_ids, growth * dot1(k, k, NT) * beta_h, 0.0))
    inverses = unit_inverses(lowers, row_ids, col_ids)
    for h, (qs, ks, vs, gs) in enumerate(parts):
        q = active(qs)
        q = (q * lax.rsqrt(jnp.sum(q * q, axis=-1, keepdims=True) + EPSILON) * DK ** (-0.5)).astype(BF16)
        v = active(vs).astype(BF16)
        inv_ref[h] = inverses[h]
        solved = dot3(inverses[h], betas[h] * v.astype(F32))
        core = dot3(growths[h] * dot1(q, keys[h], NT), solved)
        solved_ref[:, h * DV : (h + 1) * DV] = solved
        core_ref[:, h * DV : (h + 1) * DV] = core
        gate = proj_ref[:, gs]
        normed = core * lax.rsqrt(jnp.mean(core * core, axis=-1, keepdims=True) + EPSILON) * gain
        mixed_ref[:, h * DV : (h + 1) * DV] = (normed * (gate * sigmoid(gate))).astype(BF16)


def mixer_forward(proj, taps, decay, gain, heads, length):
    tokens, width = proj.shape
    seqs = tokens // length
    hv = heads * DV
    row = lambda cols: pl.BlockSpec((length, cols), lambda s: (s, 0))
    whole = lambda a: pl.BlockSpec(a.shape, lambda s: (0,) * a.ndim)
    return pl.pallas_call(
        functools.partial(mixer_forward_kernel, heads),
        grid=(seqs,),
        in_specs=[row(width), whole(taps), whole(decay), whole(gain)],
        out_specs=[row(hv), pl.BlockSpec((None, heads, length, length), lambda s: (s, 0, 0, 0)), row(hv), row(hv)],
        out_shape=[
            jax.ShapeDtypeStruct((tokens, hv), BF16),
            jax.ShapeDtypeStruct((seqs, heads, length, length), F32),
            jax.ShapeDtypeStruct((tokens, hv), F32),
            jax.ShapeDtypeStruct((tokens, hv), F32),
        ],
        cost_estimate=busy(55), compiler_params=pltpu.CompilerParams(vmem_limit_bytes=48 << 20),
    )(proj, taps, decay, gain)


def mixer_backward_kernel(
    heads, proj_ref, taps_ref, decay_ref, gain_ref, inv_ref, solved_ref, core_ref, grad_ref,
    low_ref, conv_ref, gain_grad_ref, decay_grad_ref,
):
    length = proj_ref.shape[0]
    count = taps_ref.shape[0]
    decay = decay_ref[...]
    gain = gain_ref[...]
    rows, row_ids, col_ids, raw, lanes, shifted, rate, beta, cumulated, cum_t = common(
        proj_ref[...], decay, heads, length
    )
    within = row_ids >= col_ids
    strict = row_ids > col_ids

    @pl.when(pl.program_id(0) == 0)
    def _():
        conv_ref[...] = jnp.zeros_like(conv_ref)
        gain_grad_ref[...] = jnp.zeros_like(gain_grad_ref)
        decay_grad_ref[...] = jnp.zeros_like(decay_grad_ref)

    cum_grad = jnp.zeros(raw.shape, F32)
    beta_grad = jnp.zeros(raw.shape, F32)
    for h in range(heads):
        qs, ks, vs, gs = head_parts(h, heads)
        hs = slice(h * DV, (h + 1) * DV)

        def active(cols):
            y = conv(proj_ref[:, cols], taps_ref[:, cols], rows)
            s = sigmoid(y)
            return y * s, s * (1.0 + y * (1.0 - s))

        def conv_back(cols, grad):
            c = proj_ref[:, cols]
            total = grad * taps_ref[count - 1 : count, cols]
            conv_ref[count - 1 : count, cols] += jnp.sum(grad * c, axis=0, keepdims=True)
            for j in range(count - 1):
                n = count - 1 - j
                total = total + shift_up(grad, n, rows) * taps_ref[j : j + 1, cols]
                conv_ref[j : j + 1, cols] += jnp.sum(grad * shift_down(c, n, rows), axis=0, keepdims=True)
            low_ref[:, cols] = total.astype(BF16)

        core = core_ref[:, hs]
        gate = proj_ref[:, gs]
        gate_sig = sigmoid(gate)
        grad = grad_ref[:, hs]
        root = lax.rsqrt(jnp.mean(core * core, axis=-1, keepdims=True) + EPSILON)
        normed = core * root
        silu_gate = gate * gate_sig
        gain_grad_ref[...] += jnp.sum(grad * normed * silu_gate, axis=0, keepdims=True)
        low_ref[:, gs] = (grad * normed * gain * gate_sig * (1.0 + gate * (1.0 - gate_sig))).astype(BF16)
        normed_grad = grad * gain * silu_gate
        core_grad = root * (normed_grad - normed * jnp.mean(normed_grad * normed, axis=-1, keepdims=True))

        q_act, q_slope = active(qs)
        q_root = lax.rsqrt(jnp.sum(q_act * q_act, axis=-1, keepdims=True) + EPSILON)
        q_unit = q_act * q_root
        q = (q_unit * DK ** (-0.5)).astype(BF16)
        k_act, k_slope = active(ks)
        k_root = lax.rsqrt(jnp.sum(k_act * k_act, axis=-1, keepdims=True) + EPSILON)
        k_unit = k_act * k_root
        k = k_unit.astype(BF16)
        v_act, v_slope = active(vs)
        v = v_act.astype(BF16).astype(F32)
        beta_h = beta[:, heads + h : heads + h + 1]
        gap = cumulated[:, h : h + 1] - cum_t[h : h + 1, :]
        growth = jnp.where(within, jnp.exp(jnp.where(within, gap, 0.0)), 0.0)
        decayed_gram = jnp.where(strict, growth * dot1(k, k, NT), 0.0)
        weights = growth * dot1(q, k, NT)
        inverse = inv_ref[h]
        solved = solved_ref[:, hs]
        solved_grad = dot3(weights, core_grad, TN)
        weights_grad = dot3(core_grad, solved, NT)
        value_grad = dot3(inverse, solved_grad, TN)
        lower_grad = jnp.where(strict, -dot3(value_grad, solved, NT), 0.0)
        gap_part = lower_grad * decayed_gram
        beta_col = jnp.sum(gap_part, axis=-1, keepdims=True) + jnp.sum(value_grad * v, axis=-1, keepdims=True)
        gap_grad = gap_part * beta_h + weights_grad * weights
        cum_col = jnp.sum(gap_grad, axis=-1, keepdims=True)
        cum_row = jnp.sum(gap_grad, axis=0, keepdims=True)
        cum_col = cum_col - jnp.broadcast_to(cum_row, (8, length)).T[:, 0:1]
        gram_grad = lower_grad * growth * beta_h
        score_grad = weights_grad * growth
        k_grad = dot3(gram_grad, k) + dot3(gram_grad, k, TN) + dot3(score_grad, q, TN)
        q_grad = dot3(score_grad, k)
        cum_grad = jnp.where(lanes == h, cum_col, cum_grad)
        beta_grad = jnp.where(lanes == heads + h, beta_col, beta_grad)

        q_grad = q_grad * DK ** (-0.5)
        q_grad = q_root * (q_grad - q_unit * jnp.sum(q_grad * q_unit, axis=-1, keepdims=True))
        conv_back(qs, q_grad * q_slope)
        k_grad = k_root * (k_grad - k_unit * jnp.sum(k_grad * k_unit, axis=-1, keepdims=True))
        conv_back(ks, k_grad * k_slope)
        conv_back(vs, value_grad * beta_h * v_slope)

    rate_grad = dot6(jnp.where(col_ids >= row_ids, 1.0, 0.0), cum_grad)
    bias_part = rate_grad * -jnp.exp(decay[0:1]) * sigmoid(shifted)
    raw_grad = jnp.where(lanes < heads, bias_part, beta_grad * beta * (1.0 - beta))
    low_ref[:, heads * 768 :] = raw_grad.astype(BF16)
    decay_grad_ref[0:1] += jnp.sum(jnp.where(lanes < heads, rate_grad * rate, 0.0), axis=0, keepdims=True)
    decay_grad_ref[1:2] += jnp.sum(jnp.where(lanes < heads, bias_part, 0.0), axis=0, keepdims=True)


def mixer_backward(proj, taps, decay, gain, inverse, solved, core, grad, heads, length):
    tokens, width = proj.shape
    seqs = tokens // length
    hv = heads * DV
    row = lambda cols: pl.BlockSpec((length, cols), lambda s: (s, 0))
    whole = lambda a: pl.BlockSpec(a.shape, lambda s: (0,) * a.ndim)
    return pl.pallas_call(
        functools.partial(mixer_backward_kernel, heads),
        grid=(seqs,),
        in_specs=[row(width), whole(taps), whole(decay), whole(gain),
                  pl.BlockSpec((None, heads, length, length), lambda s: (s, 0, 0, 0)), row(hv), row(hv), row(hv)],
        out_specs=[row(width), whole(taps), whole(gain), whole(decay)],
        out_shape=[
            jax.ShapeDtypeStruct((tokens, width), BF16),
            jax.ShapeDtypeStruct(taps.shape, F32),
            jax.ShapeDtypeStruct(gain.shape, F32),
            jax.ShapeDtypeStruct(decay.shape, F32),
        ],
        cost_estimate=busy(50), compiler_params=pltpu.CompilerParams(vmem_limit_bytes=56 << 20),
    )(proj, taps, decay, gain, inverse, solved, core, grad)


def busy(us):
    return pl.CostEstimate(flops=us * 1_000_000_000, bytes_accessed=0, transcendentals=0)


def _place(n_dp):
    me = lax.axis_index("dp")
    z = lax.axis_index("fsdp")
    core = lax.rem(me, 2)
    chip = me // 2
    return me, z, core, lax.rem(chip, 2), chip // 2

def ag_square(x, cid, chunks=4):
    rows, cols = x.shape
    r = rows // chunks
    def kernel(x_ref, o_ref, lsem, ssem, rsem, dssem, drsem, fs, fr):
        me, z, core, cx, cy = _place(8)
        dev = lambda dx, dy, c: 2*(2*lax.rem(cy+dy,2)+lax.rem(cx+dx,2))+c
        nx, ny, nd = dev(1,0,core), dev(0,1,core), dev(1,1,core)
        src = dev(1-core, core, core)
        tgt = dev(core, 1-core, core)
        sib = dev(0,0,1-core)
        bar = pltpu.get_barrier_semaphore()
        for d in (sib,nx,ny):
            pl.semaphore_signal(bar, inc=1, device_id=(d,z), device_id_type=MESH)
        pl.semaphore_wait(bar, 3)
        lc = pltpu.make_async_copy(x_ref, o_ref.at[me], lsem); lc.start()
        def rc(a, b, s, q, d):
            return pltpu.make_async_remote_copy(a, b, s, q, device_id=(d,z), device_id_type=MESH)
        own = []
        for c in range(chunks):
            sl = pl.ds(c*r, r)
            for i, d in ((0,nx),(1,ny)):
                cp = rc(x_ref.at[sl], o_ref.at[me,sl], ssem.at[i,c], rsem.at[i,c], d); cp.start(); own.append(cp)
        sibs=[]
        for c in range(chunks):
            sl = pl.ds(c*r, r)
            cp = rc(x_ref.at[sl], o_ref.at[me,sl], fs.at[0,c], fr.at[0,c], sib); cp.start(); sibs.append(cp)
        other = dev(core, 1-core, core)
        for c in range(chunks):
            sl = pl.ds(c*r, r)
            rc(x_ref.at[sl], o_ref.at[src,sl], ssem.at[core,c], rsem.at[core,c], sib).wait_recv()
            cp = rc(o_ref.at[src,sl], o_ref.at[src,sl], dssem.at[c], drsem.at[c], tgt); cp.start(); sibs.append((cp,))
            cp = rc(o_ref.at[src,sl], o_ref.at[src,sl], fs.at[1,c], fr.at[1,c], sib); cp.start(); sibs.append(cp)
            rc(x_ref.at[sl], o_ref.at[other,sl], ssem.at[1-core,c], rsem.at[1-core,c], sib).wait_recv()
            cp = rc(o_ref.at[other,sl], o_ref.at[other,sl], fs.at[2,c], fr.at[2,c], sib); cp.start(); sibs.append(cp)
        for c in range(chunks):
            sl = pl.ds(c*r, r)
            rc(x_ref.at[sl], o_ref.at[nd,sl], dssem.at[c], drsem.at[c], sib).wait_recv()
            cp = rc(o_ref.at[nd,sl], o_ref.at[nd,sl], fs.at[3,c], fr.at[3,c], sib); cp.start(); sibs.append(cp)
        for cp in own: cp.wait_send()
        for cp in sibs:
            if isinstance(cp, tuple): cp[0].wait_send()
            else: cp.wait()
        lc.wait()
    D=pltpu.SemaphoreType.DMA
    return pl.pallas_call(kernel, out_shape=jax.ShapeDtypeStruct((8,rows,cols),x.dtype),
        in_specs=[pl.BlockSpec(memory_space=pl.ANY)], out_specs=pl.BlockSpec(memory_space=pl.ANY),
        scratch_shapes=[D, D((2,chunks)), D((2,chunks)), D((chunks,)), D((chunks,)), D((4,chunks)), D((4,chunks))],
        cost_estimate=busy(40), compiler_params=pltpu.CompilerParams(collective_id=cid, has_side_effects=True))(x)

def rs_square(x, cid, chunks=4):
    _, rows, cols = x.shape
    r = rows // chunks
    def kernel(x_ref, o_ref, X, A, B, R, lsem, sa, ra, sb, rb):
        me, z, core, cx, cy = _place(8)
        dev = lambda dx, dy, c: 2*(2*lax.rem(cy+dy,2)+lax.rem(cx+dx,2))+c
        fdx, fdy = 1-core, core
        nf, ng = dev(fdx,fdy,core), dev(fdy,fdx,core)
        sib = dev(0,0,1-core)
        bar = pltpu.get_barrier_semaphore()
        for d in (sib,nf,ng):
            pl.semaphore_signal(bar, inc=1, device_id=(d,z), device_id_type=MESH)
        mine = [dev(1,1,core), ng, nf, me]
        s_f, s_g = dev(core,1-core,1-core), dev(1-core,core,1-core)
        theirs = [dev(1,1,1-core), s_g, s_f, sib]
        loads=[]
        for k in range(4):
            for c in range(chunks):
                sl=pl.ds(c*r,r)
                cp=pltpu.make_async_copy(x_ref.at[mine[k],sl], X.at[k,sl], lsem.at[k,c]); cp.start(); loads.append(cp)
        pl.semaphore_wait(bar, 3)
        def rc(a, b, s, q, d):
            return pltpu.make_async_remote_copy(a, b, s, q, device_id=(d,z), device_id_type=MESH)
        sends=[]; ga={}
        for k in range(4):
            for c in range(chunks):
                sl=pl.ds(c*r,r)
                cp=rc(x_ref.at[theirs[k],sl], A.at[k,sl], sa.at[k,c], ra.at[k,c], sib); cp.start(); sends.append(cp); ga[k,c]=cp
        def pair(k,c):
            sl=pl.ds(c*r,r)
            loads[k*chunks+c].wait(); ga[k,c].wait_recv()
            return X[k,sl].astype(F32)+A[k,sl].astype(F32)
        gb={}
        def ship(slot, c, d):
            sl=pl.ds(c*r,r)
            cp=rc(B.at[slot,sl], R.at[slot,sl], sb.at[slot,c], rb.at[slot,c], d); cp.start(); sends.append(cp); gb[slot,c]=cp
        for c in range(chunks):
            sl=pl.ds(c*r,r)
            B[0,sl]=pair(0,c).astype(BF16); ship(0,c,nf)
        for c in range(chunks):
            sl=pl.ds(c*r,r)
            B[2,sl]=pair(2,c).astype(BF16); ship(2,c,nf)
        for c in range(chunks):
            sl=pl.ds(c*r,r)
            v=pair(1,c)
            gb[0,c].wait_recv()
            B[1,sl]=(v+R[0,sl].astype(F32)).astype(BF16); ship(1,c,ng)
        for c in range(chunks):
            sl=pl.ds(c*r,r)
            v=pair(3,c)
            gb[2,c].wait_recv()
            o_ref[sl]=v+R[2,sl].astype(F32)
        for c in range(chunks):
            sl=pl.ds(c*r,r)
            gb[1,c].wait_recv()
            o_ref[sl]=o_ref[sl]+R[1,sl].astype(F32)
        for cp in sends: cp.wait_send()
    D=pltpu.SemaphoreType.DMA
    V=lambda n: pltpu.VMEM((n,rows,cols),x.dtype)
    return pl.pallas_call(kernel, out_shape=jax.ShapeDtypeStruct((rows,cols),F32),
        in_specs=[pl.BlockSpec(memory_space=pl.ANY)], out_specs=pl.BlockSpec(memory_space=pltpu.VMEM),
        scratch_shapes=[V(4),V(4),V(3),V(3), D((4,chunks)), D((4,chunks)), D((4,chunks)), D((3,chunks)), D((3,chunks))],
        cost_estimate=busy(40), compiler_params=pltpu.CompilerParams(collective_id=cid, has_side_effects=True, vmem_limit_bytes=40<<20))(x)

def begin(weight, decays, ups, tokens, cotangent, small, bounds, n_z, cid):
    own = weight.shape[0]
    cols = bounds[-1] + 128
    units = ups.shape[2]
    rows, width = tokens.shape
    count = 8 * n_z
    chunks = 2
    part = rows // chunks

    def kernel(
        w_ref, dec_ref, u_ref, t_ref, c_ref, small_ref, w_out, u_out, n_out, c_out, small_out,
        toks, lsem, a_send, a_recv, g_send, g_recv, up_send, up_recv, down_send, down_recv,
        small_send, small_recv, x_send, x_recv, d_send, d_recv, f_send, f_recv,
    ):
        me, z, core, cx, cy = _place(8)
        flat = me * n_z + z
        bar = pltpu.get_barrier_semaphore()

        def dev(dx, dy, c):
            return 2 * (2 * lax.rem(cy + dy, 2) + lax.rem(cx + dx, 2)) + c

        sib = dev(0, 0, 1 - core)

        def partner(o):
            return dev(o // 4, lax.rem(o // 2, 2), lax.rem(core + o, 2))

        def anyone(o):
            other = lax.rem(flat + o, count)
            return (other // n_z, lax.rem(other, n_z))

        def remote(src, dst, send, recv, device):
            return pltpu.make_async_remote_copy(src, dst, send, recv, device_id=device, device_id_type=MESH)

        def loop(first, last, body):
            def step(o, _):
                body(o)
                return 0

            lax.fori_loop(first, last, step, 0)

        def sections(q):
            for first, last in zip(bounds[:-1], bounds[1:]):
                size = last - first
                at = pl.multiple_of(8 * first + q * size, 128)
                yield w_ref.at[:, pl.ds(at, size)], w_out.at[me, z, :, pl.ds(first, size)]
            yield dec_ref.at[q], w_out.at[me, z, :, pl.ds(bounds[-1], 128)]

        def send_piece(o):
            q = partner(o)
            for src, dst in sections(q):
                remote(src, dst, a_send.at[o - 1], a_recv.at[o - 1], (q, z)).start()

        def landed(o):
            at = w_out.at[partner(o), z]
            return remote(at, at, a_send.at[o - 1], a_recv.at[o - 1], (sib, z))

        def up(t, o):
            at = w_out.at[partner(o), z - t]
            return remote(at, at, up_send.at[t, o], up_recv.at[t, o], (me, z + 1))

        def down(t, o):
            at = w_out.at[partner(o), z + t]
            return remote(at, at, down_send.at[t, o], down_recv.at[t, o], (me, z - 1))

        def pass_on(t, o):
            if t > 0:

                @pl.when(z >= t)
                def _():
                    at = w_out.at[partner(o), z - t]
                    remote(at, at, up_send.at[t - 1, o], up_recv.at[t - 1, o], (sib, z)).wait_recv()

                @pl.when(z + t < n_z)
                def _():
                    at = w_out.at[partner(o), z + t]
                    remote(at, at, down_send.at[t - 1, o], down_recv.at[t - 1, o], (sib, z)).wait_recv()

            if t < n_z - 1:

                @pl.when((z >= t) & (z < n_z - 1))
                def _():
                    up(t, o).start()

                @pl.when((z + t < n_z) & (z > 0))
                def _():
                    down(t, o).start()

        def sent(t, o):
            @pl.when((z >= t) & (z < n_z - 1))
            def _():
                up(t, o).wait_send()

            @pl.when((z + t < n_z) & (z > 0))
            def _():
                down(t, o).wait_send()

        def unit_piece(o):
            q = partner(o)
            return remote(u_ref.at[q], u_out.at[me], g_send.at[o - 1], g_recv.at[o - 1], (q, z))

        def tiny(o):
            return remote(small_ref, small_out.at[flat], small_send.at[o - 1], small_recv.at[o - 1], anyone(o))

        near = (dev(1, 0, core), dev(0, 1, core))
        source, other, across = dev(1 - core, core, core), dev(core, 1 - core, core), dev(1, 1, core)

        def gather(i, ref, out):
            def at(q, c):
                return out.at[q, pl.ds(c * part, part)]

            def mine(c):
                return ref.at[pl.ds(c * part, part)]

            def first(k, c):
                return remote(mine(c), at(me, c), x_send.at[i, k, c], x_recv.at[i, k, c], (near[k], z))

            def twin(k, q, c):
                src = mine(c) if k == 0 else at(q, c)
                return remote(src, at(q, c), f_send.at[i, k, c], f_recv.at[i, k, c], (sib, z))

            def second(c):
                return remote(at(source, c), at(source, c), d_send.at[i, c], d_recv.at[i, c], (other, z))

            def keep():
                return pltpu.make_async_copy(ref, out.at[me], lsem.at[i])

            def begin_():
                keep().start()
                for c in range(chunks):
                    for k in range(2):
                        first(k, c).start()
                for c in range(chunks):
                    twin(0, me, c).start()

            def forward():
                for c in range(chunks):
                    remote(mine(c), at(source, c), x_send.at[i, core, c], x_recv.at[i, core, c], (sib, z)).wait_recv()
                    second(c).start()
                    twin(1, source, c).start()
                    remote(
                        mine(c), at(other, c), x_send.at[i, 1 - core, c], x_recv.at[i, 1 - core, c], (sib, z)
                    ).wait_recv()
                    twin(2, other, c).start()

            def last():
                for c in range(chunks):
                    remote(at(across, c), at(across, c), d_send.at[i, c], d_recv.at[i, c], (other, z)).wait_recv()
                    twin(3, across, c).start()

            def finish():
                keep().wait()
                theirs = (sib, dev(core, 1 - core, 1 - core), dev(1 - core, core, 1 - core), dev(1, 1, 1 - core))
                for c in range(chunks):
                    for k in range(4):
                        remote(
                            at(theirs[k], c), at(theirs[k], c), f_send.at[i, k, c], f_recv.at[i, k, c], (sib, z)
                        ).wait_recv()

            def close():
                for c in range(chunks):
                    for k in range(2):
                        first(k, c).wait_send()
                    second(c).wait_send()
                    for k, q in enumerate((me, source, other, across)):
                        twin(k, q, c).wait_send()

            return begin_, forward, last, finish, close

        tok_begin, tok_forward, tok_last, tok_finish, tok_close = gather(0, t_ref, toks)
        cot_begin, cot_forward, cot_last, cot_finish, cot_close = gather(1, c_ref, c_out)

        loop(1, count, lambda o: pl.semaphore_signal(bar, inc=1, device_id=anyone(o), device_id_type=MESH))
        for src, dst in sections(me):
            pltpu.make_async_copy(src, dst, lsem.at[2]).start()
        keep_u = pltpu.make_async_copy(u_ref.at[me], u_out.at[me], lsem.at[3])
        keep_s = pltpu.make_async_copy(small_ref, small_out.at[flat], lsem.at[4])
        keep_u.start()
        keep_s.start()
        pl.semaphore_wait(bar, count - 1)

        loop(1, 8, send_piece)
        pltpu.make_async_copy(w_out.at[me, z], w_out.at[me, z], lsem.at[2]).wait()
        pass_on(0, 0)
        loop(1, count, lambda o: tiny(o).start())

        def first_leg(o):
            landed(o).wait_recv()
            pass_on(0, o)

        tok_begin()
        loop(1, 8, first_leg)
        loop(0, 8, lambda o: pass_on(1, o))
        tok_forward()
        cot_begin()
        loop(1, 8, lambda o: unit_piece(o).start())
        loop(0, 4, lambda o: pass_on(2, o))
        tok_last()
        tok_finish()
        keep_s.wait()
        loop(1, count, lambda o: tiny(o).wait_recv())

        lanes = lax.broadcasted_iota(jnp.int32, (1, 128), 1)
        per = 128 // own
        blocks = []
        for m in range(width // 128):
            block = small_out[m * per, 0:1, :].astype(F32)
            for i in range(1, per):
                block = jnp.where(lanes >= i * own, small_out[m * per + i, 0:1, :].astype(F32), block)
            blocks.append(block)
        gain = jnp.concatenate(blocks, axis=1)
        step = 32

        def norm_rows(o):
            def some(r, _):
                sl = pl.ds(r * step, step)
                v = toks[o, sl].astype(F32)
                n_out[o, sl] = (
                    v * lax.rsqrt(jnp.mean(v * v, axis=-1, keepdims=True) + EPSILON) * gain
                ).astype(BF16)
                return 0

            lax.fori_loop(0, rows // step, some, 0)

        def third_leg(o):
            pass_on(2, o)
            norm_rows(o - 4)
            norm_rows(o)

        loop(4, 8, third_leg)
        cot_forward()
        loop(0, 4, lambda o: pass_on(3, o))
        cot_last()
        loop(4, 8, lambda o: pass_on(3, o))
        cot_finish()
        for t in range(n_z - 1):
            loop(0, 8, functools.partial(sent, t))
        loop(1, 8, lambda o: landed(o).wait_send())
        loop(1, 8, lambda o: unit_piece(o).wait())
        loop(1, count, lambda o: tiny(o).wait_send())
        keep_u.wait()
        tok_close()
        cot_close()

    dma = pltpu.SemaphoreType.DMA
    anywhere, vmem = pl.BlockSpec(memory_space=pl.ANY), pl.BlockSpec(memory_space=pltpu.VMEM)
    plane = jax.ShapeDtypeStruct((8, rows, width), BF16)
    legs = n_z - 1
    return pl.pallas_call(
        kernel,
        out_shape=[
            jax.ShapeDtypeStruct((8, n_z, own, cols), BF16),
            jax.ShapeDtypeStruct((8, own, units), BF16),
            plane,
            plane,
            jax.ShapeDtypeStruct((count,) + small.shape, BF16),
        ],
        in_specs=[anywhere] * 6,
        out_specs=[anywhere, anywhere, vmem, anywhere, vmem],
        scratch_shapes=[
            pltpu.VMEM((8, rows, width), BF16),
            dma((5,)),
            dma((7,)),
            dma((7,)),
            dma((7,)),
            dma((7,)),
            dma((legs, 8)),
            dma((legs, 8)),
            dma((legs, 8)),
            dma((legs, 8)),
            dma((count - 1,)),
            dma((count - 1,)),
            dma((2, 2, chunks)),
            dma((2, 2, chunks)),
            dma((2, chunks)),
            dma((2, chunks)),
            dma((2, 4, chunks)),
            dma((2, 4, chunks)),
        ],
        cost_estimate=busy(150),
        compiler_params=pltpu.CompilerParams(
            collective_id=cid, has_side_effects=True, vmem_limit_bytes=32 << 20
        ),
    )(weight, decays, ups, tokens, cotangent, small)


def relay(left, first, second, first_dims, second_dims, gain, extras, norm_back, cid):
    _, rows, depth = left.shape
    width = gain.shape[1]
    multiply = second is not None
    out_cols = 0 if not multiply else second.shape[1] if second_dims == NN else second.shape[0]
    chunks = 4
    part = rows // chunks
    tile = 512
    out_tiles = [(a, min(a + tile, out_cols)) for a in range(0, out_cols, tile)]

    def kernel(left_ref, first_ref, gain_ref, *refs):
        extra_refs, refs = refs[: len(extras)], refs[len(extras) :]
        if multiply:
            second_ref, *refs = refs
        rows_out, all_out, *refs = refs
        if multiply:
            prod_out, *refs = refs
        if norm_back:
            gain_grad, *refs = refs
        if multiply:
            *refs, w2, stage = refs
        (T, A, B, R, S, lsem, sa, ra, sb, rb, x_send, x_recv, d_send, d_recv, f_send, f_recv) = refs
        me, z, core, cx, cy = _place(8)

        def dev(dx, dy, c):
            return 2 * (2 * lax.rem(cy + dy, 2) + lax.rem(cx + dx, 2)) + c

        def remote(src, dst, send, recv, device):
            return pltpu.make_async_remote_copy(src, dst, send, recv, device_id=(device, z), device_id_type=MESH)

        sib = dev(0, 0, 1 - core)
        nf, ng, across = dev(1 - core, core, core), dev(core, 1 - core, core), dev(1, 1, core)
        bar = pltpu.get_barrier_semaphore()
        for d in (sib, nf, ng):
            pl.semaphore_signal(bar, inc=1, device_id=(d, z), device_id_type=MESH)
        if multiply:
            load = pltpu.make_async_copy(second_ref, w2, lsem.at[2])
            load.start()

        mine = (across, ng, nf, me)
        theirs = (dev(1, 1, 1 - core), dev(1 - core, core, 1 - core), dev(core, 1 - core, 1 - core), sib)

        def partial(q, write):
            def some(n, _):
                cols = pl.ds(pl.multiple_of(n * tile, tile), tile)
                w = first_ref[:, cols] if first_dims == NN else first_ref[cols, :]
                write(cols, lax.dot_general(left_ref[q], w, first_dims, preferred_element_type=F32))
                return 0

            lax.fori_loop(0, width // tile, some, 0)

        def give(k):
            def write(cols, v):
                T[k, :, cols] = v.astype(BF16)

            partial(theirs[k], write)
            remote(T.at[k], A.at[k], sa.at[k], ra.at[k], sib).start()

        def got(k):
            remote(T.at[k], A.at[k], sa.at[k], ra.at[k], sib).wait_recv()

        def cut(c):
            return pl.ds(c * part, part)

        def ship(k, c, d):
            return remote(B.at[k, cut(c)], R.at[k, cut(c)], sb.at[k, c], rb.at[k, c], d)

        def send_sum(k):
            got(k)

            def write(cols, v):
                B[k, :, cols] = (v + A[k, :, cols].astype(F32)).astype(BF16)

            partial(mine[k], write)
            for c in range(chunks):
                ship(k, c, nf).start()

        def keep_sum(k, out):
            got(k)

            def write(cols, v):
                out[:, cols] = v + A[k, :, cols].astype(F32)

            partial(mine[k], write)

        pl.semaphore_wait(bar, 3)
        give(0)
        give(2)
        send_sum(0)
        give(1)
        send_sum(2)
        give(3)
        keep_sum(1, S)
        for c in range(chunks):
            ship(0, c, nf).wait_recv()
            B[1, cut(c)] = (S[cut(c)] + R[0, cut(c)].astype(F32)).astype(BF16)
            ship(1, c, ng).start()
        keep_sum(3, S)

        source, other = nf, ng

        def at(q, c):
            return all_out.at[q, cut(c)]

        def step(k, c):
            return remote(at(me, c), at(me, c), x_send.at[k, c], x_recv.at[k, c], (dev(1, 0, core), dev(0, 1, core))[k])

        def twin(k, q, c):
            return remote(at(q, c), at(q, c), f_send.at[k, c], f_recv.at[k, c], sib)

        def second_step(c):
            return remote(at(source, c), at(source, c), d_send.at[c], d_recv.at[c], other)

        gains = gain_ref[...]
        if norm_back:
            gain_grad[...] = jnp.zeros_like(gain_grad)
        for c in range(chunks):
            ship(2, c, nf).wait_recv()
            ship(1, c, ng).wait_recv()
            for h in range(2):
                sl = pl.ds(c * part + h * (part // 2), part // 2)
                total = S[sl] + R[2, sl].astype(F32) + R[1, sl].astype(F32)
                if norm_back:
                    v = extra_refs[0][sl]
                    root = lax.rsqrt(jnp.mean(v * v, axis=-1, keepdims=True) + EPSILON)
                    hat = v * root
                    scaled = total * gains
                    gain_grad[...] += jnp.sum(total * hat, axis=0, keepdims=True)
                    done = extra_refs[1][sl] + root * (scaled - hat * jnp.mean(scaled * hat, axis=-1, keepdims=True))
                    low = done
                else:
                    done = extra_refs[0][sl].astype(F32) + total
                    low = done * lax.rsqrt(jnp.mean(done * done, axis=-1, keepdims=True) + EPSILON) * gains
                rows_out[sl] = done
                all_out[me, sl] = low.astype(BF16)
            for k in range(2):
                step(k, c).start()
            twin(0, me, c).start()
        if multiply:
            load.wait()

        flushes = []

        def product(q):
            if not multiply:
                return
            slot = len(flushes) % 2
            if len(flushes) > 1:
                flushes[-2].wait()
            for a, b in out_tiles:
                w = w2[:, a:b] if second_dims == NN else w2[a:b, :]
                stage[slot, :, a:b] = lax.dot_general(all_out[q], w, second_dims, preferred_element_type=F32)
            flush = pltpu.make_async_copy(stage.at[slot], prod_out.at[q], lsem.at[slot])
            flush.start()
            flushes.append(flush)

        def twin_got(k):
            for c in range(chunks):
                twin(k, theirs_at[k], c).wait_recv()

        theirs_at = (sib, dev(core, 1 - core, 1 - core), dev(1 - core, core, 1 - core), dev(1, 1, 1 - core))
        product(me)
        for c in range(chunks):
            remote(at(source, c), at(source, c), x_send.at[core, c], x_recv.at[core, c], sib).wait_recv()
            second_step(c).start()
            twin(1, source, c).start()
            remote(at(other, c), at(other, c), x_send.at[1 - core, c], x_recv.at[1 - core, c], sib).wait_recv()
            twin(2, other, c).start()
            if c == 0:
                twin_got(0)
                product(sib)
        product(source)
        product(other)
        for c in range(chunks):
            remote(at(across, c), at(across, c), d_send.at[c], d_recv.at[c], sib).wait_recv()
            twin(3, across, c).start()
            if c == 0:
                twin_got(1)
                product(theirs_at[1])
            if c == 1:
                twin_got(2)
                product(theirs_at[2])
        product(across)
        twin_got(3)
        product(theirs_at[3])

        for k in range(4):
            remote(T.at[k], A.at[k], sa.at[k], ra.at[k], sib).wait_send()
        for c in range(chunks):
            for k in range(3):
                ship(k, c, nf).wait_send()
            for k in range(2):
                step(k, c).wait_send()
            second_step(c).wait_send()
            for k, q in enumerate((me, source, other, across)):
                twin(k, q, c).wait_send()
        for flush in flushes[-2:]:
            flush.wait()

    dma = pltpu.SemaphoreType.DMA
    anywhere, vmem = pl.BlockSpec(memory_space=pl.ANY), pl.BlockSpec(memory_space=pltpu.VMEM)
    block = lambda n: pltpu.VMEM((n, rows, width), BF16)
    out_shape = [
        jax.ShapeDtypeStruct((rows, width), F32),
        jax.ShapeDtypeStruct((8, rows, width), BF16),
    ]
    out_specs = [vmem, vmem]
    operands = [left, first, gain, *extras]
    in_specs = [vmem] * len(operands)
    later = []
    if multiply:
        out_shape.append(jax.ShapeDtypeStruct((8, rows, out_cols), F32))
        out_specs.append(anywhere)
        operands.append(second)
        in_specs.append(anywhere)
        later = [pltpu.VMEM(second.shape, BF16), pltpu.VMEM((2, rows, out_cols), F32)]
    if norm_back:
        out_shape.append(jax.ShapeDtypeStruct((1, width), F32))
        out_specs.append(vmem)
    return pl.pallas_call(
        kernel,
        out_shape=out_shape,
        in_specs=in_specs,
        out_specs=out_specs,
        scratch_shapes=[
            block(4),
            block(4),
            block(3),
            block(3),
            pltpu.VMEM((rows, width), F32),
            dma((3,)),
            dma((4,)),
            dma((4,)),
            dma((3, chunks)),
            dma((3, chunks)),
            dma((2, chunks)),
            dma((2, chunks)),
            dma((chunks,)),
            dma((chunks,)),
            dma((4, chunks)),
            dma((4, chunks)),
            *later,
        ],
        cost_estimate=busy(80),
        compiler_params=pltpu.CompilerParams(
            collective_id=cid, has_side_effects=True, vmem_limit_bytes=58 << 20
        ),
    )(*operands)


def unit_pairs(a, main):
    tail = a[:, 2 * main :]
    size = tail.shape[1]
    turned = pltpu.roll(tail, size // 2, 1)
    left = lax.broadcasted_iota(jnp.int32, tail.shape, 1) < size // 2
    return (a[:, :main], a[:, main : 2 * main]), (jnp.where(left, tail, turned), jnp.where(left, turned, tail)), left


def units_forward(x, weight, scales, units, main):
    blocks, rows, width = x.shape
    cols = weight.shape[1]

    def kernel(x_ref, w_ref, s_ref, up_ref, hidden_ref, scaled_ref):
        scale = s_ref[pl.ds(pl.program_id(0), 1), :][:, 0:1]
        for a in range(0, cols, 512):
            b = min(a + 512, cols)
            up_ref[:, a:b] = jnp.dot(x_ref[...], w_ref[:, a:b], preferred_element_type=F32)
        (g, u), (g_tail, u_tail), _ = unit_pairs(up_ref[...], main)
        hidden = g * sigmoid(g) * u
        tail = (g_tail * sigmoid(g_tail) * u_tail)[:, : units - main]
        hidden_ref[:, :main] = hidden.astype(BF16)
        hidden_ref[:, main:] = tail.astype(BF16)
        scaled_ref[:, :main] = (hidden * scale).astype(BF16)
        scaled_ref[:, main:] = (tail * scale).astype(BF16)

    row = lambda n: pl.BlockSpec((rows, n), lambda i: (i, 0))
    whole = lambda a: pl.BlockSpec(a.shape, lambda i: (0, 0))
    tokens = blocks * rows
    return pl.pallas_call(
        kernel,
        grid=(blocks,),
        in_specs=[row(width), whole(weight), whole(scales)],
        out_specs=[row(cols), row(units), row(units)],
        out_shape=[
            jax.ShapeDtypeStruct((tokens, cols), F32),
            jax.ShapeDtypeStruct((tokens, units), BF16),
            jax.ShapeDtypeStruct((tokens, units), BF16),
        ],
        cost_estimate=busy(20),
        compiler_params=pltpu.CompilerParams(vmem_limit_bytes=48 << 20),
    )(x.reshape(tokens, width), weight, scales)


def units_backward(cot, weight, upgate, scales, units, main):
    blocks, rows, width = cot.shape
    cols = upgate.shape[1]

    def kernel(c_ref, w_ref, up_ref, s_ref, low_ref):
        scale = s_ref[pl.ds(pl.program_id(0), 1), :][:, 0:1]
        pair, pair_tail, left = unit_pairs(up_ref[...], main)
        tail_rows = w_ref[main:, :]
        grad = dot(c_ref[...], w_ref[:main, :], NT) * scale
        grad_tail = dot(c_ref[...], jnp.concatenate([tail_rows, tail_rows], axis=0), NT) * scale

        def both(g, u, grad):
            s = sigmoid(g)
            return grad * u * s * (1.0 + g * (1.0 - s)), grad * g * s

        gate_grad, up_grad = both(*pair, grad)
        low_ref[:, :main] = gate_grad.astype(BF16)
        low_ref[:, main : 2 * main] = up_grad.astype(BF16)
        gate_grad, up_grad = both(*pair_tail, grad_tail)
        low_ref[:, 2 * main :] = jnp.where(left, gate_grad, up_grad).astype(BF16)

    row = lambda n: pl.BlockSpec((rows, n), lambda i: (i, 0))
    whole = lambda a: pl.BlockSpec(a.shape, lambda i: (0, 0))
    tokens = blocks * rows
    return pl.pallas_call(
        kernel,
        grid=(blocks,),
        in_specs=[row(width), whole(weight), row(cols), whole(scales)],
        out_specs=row(cols),
        out_shape=jax.ShapeDtypeStruct((tokens, cols), BF16),
        cost_estimate=busy(12),
        compiler_params=pltpu.CompilerParams(vmem_limit_bytes=48 << 20),
    )(cot.reshape(tokens, width), weight, upgate, scales)


def conclude(grad, left, weight, block, ups, tokens, middle, middle_grad, gain, lines, conv, bounds, cid):
    n_z = 4
    _, _, own, cols = grad.shape
    units = ups.shape[2]
    rows, width = tokens.shape
    count = 8 * n_z
    per = 128 * count // width
    conv_cols = conv.shape[1] // count
    chunks = 2
    part = rows // chunks
    tile = 512
    last = n_z - 1

    def kernel(
        g_ref, l_ref, w_ref, b_ref, u_ref, t_ref, m_ref, mg_ref, gain_ref, lines_ref, conv_ref,
        result, tg, in_out, dec_out, u_out, lines_out, conv_out,
        W, L, own_buf, UD, T, A, B, R, S, A7, B7, R7, X7, line_buf,
        lsem, wsem, osem, mine_sem, us, ur, ds, dr, i_send, i_recv, u_send, u_recv, p_send, p_recv, c_send, c_recv,
        sa, ra, sb, rb, sa7, ra7, sb7, rb7,
    ):
        me, z, core, cx, cy = _place(8)
        flat = me * n_z + z

        def dev(dx, dy, c):
            return 2 * (2 * lax.rem(cy + dy, 2) + lax.rem(cx + dx, 2)) + c

        sib = dev(0, 0, 1 - core)
        nf, ng, across = dev(1 - core, core, core), dev(core, 1 - core, core), dev(1, 1, core)

        def partner(o):
            return dev(o // 4, lax.rem(o // 2, 2), lax.rem(core + o, 2))

        def anyone(o):
            other = lax.rem(flat + o, count)
            return (other // n_z, lax.rem(other, n_z))

        def remote(src, dst, send, recv, device):
            return pltpu.make_async_remote_copy(src, dst, send, recv, device_id=device, device_id_type=MESH)

        def loop(first, end, body):
            def step(o, _):
                body(o)
                return 0

            lax.fori_loop(first, end, step, 0)

        bar = pltpu.get_barrier_semaphore()
        loop(1, count, lambda o: pl.semaphore_signal(bar, inc=1, device_id=anyone(o), device_id_type=MESH))

        mine = (across, ng, nf, me)
        theirs = (dev(1, 1, 1 - core), dev(1 - core, core, 1 - core), dev(core, 1 - core, 1 - core), sib)
        turns = (theirs[0], theirs[2], mine[0], theirs[1], mine[2], theirs[3], mine[1], mine[3])

        def load_left(i):
            return pltpu.make_async_copy(l_ref.at[turns[i]], L.at[i % 2], lsem.at[i % 2])

        load_weight = pltpu.make_async_copy(w_ref, W, wsem.at[0])
        load_middle = pltpu.make_async_copy(m_ref, result, wsem.at[1])
        load_grad = pltpu.make_async_copy(mg_ref, tg, wsem.at[2])

        def load_own(zz):
            return pltpu.make_async_copy(g_ref.at[:, zz], own_buf.at[zz], osem.at[zz])

        load_left(0).start()
        load_weight.start()
        for zz in (0, 3, 2, 1):
            load_own(zz).start()
        load_left(1).start()
        load_middle.start()
        load_grad.start()
        pl.semaphore_wait(bar, count - 1)

        def up_slot(s, o):
            return s * 8 + o

        def down_slot(s, o):
            return 39 - (s * 8 + o)

        def up(s, o, src):
            return remote(src, UD.at[up_slot(s, o)], us.at[s, o], ur.at[s, o], (me, z + 1))

        def down(s, o, src):
            return remote(src, UD.at[down_slot(s, o)], ds.at[s, o], dr.at[s, o], (me, z - 1))

        def start_line(s, o):
            q = partner(o)

            @pl.when(z == 0)
            def _():
                up(s, o, g_ref.at[q, last - s]).start()

            @pl.when(z == last)
            def _():
                down(s, o, g_ref.at[q, s]).start()

        for s in range(last):
            loop(0, 8, functools.partial(start_line, s))
        for zz in range(n_z):
            load_own(zz).wait()

        def sections(q):
            for a, b in zip(bounds[:-1], bounds[1:]):
                at = pl.multiple_of(8 * a + q * (b - a), 128)
                yield pl.ds(a, b - a), in_out.at[:, pl.ds(at, b - a)]
            yield pl.ds(bounds[-1], 128), dec_out.at[q]

        def deliver(o, slot):
            @pl.when(o == 0)
            def _():
                for src, dst in sections(me):
                    pltpu.make_async_copy(UD.at[slot, :, src], dst, wsem.at[3]).start()

            @pl.when(o > 0)
            def _():
                for src, dst in sections(me):
                    remote(UD.at[slot, :, src], dst, i_send.at[o - 1], i_recv.at[o - 1], (partner(o), z)).start()

        def add(slot, *others):
            total = UD[slot].astype(F32)
            for other in others:
                total = total + other.astype(F32)
            UD[slot] = total.astype(BF16)

        def up_tick(i):
            s, o = i // 8, lax.rem(i, 8)
            q, u = partner(o), up_slot(s, o)

            @pl.when((z >= 1) & (z <= last - s))
            def _():
                remote(UD.at[u], UD.at[u], us.at[s, o], ur.at[s, o], (sib, z)).wait_recv()

            @pl.when((z >= 1) & (z < last - s))
            def _():
                add(u, own_buf[last - s, q])
                up(s, o, UD.at[u]).start()

            @pl.when((z == last) & (s == 0))
            def _():
                add(u, own_buf[last, q])
                deliver(o, u)

            @pl.when((z == 1) & (s == 2))
            def _():
                add(u, UD[down_slot(1, o)], own_buf[1, q])
                deliver(o, u)

        def down_tick(i):
            s, o = i // 8, lax.rem(i, 8)
            q, d = partner(o), down_slot(s, o)

            @pl.when((z <= last - 1) & (z >= s))
            def _():
                remote(UD.at[d], UD.at[d], ds.at[s, o], dr.at[s, o], (sib, z)).wait_recv()

            @pl.when((z <= last - 1) & (z > s))
            def _():
                add(d, own_buf[s, q])
                down(s, o, UD.at[d]).start()

            @pl.when((z == 0) & (s == 0))
            def _():
                add(d, own_buf[0, q])
                deliver(o, d)

            @pl.when((z == 2) & (s == 2))
            def _():
                add(d, UD[up_slot(1, o)], own_buf[2, q])
                deliver(o, d)

        lag = 4
        low = 1 - z // 2

        def tick(i):
            at_up, at_down = i - lag * (1 - low), i - lag * low

            @pl.when((at_up >= 0) & (at_up < 24))
            def _():
                up_tick(at_up)

            @pl.when((at_down >= 0) & (at_down < 24))
            def _():
                down_tick(at_down)

        def cut(c):
            return pl.ds(c * part, part)

        def partial(i, write):
            load_left(i).wait()

            def some(n, _):
                at = pl.ds(pl.multiple_of(n * tile, tile), tile)
                write(at, lax.dot_general(L[i % 2], W[at, :], NT, preferred_element_type=F32))
                return 0

            lax.fori_loop(0, width // tile, some, 0)
            if i + 2 < 8:
                load_left(i + 2).start()

        def give(i, k, slot, before):
            if before is not None:
                remote(T.at[slot], A.at[before], sa.at[before], ra.at[before], (sib, z)).wait_send()

            def write(at, v):
                T[slot, :, at] = v.astype(BF16)

            partial(i, write)
            remote(T.at[slot], A.at[k], sa.at[k], ra.at[k], (sib, z)).start()

        def got(k):
            remote(T.at[0], A.at[k], sa.at[k], ra.at[k], (sib, z)).wait_recv()

        def ship(k, c, d):
            return remote(B.at[k, cut(c)], R.at[k, cut(c)], sb.at[k, c], rb.at[k, c], (d, z))

        def ship7(k, c, d):
            return remote(B7.at[k, cut(c)], R7.at[k, cut(c)], sb7.at[k, c], rb7.at[k, c], (d, z))

        def send_sum(i, k):
            got(k)

            def write(at, v):
                B[k, :, at] = (v + A[k, :, at].astype(F32)).astype(BF16)

            partial(i, write)
            for c in range(chunks):
                ship(k, c, nf).start()

        def keep_sum(i, k):
            got(k)

            def write(at, v):
                S[:, at] = v + A[k, :, at].astype(F32)

            partial(i, write)

        def second_hop():
            for c in range(chunks):
                ship(0, c, nf).wait_recv()
                B[1, cut(c)] = (S[cut(c)] + R[0, cut(c)].astype(F32)).astype(BF16)
                ship(1, c, ng).start()

        def give7(k):
            return remote(b_ref.at[theirs[k]], A7.at[k], sa7.at[k], ra7.at[k], (sib, z))

        def mine7(k):
            return pltpu.make_async_copy(b_ref.at[mine[k]], X7 if k == 3 else B7.at[k], mine_sem.at[k])

        def start7():
            for k in (0, 2, 1, 3):
                give7(k).start()
                mine7(k).start()

        def send7(k):
            mine7(k).wait()
            give7(k).wait_recv()
            for c in range(chunks):
                B7[k, cut(c)] = (B7[k, cut(c)].astype(F32) + A7[k, cut(c)].astype(F32)).astype(BF16)
                ship7(k, c, nf).start()

        def second_hop7():
            mine7(1).wait()
            give7(1).wait_recv()
            for c in range(chunks):
                ship7(0, c, nf).wait_recv()
                sl = cut(c)
                B7[1, sl] = (B7[1, sl].astype(F32) + A7[1, sl].astype(F32) + R7[0, sl].astype(F32)).astype(BF16)
                ship7(1, c, ng).start()

        small = 32

        def finish_rows():
            load_grad.wait()
            line_buf[...] = lines_ref[...]
            line_buf[0:1] = jnp.zeros((1, width), F32)
            gains = gain_ref[...]
            for c in range(chunks):
                ship(2, c, nf).wait_recv()
                ship(1, c, ng).wait_recv()

                def some(r, _):
                    sl = pl.ds(pl.multiple_of(c * part + r * small, small), small)
                    total = S[sl] + R[2, sl].astype(F32) + R[1, sl].astype(F32)
                    v = t_ref[sl].astype(F32)
                    root = lax.rsqrt(jnp.mean(v * v, axis=-1, keepdims=True) + EPSILON)
                    hat = v * root
                    scaled = total * gains
                    line_buf[0:1] += jnp.sum(total * hat, axis=0, keepdims=True)
                    tg[sl] += root * (scaled - hat * jnp.mean(scaled * hat, axis=-1, keepdims=True))
                    return 0

                lax.fori_loop(0, part // small, some, 0)

        def finish7():
            load_middle.wait()
            mine7(3).wait()
            give7(3).wait_recv()
            for c in range(chunks):
                ship7(2, c, nf).wait_recv()
                ship7(1, c, ng).wait_recv()

                def some(r, _):
                    sl = pl.ds(pl.multiple_of(c * part + r * small, small), small)
                    result[sl] += (
                        X7[sl].astype(F32) + A7[3, sl].astype(F32) + R7[2, sl].astype(F32) + R7[1, sl].astype(F32)
                    )
                    return 0

                lax.fori_loop(0, part // small, some, 0)

        def line_part(d):
            return line_buf.at[:, pl.ds(pl.multiple_of((d // per) * 128, 128), 128)]

        def conv_part(d):
            return conv_ref.at[:, pl.ds(pl.multiple_of(d * conv_cols, conv_cols), conv_cols)]

        def packet(o):
            d = lax.rem(flat + o, count)
            return remote(line_part(d), lines_out.at[flat], p_send.at[o - 1], p_recv.at[o - 1], anyone(o))

        def conv_packet(o):
            d = lax.rem(flat + o, count)
            return remote(conv_part(d), conv_out.at[flat], c_send.at[o - 1], c_recv.at[o - 1], anyone(o))

        keep_line = pltpu.make_async_copy(line_part(flat), lines_out.at[flat], wsem.at[4])
        keep_conv = pltpu.make_async_copy(conv_part(flat), conv_out.at[flat], wsem.at[5])
        keep_up = pltpu.make_async_copy(u_ref.at[me], u_out.at[me], wsem.at[6])

        def unit_piece(o):
            q = partner(o)
            return remote(u_ref.at[q], u_out.at[me], u_send.at[o - 1], u_recv.at[o - 1], (q, z))

        def send_packets():
            keep_line.start()
            loop(1, count, lambda o: packet(o).start())

        def others():
            keep_conv.start()
            keep_up.start()
            loop(1, count, lambda o: conv_packet(o).start())

        def first_work():
            load_weight.wait()
            give(0, 0, 0, None)
            give(1, 2, 1, None)

        work = (
            first_work,
            lambda: (send_sum(2, 0), give(3, 1, 0, 0)),
            lambda: (send_sum(4, 2), give(5, 3, 1, 2), start7()),
            lambda: (keep_sum(6, 1), others()),
            lambda: (second_hop(), keep_sum(7, 3)),
            lambda: (send7(0), send7(2)),
            lambda: finish_rows(),
            lambda: (send_packets(), loop(1, 8, lambda o: unit_piece(o).start())),
            lambda: second_hop7(),
            lambda: None,
            lambda: finish7(),
            lambda: None,
            lambda: None,
            lambda: None,
        )
        for g, item in enumerate(work):
            item()
            loop(2 * g, 2 * g + 2, tick)

        def line_sent(s, o):
            @pl.when(z < last - s)
            def _():
                up(s, o, UD.at[up_slot(s, o)]).wait_send()

            @pl.when(z > s)
            def _():
                down(s, o, UD.at[down_slot(s, o)]).wait_send()

        for s in range(last):
            loop(0, 8, functools.partial(line_sent, s))
        for k, slot in ((1, 0), (3, 1)):
            remote(T.at[slot], A.at[k], sa.at[k], ra.at[k], (sib, z)).wait_send()
        for k in range(4):
            give7(k).wait_send()
        for c in range(chunks):
            for k in range(3):
                ship(k, c, nf).wait_send()
                ship7(k, c, nf).wait_send()
        piece = UD.at[0]

        def arrived(o):
            remote(piece, piece, i_send.at[o - 1], i_recv.at[o - 1], (sib, z)).wait()

        pltpu.make_async_copy(piece, piece, wsem.at[3]).wait()
        loop(1, 8, arrived)
        loop(1, 8, lambda o: unit_piece(o).wait())
        loop(1, count, lambda o: packet(o).wait())
        loop(1, count, lambda o: conv_packet(o).wait())
        keep_line.wait()
        keep_conv.wait()
        keep_up.wait()

    dma = pltpu.SemaphoreType.DMA
    anywhere, vmem = pl.BlockSpec(memory_space=pl.ANY), pl.BlockSpec(memory_space=pltpu.VMEM)
    blocks = lambda n: pltpu.VMEM((n, rows, width), BF16)
    f32_rows = jax.ShapeDtypeStruct((rows, width), F32)
    return pl.pallas_call(
        kernel,
        out_shape=[
            f32_rows,
            f32_rows,
            jax.ShapeDtypeStruct((own, 8 * bounds[-1]), BF16),
            jax.ShapeDtypeStruct((8, own, 128), BF16),
            jax.ShapeDtypeStruct((8, own, units), BF16),
            jax.ShapeDtypeStruct((count, 8, 128), F32),
            jax.ShapeDtypeStruct((count, conv.shape[0], conv_cols), F32),
        ],
        in_specs=[anywhere] * 5 + [vmem, anywhere, anywhere, vmem, vmem, anywhere],
        out_specs=[vmem, vmem] + [anywhere] * 5,
        scratch_shapes=[
            pltpu.VMEM((width, cols), BF16),
            pltpu.VMEM((2, rows, cols), BF16),
            pltpu.VMEM((n_z, 8, own, cols), BF16),
            pltpu.VMEM((40, own, cols), BF16),
            blocks(2),
            blocks(4),
            blocks(3),
            blocks(3),
            pltpu.VMEM((rows, width), F32),
            blocks(4),
            blocks(3),
            blocks(3),
            pltpu.VMEM((rows, width), BF16),
            pltpu.VMEM((8, width), F32),
            dma((2,)),
            dma((7,)),
            dma((n_z,)),
            dma((4,)),
            dma((3, 8)),
            dma((3, 8)),
            dma((3, 8)),
            dma((3, 8)),
            dma((7,)),
            dma((7,)),
            dma((7,)),
            dma((7,)),
            dma((count - 1,)),
            dma((count - 1,)),
            dma((count - 1,)),
            dma((count - 1,)),
            dma((4,)),
            dma((4,)),
            dma((3, chunks)),
            dma((3, chunks)),
            dma((4,)),
            dma((4,)),
            dma((3, chunks)),
            dma((3, chunks)),
        ],
        cost_estimate=busy(120),
        compiler_params=pltpu.CompilerParams(
            collective_id=cid, has_side_effects=True, vmem_limit_bytes=60 << 20
        ),
    )(grad, left, weight, block, ups, tokens, middle, middle_grad, gain, lines, conv)


def gather_small(x, n_dp, n_z, cid):
    rows, cols = x.shape
    count = n_dp * n_z

    def kernel(x_ref, o_ref, lsem, ssem, rsem):
        flat = lax.axis_index("dp") * n_z + lax.axis_index("fsdp")
        bar = pltpu.get_barrier_semaphore()

        def device(o):
            other = lax.rem(flat + o, count)
            return (other // n_z, lax.rem(other, n_z))

        def copy(o):
            return pltpu.make_async_remote_copy(
                x_ref, o_ref.at[flat], ssem.at[o - 1], rsem.at[o - 1], device_id=device(o), device_id_type=MESH
            )

        def greet(o, _):
            pl.semaphore_signal(bar, inc=1, device_id=device(o), device_id_type=MESH)
            return 0

        def send(o, _):
            copy(o).start()
            return 0

        def wait(o, _):
            copy(o).wait()
            return 0

        lax.fori_loop(1, count, greet, 0)
        local = pltpu.make_async_copy(x_ref, o_ref.at[flat], lsem)
        local.start()
        pl.semaphore_wait(bar, count - 1)
        lax.fori_loop(1, count, send, 0)
        lax.fori_loop(1, count, wait, 0)
        local.wait()

    dma = pltpu.SemaphoreType.DMA
    return pl.pallas_call(
        kernel,
        out_shape=jax.ShapeDtypeStruct((count, rows, cols), x.dtype),
        in_specs=[pl.BlockSpec(memory_space=pl.ANY)],
        out_specs=pl.BlockSpec(memory_space=pl.ANY),
        scratch_shapes=[dma, dma((count - 1,)), dma((count - 1,))],
        cost_estimate=busy(15),
        compiler_params=pltpu.CompilerParams(collective_id=cid, has_side_effects=True),
    )(x)


def scatter_small(x, n_dp, n_z, cid):
    count, rows, cols = x.shape

    def kernel(x_ref, o_ref, lsem, ssem, rsem):
        flat = lax.axis_index("dp") * n_z + lax.axis_index("fsdp")
        bar = pltpu.get_barrier_semaphore()

        def device(o):
            other = lax.rem(flat + o, count)
            return (other // n_z, lax.rem(other, n_z))

        def copy(o):
            return pltpu.make_async_remote_copy(
                x_ref.at[lax.rem(flat + o, count)], o_ref.at[flat], ssem.at[o - 1], rsem.at[o - 1], device_id=device(o), device_id_type=MESH
            )

        def greet(o, _):
            pl.semaphore_signal(bar, inc=1, device_id=device(o), device_id_type=MESH)
            return 0

        def send(o, _):
            copy(o).start()
            return 0

        def wait(o, _):
            copy(o).wait()
            return 0

        lax.fori_loop(1, count, greet, 0)
        local = pltpu.make_async_copy(x_ref.at[flat], o_ref.at[flat], lsem)
        local.start()
        pl.semaphore_wait(bar, count - 1)
        lax.fori_loop(1, count, send, 0)
        lax.fori_loop(1, count, wait, 0)
        local.wait()

    dma = pltpu.SemaphoreType.DMA
    return pl.pallas_call(
        kernel,
        out_shape=jax.ShapeDtypeStruct((count, rows, cols), x.dtype),
        in_specs=[pl.BlockSpec(memory_space=pl.ANY)],
        out_specs=pl.BlockSpec(memory_space=pl.ANY),
        scratch_shapes=[dma, dma((count - 1,)), dma((count - 1,))],
        cost_estimate=busy(15),
        compiler_params=pltpu.CompilerParams(collective_id=cid, has_side_effects=True),
    )(x)


def pack(parts, unit):
    flat = jnp.concatenate([part.reshape(-1) for part in parts])
    size = flat.shape[0]
    full = -(-size // (128 * unit)) * 128 * unit
    return jnp.pad(flat, (0, full - size)).reshape(-1, 128)


def dot(a, b, dims=NN, out=F32):
    return lax.dot_general(a, b, dims, preferred_element_type=F32).astype(out)


def local(
    n_dp,
    n_z,
    tokens,
    cotangent,
    group_ids,
    norm_first,
    input_weight,
    decay_weight,
    conv_weight,
    decay_scale,
    decay_bias,
    output_gain,
    output_weight,
    norm_second,
    upgate_weight,
    down_weight,
):
    count = n_dp * n_z
    rows, width = tokens.shape
    all_heads = decay_scale.shape[0]
    heads = all_heads // n_dp
    taps = conv_weight.shape[0]
    own_conv = conv_weight.shape[1]
    own_d = norm_first.shape[0]
    units = upgate_weight.shape[1] // (2 * n_dp)
    key, value = heads * DK, heads * DV
    cols = 2 * key + 2 * value + 128
    square = n_dp == 8 and n_z == 4
    here = lax.axis_index("dp")
    flat = here * n_z + lax.axis_index("fsdp")

    def spread(x, cid):
        if square:
            return ag_square(x, cid).reshape(n_dp * rows, width)
        return lax.all_gather(x, "dp", axis=0, tiled=True)

    def total(x, cid):
        if square:
            return rs_square(x.reshape(n_dp, rows, width), cid)
        return lax.psum_scatter(x, "dp", scatter_dimension=0, tiled=True).astype(F32)

    def by_dp(a, parts):
        return a.reshape(a.shape[0], n_dp, parts)

    main = units // 128 * 128
    bounds = (0, key, 2 * key, 2 * key + value, 2 * key + 2 * value)
    gates = by_dp(upgate_weight[:, : n_dp * units], units)
    ups = by_dp(upgate_weight[:, n_dp * units :], units)
    up_mine = jnp.concatenate(
        [gates[:, :, :main], ups[:, :, :main], gates[:, :, main:], ups[:, :, main:]], axis=2
    ).transpose(1, 0, 2)
    decay_cols = jnp.concatenate(
        [
            by_dp(decay_weight[:, :all_heads], heads),
            by_dp(decay_weight[:, all_heads:], heads),
            jnp.zeros((own_d, n_dp, 128 - 2 * heads), BF16),
        ],
        axis=2,
    ).transpose(1, 0, 2)

    def whole_rows(a):
        a = lax.all_gather(a[:, None], "fsdp", axis=1, tiled=True)
        return a.reshape(width, a.shape[-1])

    conv_size = taps * own_conv
    inputs = tokens.astype(F32)
    first_root = lax.rsqrt(jnp.mean(inputs * inputs, axis=-1, keepdims=True) + EPSILON)
    if square:
        small = jnp.concatenate(
            [norm_first] * (128 // own_d)
            + [norm_second] * (128 // own_d)
            + [jnp.broadcast_to(group_ids.astype(BF16), (128,)), jnp.zeros((640,), BF16), conv_weight.reshape(-1)]
        ).reshape(16, 128)
        in_full, up_plane, normed_all, cot_all, small = begin(
            input_weight, decay_cols, up_mine, tokens, cotangent, small, bounds, n_z, 1
        )
        in_full = in_full.reshape(width, cols)
        normed_all = normed_all.reshape(n_dp * rows, width)
        cot_all = cot_all.reshape(n_dp * rows, width)
        conv_full = small[:, 8:].reshape(count, taps, own_conv)
        first_full = small[:, 0, :own_d]
        second_full = small[:, 1, :own_d]
        every_id = small[:, 2, 0]
        output_weight, down_weight, up_plane = lax.optimization_barrier(
            (output_weight, down_weight, up_plane, small)
        )[:3]
    else:
        in_mine = [
            by_dp(input_weight[:, n_dp * a : n_dp * b], b - a).transpose(1, 0, 2)
            for a, b in zip(bounds[:-1], bounds[1:])
        ]
        in_mine = jnp.concatenate(in_mine + [decay_cols], axis=2)
        in_full = whole_rows(lax.all_to_all(in_mine, "dp", 0, 0, tiled=True))
        up_plane = lax.all_to_all(up_mine, "dp", 0, 0, tiled=True)
        small = gather_small(
            pack((conv_weight, norm_first, norm_second, group_ids.astype(BF16)), 16), n_dp, n_z, 1
        ).reshape(count, -1)
        conv_full = small[:, :conv_size].reshape(count, taps, own_conv)
        first_full = small[:, conv_size : conv_size + own_d]
        second_full = small[:, conv_size + own_d : conv_size + 2 * own_d]
        every_id = small[:, conv_size + 2 * own_d]
    out_full = lax.all_gather(output_weight, "fsdp", axis=0, tiled=True)
    up_full = whole_rows(up_plane)
    down_full = lax.all_gather(down_weight, "fsdp", axis=0, tiled=True)
    conv_full = conv_full.transpose(1, 0, 2).reshape(taps, -1)
    first_full = first_full.reshape(1, width).astype(F32)
    second_full = second_full.reshape(1, width).astype(F32)
    every_id = every_id.astype(jnp.int32)
    scales = 1.0 / jnp.sum((every_id[:, None] == every_id[None, :]).astype(F32), axis=0).reshape(n_dp, n_z)
    scales = lax.dynamic_index_in_dim(scales, lax.axis_index("fsdp"), axis=1, keepdims=False)
    seed = cotangent.astype(F32) * lax.dynamic_index_in_dim(scales, here, axis=0, keepdims=False)
    lanes_of_scales = jnp.broadcast_to(scales[:, None], (n_dp, 128))
    scales = jnp.broadcast_to(scales[:, None, None], (n_dp, rows, 1)).reshape(n_dp * rows, 1)
    if not square:
        normed_all = spread((inputs * first_root * first_full).astype(BF16), 2)
        cot_all = spread(cotangent, 3)

    def conv_columns(start, size):
        return lax.dynamic_slice_in_dim(conv_full, start + here * size, size, axis=1)

    conv_mine = jnp.concatenate(
        [conv_columns(0, key), conv_columns(n_dp * key, key), conv_columns(2 * n_dp * key, value)], axis=1
    ).astype(F32)
    decay_mine = jnp.pad(
        jnp.stack(
            [
                lax.dynamic_slice_in_dim(decay_scale, here * heads, heads),
                lax.dynamic_slice_in_dim(decay_bias, here * heads, heads),
            ]
        ),
        ((0, 0), (0, 128 - heads)),
    )
    gain = output_gain[None, :]

    projected = dot(normed_all, in_full)
    mixed, inverse, solved, core = mixer_forward(projected, conv_mine, decay_mine, gain, heads, rows)
    if square:
        middle, second_all = relay(
            mixed.reshape(n_dp, rows, value), out_full, None, NN, NN, second_full, (tokens,), False, 4
        )
        upgate, hidden, hidden_seed = units_forward(second_all, up_full, lanes_of_scales, units, main)
        second_all = second_all.reshape(n_dp * rows, width)
    else:
        middle = inputs + total(dot(mixed, out_full, out=BF16), 4)
        second_root = lax.rsqrt(jnp.mean(middle * middle, axis=-1, keepdims=True) + EPSILON)
        second_all = spread((middle * second_root * second_full).astype(BF16), 5)
        upgate = dot(second_all, up_full)

        def halves_of(a):
            return (a[:, :main], a[:, main : 2 * main]), (a[:, 2 * main : main + units], a[:, main + units :])

        acts = [(g, u, jax.nn.sigmoid(g)) for g, u in halves_of(upgate)]
        hidden = jnp.concatenate([g * s * u for g, u, s in acts], axis=1)
        hidden_seed = (hidden * scales).astype(BF16)
        hidden = hidden.astype(BF16)

    down_grad = dot(hidden_seed, cot_all, TN, out=BF16)
    down_grad, cot_all = lax.optimization_barrier((down_grad, cot_all))
    if square:
        upgate_low = units_backward(
            cot_all.reshape(n_dp, rows, width), down_full, upgate, lanes_of_scales, units, main
        )
    else:
        hidden_grad = dot(cot_all, down_full, NT) * scales
        parts = list(zip(acts, (hidden_grad[:, :main], hidden_grad[:, main:])))
        upgate_low = jnp.concatenate(
            [x for (g, u, s), grad in parts for x in (grad * u * s * (1.0 + g * (1.0 - s)), grad * g * s)], axis=1
        ).astype(BF16)
    upgate_grad = dot(second_all, upgate_low, TN, out=BF16)
    upgate_low, upgate_grad = lax.optimization_barrier((upgate_low, upgate_grad))

    def norm_back(v, root, gain_row, grad):
        hat = v * root
        scaled = grad * gain_row
        gain_grad = jnp.sum(grad * hat, axis=0)
        return root * (scaled - hat * jnp.mean(scaled * hat, axis=-1, keepdims=True)), gain_grad

    def owned_rows(a):
        return lax.psum_scatter(a, "fsdp", scatter_dimension=0, tiled=True)

    def owned_parts(a):
        a = a.reshape(n_dp, n_z, own_d, a.shape[-1]).transpose(1, 0, 2, 3)
        return lax.psum_scatter(a.reshape(width, -1), "fsdp", scatter_dimension=0, tiled=True)

    down_total = owned_rows(down_grad)
    block_part = dot(hidden, down_full, out=BF16)
    upgate_low, upgate_grad, down_total, block_part = lax.optimization_barrier(
        (upgate_low, upgate_grad, down_total, block_part)
    )
    upgate_sum = owned_parts(upgate_grad)
    if square:
        middle_grad, middle_all, mixed_grad, second_grad = relay(
            upgate_low.reshape(n_dp, rows, 2 * units), up_full, out_full, NT, NT, second_full, (middle, seed), True, 6
        )
        middle_all = middle_all.reshape(n_dp * rows, width)
        mixed_grad = mixed_grad.reshape(n_dp * rows, value)
    else:
        normed_two_grad = total(dot(upgate_low, up_full, NT, out=BF16), 6)
        middle_part, second_grad = norm_back(middle, second_root, second_full, normed_two_grad)
        middle_grad = seed + middle_part
        middle_all = spread(middle_grad.astype(BF16), 8)
        mixed_grad = dot(middle_all, out_full, NT)
    output_grad = dot(mixed, middle_all, TN, out=BF16)
    mixed_grad, output_grad, upgate_sum = lax.optimization_barrier((mixed_grad, output_grad, upgate_sum))
    output_total = owned_rows(output_grad)
    projected_low, conv_grad, gain_grad, decay_grad = mixer_backward(
        projected, conv_mine, decay_mine, gain, inverse, solved, core, mixed_grad, heads, rows
    )
    projected_low, output_total = lax.optimization_barrier((projected_low, output_total))
    def upgate_rows(a):
        return jnp.concatenate(
            [
                jnp.concatenate([x, y], axis=2).transpose(1, 0, 2).reshape(own_d, -1)
                for x, y in (
                    (a[:, :, :main], a[:, :, 2 * main : main + units]),
                    (a[:, :, main : 2 * main], a[:, :, main + units :]),
                )
            ],
            axis=1,
        ).astype(F32)

    def decay_rows(a):
        a = a.transpose(1, 0, 2).astype(F32)
        return jnp.concatenate(
            [a[:, :, :heads].reshape(own_d, -1), a[:, :, heads : 2 * heads].reshape(own_d, -1)], axis=1
        )

    in_grad = dot(normed_all, projected_low, TN, out=BF16)
    down_total = down_total.astype(F32)
    output_total = output_total.astype(F32)
    if square:
        lines = jnp.concatenate(
            [
                jnp.zeros((1, width), F32),
                second_grad.reshape(1, width),
                jnp.tile(gain_grad[:, :128], (1, width // 128)),
                jnp.tile(gain_grad[:, 128:], (1, width // 128)),
                jnp.tile(jnp.pad(decay_grad[:, :heads].reshape(1, -1), ((0, 0), (0, 128 - 2 * heads))), (1, width // 128)),
                jnp.zeros((3, width), F32),
            ],
            axis=0,
        )
        conv_lines = jnp.zeros((8, n_dp * (2 * key + value)), F32)
        for at, a, b in (
            (here * key, 0, key),
            (n_dp * key + here * key, key, 2 * key),
            (2 * n_dp * key + here * value, 2 * key, 2 * key + value),
        ):
            conv_lines = lax.dynamic_update_slice(conv_lines, conv_grad[:, a:b], (0, at))
        result, tokens_grad, input_total, decay_total, up_total, lines, conv_lines = conclude(
            in_grad.reshape(n_dp, n_z, own_d, cols),
            projected_low.reshape(n_dp, rows, cols),
            in_full,
            block_part.reshape(n_dp, rows, width),
            upgate_sum.reshape(n_dp, own_d, 2 * units),
            tokens,
            middle,
            middle_grad,
            first_full,
            lines,
            conv_lines,
            bounds,
            9,
        )
        input_total = input_total.astype(F32)
        decay_total = decay_rows(decay_total)
        upgate_total = upgate_rows(up_total)
        summed = jnp.sum(lines, axis=0)
        per = 128 // own_d
        place = lax.rem(flat, per) * own_d
        first_total = lax.dynamic_slice_in_dim(summed[0], place, own_d)
        second_total = lax.dynamic_slice_in_dim(summed[1], place, own_d)
        gain_total = summed[2:4].reshape(-1)
        scale_bias = jnp.sum(lines[:, 4, : 2 * heads].reshape(n_dp, n_z, 2, heads), axis=1)
        scale_total = scale_bias[:, 0].reshape(-1)
        bias_total = scale_bias[:, 1].reshape(-1)
        conv_total = jnp.sum(conv_lines, axis=0)[:taps]
    else:
        projected_low, in_grad = lax.optimization_barrier((projected_low, in_grad))
        back_one = dot(projected_low, in_full, NT, out=BF16)
        in_sum = owned_parts(in_grad)
        normed_one_grad = total(back_one, 9)
        result = middle + total(block_part, 7)
        input_part, first_grad = norm_back(inputs, first_root, first_full, normed_one_grad)
        tokens_grad = middle_grad + input_part

        up_total = lax.all_to_all(upgate_sum.reshape(n_dp, own_d, -1), "dp", 0, 0, tiled=True)
        upgate_total = upgate_rows(up_total)
        in_total = lax.all_to_all(in_sum.reshape(n_dp, own_d, -1), "dp", 0, 0, tiled=True)
        decay_total = decay_rows(in_total[:, :, bounds[-1] :])
        in_total = in_total.transpose(1, 0, 2).astype(F32)
        input_total = jnp.concatenate(
            [in_total[:, :, a:b].reshape(own_d, -1) for a, b in zip(bounds[:-1], bounds[1:])], axis=1
        )

        share = key // own_conv, value // own_conv
        owner = jnp.concatenate(
            [
                here * share[0] + jnp.arange(share[0]),
                (n_dp + here) * share[0] + jnp.arange(share[0]),
                2 * n_dp * share[0] + here * share[1] + jnp.arange(share[1]),
            ]
        )
        blocks = conv_grad.reshape(taps, -1, own_conv).transpose(1, 0, 2).reshape(-1, taps * own_conv)
        for_owner = owner[None, :] == jnp.arange(count)[:, None]
        everyone = jnp.concatenate([gain_grad.reshape(-1), decay_grad[:, :heads].reshape(-1)])
        packets = jnp.concatenate(
            [
                first_grad.reshape(count, own_d),
                second_grad.reshape(count, own_d),
                jnp.sum(jnp.where(for_owner[:, :, None], blocks[None], 0.0), axis=1),
                jnp.broadcast_to(everyone[None], (count, everyone.size)),
            ],
            axis=1,
        )
        size = packets.shape[1]
        lines = -(-size // 1024) * 8
        packets = jnp.pad(packets, ((0, 0), (0, lines * 128 - size))).reshape(count, lines, 128)
        shared = scatter_small(packets, n_dp, n_z, 10).reshape(count, -1)
        summed = jnp.sum(shared, axis=0)
        first_total = summed[:own_d]
        second_total = summed[own_d : 2 * own_d]
        start = 2 * own_d + taps * own_conv
        conv_total = summed[2 * own_d : start].reshape(taps, own_conv)
        gain_total = summed[start : start + gain_grad.size]
        start += gain_grad.size
        scale_bias = jnp.sum(shared[:, start : start + 2 * heads].reshape(n_dp, n_z, 2, heads), axis=1)
        scale_total = scale_bias[:, 0].reshape(-1)
        bias_total = scale_bias[:, 1].reshape(-1)
    return (
        result,
        tokens_grad,
        first_total,
        input_total,
        decay_total,
        conv_total,
        scale_total,
        bias_total,
        gain_total,
        output_total,
        second_total,
        upgate_total,
        down_total,
    )


def solution(mesh):
    both = ("dp", "fsdp")
    rows, vector = P(both, None), P(both)
    return jax.shard_map(
        functools.partial(local, mesh.shape["dp"], mesh.shape["fsdp"]),
        mesh=mesh,
        in_specs=(
            rows, rows, vector, vector, rows, rows, P(None, both), P(), P(), P(), rows, vector, rows, rows,
        ),
        out_specs=(
            rows, rows, vector, rows, rows, P(None, both), P(), P(), P(), rows, vector, rows, rows,
        ),
        check_vma=False,
    )
```

```python
import functools

import jax
import jax.numpy as jnp
from jax import lax
from jax.experimental import pallas as pl
from jax.experimental.pallas import tpu as pltpu
from jax.sharding import PartitionSpec as P

MESH = pl.DeviceIdType.MESH
F32 = jnp.float32
BF16 = jnp.bfloat16
EPSILON = 1e-06
DK = 128
DV = 256
BASE = 8
NN = (((1,), (0,)), ((), ()))
NT = (((1,), (1,)), ((), ()))
TN = (((0,), (0,)), ((), ()))


def dot1(a, b, dims=NN):
    return lax.dot_general(a.astype(BF16), b.astype(BF16), dims, preferred_element_type=F32)


def halves(a):
    if a.dtype == BF16:
        return (a,)
    high = a.astype(BF16)
    return (high, (a - high.astype(F32)).astype(BF16))


def dot3(a, b, dims=NN):
    a, b = halves(a), halves(b)
    total = lax.dot_general(a[0], b[0], dims, preferred_element_type=F32)
    if len(a) > 1:
        total = total + lax.dot_general(a[1], b[0], dims, preferred_element_type=F32)
    if len(b) > 1:
        total = total + lax.dot_general(a[0], b[1], dims, preferred_element_type=F32)
    return total


def sum_rows(mask, b):
    mask = jnp.where(mask, 1.0, 0.0).astype(BF16)
    high = b.astype(BF16)
    rest = b - high.astype(F32)
    middle = rest.astype(BF16)
    low = (rest - middle.astype(F32)).astype(BF16)
    return dot1(mask, high) + (dot1(mask, middle) + dot1(mask, low))


def shift_down(v, n):
    turned = pltpu.roll(v, n, 0)
    places = lax.broadcasted_iota(jnp.int32, (8, 1), 0)
    return jnp.concatenate([jnp.where(places >= n, turned[:8], 0.0), turned[8:]], axis=0)


def shift_up(v, n):
    length = v.shape[0]
    turned = pltpu.roll(v, length - n, 0)
    places = lax.broadcasted_iota(jnp.int32, (8, 1), 0)
    return jnp.concatenate([turned[:-8], jnp.where(places < 8 - n, turned[-8:], 0.0)], axis=0)


def conv(c, taps):
    count = taps.shape[0]
    total = c * taps[count - 1 : count]
    for j in range(count - 1):
        total = total + shift_down(c, count - 1 - j) * taps[j : j + 1]
    return total


def sigmoid(v):
    return 1.0 / (1.0 + jnp.exp(-v))


def gate_of(v):
    return 0.5 * jnp.tanh(0.5 * v) + 0.5


def softplus(v):
    return jnp.maximum(v, 0.0) + jnp.log1p(jnp.exp(-jnp.abs(v)))


def unit_inverses(lowers, row_ids, col_ids):
    length = lowers[0].shape[0]
    size = BASE
    same = row_ids // size == col_ids // size
    pick = jnp.where(col_ids[:, :128] == lax.rem(row_ids[:, :128], size), 1.0, 0.0).astype(BF16)
    lanes = lax.broadcasted_iota(jnp.int32, (length // size, size, 128), 2)
    places = lax.broadcasted_iota(jnp.int32, (length // size, size, 128), 1)
    compact = [dot3(jnp.where(same, lower, 0.0), pick).reshape(length // size, size, 128) for lower in lowers]
    solved = [jnp.where(lanes == places, 1.0, 0.0) for _ in lowers]
    for j in range(size - 1):
        solved = [x - a[:, :, j : j + 1] * x[:, j : j + 1, :] for a, x in zip(compact, solved)]
    inverses = [jnp.where(same, dot3(x.reshape(length, 128), pick, NT), 0.0) for x in solved]
    while size < length:
        wide = 2 * size
        off = (row_ids // wide == col_ids // wide) & (row_ids // size != col_ids // size)
        inner = [dot3(jnp.where(off, lower, 0.0), inverse) for lower, inverse in zip(lowers, inverses)]
        inverses = [inverse - dot3(inverse, x) for inverse, x in zip(inverses, inner)]
        size = wide
    return inverses


def common(raw, decay, heads, length):
    rows = lax.broadcasted_iota(jnp.int32, (length, 1), 0)
    row_ids = lax.broadcasted_iota(jnp.int32, (length, length), 0)
    col_ids = lax.broadcasted_iota(jnp.int32, (length, length), 1)
    lanes = lax.broadcasted_iota(jnp.int32, raw.shape, 1)
    shifted = raw + decay[1:2]
    rate = jnp.where(lanes < heads, -jnp.exp(decay[0:1]) * softplus(shifted), 0.0)
    beta = sigmoid(raw)
    cumulated = sum_rows(row_ids >= col_ids, rate)
    return rows, row_ids, col_ids, lanes, shifted, rate, beta, cumulated, cumulated.T


def head_parts(h, heads):
    key = slice(h * DK, (h + 1) * DK)
    keyk = slice((heads + h) * DK, (heads + h + 1) * DK)
    val = slice(heads * DV + h * DV, heads * DV + (h + 1) * DV)
    gat = slice(2 * heads * DV + h * DV, 2 * heads * DV + (h + 1) * DV)
    return key, keyk, val, gat


def mixer_forward_kernel(heads, proj_ref, raw_ref, taps_ref, decay_ref, gain_ref, mixed_ref, inv_ref, solved_ref, core_ref, conv_ref):
    length = proj_ref.shape[0]
    decay = decay_ref[...]
    gain = gain_ref[...]
    raw = raw_ref[...]
    rows, row_ids, col_ids, lanes, shifted, rate, beta, cumulated, cum_t = common(raw, decay, heads, length)
    def active(cols):
        y = conv(proj_ref[:, cols], taps_ref[:, cols])
        conv_ref[:, cols] = y
        return y * gate_of(y)

    parts = [head_parts(h, heads) for h in range(heads)]
    queries, keys, values, growths, betas, lowers = [], [], [], [], [], []
    for h, (qs, ks, vs, gs) in enumerate(parts):
        k = active(ks)
        k = (k * lax.rsqrt(jnp.sum(k * k, axis=-1, keepdims=True) + EPSILON)).astype(BF16)
        beta_h = beta[:, heads + h : heads + h + 1]
        gap = cumulated[:, h : h + 1] - cum_t[h : h + 1, :]
        growth = jnp.where(row_ids >= col_ids, jnp.exp(jnp.where(row_ids >= col_ids, gap, 0.0)), 0.0)
        keys.append(k)
        growths.append(growth)
        betas.append(beta_h)
        lowers.append(jnp.where(row_ids > col_ids, growth * dot1(k, k, NT) * beta_h, 0.0))
    inverses = unit_inverses(lowers, row_ids, col_ids)
    for h, (qs, ks, vs, gs) in enumerate(parts):
        q = active(qs)
        q = (q * lax.rsqrt(jnp.sum(q * q, axis=-1, keepdims=True) + EPSILON) * DK ** (-0.5)).astype(BF16)
        v = active(vs).astype(BF16)
        inv_ref[h] = inverses[h]
        solved = dot3(inverses[h], betas[h] * v.astype(F32))
        core = dot3(growths[h] * dot1(q, keys[h], NT), solved)
        solved_ref[:, h * DV : (h + 1) * DV] = solved
        core_ref[:, h * DV : (h + 1) * DV] = core
        gate = proj_ref[:, gs]
        normed = core * lax.rsqrt(jnp.mean(core * core, axis=-1, keepdims=True) + EPSILON) * gain
        mixed_ref[:, h * DV : (h + 1) * DV] = (normed * (gate * gate_of(gate))).astype(BF16)


def mixer_forward(proj, raw, taps, decay, gain, heads, length):
    tokens, width = proj.shape
    seqs = tokens // length
    hv = heads * DV
    row = lambda cols: pl.BlockSpec((length, cols), lambda s: (s, 0))
    whole = lambda a: pl.BlockSpec(a.shape, lambda s: (0,) * a.ndim)
    return pl.pallas_call(
        functools.partial(mixer_forward_kernel, heads),
        grid=(seqs,),
        in_specs=[row(width), row(128), whole(taps), whole(decay), whole(gain)],
        out_specs=[row(hv), pl.BlockSpec((None, heads, length, length), lambda s: (s, 0, 0, 0)), row(hv), row(hv), row(taps.shape[1])],
        out_shape=[
            jax.ShapeDtypeStruct((tokens, hv), BF16),
            jax.ShapeDtypeStruct((seqs, heads, length, length), F32),
            jax.ShapeDtypeStruct((tokens, hv), F32),
            jax.ShapeDtypeStruct((tokens, hv), F32),
            jax.ShapeDtypeStruct((tokens, taps.shape[1]), F32),
        ],
        cost_estimate=busy(55), compiler_params=pltpu.CompilerParams(vmem_limit_bytes=48 << 20),
    )(proj, raw, taps, decay, gain)


def mixer_backward_kernel(
    heads, proj_ref, raw_ref, taps_ref, decay_ref, gain_ref, inv_ref, solved_ref, core_ref, pre_ref, grad_ref,
    low_ref, raw_low_ref, conv_ref, gain_grad_ref, decay_grad_ref,
):
    length = proj_ref.shape[0]
    count = taps_ref.shape[0]
    decay = decay_ref[...]
    gain = gain_ref[...]
    raw = raw_ref[...]
    rows, row_ids, col_ids, lanes, shifted, rate, beta, cumulated, cum_t = common(raw, decay, heads, length)
    within = row_ids >= col_ids
    strict = row_ids > col_ids

    @pl.when(pl.program_id(0) == 0)
    def _():
        conv_ref[...] = jnp.zeros_like(conv_ref)
        gain_grad_ref[...] = jnp.zeros_like(gain_grad_ref)
        decay_grad_ref[...] = jnp.zeros_like(decay_grad_ref)

    cum_grad = jnp.zeros(raw.shape, F32)
    beta_grad = jnp.zeros(raw.shape, F32)
    for h in range(heads):
        qs, ks, vs, gs = head_parts(h, heads)
        hs = slice(h * DV, (h + 1) * DV)

        def active(cols):
            y = pre_ref[:, cols]
            s = gate_of(y)
            return y * s, s * (1.0 + y * (1.0 - s))

        def conv_back(cols, grad):
            c = proj_ref[:, cols]
            total = grad * taps_ref[count - 1 : count, cols]
            conv_ref[count - 1 : count, cols] += jnp.sum(grad * c, axis=0, keepdims=True)
            for j in range(count - 1):
                n = count - 1 - j
                later = shift_up(grad, n)
                total = total + later * taps_ref[j : j + 1, cols]
                conv_ref[j : j + 1, cols] += jnp.sum(later * c, axis=0, keepdims=True)
            low_ref[:, cols] = total.astype(BF16)

        core = core_ref[:, hs]
        gate = proj_ref[:, gs]
        gate_sig = gate_of(gate)
        grad = grad_ref[:, hs]
        root = lax.rsqrt(jnp.mean(core * core, axis=-1, keepdims=True) + EPSILON)
        normed = core * root
        silu_gate = gate * gate_sig
        gain_grad_ref[...] += jnp.sum(grad * normed * silu_gate, axis=0, keepdims=True)
        low_ref[:, gs] = (grad * normed * gain * gate_sig * (1.0 + gate * (1.0 - gate_sig))).astype(BF16)
        normed_grad = grad * gain * silu_gate
        core_grad = root * (normed_grad - normed * jnp.mean(normed_grad * normed, axis=-1, keepdims=True))

        q_act, q_slope = active(qs)
        q_root = lax.rsqrt(jnp.sum(q_act * q_act, axis=-1, keepdims=True) + EPSILON)
        q_unit = q_act * q_root
        q = (q_unit * DK ** (-0.5)).astype(BF16)
        k_act, k_slope = active(ks)
        k_root = lax.rsqrt(jnp.sum(k_act * k_act, axis=-1, keepdims=True) + EPSILON)
        k_unit = k_act * k_root
        k = k_unit.astype(BF16)
        v_act, v_slope = active(vs)
        v = v_act.astype(BF16).astype(F32)
        beta_h = beta[:, heads + h : heads + h + 1]
        gap = cumulated[:, h : h + 1] - cum_t[h : h + 1, :]
        growth = jnp.where(within, jnp.exp(jnp.where(within, gap, 0.0)), 0.0)
        decayed_gram = jnp.where(strict, growth * dot1(k, k, NT), 0.0)
        weights = growth * dot1(q, k, NT)
        inverse = inv_ref[h]
        solved = solved_ref[:, hs]
        core_low = core_grad.astype(BF16)
        solved_grad = dot3(weights, core_low, TN)
        weights_grad = dot3(core_low, solved, NT)
        value_grad = dot3(inverse, solved_grad.astype(BF16), TN)
        lower_grad = jnp.where(strict, -dot3(value_grad.astype(BF16), solved, NT), 0.0)
        gap_part = lower_grad * decayed_gram
        beta_col = jnp.sum(gap_part, axis=-1, keepdims=True) + jnp.sum(value_grad * v, axis=-1, keepdims=True)
        gap_grad = gap_part * beta_h + weights_grad * weights
        cum_col = jnp.sum(gap_grad, axis=-1, keepdims=True)
        cum_row = jnp.sum(gap_grad, axis=0, keepdims=True)
        cum_col = cum_col - jnp.broadcast_to(cum_row, (8, length)).T[:, 0:1]
        gram_grad = lower_grad * growth * beta_h
        score_grad = weights_grad * growth
        k_grad = dot3(gram_grad, k) + dot3(gram_grad, k, TN) + dot3(score_grad, q, TN)
        q_grad = dot3(score_grad, k)
        cum_grad = jnp.where(lanes == h, cum_col, cum_grad)
        beta_grad = jnp.where(lanes == heads + h, beta_col, beta_grad)

        q_grad = q_grad * DK ** (-0.5)
        q_grad = q_root * (q_grad - q_unit * jnp.sum(q_grad * q_unit, axis=-1, keepdims=True))
        conv_back(qs, q_grad * q_slope)
        k_grad = k_root * (k_grad - k_unit * jnp.sum(k_grad * k_unit, axis=-1, keepdims=True))
        conv_back(ks, k_grad * k_slope)
        conv_back(vs, value_grad * beta_h * v_slope)

    rate_grad = sum_rows(col_ids >= row_ids, cum_grad)
    bias_part = rate_grad * -jnp.exp(decay[0:1]) * sigmoid(shifted)
    raw_grad = jnp.where(lanes < heads, bias_part, beta_grad * beta * (1.0 - beta))
    raw_low_ref[...] = raw_grad.astype(BF16)
    decay_grad_ref[0:1] += jnp.sum(jnp.where(lanes < heads, rate_grad * rate, 0.0), axis=0, keepdims=True)
    decay_grad_ref[1:2] += jnp.sum(jnp.where(lanes < heads, bias_part, 0.0), axis=0, keepdims=True)


def mixer_backward(proj, raw, taps, decay, gain, inverse, solved, core, pre, grad, heads, length):
    tokens, width = proj.shape
    seqs = tokens // length
    hv = heads * DV
    row = lambda cols: pl.BlockSpec((length, cols), lambda s: (s, 0))
    whole = lambda a: pl.BlockSpec(a.shape, lambda s: (0,) * a.ndim)
    return pl.pallas_call(
        functools.partial(mixer_backward_kernel, heads),
        grid=(seqs,),
        in_specs=[row(width), row(128), whole(taps), whole(decay), whole(gain),
                  pl.BlockSpec((None, heads, length, length), lambda s: (s, 0, 0, 0)), row(hv), row(hv), row(taps.shape[1]), row(hv)],
        out_specs=[row(width), row(128), whole(taps), whole(gain), whole(decay)],
        out_shape=[
            jax.ShapeDtypeStruct((tokens, width), BF16),
            jax.ShapeDtypeStruct((tokens, 128), BF16),
            jax.ShapeDtypeStruct(taps.shape, F32),
            jax.ShapeDtypeStruct(gain.shape, F32),
            jax.ShapeDtypeStruct(decay.shape, F32),
        ],
        cost_estimate=busy(50), compiler_params=pltpu.CompilerParams(vmem_limit_bytes=56 << 20),
    )(proj, raw, taps, decay, gain, inverse, solved, core, pre, grad)


def busy(us):
    return pl.CostEstimate(flops=us * 1_000_000_000, bytes_accessed=0, transcendentals=0)


def _place(n_dp):
    me = lax.axis_index("dp")
    z = lax.axis_index("fsdp")
    core = lax.rem(me, 2)
    chip = me // 2
    return me, z, core, lax.rem(chip, 2), chip // 2

def ag_square(x, cid, chunks=4):
    rows, cols = x.shape
    r = rows // chunks
    def kernel(x_ref, o_ref, lsem, ssem, rsem, dssem, drsem, fs, fr):
        me, z, core, cx, cy = _place(8)
        dev = lambda dx, dy, c: 2*(2*lax.rem(cy+dy,2)+lax.rem(cx+dx,2))+c
        nx, ny, nd = dev(1,0,core), dev(0,1,core), dev(1,1,core)
        src = dev(1-core, core, core)
        tgt = dev(core, 1-core, core)
        sib = dev(0,0,1-core)
        bar = pltpu.get_barrier_semaphore()
        for d in (sib,nx,ny):
            pl.semaphore_signal(bar, inc=1, device_id=(d,z), device_id_type=MESH)
        pl.semaphore_wait(bar, 3)
        lc = pltpu.make_async_copy(x_ref, o_ref.at[me], lsem); lc.start()
        def rc(a, b, s, q, d):
            return pltpu.make_async_remote_copy(a, b, s, q, device_id=(d,z), device_id_type=MESH)
        own = []
        for c in range(chunks):
            sl = pl.ds(c*r, r)
            for i, d in ((0,nx),(1,ny)):
                cp = rc(x_ref.at[sl], o_ref.at[me,sl], ssem.at[i,c], rsem.at[i,c], d); cp.start(); own.append(cp)
        sibs=[]
        for c in range(chunks):
            sl = pl.ds(c*r, r)
            cp = rc(x_ref.at[sl], o_ref.at[me,sl], fs.at[0,c], fr.at[0,c], sib); cp.start(); sibs.append(cp)
        other = dev(core, 1-core, core)
        for c in range(chunks):
            sl = pl.ds(c*r, r)
            rc(x_ref.at[sl], o_ref.at[src,sl], ssem.at[core,c], rsem.at[core,c], sib).wait_recv()
            cp = rc(o_ref.at[src,sl], o_ref.at[src,sl], dssem.at[c], drsem.at[c], tgt); cp.start(); sibs.append((cp,))
            cp = rc(o_ref.at[src,sl], o_ref.at[src,sl], fs.at[1,c], fr.at[1,c], sib); cp.start(); sibs.append(cp)
            rc(x_ref.at[sl], o_ref.at[other,sl], ssem.at[1-core,c], rsem.at[1-core,c], sib).wait_recv()
            cp = rc(o_ref.at[other,sl], o_ref.at[other,sl], fs.at[2,c], fr.at[2,c], sib); cp.start(); sibs.append(cp)
        for c in range(chunks):
            sl = pl.ds(c*r, r)
            rc(x_ref.at[sl], o_ref.at[nd,sl], dssem.at[c], drsem.at[c], sib).wait_recv()
            cp = rc(o_ref.at[nd,sl], o_ref.at[nd,sl], fs.at[3,c], fr.at[3,c], sib); cp.start(); sibs.append(cp)
        for cp in own: cp.wait_send()
        for cp in sibs:
            if isinstance(cp, tuple): cp[0].wait_send()
            else: cp.wait()
        lc.wait()
    D=pltpu.SemaphoreType.DMA
    return pl.pallas_call(kernel, out_shape=jax.ShapeDtypeStruct((8,rows,cols),x.dtype),
        in_specs=[pl.BlockSpec(memory_space=pl.ANY)], out_specs=pl.BlockSpec(memory_space=pl.ANY),
        scratch_shapes=[D, D((2,chunks)), D((2,chunks)), D((chunks,)), D((chunks,)), D((4,chunks)), D((4,chunks))],
        cost_estimate=busy(40), compiler_params=pltpu.CompilerParams(collective_id=cid, has_side_effects=True))(x)

def rs_square(x, cid, chunks=4):
    _, rows, cols = x.shape
    r = rows // chunks
    def kernel(x_ref, o_ref, X, A, B, R, lsem, sa, ra, sb, rb):
        me, z, core, cx, cy = _place(8)
        dev = lambda dx, dy, c: 2*(2*lax.rem(cy+dy,2)+lax.rem(cx+dx,2))+c
        fdx, fdy = 1-core, core
        nf, ng = dev(fdx,fdy,core), dev(fdy,fdx,core)
        sib = dev(0,0,1-core)
        bar = pltpu.get_barrier_semaphore()
        for d in (sib,nf,ng):
            pl.semaphore_signal(bar, inc=1, device_id=(d,z), device_id_type=MESH)
        mine = [dev(1,1,core), ng, nf, me]
        s_f, s_g = dev(core,1-core,1-core), dev(1-core,core,1-core)
        theirs = [dev(1,1,1-core), s_g, s_f, sib]
        loads=[]
        for k in range(4):
            for c in range(chunks):
                sl=pl.ds(c*r,r)
                cp=pltpu.make_async_copy(x_ref.at[mine[k],sl], X.at[k,sl], lsem.at[k,c]); cp.start(); loads.append(cp)
        pl.semaphore_wait(bar, 3)
        def rc(a, b, s, q, d):
            return pltpu.make_async_remote_copy(a, b, s, q, device_id=(d,z), device_id_type=MESH)
        sends=[]; ga={}
        for k in range(4):
            for c in range(chunks):
                sl=pl.ds(c*r,r)
                cp=rc(x_ref.at[theirs[k],sl], A.at[k,sl], sa.at[k,c], ra.at[k,c], sib); cp.start(); sends.append(cp); ga[k,c]=cp
        def pair(k,c):
            sl=pl.ds(c*r,r)
            loads[k*chunks+c].wait(); ga[k,c].wait_recv()
            return X[k,sl].astype(F32)+A[k,sl].astype(F32)
        gb={}
        def ship(slot, c, d):
            sl=pl.ds(c*r,r)
            cp=rc(B.at[slot,sl], R.at[slot,sl], sb.at[slot,c], rb.at[slot,c], d); cp.start(); sends.append(cp); gb[slot,c]=cp
        for c in range(chunks):
            sl=pl.ds(c*r,r)
            B[0,sl]=pair(0,c).astype(BF16); ship(0,c,nf)
        for c in range(chunks):
            sl=pl.ds(c*r,r)
            B[2,sl]=pair(2,c).astype(BF16); ship(2,c,nf)
        for c in range(chunks):
            sl=pl.ds(c*r,r)
            v=pair(1,c)
            gb[0,c].wait_recv()
            B[1,sl]=(v+R[0,sl].astype(F32)).astype(BF16); ship(1,c,ng)
        for c in range(chunks):
            sl=pl.ds(c*r,r)
            v=pair(3,c)
            gb[2,c].wait_recv()
            o_ref[sl]=v+R[2,sl].astype(F32)
        for c in range(chunks):
            sl=pl.ds(c*r,r)
            gb[1,c].wait_recv()
            o_ref[sl]=o_ref[sl]+R[1,sl].astype(F32)
        for cp in sends: cp.wait_send()
    D=pltpu.SemaphoreType.DMA
    V=lambda n: pltpu.VMEM((n,rows,cols),x.dtype)
    return pl.pallas_call(kernel, out_shape=jax.ShapeDtypeStruct((rows,cols),F32),
        in_specs=[pl.BlockSpec(memory_space=pl.ANY)], out_specs=pl.BlockSpec(memory_space=pltpu.VMEM),
        scratch_shapes=[V(4),V(4),V(3),V(3), D((4,chunks)), D((4,chunks)), D((4,chunks)), D((3,chunks)), D((3,chunks))],
        cost_estimate=busy(40), compiler_params=pltpu.CompilerParams(collective_id=cid, has_side_effects=True, vmem_limit_bytes=40<<20))(x)

def begin(weight, ups, tokens, cotangent, small, bounds, n_z, cid):
    own = weight.shape[0]
    cols = bounds[-1]
    units = ups.shape[2]
    rows, width = tokens.shape
    count = 8 * n_z
    chunks = 2
    part = rows // chunks

    def kernel(
        w_ref, u_ref, t_ref, c_ref, small_ref, w_out, u_out, n_out, c_out, small_out,
        toks, lsem, a_send, a_recv, g_send, g_recv, up_send, up_recv, down_send, down_recv,
        small_send, small_recv, x_send, x_recv, d_send, d_recv, f_send, f_recv,
    ):
        me, z, core, cx, cy = _place(8)
        flat = me * n_z + z
        bar = pltpu.get_barrier_semaphore()

        def dev(dx, dy, c):
            return 2 * (2 * lax.rem(cy + dy, 2) + lax.rem(cx + dx, 2)) + c

        sib = dev(0, 0, 1 - core)

        def partner(o):
            return dev(o // 4, lax.rem(o // 2, 2), lax.rem(core + o, 2))

        def anyone(o):
            other = lax.rem(flat + o, count)
            return (other // n_z, lax.rem(other, n_z))

        def remote(src, dst, send, recv, device):
            return pltpu.make_async_remote_copy(src, dst, send, recv, device_id=device, device_id_type=MESH)

        def loop(first, last, body):
            def step(o, _):
                body(o)
                return 0

            lax.fori_loop(first, last, step, 0)

        def sections(q):
            for first, last in zip(bounds[:-1], bounds[1:]):
                size = last - first
                at = pl.multiple_of(8 * first + q * size, 128)
                yield w_ref.at[:, pl.ds(at, size)], w_out.at[me, z, :, pl.ds(first, size)]

        def send_piece(o):
            q = partner(o)
            for src, dst in sections(q):
                remote(src, dst, a_send.at[o - 1], a_recv.at[o - 1], (q, z)).start()

        def landed(o):
            at = w_out.at[partner(o), z]
            return remote(at, at, a_send.at[o - 1], a_recv.at[o - 1], (sib, z))

        def up(t, o):
            at = w_out.at[partner(o), z - t]
            return remote(at, at, up_send.at[t, o], up_recv.at[t, o], (me, z + 1))

        def down(t, o):
            at = w_out.at[partner(o), z + t]
            return remote(at, at, down_send.at[t, o], down_recv.at[t, o], (me, z - 1))

        def pass_on(t, o):
            if t > 0:

                @pl.when(z >= t)
                def _():
                    at = w_out.at[partner(o), z - t]
                    remote(at, at, up_send.at[t - 1, o], up_recv.at[t - 1, o], (sib, z)).wait_recv()

                @pl.when(z + t < n_z)
                def _():
                    at = w_out.at[partner(o), z + t]
                    remote(at, at, down_send.at[t - 1, o], down_recv.at[t - 1, o], (sib, z)).wait_recv()

            if t < n_z - 1:

                @pl.when((z >= t) & (z < n_z - 1))
                def _():
                    up(t, o).start()

                @pl.when((z + t < n_z) & (z > 0))
                def _():
                    down(t, o).start()

        def sent(t, o):
            @pl.when((z >= t) & (z < n_z - 1))
            def _():
                up(t, o).wait_send()

            @pl.when((z + t < n_z) & (z > 0))
            def _():
                down(t, o).wait_send()

        def unit_piece(o):
            q = partner(o)
            return remote(u_ref.at[q], u_out.at[me], g_send.at[o - 1], g_recv.at[o - 1], (q, z))

        def tiny(o):
            return remote(small_ref, small_out.at[flat], small_send.at[o - 1], small_recv.at[o - 1], anyone(o))

        near = (dev(1, 0, core), dev(0, 1, core))
        source, other, across = dev(1 - core, core, core), dev(core, 1 - core, core), dev(1, 1, core)

        def gather(i, ref, out):
            def at(q, c):
                return out.at[q, pl.ds(c * part, part)]

            def mine(c):
                return ref.at[pl.ds(c * part, part)]

            def first(k, c):
                return remote(mine(c), at(me, c), x_send.at[i, k, c], x_recv.at[i, k, c], (near[k], z))

            def twin(k, q, c):
                src = mine(c) if k == 0 else at(q, c)
                return remote(src, at(q, c), f_send.at[i, k, c], f_recv.at[i, k, c], (sib, z))

            def second(c):
                return remote(at(source, c), at(source, c), d_send.at[i, c], d_recv.at[i, c], (other, z))

            def keep():
                return pltpu.make_async_copy(ref, out.at[me], lsem.at[i])

            def begin_():
                keep().start()
                for c in range(chunks):
                    for k in range(2):
                        first(k, c).start()
                for c in range(chunks):
                    twin(0, me, c).start()

            def forward():
                for c in range(chunks):
                    remote(mine(c), at(source, c), x_send.at[i, core, c], x_recv.at[i, core, c], (sib, z)).wait_recv()
                    second(c).start()
                    twin(1, source, c).start()
                    remote(
                        mine(c), at(other, c), x_send.at[i, 1 - core, c], x_recv.at[i, 1 - core, c], (sib, z)
                    ).wait_recv()
                    twin(2, other, c).start()

            def last():
                for c in range(chunks):
                    remote(at(across, c), at(across, c), d_send.at[i, c], d_recv.at[i, c], (other, z)).wait_recv()
                    twin(3, across, c).start()

            def finish():
                keep().wait()
                theirs = (sib, dev(core, 1 - core, 1 - core), dev(1 - core, core, 1 - core), dev(1, 1, 1 - core))
                for c in range(chunks):
                    for k in range(4):
                        remote(
                            at(theirs[k], c), at(theirs[k], c), f_send.at[i, k, c], f_recv.at[i, k, c], (sib, z)
                        ).wait_recv()

            def close():
                for c in range(chunks):
                    for k in range(2):
                        first(k, c).wait_send()
                    second(c).wait_send()
                    for k, q in enumerate((me, source, other, across)):
                        twin(k, q, c).wait_send()

            return begin_, forward, last, finish, close

        tok_begin, tok_forward, tok_last, tok_finish, tok_close = gather(0, t_ref, toks)
        cot_begin, cot_forward, cot_last, cot_finish, cot_close = gather(1, c_ref, c_out)

        loop(1, count, lambda o: pl.semaphore_signal(bar, inc=1, device_id=anyone(o), device_id_type=MESH))
        for src, dst in sections(me):
            pltpu.make_async_copy(src, dst, lsem.at[2]).start()
        keep_u = pltpu.make_async_copy(u_ref.at[me], u_out.at[me], lsem.at[3])
        keep_s = pltpu.make_async_copy(small_ref, small_out.at[flat], lsem.at[4])
        keep_u.start()
        keep_s.start()
        pl.semaphore_wait(bar, count - 1)

        loop(1, 8, send_piece)
        pltpu.make_async_copy(w_out.at[me, z], w_out.at[me, z], lsem.at[2]).wait()
        pass_on(0, 0)
        loop(1, count, lambda o: tiny(o).start())

        def first_leg(o):
            landed(o).wait_recv()
            pass_on(0, o)

        tok_begin()
        loop(1, 8, first_leg)
        loop(0, 8, lambda o: pass_on(1, o))
        tok_forward()
        cot_begin()
        loop(1, 8, lambda o: unit_piece(o).start())
        loop(0, 4, lambda o: pass_on(2, o))
        tok_last()
        tok_finish()
        keep_s.wait()
        loop(1, count, lambda o: tiny(o).wait_recv())

        lanes = lax.broadcasted_iota(jnp.int32, (1, 128), 1)
        per = 128 // own
        blocks = []
        for m in range(width // 128):
            block = small_out[m * per, 0:1, :].astype(F32)
            for i in range(1, per):
                block = jnp.where(lanes >= i * own, small_out[m * per + i, 0:1, :].astype(F32), block)
            blocks.append(block)
        gain = jnp.concatenate(blocks, axis=1)
        step = 32

        def norm_rows(o):
            def some(r, _):
                sl = pl.ds(r * step, step)
                v = toks[o, sl].astype(F32)
                n_out[o, sl] = (
                    v * lax.rsqrt(jnp.mean(v * v, axis=-1, keepdims=True) + EPSILON) * gain
                ).astype(BF16)
                return 0

            lax.fori_loop(0, rows // step, some, 0)

        def third_leg(o):
            pass_on(2, o)
            norm_rows(o - 4)
            norm_rows(o)

        loop(4, 8, third_leg)
        cot_forward()
        loop(0, 4, lambda o: pass_on(3, o))
        cot_last()
        loop(4, 8, lambda o: pass_on(3, o))
        cot_finish()
        for t in range(n_z - 1):
            loop(0, 8, functools.partial(sent, t))
        loop(1, 8, lambda o: landed(o).wait_send())
        loop(1, 8, lambda o: unit_piece(o).wait())
        loop(1, count, lambda o: tiny(o).wait_send())
        keep_u.wait()
        tok_close()
        cot_close()

    dma = pltpu.SemaphoreType.DMA
    anywhere, vmem = pl.BlockSpec(memory_space=pl.ANY), pl.BlockSpec(memory_space=pltpu.VMEM)
    plane = jax.ShapeDtypeStruct((8, rows, width), BF16)
    legs = n_z - 1
    return pl.pallas_call(
        kernel,
        out_shape=[
            jax.ShapeDtypeStruct((8, n_z, own, cols), BF16),
            jax.ShapeDtypeStruct((8, own, units), BF16),
            plane,
            plane,
            jax.ShapeDtypeStruct((count,) + small.shape, BF16),
        ],
        in_specs=[anywhere] * 5,
        out_specs=[anywhere, anywhere, vmem, anywhere, vmem],
        scratch_shapes=[
            pltpu.VMEM((8, rows, width), BF16),
            dma((5,)),
            dma((7,)),
            dma((7,)),
            dma((7,)),
            dma((7,)),
            dma((legs, 8)),
            dma((legs, 8)),
            dma((legs, 8)),
            dma((legs, 8)),
            dma((count - 1,)),
            dma((count - 1,)),
            dma((2, 2, chunks)),
            dma((2, 2, chunks)),
            dma((2, chunks)),
            dma((2, chunks)),
            dma((2, 4, chunks)),
            dma((2, 4, chunks)),
        ],
        cost_estimate=busy(150),
        compiler_params=pltpu.CompilerParams(
            collective_id=cid, has_side_effects=True, vmem_limit_bytes=58 << 20
        ),
    )(weight, ups, tokens, cotangent, small)


def relay(left, first, second, first_dims, second_dims, gain, extras, norm_back, cid):
    _, rows, depth = left.shape
    width = gain.shape[1]
    multiply = second is not None
    out_cols = 0 if not multiply else second.shape[1] if second_dims == NN else second.shape[0]
    chunks = 4
    part = rows // chunks
    tile = 512
    out_tiles = [(a, min(a + tile, out_cols)) for a in range(0, out_cols, tile)]

    def kernel(left_ref, first_ref, gain_ref, *refs):
        extra_refs, refs = refs[: len(extras)], refs[len(extras) :]
        if multiply:
            second_ref, *refs = refs
        rows_out, all_ref, *refs = refs
        if multiply:
            prod_out, *refs = refs
        if norm_back:
            gain_grad, *refs = refs
        if multiply:
            *refs, w2, stage = refs
        (L, W, plane, T, A, B, R, S, msem, fsem, lsem, sa, ra, sb, rb, x_send, x_recv, d_send, d_recv, f_send, f_recv) = refs
        me, z, core, cx, cy = _place(8)

        def dev(dx, dy, c):
            return 2 * (2 * lax.rem(cy + dy, 2) + lax.rem(cx + dx, 2)) + c

        def remote(src, dst, send, recv, device):
            return pltpu.make_async_remote_copy(src, dst, send, recv, device_id=(device, z), device_id_type=MESH)

        sib = dev(0, 0, 1 - core)
        nf, ng, across = dev(1 - core, core, core), dev(core, 1 - core, core), dev(1, 1, core)
        bar = pltpu.get_barrier_semaphore()
        for d in (sib, nf, ng):
            pl.semaphore_signal(bar, inc=1, device_id=(d, z), device_id_type=MESH)
        if multiply:
            load = pltpu.make_async_copy(second_ref, w2, lsem.at[2])
            load.start()

        load_first = pltpu.make_async_copy(first_ref, W, lsem.at[3])
        load_first.start()

        mine = (across, ng, nf, me)
        theirs = (dev(1, 1, 1 - core), dev(1 - core, core, 1 - core), dev(core, 1 - core, 1 - core), sib)

        turns = (theirs[0], mine[0], theirs[2], mine[2], theirs[1], theirs[3], mine[1], mine[3])

        def load_left(i):
            return pltpu.make_async_copy(left_ref.at[turns[i]], L.at[i], msem.at[i])

        for i in range(8):
            load_left(i).start()

        def partial(i, write):
            load_left(i).wait()

            def some(n, _):
                cols = pl.ds(pl.multiple_of(n * tile, tile), tile)
                w = W[:, cols] if first_dims == NN else W[cols, :]
                write(cols, lax.dot_general(L[i], w, first_dims, preferred_element_type=F32))
                return 0

            lax.fori_loop(0, width // tile, some, 0)

        def give(i, k):
            def write(cols, v):
                T[k, :, cols] = v.astype(BF16)

            partial(i, write)
            remote(T.at[k], A.at[k], sa.at[k], ra.at[k], sib).start()

        def got(k):
            remote(T.at[k], A.at[k], sa.at[k], ra.at[k], sib).wait_recv()

        def cut(c):
            return pl.ds(c * part, part)

        def ship(k, c, d):
            return remote(B.at[k, cut(c)], R.at[k, cut(c)], sb.at[k, c], rb.at[k, c], d)

        def send_sum(i, k):
            def write(cols, v):
                S[:, cols] = v

            partial(i, write)
            got(k)
            for c in range(chunks):
                B[k, cut(c)] = (S[cut(c)] + A[k, cut(c)].astype(F32)).astype(BF16)
                ship(k, c, nf).start()

        def keep_sum(i, k):
            got(k)

            def write(cols, v):
                S[:, cols] = v + A[k, :, cols].astype(F32)

            partial(i, write)

        pl.semaphore_wait(bar, 3)
        load_first.wait()
        give(0, 0)
        send_sum(1, 0)
        give(2, 2)
        send_sum(3, 2)
        give(4, 1)
        give(5, 3)
        keep_sum(6, 1)
        for c in range(chunks):
            ship(0, c, nf).wait_recv()
            B[1, cut(c)] = (S[cut(c)] + R[0, cut(c)].astype(F32)).astype(BF16)
            ship(1, c, ng).start()
        keep_sum(7, 3)

        source, other = nf, ng

        def at(q, c):
            return plane.at[q, cut(c)]

        def step(k, c):
            return remote(at(me, c), at(me, c), x_send.at[k, c], x_recv.at[k, c], (dev(1, 0, core), dev(0, 1, core))[k])

        def twin(k, q, c):
            return remote(at(q, c), at(q, c), f_send.at[k, c], f_recv.at[k, c], sib)

        def second_step(c):
            return remote(at(source, c), at(source, c), d_send.at[c], d_recv.at[c], other)

        gains = gain_ref[...]
        if norm_back:
            gain_grad[...] = jnp.zeros_like(gain_grad)
        for c in range(chunks):
            ship(2, c, nf).wait_recv()
            ship(1, c, ng).wait_recv()
            for h in range(2):
                sl = pl.ds(c * part + h * (part // 2), part // 2)
                total = S[sl] + R[2, sl].astype(F32) + R[1, sl].astype(F32)
                if norm_back:
                    v = extra_refs[0][sl]
                    root = lax.rsqrt(jnp.mean(v * v, axis=-1, keepdims=True) + EPSILON)
                    hat = v * root
                    scaled = total * gains
                    gain_grad[...] += jnp.sum(total * hat, axis=0, keepdims=True)
                    done = extra_refs[1][sl] + root * (scaled - hat * jnp.mean(scaled * hat, axis=-1, keepdims=True))
                    low = done
                else:
                    done = extra_refs[0][sl].astype(F32) + total
                    low = done * lax.rsqrt(jnp.mean(done * done, axis=-1, keepdims=True) + EPSILON) * gains
                rows_out[sl] = done
                plane[me, sl] = low.astype(BF16)
            for k in range(2):
                step(k, c).start()
            twin(0, me, c).start()
        if multiply:
            load.wait()

        flushes = []

        kept = []

        def product(q):
            keep = pltpu.make_async_copy(plane.at[q], all_ref.at[q], fsem.at[len(kept)])
            keep.start()
            kept.append(keep)
            if not multiply:
                return
            slot = len(flushes) % 2
            if len(flushes) > 1:
                flushes[-2].wait()
            for a, b in out_tiles:
                w = w2[:, a:b] if second_dims == NN else w2[a:b, :]
                stage[slot, :, a:b] = lax.dot_general(plane[q], w, second_dims, preferred_element_type=F32)
            flush = pltpu.make_async_copy(stage.at[slot], prod_out.at[q], lsem.at[slot])
            flush.start()
            flushes.append(flush)

        def twin_got(k):
            for c in range(chunks):
                twin(k, theirs_at[k], c).wait_recv()

        theirs_at = (sib, dev(core, 1 - core, 1 - core), dev(1 - core, core, 1 - core), dev(1, 1, 1 - core))
        product(me)
        for c in range(chunks):
            remote(at(source, c), at(source, c), x_send.at[core, c], x_recv.at[core, c], sib).wait_recv()
            second_step(c).start()
            twin(1, source, c).start()
            remote(at(other, c), at(other, c), x_send.at[1 - core, c], x_recv.at[1 - core, c], sib).wait_recv()
            twin(2, other, c).start()
            if c == 0:
                twin_got(0)
                product(sib)
        product(source)
        product(other)
        for c in range(chunks):
            remote(at(across, c), at(across, c), d_send.at[c], d_recv.at[c], sib).wait_recv()
            twin(3, across, c).start()
            if c == 0:
                twin_got(1)
                product(theirs_at[1])
            if c == 1:
                twin_got(2)
                product(theirs_at[2])
        product(across)
        twin_got(3)
        product(theirs_at[3])

        for k in range(4):
            remote(T.at[k], A.at[k], sa.at[k], ra.at[k], sib).wait_send()
        for c in range(chunks):
            for k in range(3):
                ship(k, c, nf).wait_send()
            for k in range(2):
                step(k, c).wait_send()
            second_step(c).wait_send()
            for k, q in enumerate((me, source, other, across)):
                twin(k, q, c).wait_send()
        for flush in flushes[-2:] + kept:
            flush.wait()

    dma = pltpu.SemaphoreType.DMA
    anywhere, vmem = pl.BlockSpec(memory_space=pl.ANY), pl.BlockSpec(memory_space=pltpu.VMEM)
    block = lambda n: pltpu.VMEM((n, rows, width), BF16)
    out_shape = [
        jax.ShapeDtypeStruct((rows, width), F32),
        jax.ShapeDtypeStruct((8, rows, width), BF16),
    ]
    out_specs = [vmem, anywhere]
    operands = [left, first, gain, *extras]
    in_specs = [anywhere, anywhere] + [vmem] * (1 + len(extras))
    later = []
    if multiply:
        out_shape.append(jax.ShapeDtypeStruct((8, rows, out_cols), F32))
        out_specs.append(anywhere)
        operands.append(second)
        in_specs.append(anywhere)
        later = [pltpu.VMEM(second.shape, BF16), pltpu.VMEM((2, rows, out_cols), F32)]
    if norm_back:
        out_shape.append(jax.ShapeDtypeStruct((1, width), F32))
        out_specs.append(vmem)
    return pl.pallas_call(
        kernel,
        out_shape=out_shape,
        in_specs=in_specs,
        out_specs=out_specs,
        scratch_shapes=[
            pltpu.VMEM(left.shape, BF16),
            pltpu.VMEM(first.shape, BF16),
            block(8),
            block(4),
            block(4),
            block(3),
            block(3),
            pltpu.VMEM((rows, width), F32),
            dma((8,)),
            dma((8,)),
            dma((4,)),
            dma((4,)),
            dma((4,)),
            dma((3, chunks)),
            dma((3, chunks)),
            dma((2, chunks)),
            dma((2, chunks)),
            dma((chunks,)),
            dma((chunks,)),
            dma((4, chunks)),
            dma((4, chunks)),
            *later,
        ],
        cost_estimate=busy(80),
        compiler_params=pltpu.CompilerParams(
            collective_id=cid, has_side_effects=True, vmem_limit_bytes=58 << 20
        ),
    )(*operands)


def unit_pairs(a, main):
    tail = a[:, 2 * main :]
    size = tail.shape[1]
    turned = pltpu.roll(tail, size // 2, 1)
    left = lax.broadcasted_iota(jnp.int32, tail.shape, 1) < size // 2
    return (a[:, :main], a[:, main : 2 * main]), (jnp.where(left, tail, turned), jnp.where(left, turned, tail)), left


def units_forward(x, weight, scales, units, main):
    blocks, rows, width = x.shape
    cols = weight.shape[1]

    def kernel(x_ref, w_ref, s_ref, up_ref, hidden_ref, scaled_ref):
        scale = s_ref[pl.ds(pl.program_id(0), 1), :][:, 0:1]
        for a in range(0, cols, 512):
            b = min(a + 512, cols)
            up_ref[:, a:b] = jnp.dot(x_ref[...], w_ref[:, a:b], preferred_element_type=F32)
        (g, u), (g_tail, u_tail), _ = unit_pairs(up_ref[...], main)
        hidden = g * sigmoid(g) * u
        tail = (g_tail * sigmoid(g_tail) * u_tail)[:, : units - main]
        hidden_ref[:, :main] = hidden.astype(BF16)
        hidden_ref[:, main:] = tail.astype(BF16)
        scaled_ref[:, :main] = (hidden * scale).astype(BF16)
        scaled_ref[:, main:] = (tail * scale).astype(BF16)

    row = lambda n: pl.BlockSpec((rows, n), lambda i: (i, 0))
    whole = lambda a: pl.BlockSpec(a.shape, lambda i: (0, 0))
    tokens = blocks * rows
    return pl.pallas_call(
        kernel,
        grid=(blocks,),
        in_specs=[row(width), whole(weight), whole(scales)],
        out_specs=[row(cols), row(units), row(units)],
        out_shape=[
            jax.ShapeDtypeStruct((tokens, cols), F32),
            jax.ShapeDtypeStruct((tokens, units), BF16),
            jax.ShapeDtypeStruct((tokens, units), BF16),
        ],
        cost_estimate=busy(20),
        compiler_params=pltpu.CompilerParams(vmem_limit_bytes=48 << 20),
    )(x.reshape(tokens, width), weight, scales)


def units_backward(cot, weight, upgate, scales, units, main):
    blocks, rows, width = cot.shape
    cols = upgate.shape[1]

    def kernel(c_ref, w_ref, up_ref, s_ref, low_ref):
        scale = s_ref[pl.ds(pl.program_id(0), 1), :][:, 0:1]
        pair, pair_tail, left = unit_pairs(up_ref[...], main)
        tail_rows = w_ref[main:, :]
        grad = dot(c_ref[...], w_ref[:main, :], NT) * scale
        grad_tail = dot(c_ref[...], jnp.concatenate([tail_rows, tail_rows], axis=0), NT) * scale

        def both(g, u, grad):
            s = sigmoid(g)
            return grad * u * s * (1.0 + g * (1.0 - s)), grad * g * s

        gate_grad, up_grad = both(*pair, grad)
        low_ref[:, :main] = gate_grad.astype(BF16)
        low_ref[:, main : 2 * main] = up_grad.astype(BF16)
        gate_grad, up_grad = both(*pair_tail, grad_tail)
        low_ref[:, 2 * main :] = jnp.where(left, gate_grad, up_grad).astype(BF16)

    row = lambda n: pl.BlockSpec((rows, n), lambda i: (i, 0))
    whole = lambda a: pl.BlockSpec(a.shape, lambda i: (0, 0))
    tokens = blocks * rows
    return pl.pallas_call(
        kernel,
        grid=(blocks,),
        in_specs=[row(width), whole(weight), row(cols), whole(scales)],
        out_specs=row(cols),
        out_shape=jax.ShapeDtypeStruct((tokens, cols), BF16),
        cost_estimate=busy(12),
        compiler_params=pltpu.CompilerParams(vmem_limit_bytes=48 << 20),
    )(cot.reshape(tokens, width), weight, upgate, scales)


def conclude(grad, left, raw_left, weight, raw_weight, block, ups, tokens, middle, middle_grad, gain, lines, conv, bounds, cid):
    n_z = 4
    _, _, own, cols = grad.shape
    units = ups.shape[2]
    rows, width = tokens.shape
    count = 8 * n_z
    per = 128 * count // width
    conv_cols = conv.shape[1] // count
    chunks = 2
    part = rows // chunks
    tile = 512
    last = n_z - 1

    def kernel(
        g_ref, l_ref, lr_ref, w_ref, wr_ref, b_ref, u_ref, t_ref, m_ref, mg_ref, gain_ref, lines_ref, conv_ref,
        result, tg, in_out, u_out, line_sum, line_planes, conv_sum, conv_planes,
        lines_out, conv_out, W, L, own_buf, UD, T, A, B, R, S, A7, B7, R7, X7, line_buf,
        lsem, wsem, osem, mine_sem, us, ur, ds, dr, i_send, i_recv, u_send, u_recv, p_send, p_recv, c_send, c_recv,
        sa, ra, sb, rb, sa7, ra7, sb7, rb7,
    ):
        me, z, core, cx, cy = _place(8)
        flat = me * n_z + z

        def dev(dx, dy, c):
            return 2 * (2 * lax.rem(cy + dy, 2) + lax.rem(cx + dx, 2)) + c

        sib = dev(0, 0, 1 - core)
        nf, ng, across = dev(1 - core, core, core), dev(core, 1 - core, core), dev(1, 1, core)

        def partner(o):
            return dev(o // 4, lax.rem(o // 2, 2), lax.rem(core + o, 2))

        def anyone(o):
            other = lax.rem(flat + o, count)
            return (other // n_z, lax.rem(other, n_z))

        def remote(src, dst, send, recv, device):
            return pltpu.make_async_remote_copy(src, dst, send, recv, device_id=device, device_id_type=MESH)

        def loop(first, end, body):
            def step(o, _):
                body(o)
                return 0

            lax.fori_loop(first, end, step, 0)

        bar = pltpu.get_barrier_semaphore()
        loop(1, count, lambda o: pl.semaphore_signal(bar, inc=1, device_id=anyone(o), device_id_type=MESH))

        mine = (across, ng, nf, me)
        theirs = (dev(1, 1, 1 - core), dev(1 - core, core, 1 - core), dev(core, 1 - core, 1 - core), sib)
        turns = (theirs[0], theirs[2], mine[0], theirs[1], mine[2], theirs[3], mine[1], mine[3])

        def load_left(i):
            q, slot = turns[i], i % 2
            return (
                pltpu.make_async_copy(l_ref.at[q], L.at[slot, :, pl.ds(0, cols)], lsem.at[slot]),
                pltpu.make_async_copy(lr_ref.at[q], L.at[slot, :, pl.ds(cols, 128)], lsem.at[2 + slot]),
            )

        def start(copies):
            for copy in copies:
                copy.start()

        def wait(copies):
            for copy in copies:
                copy.wait()

        load_weight = (
            pltpu.make_async_copy(w_ref, W.at[:, pl.ds(0, cols)], wsem.at[0]),
            pltpu.make_async_copy(wr_ref, W.at[:, pl.ds(cols, 128)], wsem.at[7]),
        )
        load_middle = pltpu.make_async_copy(m_ref, result, wsem.at[1])
        load_grad = pltpu.make_async_copy(mg_ref, tg, wsem.at[2])

        def load_own(zz):
            return pltpu.make_async_copy(g_ref.at[:, zz], own_buf.at[zz], osem.at[zz])

        start(load_left(0))
        start(load_weight)
        for zz in (0, 3, 2, 1):
            load_own(zz).start()
        start(load_left(1))
        load_middle.start()
        load_grad.start()
        pl.semaphore_wait(bar, count - 1)

        def up_slot(s, o):
            return s * 8 + o

        def down_slot(s, o):
            return 39 - (s * 8 + o)

        def up(s, o, src):
            return remote(src, UD.at[up_slot(s, o)], us.at[s, o], ur.at[s, o], (me, z + 1))

        def down(s, o, src):
            return remote(src, UD.at[down_slot(s, o)], ds.at[s, o], dr.at[s, o], (me, z - 1))

        def start_line(s, o):
            q = partner(o)

            @pl.when(z == 0)
            def _():
                up(s, o, g_ref.at[q, last - s]).start()

            @pl.when(z == last)
            def _():
                down(s, o, g_ref.at[q, s]).start()

        for s in range(last):
            loop(0, 8, functools.partial(start_line, s))
        for zz in range(n_z):
            load_own(zz).wait()

        def sections(q):
            for a, b in zip(bounds[:-1], bounds[1:]):
                at = pl.multiple_of(8 * a + q * (b - a), 128)
                yield pl.ds(a, b - a), in_out.at[:, pl.ds(at, b - a)]

        def deliver(o, slot):
            @pl.when(o == 0)
            def _():
                for src, dst in sections(me):
                    pltpu.make_async_copy(UD.at[slot, :, src], dst, wsem.at[3]).start()

            @pl.when(o > 0)
            def _():
                for src, dst in sections(me):
                    remote(UD.at[slot, :, src], dst, i_send.at[o - 1], i_recv.at[o - 1], (partner(o), z)).start()

        def add(slot, *others):
            total = UD[slot].astype(F32)
            for other in others:
                total = total + other.astype(F32)
            UD[slot] = total.astype(BF16)

        def up_tick(i):
            s, o = i // 8, lax.rem(i, 8)
            q, u = partner(o), up_slot(s, o)

            @pl.when((z >= 1) & (z <= last - s))
            def _():
                remote(UD.at[u], UD.at[u], us.at[s, o], ur.at[s, o], (sib, z)).wait_recv()

            @pl.when((z >= 1) & (z < last - s))
            def _():
                add(u, own_buf[last - s, q])
                up(s, o, UD.at[u]).start()

            @pl.when((z == last) & (s == 0))
            def _():
                add(u, own_buf[last, q])
                deliver(o, u)

            @pl.when((z == 1) & (s == 2))
            def _():
                add(u, UD[down_slot(1, o)], own_buf[1, q])
                deliver(o, u)

        def down_tick(i):
            s, o = i // 8, lax.rem(i, 8)
            q, d = partner(o), down_slot(s, o)

            @pl.when((z <= last - 1) & (z >= s))
            def _():
                remote(UD.at[d], UD.at[d], ds.at[s, o], dr.at[s, o], (sib, z)).wait_recv()

            @pl.when((z <= last - 1) & (z > s))
            def _():
                add(d, own_buf[s, q])
                down(s, o, UD.at[d]).start()

            @pl.when((z == 0) & (s == 0))
            def _():
                add(d, own_buf[0, q])
                deliver(o, d)

            @pl.when((z == 2) & (s == 2))
            def _():
                add(d, UD[up_slot(1, o)], own_buf[2, q])
                deliver(o, d)

        lag = 4
        low = 1 - z // 2

        def tick(i):
            at_up, at_down = i - lag * (1 - low), i - lag * low

            @pl.when((at_up >= 0) & (at_up < 24))
            def _():
                up_tick(at_up)

            @pl.when((at_down >= 0) & (at_down < 24))
            def _():
                down_tick(at_down)

        def cut(c):
            return pl.ds(c * part, part)

        def partial(i, write):
            wait(load_left(i))

            def some(n, _):
                at = pl.ds(pl.multiple_of(n * tile, tile), tile)
                write(at, lax.dot_general(L[i % 2], W[at, :], NT, preferred_element_type=F32))
                return 0

            lax.fori_loop(0, width // tile, some, 0)
            if i + 2 < 8:
                start(load_left(i + 2))

        def give(i, k, slot, before):
            if before is not None:
                remote(T.at[slot], A.at[before], sa.at[before], ra.at[before], (sib, z)).wait_send()

            def write(at, v):
                T[slot, :, at] = v.astype(BF16)

            partial(i, write)
            remote(T.at[slot], A.at[k], sa.at[k], ra.at[k], (sib, z)).start()

        def got(k):
            remote(T.at[0], A.at[k], sa.at[k], ra.at[k], (sib, z)).wait_recv()

        def ship(k, c, d):
            return remote(B.at[k, cut(c)], R.at[k, cut(c)], sb.at[k, c], rb.at[k, c], (d, z))

        def ship7(k, c, d):
            return remote(B7.at[k, cut(c)], R7.at[k, cut(c)], sb7.at[k, c], rb7.at[k, c], (d, z))

        def send_sum(i, k):
            got(k)

            def write(at, v):
                B[k, :, at] = (v + A[k, :, at].astype(F32)).astype(BF16)

            partial(i, write)
            for c in range(chunks):
                ship(k, c, nf).start()

        def keep_sum(i, k):
            got(k)

            def write(at, v):
                S[:, at] = v + A[k, :, at].astype(F32)

            partial(i, write)

        def second_hop():
            for c in range(chunks):
                ship(0, c, nf).wait_recv()
                B[1, cut(c)] = (S[cut(c)] + R[0, cut(c)].astype(F32)).astype(BF16)
                ship(1, c, ng).start()

        def give7(k):
            return remote(b_ref.at[theirs[k]], A7.at[k], sa7.at[k], ra7.at[k], (sib, z))

        def mine7(k):
            return pltpu.make_async_copy(b_ref.at[mine[k]], X7 if k == 3 else B7.at[k], mine_sem.at[k])

        def start7():
            for k in (0, 2, 1, 3):
                give7(k).start()
                mine7(k).start()

        def send7(k):
            mine7(k).wait()
            give7(k).wait_recv()
            for c in range(chunks):
                B7[k, cut(c)] = (B7[k, cut(c)].astype(F32) + A7[k, cut(c)].astype(F32)).astype(BF16)
                ship7(k, c, nf).start()

        def second_hop7():
            mine7(1).wait()
            give7(1).wait_recv()
            for c in range(chunks):
                ship7(0, c, nf).wait_recv()
                sl = cut(c)
                B7[1, sl] = (B7[1, sl].astype(F32) + A7[1, sl].astype(F32) + R7[0, sl].astype(F32)).astype(BF16)
                ship7(1, c, ng).start()

        small = 32

        def finish_rows():
            load_grad.wait()
            line_buf[...] = lines_ref[...]
            line_buf[0:1] = jnp.zeros((1, width), F32)
            gains = gain_ref[...]
            for c in range(chunks):
                ship(2, c, nf).wait_recv()
                ship(1, c, ng).wait_recv()

                def some(r, _):
                    sl = pl.ds(pl.multiple_of(c * part + r * small, small), small)
                    total = S[sl] + R[2, sl].astype(F32) + R[1, sl].astype(F32)
                    v = t_ref[sl].astype(F32)
                    root = lax.rsqrt(jnp.mean(v * v, axis=-1, keepdims=True) + EPSILON)
                    hat = v * root
                    scaled = total * gains
                    line_buf[0:1] += jnp.sum(total * hat, axis=0, keepdims=True)
                    tg[sl] += root * (scaled - hat * jnp.mean(scaled * hat, axis=-1, keepdims=True))
                    return 0

                lax.fori_loop(0, part // small, some, 0)

        def finish7():
            load_middle.wait()
            mine7(3).wait()
            give7(3).wait_recv()
            for c in range(chunks):
                ship7(2, c, nf).wait_recv()
                ship7(1, c, ng).wait_recv()

                def some(r, _):
                    sl = pl.ds(pl.multiple_of(c * part + r * small, small), small)
                    result[sl] += (
                        X7[sl].astype(F32) + A7[3, sl].astype(F32) + R7[2, sl].astype(F32) + R7[1, sl].astype(F32)
                    )
                    return 0

                lax.fori_loop(0, part // small, some, 0)

        def line_part(d):
            return line_buf.at[:, pl.ds(pl.multiple_of((d // per) * 128, 128), 128)]

        def conv_part(d):
            return conv_ref.at[:, pl.ds(pl.multiple_of(d * conv_cols, conv_cols), conv_cols)]

        def packet(o):
            d = lax.rem(flat + o, count)
            return remote(line_part(d), lines_out.at[flat], p_send.at[o - 1], p_recv.at[o - 1], anyone(o))

        def conv_packet(o):
            d = lax.rem(flat + o, count)
            return remote(conv_part(d), conv_out.at[flat], c_send.at[o - 1], c_recv.at[o - 1], anyone(o))

        keep_line = pltpu.make_async_copy(line_part(flat), lines_out.at[flat], wsem.at[4])
        keep_conv = pltpu.make_async_copy(conv_part(flat), conv_out.at[flat], wsem.at[5])
        keep_up = pltpu.make_async_copy(u_ref.at[me], u_out.at[me], wsem.at[6])

        def unit_piece(o):
            q = partner(o)
            return remote(u_ref.at[q], u_out.at[me], u_send.at[o - 1], u_recv.at[o - 1], (q, z))

        def send_packets():
            keep_line.start()
            loop(1, count, lambda o: packet(o).start())

        def others():
            keep_conv.start()
            keep_up.start()
            loop(1, count, lambda o: conv_packet(o).start())

        def first_work():
            wait(load_weight)
            give(0, 0, 0, None)
            give(1, 2, 1, None)

        work = (
            first_work,
            lambda: (send_sum(2, 0), give(3, 1, 0, 0)),
            lambda: (send_sum(4, 2), give(5, 3, 1, 2), start7()),
            lambda: (keep_sum(6, 1), others()),
            lambda: (second_hop(), keep_sum(7, 3)),
            lambda: (send7(0), send7(2)),
            lambda: finish_rows(),
            lambda: (send_packets(), loop(1, 8, lambda o: unit_piece(o).start())),
            lambda: second_hop7(),
            lambda: None,
            lambda: finish7(),
            lambda: None,
            lambda: None,
            lambda: None,
        )
        for g, item in enumerate(work):
            item()
            loop(2 * g, 2 * g + 2, tick)

        def line_sent(s, o):
            @pl.when(z < last - s)
            def _():
                up(s, o, UD.at[up_slot(s, o)]).wait_send()

            @pl.when(z > s)
            def _():
                down(s, o, UD.at[down_slot(s, o)]).wait_send()

        for s in range(last):
            loop(0, 8, functools.partial(line_sent, s))
        for k, slot in ((1, 0), (3, 1)):
            remote(T.at[slot], A.at[k], sa.at[k], ra.at[k], (sib, z)).wait_send()
        for k in range(4):
            give7(k).wait_send()
        for c in range(chunks):
            for k in range(3):
                ship(k, c, nf).wait_send()
                ship7(k, c, nf).wait_send()
        piece = UD.at[0]

        def arrived(o):
            remote(piece, piece, i_send.at[o - 1], i_recv.at[o - 1], (sib, z)).wait()

        pltpu.make_async_copy(piece, piece, wsem.at[3]).wait()
        loop(1, 8, arrived)
        loop(1, 8, lambda o: unit_piece(o).wait())
        loop(1, count, lambda o: packet(o).wait())
        loop(1, count, lambda o: conv_packet(o).wait())
        keep_line.wait()
        keep_conv.wait()
        keep_up.wait()
        all_lines, all_conv = lines_out[0], conv_out[0]
        for d in range(1, count):
            all_lines, all_conv = all_lines + lines_out[d], all_conv + conv_out[d]
        line_sum[...] = all_lines
        conv_sum[...] = all_conv
        for d in range(8):
            line_planes[d : d + 1] = sum(lines_out[d * n_z + i, 4:5] for i in range(n_z))
            conv_planes[d : d + 1] = sum(conv_out[d * n_z + i, 4:5] for i in range(n_z))

    dma = pltpu.SemaphoreType.DMA
    anywhere, vmem = pl.BlockSpec(memory_space=pl.ANY), pl.BlockSpec(memory_space=pltpu.VMEM)
    blocks = lambda n: pltpu.VMEM((n, rows, width), BF16)
    f32_rows = jax.ShapeDtypeStruct((rows, width), F32)
    return pl.pallas_call(
        kernel,
        out_shape=[
            f32_rows,
            f32_rows,
            jax.ShapeDtypeStruct((own, 8 * bounds[-1]), BF16),
            jax.ShapeDtypeStruct((8, own, units), BF16),
            jax.ShapeDtypeStruct((8, 128), F32),
            jax.ShapeDtypeStruct((8, 128), F32),
            jax.ShapeDtypeStruct((8, conv_cols), F32),
            jax.ShapeDtypeStruct((8, conv_cols), F32),
        ],
        in_specs=[anywhere] * 7 + [vmem, anywhere, anywhere, vmem, vmem, anywhere],
        out_specs=[vmem, vmem, anywhere, anywhere] + [vmem] * 4,
        scratch_shapes=[
            pltpu.VMEM((count, 8, 128), F32),
            pltpu.VMEM((count, 8, conv_cols), F32),
            pltpu.VMEM((width, cols + 128), BF16),
            pltpu.VMEM((2, rows, cols + 128), BF16),
            pltpu.VMEM((n_z, 8, own, cols), BF16),
            pltpu.VMEM((40, own, cols), BF16),
            blocks(2),
            blocks(4),
            blocks(3),
            blocks(3),
            pltpu.VMEM((rows, width), F32),
            blocks(4),
            blocks(3),
            blocks(3),
            pltpu.VMEM((rows, width), BF16),
            pltpu.VMEM((8, width), F32),
            dma((4,)),
            dma((8,)),
            dma((n_z,)),
            dma((4,)),
            dma((3, 8)),
            dma((3, 8)),
            dma((3, 8)),
            dma((3, 8)),
            dma((7,)),
            dma((7,)),
            dma((7,)),
            dma((7,)),
            dma((count - 1,)),
            dma((count - 1,)),
            dma((count - 1,)),
            dma((count - 1,)),
            dma((4,)),
            dma((4,)),
            dma((3, chunks)),
            dma((3, chunks)),
            dma((4,)),
            dma((4,)),
            dma((3, chunks)),
            dma((3, chunks)),
        ],
        cost_estimate=busy(120),
        compiler_params=pltpu.CompilerParams(
            collective_id=cid, has_side_effects=True, vmem_limit_bytes=60 << 20
        ),
    )(grad, left, raw_left, weight, raw_weight, block, ups, tokens, middle, middle_grad, gain, lines, conv)


def gather_small(x, n_dp, n_z, cid):
    rows, cols = x.shape
    count = n_dp * n_z

    def kernel(x_ref, o_ref, lsem, ssem, rsem):
        flat = lax.axis_index("dp") * n_z + lax.axis_index("fsdp")
        bar = pltpu.get_barrier_semaphore()

        def device(o):
            other = lax.rem(flat + o, count)
            return (other // n_z, lax.rem(other, n_z))

        def copy(o):
            return pltpu.make_async_remote_copy(
                x_ref, o_ref.at[flat], ssem.at[o - 1], rsem.at[o - 1], device_id=device(o), device_id_type=MESH
            )

        def greet(o, _):
            pl.semaphore_signal(bar, inc=1, device_id=device(o), device_id_type=MESH)
            return 0

        def send(o, _):
            copy(o).start()
            return 0

        def wait(o, _):
            copy(o).wait()
            return 0

        lax.fori_loop(1, count, greet, 0)
        local = pltpu.make_async_copy(x_ref, o_ref.at[flat], lsem)
        local.start()
        pl.semaphore_wait(bar, count - 1)
        lax.fori_loop(1, count, send, 0)
        lax.fori_loop(1, count, wait, 0)
        local.wait()

    dma = pltpu.SemaphoreType.DMA
    return pl.pallas_call(
        kernel,
        out_shape=jax.ShapeDtypeStruct((count, rows, cols), x.dtype),
        in_specs=[pl.BlockSpec(memory_space=pl.ANY)],
        out_specs=pl.BlockSpec(memory_space=pl.ANY),
        scratch_shapes=[dma, dma((count - 1,)), dma((count - 1,))],
        cost_estimate=busy(15),
        compiler_params=pltpu.CompilerParams(collective_id=cid, has_side_effects=True),
    )(x)


def scatter_small(x, n_dp, n_z, cid):
    count, rows, cols = x.shape

    def kernel(x_ref, o_ref, lsem, ssem, rsem):
        flat = lax.axis_index("dp") * n_z + lax.axis_index("fsdp")
        bar = pltpu.get_barrier_semaphore()

        def device(o):
            other = lax.rem(flat + o, count)
            return (other // n_z, lax.rem(other, n_z))

        def copy(o):
            return pltpu.make_async_remote_copy(
                x_ref.at[lax.rem(flat + o, count)], o_ref.at[flat], ssem.at[o - 1], rsem.at[o - 1], device_id=device(o), device_id_type=MESH
            )

        def greet(o, _):
            pl.semaphore_signal(bar, inc=1, device_id=device(o), device_id_type=MESH)
            return 0

        def send(o, _):
            copy(o).start()
            return 0

        def wait(o, _):
            copy(o).wait()
            return 0

        lax.fori_loop(1, count, greet, 0)
        local = pltpu.make_async_copy(x_ref.at[flat], o_ref.at[flat], lsem)
        local.start()
        pl.semaphore_wait(bar, count - 1)
        lax.fori_loop(1, count, send, 0)
        lax.fori_loop(1, count, wait, 0)
        local.wait()

    dma = pltpu.SemaphoreType.DMA
    return pl.pallas_call(
        kernel,
        out_shape=jax.ShapeDtypeStruct((count, rows, cols), x.dtype),
        in_specs=[pl.BlockSpec(memory_space=pl.ANY)],
        out_specs=pl.BlockSpec(memory_space=pl.ANY),
        scratch_shapes=[dma, dma((count - 1,)), dma((count - 1,))],
        cost_estimate=busy(15),
        compiler_params=pltpu.CompilerParams(collective_id=cid, has_side_effects=True),
    )(x)


def pack(parts, unit):
    flat = jnp.concatenate([part.reshape(-1) for part in parts])
    size = flat.shape[0]
    full = -(-size // (128 * unit)) * 128 * unit
    return jnp.pad(flat, (0, full - size)).reshape(-1, 128)


def dot(a, b, dims=NN, out=F32):
    return lax.dot_general(a, b, dims, preferred_element_type=F32).astype(out)


def local(
    n_dp,
    n_z,
    tokens,
    cotangent,
    group_ids,
    norm_first,
    input_weight,
    decay_weight,
    conv_weight,
    decay_scale,
    decay_bias,
    output_gain,
    output_weight,
    norm_second,
    upgate_weight,
    down_weight,
):
    count = n_dp * n_z
    rows, width = tokens.shape
    all_heads = decay_scale.shape[0]
    heads = all_heads // n_dp
    taps = conv_weight.shape[0]
    own_conv = conv_weight.shape[1]
    own_d = norm_first.shape[0]
    units = upgate_weight.shape[1] // (2 * n_dp)
    key, value = heads * DK, heads * DV
    cols = 2 * key + 2 * value
    square = n_dp == 8 and n_z == 4
    here = lax.axis_index("dp")
    flat = here * n_z + lax.axis_index("fsdp")

    def spread(x, cid):
        if square:
            return ag_square(x, cid).reshape(n_dp * rows, width)
        return lax.all_gather(x, "dp", axis=0, tiled=True)

    def total(x, cid):
        if square:
            return rs_square(x.reshape(n_dp, rows, width), cid)
        return lax.psum_scatter(x, "dp", scatter_dimension=0, tiled=True).astype(F32)

    def by_dp(a, parts):
        return a.reshape(a.shape[0], n_dp, parts)

    main = units // 128 * 128
    bounds = (0, key, 2 * key, 2 * key + value, 2 * key + 2 * value)
    gates = by_dp(upgate_weight[:, : n_dp * units], units)
    ups = by_dp(upgate_weight[:, n_dp * units :], units)
    up_mine = jnp.concatenate(
        [gates[:, :, :main], ups[:, :, :main], gates[:, :, main:], ups[:, :, main:]], axis=2
    ).transpose(1, 0, 2)
    def whole_rows(a):
        a = lax.all_gather(a[:, None], "fsdp", axis=1, tiled=True)
        return a.reshape(width, a.shape[-1])

    conv_size = taps * own_conv
    inputs = tokens.astype(F32)
    first_root = lax.rsqrt(jnp.mean(inputs * inputs, axis=-1, keepdims=True) + EPSILON)
    if square:
        small = jnp.concatenate(
            [norm_first] * (128 // own_d)
            + [norm_second] * (128 // own_d)
            + [jnp.broadcast_to(group_ids.astype(BF16), (128,)), jnp.zeros((640,), BF16), conv_weight.reshape(-1)]
            + [decay_weight.reshape(-1)]
        ).reshape(32, 128)
        in_full, up_plane, normed_all, cot_all, small = begin(
            input_weight, up_mine, tokens, cotangent, small, bounds, n_z, 1
        )
        in_full = in_full.reshape(width, cols)
        normed_all = normed_all.reshape(n_dp * rows, width)
        cot_all = cot_all.reshape(n_dp * rows, width)
        conv_full = small[:, 8:16].reshape(count, taps, own_conv)
        decay_full = small[:, 16:].reshape(width, 2 * all_heads)
        first_full = small[:, 0, :own_d]
        second_full = small[:, 1, :own_d]
        every_id = small[:, 2, 0]
        output_weight, down_weight, up_plane = lax.optimization_barrier(
            (output_weight, down_weight, up_plane, small)
        )[:3]
    else:
        in_mine = [
            by_dp(input_weight[:, n_dp * a : n_dp * b], b - a).transpose(1, 0, 2)
            for a, b in zip(bounds[:-1], bounds[1:])
        ]
        in_mine = jnp.concatenate(in_mine, axis=2)
        decay_full = lax.all_gather(decay_weight, ("dp", "fsdp"), axis=0, tiled=True)
        in_full = whole_rows(lax.all_to_all(in_mine, "dp", 0, 0, tiled=True))
        up_plane = lax.all_to_all(up_mine, "dp", 0, 0, tiled=True)
        small = gather_small(
            pack((conv_weight, norm_first, norm_second, group_ids.astype(BF16)), 16), n_dp, n_z, 1
        ).reshape(count, -1)
        conv_full = small[:, :conv_size].reshape(count, taps, own_conv)
        first_full = small[:, conv_size : conv_size + own_d]
        second_full = small[:, conv_size + own_d : conv_size + 2 * own_d]
        every_id = small[:, conv_size + 2 * own_d]
    out_full = lax.all_gather(output_weight, "fsdp", axis=0, tiled=True)
    up_full = whole_rows(up_plane)
    down_full = lax.all_gather(down_weight, "fsdp", axis=0, tiled=True)
    conv_full = conv_full.transpose(1, 0, 2).reshape(taps, -1)
    first_full = first_full.reshape(1, width).astype(F32)
    second_full = second_full.reshape(1, width).astype(F32)
    every_id = every_id.astype(jnp.int32)
    scales = 1.0 / jnp.sum((every_id[:, None] == every_id[None, :]).astype(F32), axis=0).reshape(n_dp, n_z)
    scales = lax.dynamic_index_in_dim(scales, lax.axis_index("fsdp"), axis=1, keepdims=False)
    seed = cotangent.astype(F32) * lax.dynamic_index_in_dim(scales, here, axis=0, keepdims=False)
    lanes_of_scales = jnp.broadcast_to(scales[:, None], (n_dp, 128))
    scales = jnp.broadcast_to(scales[:, None, None], (n_dp, rows, 1)).reshape(n_dp * rows, 1)
    if not square:
        normed_all = spread((inputs * first_root * first_full).astype(BF16), 2)
        cot_all = spread(cotangent, 3)

    def conv_columns(start, size):
        return lax.dynamic_slice_in_dim(conv_full, start + here * size, size, axis=1)

    conv_mine = jnp.concatenate(
        [conv_columns(0, key), conv_columns(n_dp * key, key), conv_columns(2 * n_dp * key, value)], axis=1
    ).astype(F32)
    decay_mine = jnp.pad(
        jnp.stack(
            [
                lax.dynamic_slice_in_dim(decay_scale, here * heads, heads),
                lax.dynamic_slice_in_dim(decay_bias, here * heads, heads),
            ]
        ),
        ((0, 0), (0, 128 - heads)),
    )
    gain = output_gain[None, :]

    raw_weight = jnp.pad(
        jnp.concatenate(
            [lax.dynamic_slice_in_dim(decay_full, i * all_heads + here * heads, heads, axis=1) for i in range(2)], axis=1
        ),
        ((0, 0), (0, 128 - 2 * heads)),
    )
    projected = dot(normed_all, in_full)
    raw = dot(normed_all, raw_weight)
    mixed, inverse, solved, core, before_silu = mixer_forward(projected, raw, conv_mine, decay_mine, gain, heads, rows)
    if square:
        middle, second_all = relay(
            mixed.reshape(n_dp, rows, value), out_full, None, NN, NN, second_full, (tokens,), False, 4
        )
        upgate, hidden, hidden_seed = units_forward(second_all, up_full, lanes_of_scales, units, main)
        second_all = second_all.reshape(n_dp * rows, width)
    else:
        middle = inputs + total(dot(mixed, out_full, out=BF16), 4)
        second_root = lax.rsqrt(jnp.mean(middle * middle, axis=-1, keepdims=True) + EPSILON)
        second_all = spread((middle * second_root * second_full).astype(BF16), 5)
        upgate = dot(second_all, up_full)

        def halves_of(a):
            return (a[:, :main], a[:, main : 2 * main]), (a[:, 2 * main : main + units], a[:, main + units :])

        acts = [(g, u, jax.nn.sigmoid(g)) for g, u in halves_of(upgate)]
        hidden = jnp.concatenate([g * s * u for g, u, s in acts], axis=1)
        hidden_seed = (hidden * scales).astype(BF16)
        hidden = hidden.astype(BF16)

    down_grad = dot(hidden_seed, cot_all, TN, out=BF16)
    down_grad, cot_all = lax.optimization_barrier((down_grad, cot_all))
    if square:
        upgate_low = units_backward(
            cot_all.reshape(n_dp, rows, width), down_full, upgate, lanes_of_scales, units, main
        )
    else:
        hidden_grad = dot(cot_all, down_full, NT) * scales
        parts = list(zip(acts, (hidden_grad[:, :main], hidden_grad[:, main:])))
        upgate_low = jnp.concatenate(
            [x for (g, u, s), grad in parts for x in (grad * u * s * (1.0 + g * (1.0 - s)), grad * g * s)], axis=1
        ).astype(BF16)
    upgate_grad = dot(second_all, upgate_low, TN, out=BF16)
    upgate_low, upgate_grad = lax.optimization_barrier((upgate_low, upgate_grad))

    def norm_back(v, root, gain_row, grad):
        hat = v * root
        scaled = grad * gain_row
        gain_grad = jnp.sum(grad * hat, axis=0)
        return root * (scaled - hat * jnp.mean(scaled * hat, axis=-1, keepdims=True)), gain_grad

    def owned_rows(a):
        return lax.psum_scatter(a, "fsdp", scatter_dimension=0, tiled=True)

    def owned_parts(a):
        return lax.psum_scatter(a, "fsdp", scatter_dimension=0, tiled=True)

    def by_plane(a):
        return a.reshape(n_dp, n_z, own_d, a.shape[-1]).transpose(1, 0, 2, 3).reshape(width, -1)

    down_total = owned_rows(down_grad)
    block_part = dot(hidden, down_full, out=BF16)
    upgate_low, upgate_grad, down_total, block_part, seed = lax.optimization_barrier(
        (upgate_low, by_plane(upgate_grad), down_total, block_part, seed)
    )
    upgate_sum = owned_parts(upgate_grad)
    if square:
        middle_grad, middle_all, mixed_grad, second_grad = relay(
            upgate_low.reshape(n_dp, rows, 2 * units), up_full, out_full, NT, NT, second_full, (middle, seed), True, 6
        )
        middle_all = middle_all.reshape(n_dp * rows, width)
        mixed_grad = mixed_grad.reshape(n_dp * rows, value)
    else:
        normed_two_grad = total(dot(upgate_low, up_full, NT, out=BF16), 6)
        middle_part, second_grad = norm_back(middle, second_root, second_full, normed_two_grad)
        middle_grad = seed + middle_part
        middle_all = spread(middle_grad.astype(BF16), 8)
        mixed_grad = dot(middle_all, out_full, NT)
    output_grad = dot(mixed, middle_all, TN, out=BF16)
    mixed_grad, output_grad, upgate_sum = lax.optimization_barrier((mixed_grad, output_grad, upgate_sum))
    output_total = owned_rows(output_grad)
    projected_low, raw_low, conv_grad, gain_grad, decay_grad = mixer_backward(
        projected, raw, conv_mine, decay_mine, gain, inverse, solved, core, before_silu, mixed_grad, heads, rows
    )
    projected_low, output_total = lax.optimization_barrier((projected_low, output_total))
    def upgate_rows(a):
        return jnp.concatenate(
            [
                jnp.concatenate([x, y], axis=2).transpose(1, 0, 2).reshape(own_d, -1)
                for x, y in (
                    (a[:, :, :main], a[:, :, 2 * main : main + units]),
                    (a[:, :, main : 2 * main], a[:, :, main + units :]),
                )
            ],
            axis=1,
        ).astype(F32)

    in_grad = dot(normed_all, projected_low, TN, out=BF16)
    raw_grad = dot(normed_all, raw_low, TN)[:, : 2 * heads]
    down_total = down_total.astype(F32)
    output_total = output_total.astype(F32)
    if square:
        lines = jnp.concatenate(
            [
                jnp.zeros((1, width), F32),
                second_grad.reshape(1, width),
                jnp.tile(gain_grad[:, :128], (1, width // 128)),
                jnp.tile(gain_grad[:, 128:], (1, width // 128)),
                jnp.tile(jnp.pad(decay_grad[:, :heads].reshape(1, -1), ((0, 0), (0, 128 - 2 * heads))), (1, width // 128)),
                jnp.zeros((3, width), F32),
            ],
            axis=0,
        )
        conv_lines = jnp.zeros((8, n_dp * (2 * key + value)), F32)
        for at, a, b in (
            (here * key, 0, key),
            (n_dp * key + here * key, key, 2 * key),
            (2 * n_dp * key + here * value, 2 * key, 2 * key + value),
        ):
            conv_lines = lax.dynamic_update_slice(conv_lines, conv_grad[:, a:b], (0, at))
        conv_lines = lax.dynamic_update_slice(conv_lines, raw_grad.reshape(1, -1), (taps, 0))
        result, tokens_grad, input_total, up_total, summed, planes, conv_total, raw_planes = conclude(
            in_grad.reshape(n_dp, n_z, own_d, cols),
            projected_low.reshape(n_dp, rows, cols),
            raw_low.reshape(n_dp, rows, 128),
            in_full,
            raw_weight,
            block_part.reshape(n_dp, rows, width),
            upgate_sum.reshape(n_dp, own_d, 2 * units),
            tokens,
            middle,
            middle_grad,
            first_full,
            lines,
            conv_lines,
            bounds,
            9,
        )
        input_total = input_total.astype(F32)
        decay_total = raw_planes.reshape(n_dp, own_d, 2, heads).transpose(1, 2, 0, 3).reshape(own_d, 2 * all_heads)
        upgate_total = upgate_rows(up_total)
        per = 128 // own_d
        place = lax.rem(flat, per) * own_d
        first_total = lax.dynamic_slice_in_dim(summed[0], place, own_d)
        second_total = lax.dynamic_slice_in_dim(summed[1], place, own_d)
        gain_total = summed[2:4].reshape(-1)
        scale_total = planes[:, :heads].reshape(-1)
        bias_total = planes[:, heads : 2 * heads].reshape(-1)
        conv_total = conv_total[:taps]
    else:
        projected_low, in_grad = lax.optimization_barrier((projected_low, in_grad))
        back_one = (dot(projected_low, in_full, NT) + dot(raw_low, raw_weight, NT)).astype(BF16)
        in_sum = owned_parts(by_plane(in_grad))
        normed_one_grad = total(back_one, 9)
        result = middle + total(block_part, 7)
        input_part, first_grad = norm_back(inputs, first_root, first_full, normed_one_grad)
        tokens_grad = middle_grad + input_part

        up_total = lax.all_to_all(upgate_sum.reshape(n_dp, own_d, -1), "dp", 0, 0, tiled=True)
        upgate_total = upgate_rows(up_total)
        in_total = lax.all_to_all(in_sum.reshape(n_dp, own_d, -1), "dp", 0, 0, tiled=True)
        raw_rows = jnp.zeros((width, 2, all_heads), F32)
        raw_rows = lax.dynamic_update_slice(raw_rows, raw_grad.reshape(width, 2, heads), (0, 0, here * heads))
        decay_total = lax.psum_scatter(raw_rows.reshape(width, -1), ("dp", "fsdp"), scatter_dimension=0, tiled=True)
        in_total = in_total.transpose(1, 0, 2).astype(F32)
        input_total = jnp.concatenate(
            [in_total[:, :, a:b].reshape(own_d, -1) for a, b in zip(bounds[:-1], bounds[1:])], axis=1
        )

        share = key // own_conv, value // own_conv
        owner = jnp.concatenate(
            [
                here * share[0] + jnp.arange(share[0]),
                (n_dp + here) * share[0] + jnp.arange(share[0]),
                2 * n_dp * share[0] + here * share[1] + jnp.arange(share[1]),
            ]
        )
        blocks = conv_grad.reshape(taps, -1, own_conv).transpose(1, 0, 2).reshape(-1, taps * own_conv)
        for_owner = owner[None, :] == jnp.arange(count)[:, None]
        everyone = jnp.concatenate([gain_grad.reshape(-1), decay_grad[:, :heads].reshape(-1)])
        packets = jnp.concatenate(
            [
                first_grad.reshape(count, own_d),
                second_grad.reshape(count, own_d),
                jnp.sum(jnp.where(for_owner[:, :, None], blocks[None], 0.0), axis=1),
                jnp.broadcast_to(everyone[None], (count, everyone.size)),
            ],
            axis=1,
        )
        size = packets.shape[1]
        lines = -(-size // 1024) * 8
        packets = jnp.pad(packets, ((0, 0), (0, lines * 128 - size))).reshape(count, lines, 128)
        shared = scatter_small(packets, n_dp, n_z, 10).reshape(count, -1)
        summed = jnp.sum(shared, axis=0)
        first_total = summed[:own_d]
        second_total = summed[own_d : 2 * own_d]
        start = 2 * own_d + taps * own_conv
        conv_total = summed[2 * own_d : start].reshape(taps, own_conv)
        gain_total = summed[start : start + gain_grad.size]
        start += gain_grad.size
        scale_bias = jnp.sum(shared[:, start : start + 2 * heads].reshape(n_dp, n_z, 2, heads), axis=1)
        scale_total = scale_bias[:, 0].reshape(-1)
        bias_total = scale_bias[:, 1].reshape(-1)
    return (
        result,
        tokens_grad,
        first_total,
        input_total,
        decay_total,
        conv_total,
        scale_total,
        bias_total,
        gain_total,
        output_total,
        second_total,
        upgate_total,
        down_total,
    )


def solution(mesh):
    both = ("dp", "fsdp")
    rows, vector = P(both, None), P(both)
    return jax.shard_map(
        functools.partial(local, mesh.shape["dp"], mesh.shape["fsdp"]),
        mesh=mesh,
        in_specs=(
            rows, rows, vector, vector, rows, rows, P(None, both), P(), P(), P(), rows, vector, rows, rows,
        ),
        out_specs=(
            rows, rows, vector, rows, rows, P(None, both), P(), P(), P(), rows, vector, rows, rows,
        ),
        check_vma=False,
    )
```

```python
import functools

import jax
import jax.numpy as jnp
from jax import lax
from jax.experimental import pallas as pl
from jax.experimental.pallas import tpu as pltpu
from jax.sharding import PartitionSpec as P

MESH = pl.DeviceIdType.MESH
F32 = jnp.float32
BF16 = jnp.bfloat16
EPSILON = 1e-06
DK = 128
DV = 256
BASE = 8
NN = (((1,), (0,)), ((), ()))
NT = (((1,), (1,)), ((), ()))
TN = (((0,), (0,)), ((), ()))


def dot1(a, b, dims=NN):
    return lax.dot_general(a.astype(BF16), b.astype(BF16), dims, preferred_element_type=F32)


def halves(a):
    if a.dtype == BF16:
        return (a,)
    high = a.astype(BF16)
    return (high, (a - high.astype(F32)).astype(BF16))


def dot3(a, b, dims=NN):
    a, b = halves(a), halves(b)
    total = lax.dot_general(a[0], b[0], dims, preferred_element_type=F32)
    if len(a) > 1:
        total = total + lax.dot_general(a[1], b[0], dims, preferred_element_type=F32)
    if len(b) > 1:
        total = total + lax.dot_general(a[0], b[1], dims, preferred_element_type=F32)
    return total


def sum_rows(mask, b):
    mask = jnp.where(mask, 1.0, 0.0).astype(BF16)
    high = b.astype(BF16)
    rest = b - high.astype(F32)
    middle = rest.astype(BF16)
    low = (rest - middle.astype(F32)).astype(BF16)
    return dot1(mask, high) + (dot1(mask, middle) + dot1(mask, low))


def shift_down(v, n):
    turned = pltpu.roll(v, n, 0)
    places = lax.broadcasted_iota(jnp.int32, (8, 1), 0)
    return jnp.concatenate([jnp.where(places >= n, turned[:8], 0.0), turned[8:]], axis=0)


def shift_up(v, n):
    length = v.shape[0]
    turned = pltpu.roll(v, length - n, 0)
    places = lax.broadcasted_iota(jnp.int32, (8, 1), 0)
    return jnp.concatenate([turned[:-8], jnp.where(places < 8 - n, turned[-8:], 0.0)], axis=0)


def conv(c, taps):
    count = taps.shape[0]
    total = c * taps[count - 1 : count]
    for j in range(count - 1):
        total = total + shift_down(c, count - 1 - j) * taps[j : j + 1]
    return total


def sigmoid(v):
    return 1.0 / (1.0 + jnp.exp(-v))


def gate_of(v):
    return 0.5 * jnp.tanh(0.5 * v) + 0.5


def softplus(v):
    return jnp.maximum(v, 0.0) + jnp.log1p(jnp.exp(-jnp.abs(v)))


def unit_inverses(lowers, row_ids, col_ids):
    length = lowers[0].shape[0]
    size = BASE
    same = row_ids // size == col_ids // size
    pick = jnp.where(col_ids[:, :128] == lax.rem(row_ids[:, :128], size), 1.0, 0.0).astype(BF16)
    lanes = lax.broadcasted_iota(jnp.int32, (length // size, size, 128), 2)
    places = lax.broadcasted_iota(jnp.int32, (length // size, size, 128), 1)
    compact = [dot3(jnp.where(same, lower, 0.0), pick).reshape(length // size, size, 128) for lower in lowers]
    solved = [jnp.where(lanes == places, 1.0, 0.0) for _ in lowers]
    for j in range(size - 1):
        solved = [x - a[:, :, j : j + 1] * x[:, j : j + 1, :] for a, x in zip(compact, solved)]
    inverses = [jnp.where(same, dot3(x.reshape(length, 128), pick, NT), 0.0) for x in solved]
    while size < length:
        wide = 2 * size
        off = (row_ids // wide == col_ids // wide) & (row_ids // size != col_ids // size)
        inner = [dot3(jnp.where(off, lower, 0.0), inverse) for lower, inverse in zip(lowers, inverses)]
        inverses = [inverse - dot3(inverse, x) for inverse, x in zip(inverses, inner)]
        size = wide
    return inverses


def common(raw, decay, heads, length):
    rows = lax.broadcasted_iota(jnp.int32, (length, 1), 0)
    row_ids = lax.broadcasted_iota(jnp.int32, (length, length), 0)
    col_ids = lax.broadcasted_iota(jnp.int32, (length, length), 1)
    lanes = lax.broadcasted_iota(jnp.int32, raw.shape, 1)
    shifted = raw + decay[1:2]
    rate = jnp.where(lanes < heads, -jnp.exp(decay[0:1]) * softplus(shifted), 0.0)
    beta = sigmoid(raw)
    cumulated = sum_rows(row_ids >= col_ids, rate)
    return rows, row_ids, col_ids, lanes, shifted, rate, beta, cumulated, cumulated.T


def head_parts(h, heads):
    key = slice(h * DK, (h + 1) * DK)
    keyk = slice((heads + h) * DK, (heads + h + 1) * DK)
    val = slice(heads * DV + h * DV, heads * DV + (h + 1) * DV)
    gat = slice(2 * heads * DV + h * DV, 2 * heads * DV + (h + 1) * DV)
    return key, keyk, val, gat


def mixer_forward_kernel(heads, proj_ref, raw_ref, taps_ref, decay_ref, gain_ref, mixed_ref, inv_ref, solved_ref, core_ref, conv_ref):
    length = proj_ref.shape[0]
    decay = decay_ref[...]
    gain = gain_ref[...]
    raw = raw_ref[...]
    rows, row_ids, col_ids, lanes, shifted, rate, beta, cumulated, cum_t = common(raw, decay, heads, length)
    def active(cols):
        y = conv(proj_ref[:, cols], taps_ref[:, cols])
        conv_ref[:, cols] = y
        return y * gate_of(y)

    parts = [head_parts(h, heads) for h in range(heads)]
    queries, keys, values, growths, betas, lowers = [], [], [], [], [], []
    for h, (qs, ks, vs, gs) in enumerate(parts):
        k = active(ks)
        k = (k * lax.rsqrt(jnp.sum(k * k, axis=-1, keepdims=True) + EPSILON)).astype(BF16)
        beta_h = beta[:, heads + h : heads + h + 1]
        gap = cumulated[:, h : h + 1] - cum_t[h : h + 1, :]
        growth = jnp.where(row_ids >= col_ids, jnp.exp(jnp.where(row_ids >= col_ids, gap, 0.0)), 0.0)
        keys.append(k)
        growths.append(growth)
        betas.append(beta_h)
        lowers.append(jnp.where(row_ids > col_ids, growth * dot1(k, k, NT) * beta_h, 0.0))
    inverses = unit_inverses(lowers, row_ids, col_ids)
    for h, (qs, ks, vs, gs) in enumerate(parts):
        q = active(qs)
        q = (q * lax.rsqrt(jnp.sum(q * q, axis=-1, keepdims=True) + EPSILON) * DK ** (-0.5)).astype(BF16)
        v = active(vs).astype(BF16)
        inv_ref[h] = inverses[h]
        solved = dot3(inverses[h], betas[h] * v.astype(F32))
        core = dot3(growths[h] * dot1(q, keys[h], NT), solved)
        solved_ref[:, h * DV : (h + 1) * DV] = solved
        core_ref[:, h * DV : (h + 1) * DV] = core
        gate = proj_ref[:, gs]
        normed = core * lax.rsqrt(jnp.mean(core * core, axis=-1, keepdims=True) + EPSILON) * gain
        mixed_ref[:, h * DV : (h + 1) * DV] = (normed * (gate * gate_of(gate))).astype(BF16)


def mixer_forward(proj, raw, taps, decay, gain, heads, length):
    tokens, width = proj.shape
    seqs = tokens // length
    hv = heads * DV
    row = lambda cols: pl.BlockSpec((length, cols), lambda s: (s, 0))
    whole = lambda a: pl.BlockSpec(a.shape, lambda s: (0,) * a.ndim)
    return pl.pallas_call(
        functools.partial(mixer_forward_kernel, heads),
        grid=(seqs,),
        in_specs=[row(width), row(128), whole(taps), whole(decay), whole(gain)],
        out_specs=[row(hv), pl.BlockSpec((None, heads, length, length), lambda s: (s, 0, 0, 0)), row(hv), row(hv), row(taps.shape[1])],
        out_shape=[
            jax.ShapeDtypeStruct((tokens, hv), BF16),
            jax.ShapeDtypeStruct((seqs, heads, length, length), F32),
            jax.ShapeDtypeStruct((tokens, hv), F32),
            jax.ShapeDtypeStruct((tokens, hv), F32),
            jax.ShapeDtypeStruct((tokens, taps.shape[1]), F32),
        ],
        cost_estimate=busy(55), compiler_params=pltpu.CompilerParams(vmem_limit_bytes=48 << 20),
    )(proj, raw, taps, decay, gain)


def mixer_backward_kernel(
    heads, proj_ref, raw_ref, taps_ref, decay_ref, gain_ref, inv_ref, solved_ref, core_ref, pre_ref, grad_ref,
    low_ref, conv_ref, gain_grad_ref, decay_grad_ref,
):
    length = proj_ref.shape[0]
    count = taps_ref.shape[0]
    decay = decay_ref[...]
    gain = gain_ref[...]
    raw = raw_ref[...]
    rows, row_ids, col_ids, lanes, shifted, rate, beta, cumulated, cum_t = common(raw, decay, heads, length)
    within = row_ids >= col_ids
    strict = row_ids > col_ids

    @pl.when(pl.program_id(0) == 0)
    def _():
        conv_ref[...] = jnp.zeros_like(conv_ref)
        gain_grad_ref[...] = jnp.zeros_like(gain_grad_ref)
        decay_grad_ref[...] = jnp.zeros_like(decay_grad_ref)

    cum_grad = jnp.zeros(raw.shape, F32)
    beta_grad = jnp.zeros(raw.shape, F32)
    for h in range(heads):
        qs, ks, vs, gs = head_parts(h, heads)
        hs = slice(h * DV, (h + 1) * DV)

        def active(cols):
            y = pre_ref[:, cols]
            s = gate_of(y)
            return y * s, s * (1.0 + y * (1.0 - s))

        def conv_back(cols, grad):
            c = proj_ref[:, cols]
            total = grad * taps_ref[count - 1 : count, cols]
            conv_ref[count - 1 : count, cols] += jnp.sum(grad * c, axis=0, keepdims=True)
            for j in range(count - 1):
                n = count - 1 - j
                later = shift_up(grad, n)
                total = total + later * taps_ref[j : j + 1, cols]
                conv_ref[j : j + 1, cols] += jnp.sum(later * c, axis=0, keepdims=True)
            low_ref[:, cols] = total.astype(BF16)

        core = core_ref[:, hs]
        gate = proj_ref[:, gs]
        gate_sig = gate_of(gate)
        grad = grad_ref[:, hs]
        root = lax.rsqrt(jnp.mean(core * core, axis=-1, keepdims=True) + EPSILON)
        normed = core * root
        silu_gate = gate * gate_sig
        gain_grad_ref[...] += jnp.sum(grad * normed * silu_gate, axis=0, keepdims=True)
        low_ref[:, gs] = (grad * normed * gain * gate_sig * (1.0 + gate * (1.0 - gate_sig))).astype(BF16)
        normed_grad = grad * gain * silu_gate
        core_grad = root * (normed_grad - normed * jnp.mean(normed_grad * normed, axis=-1, keepdims=True))

        q_act, q_slope = active(qs)
        q_root = lax.rsqrt(jnp.sum(q_act * q_act, axis=-1, keepdims=True) + EPSILON)
        q_unit = q_act * q_root
        q = (q_unit * DK ** (-0.5)).astype(BF16)
        k_act, k_slope = active(ks)
        k_root = lax.rsqrt(jnp.sum(k_act * k_act, axis=-1, keepdims=True) + EPSILON)
        k_unit = k_act * k_root
        k = k_unit.astype(BF16)
        v_act, v_slope = active(vs)
        v = v_act.astype(BF16).astype(F32)
        beta_h = beta[:, heads + h : heads + h + 1]
        gap = cumulated[:, h : h + 1] - cum_t[h : h + 1, :]
        growth = jnp.where(within, jnp.exp(jnp.where(within, gap, 0.0)), 0.0)
        decayed_gram = jnp.where(strict, growth * dot1(k, k, NT), 0.0)
        weights = growth * dot1(q, k, NT)
        inverse = inv_ref[h]
        solved = solved_ref[:, hs]
        core_low = core_grad.astype(BF16)
        solved_grad = dot3(weights, core_low, TN)
        weights_grad = dot3(core_low, solved, NT)
        value_grad = dot3(inverse, solved_grad.astype(BF16), TN)
        lower_grad = jnp.where(strict, -dot3(value_grad.astype(BF16), solved, NT), 0.0)
        gap_part = lower_grad * decayed_gram
        beta_col = jnp.sum(gap_part, axis=-1, keepdims=True) + jnp.sum(value_grad * v, axis=-1, keepdims=True)
        gap_grad = gap_part * beta_h + weights_grad * weights
        cum_col = jnp.sum(gap_grad, axis=-1, keepdims=True)
        cum_row = jnp.sum(gap_grad, axis=0, keepdims=True)
        cum_col = cum_col - jnp.broadcast_to(cum_row, (8, length)).T[:, 0:1]
        gram_grad = lower_grad * growth * beta_h
        score_grad = weights_grad * growth
        k_grad = dot3(gram_grad, k) + dot3(gram_grad, k, TN) + dot3(score_grad, q, TN)
        q_grad = dot3(score_grad, k)
        cum_grad = jnp.where(lanes == h, cum_col, cum_grad)
        beta_grad = jnp.where(lanes == heads + h, beta_col, beta_grad)

        q_grad = q_grad * DK ** (-0.5)
        q_grad = q_root * (q_grad - q_unit * jnp.sum(q_grad * q_unit, axis=-1, keepdims=True))
        conv_back(qs, q_grad * q_slope)
        k_grad = k_root * (k_grad - k_unit * jnp.sum(k_grad * k_unit, axis=-1, keepdims=True))
        conv_back(ks, k_grad * k_slope)
        conv_back(vs, value_grad * beta_h * v_slope)

    rate_grad = sum_rows(col_ids >= row_ids, cum_grad)
    bias_part = rate_grad * -jnp.exp(decay[0:1]) * sigmoid(shifted)
    raw_grad = jnp.where(lanes < heads, bias_part, beta_grad * beta * (1.0 - beta))
    low_ref[:, heads * 768 :] = raw_grad.astype(BF16)
    decay_grad_ref[0:1] += jnp.sum(jnp.where(lanes < heads, rate_grad * rate, 0.0), axis=0, keepdims=True)
    decay_grad_ref[1:2] += jnp.sum(jnp.where(lanes < heads, bias_part, 0.0), axis=0, keepdims=True)


def mixer_backward(proj, raw, taps, decay, gain, inverse, solved, core, pre, grad, heads, length):
    tokens, width = proj.shape
    seqs = tokens // length
    hv = heads * DV
    row = lambda cols: pl.BlockSpec((length, cols), lambda s: (s, 0))
    whole = lambda a: pl.BlockSpec(a.shape, lambda s: (0,) * a.ndim)
    return pl.pallas_call(
        functools.partial(mixer_backward_kernel, heads),
        grid=(seqs,),
        in_specs=[row(width), row(128), whole(taps), whole(decay), whole(gain),
                  pl.BlockSpec((None, heads, length, length), lambda s: (s, 0, 0, 0)), row(hv), row(hv), row(taps.shape[1]), row(hv)],
        out_specs=[row(width + 128), whole(taps), whole(gain), whole(decay)],
        out_shape=[
            jax.ShapeDtypeStruct((tokens, width + 128), BF16),
            jax.ShapeDtypeStruct(taps.shape, F32),
            jax.ShapeDtypeStruct(gain.shape, F32),
            jax.ShapeDtypeStruct(decay.shape, F32),
        ],
        cost_estimate=busy(50), compiler_params=pltpu.CompilerParams(vmem_limit_bytes=56 << 20),
    )(proj, raw, taps, decay, gain, inverse, solved, core, pre, grad)


def busy(us):
    return pl.CostEstimate(flops=us * 1_000_000_000, bytes_accessed=0, transcendentals=0)


def _place(n_dp):
    me = lax.axis_index("dp")
    z = lax.axis_index("fsdp")
    core = lax.rem(me, 2)
    chip = me // 2
    return me, z, core, lax.rem(chip, 2), chip // 2

def ag_square(x, cid, chunks=4):
    rows, cols = x.shape
    r = rows // chunks
    def kernel(x_ref, o_ref, lsem, ssem, rsem, dssem, drsem, fs, fr):
        me, z, core, cx, cy = _place(8)
        dev = lambda dx, dy, c: 2*(2*lax.rem(cy+dy,2)+lax.rem(cx+dx,2))+c
        nx, ny, nd = dev(1,0,core), dev(0,1,core), dev(1,1,core)
        src = dev(1-core, core, core)
        tgt = dev(core, 1-core, core)
        sib = dev(0,0,1-core)
        bar = pltpu.get_barrier_semaphore()
        for d in (sib,nx,ny):
            pl.semaphore_signal(bar, inc=1, device_id=(d,z), device_id_type=MESH)
        pl.semaphore_wait(bar, 3)
        lc = pltpu.make_async_copy(x_ref, o_ref.at[me], lsem); lc.start()
        def rc(a, b, s, q, d):
            return pltpu.make_async_remote_copy(a, b, s, q, device_id=(d,z), device_id_type=MESH)
        own = []
        for c in range(chunks):
            sl = pl.ds(c*r, r)
            for i, d in ((0,nx),(1,ny)):
                cp = rc(x_ref.at[sl], o_ref.at[me,sl], ssem.at[i,c], rsem.at[i,c], d); cp.start(); own.append(cp)
        sibs=[]
        for c in range(chunks):
            sl = pl.ds(c*r, r)
            cp = rc(x_ref.at[sl], o_ref.at[me,sl], fs.at[0,c], fr.at[0,c], sib); cp.start(); sibs.append(cp)
        other = dev(core, 1-core, core)
        for c in range(chunks):
            sl = pl.ds(c*r, r)
            rc(x_ref.at[sl], o_ref.at[src,sl], ssem.at[core,c], rsem.at[core,c], sib).wait_recv()
            cp = rc(o_ref.at[src,sl], o_ref.at[src,sl], dssem.at[c], drsem.at[c], tgt); cp.start(); sibs.append((cp,))
            cp = rc(o_ref.at[src,sl], o_ref.at[src,sl], fs.at[1,c], fr.at[1,c], sib); cp.start(); sibs.append(cp)
            rc(x_ref.at[sl], o_ref.at[other,sl], ssem.at[1-core,c], rsem.at[1-core,c], sib).wait_recv()
            cp = rc(o_ref.at[other,sl], o_ref.at[other,sl], fs.at[2,c], fr.at[2,c], sib); cp.start(); sibs.append(cp)
        for c in range(chunks):
            sl = pl.ds(c*r, r)
            rc(x_ref.at[sl], o_ref.at[nd,sl], dssem.at[c], drsem.at[c], sib).wait_recv()
            cp = rc(o_ref.at[nd,sl], o_ref.at[nd,sl], fs.at[3,c], fr.at[3,c], sib); cp.start(); sibs.append(cp)
        for cp in own: cp.wait_send()
        for cp in sibs:
            if isinstance(cp, tuple): cp[0].wait_send()
            else: cp.wait()
        lc.wait()
    D=pltpu.SemaphoreType.DMA
    return pl.pallas_call(kernel, out_shape=jax.ShapeDtypeStruct((8,rows,cols),x.dtype),
        in_specs=[pl.BlockSpec(memory_space=pl.ANY)], out_specs=pl.BlockSpec(memory_space=pl.ANY),
        scratch_shapes=[D, D((2,chunks)), D((2,chunks)), D((chunks,)), D((chunks,)), D((4,chunks)), D((4,chunks))],
        cost_estimate=busy(40), compiler_params=pltpu.CompilerParams(collective_id=cid, has_side_effects=True))(x)

def rs_square(x, cid, chunks=4):
    _, rows, cols = x.shape
    r = rows // chunks
    def kernel(x_ref, o_ref, X, A, B, R, lsem, sa, ra, sb, rb):
        me, z, core, cx, cy = _place(8)
        dev = lambda dx, dy, c: 2*(2*lax.rem(cy+dy,2)+lax.rem(cx+dx,2))+c
        fdx, fdy = 1-core, core
        nf, ng = dev(fdx,fdy,core), dev(fdy,fdx,core)
        sib = dev(0,0,1-core)
        bar = pltpu.get_barrier_semaphore()
        for d in (sib,nf,ng):
            pl.semaphore_signal(bar, inc=1, device_id=(d,z), device_id_type=MESH)
        mine = [dev(1,1,core), ng, nf, me]
        s_f, s_g = dev(core,1-core,1-core), dev(1-core,core,1-core)
        theirs = [dev(1,1,1-core), s_g, s_f, sib]
        loads=[]
        for k in range(4):
            for c in range(chunks):
                sl=pl.ds(c*r,r)
                cp=pltpu.make_async_copy(x_ref.at[mine[k],sl], X.at[k,sl], lsem.at[k,c]); cp.start(); loads.append(cp)
        pl.semaphore_wait(bar, 3)
        def rc(a, b, s, q, d):
            return pltpu.make_async_remote_copy(a, b, s, q, device_id=(d,z), device_id_type=MESH)
        sends=[]; ga={}
        for k in range(4):
            for c in range(chunks):
                sl=pl.ds(c*r,r)
                cp=rc(x_ref.at[theirs[k],sl], A.at[k,sl], sa.at[k,c], ra.at[k,c], sib); cp.start(); sends.append(cp); ga[k,c]=cp
        def pair(k,c):
            sl=pl.ds(c*r,r)
            loads[k*chunks+c].wait(); ga[k,c].wait_recv()
            return X[k,sl].astype(F32)+A[k,sl].astype(F32)
        gb={}
        def ship(slot, c, d):
            sl=pl.ds(c*r,r)
            cp=rc(B.at[slot,sl], R.at[slot,sl], sb.at[slot,c], rb.at[slot,c], d); cp.start(); sends.append(cp); gb[slot,c]=cp
        for c in range(chunks):
            sl=pl.ds(c*r,r)
            B[0,sl]=pair(0,c).astype(BF16); ship(0,c,nf)
        for c in range(chunks):
            sl=pl.ds(c*r,r)
            B[2,sl]=pair(2,c).astype(BF16); ship(2,c,nf)
        for c in range(chunks):
            sl=pl.ds(c*r,r)
            v=pair(1,c)
            gb[0,c].wait_recv()
            B[1,sl]=(v+R[0,sl].astype(F32)).astype(BF16); ship(1,c,ng)
        for c in range(chunks):
            sl=pl.ds(c*r,r)
            v=pair(3,c)
            gb[2,c].wait_recv()
            o_ref[sl]=v+R[2,sl].astype(F32)
        for c in range(chunks):
            sl=pl.ds(c*r,r)
            gb[1,c].wait_recv()
            o_ref[sl]=o_ref[sl]+R[1,sl].astype(F32)
        for cp in sends: cp.wait_send()
    D=pltpu.SemaphoreType.DMA
    V=lambda n: pltpu.VMEM((n,rows,cols),x.dtype)
    return pl.pallas_call(kernel, out_shape=jax.ShapeDtypeStruct((rows,cols),F32),
        in_specs=[pl.BlockSpec(memory_space=pl.ANY)], out_specs=pl.BlockSpec(memory_space=pltpu.VMEM),
        scratch_shapes=[V(4),V(4),V(3),V(3), D((4,chunks)), D((4,chunks)), D((4,chunks)), D((3,chunks)), D((3,chunks))],
        cost_estimate=busy(40), compiler_params=pltpu.CompilerParams(collective_id=cid, has_side_effects=True, vmem_limit_bytes=40<<20))(x)

def begin(weight, ups, tokens, cotangent, small, bounds, n_z, cid):
    own = weight.shape[0]
    cols = bounds[-1]
    units = ups.shape[2]
    rows, width = tokens.shape
    count = 8 * n_z
    chunks = 2
    part = rows // chunks

    def kernel(
        w_ref, u_ref, t_ref, c_ref, small_ref, w_out, u_out, n_out, c_out, small_out,
        toks, lsem, a_send, a_recv, g_send, g_recv, up_send, up_recv, down_send, down_recv,
        small_send, small_recv, x_send, x_recv, d_send, d_recv, f_send, f_recv,
    ):
        me, z, core, cx, cy = _place(8)
        flat = me * n_z + z
        bar = pltpu.get_barrier_semaphore()

        def dev(dx, dy, c):
            return 2 * (2 * lax.rem(cy + dy, 2) + lax.rem(cx + dx, 2)) + c

        sib = dev(0, 0, 1 - core)

        def partner(o):
            return dev(o // 4, lax.rem(o // 2, 2), lax.rem(core + o, 2))

        def anyone(o):
            other = lax.rem(flat + o, count)
            return (other // n_z, lax.rem(other, n_z))

        def remote(src, dst, send, recv, device):
            return pltpu.make_async_remote_copy(src, dst, send, recv, device_id=device, device_id_type=MESH)

        def loop(first, last, body):
            def step(o, _):
                body(o)
                return 0

            lax.fori_loop(first, last, step, 0)

        def sections(q):
            for first, last in zip(bounds[:-1], bounds[1:]):
                size = last - first
                at = pl.multiple_of(8 * first + q * size, 128)
                yield w_ref.at[:, pl.ds(at, size)], w_out.at[me, z, :, pl.ds(first, size)]

        def send_piece(o):
            q = partner(o)
            for src, dst in sections(q):
                remote(src, dst, a_send.at[o - 1], a_recv.at[o - 1], (q, z)).start()

        def landed(o):
            at = w_out.at[partner(o), z]
            return remote(at, at, a_send.at[o - 1], a_recv.at[o - 1], (sib, z))

        def up(t, o):
            at = w_out.at[partner(o), z - t]
            return remote(at, at, up_send.at[t, o], up_recv.at[t, o], (me, z + 1))

        def down(t, o):
            at = w_out.at[partner(o), z + t]
            return remote(at, at, down_send.at[t, o], down_recv.at[t, o], (me, z - 1))

        def pass_on(t, o):
            if t > 0:

                @pl.when(z >= t)
                def _():
                    at = w_out.at[partner(o), z - t]
                    remote(at, at, up_send.at[t - 1, o], up_recv.at[t - 1, o], (sib, z)).wait_recv()

                @pl.when(z + t < n_z)
                def _():
                    at = w_out.at[partner(o), z + t]
                    remote(at, at, down_send.at[t - 1, o], down_recv.at[t - 1, o], (sib, z)).wait_recv()

            if t < n_z - 1:

                @pl.when((z >= t) & (z < n_z - 1))
                def _():
                    up(t, o).start()

                @pl.when((z + t < n_z) & (z > 0))
                def _():
                    down(t, o).start()

        def sent(t, o):
            @pl.when((z >= t) & (z < n_z - 1))
            def _():
                up(t, o).wait_send()

            @pl.when((z + t < n_z) & (z > 0))
            def _():
                down(t, o).wait_send()

        def unit_piece(o):
            q = partner(o)
            return remote(u_ref.at[q], u_out.at[me], g_send.at[o - 1], g_recv.at[o - 1], (q, z))

        def tiny(o):
            return remote(small_ref, small_out.at[flat], small_send.at[o - 1], small_recv.at[o - 1], anyone(o))

        near = (dev(1, 0, core), dev(0, 1, core))
        source, other, across = dev(1 - core, core, core), dev(core, 1 - core, core), dev(1, 1, core)

        def gather(i, ref, out):
            def at(q, c):
                return out.at[q, pl.ds(c * part, part)]

            def mine(c):
                return ref.at[pl.ds(c * part, part)]

            def first(k, c):
                return remote(mine(c), at(me, c), x_send.at[i, k, c], x_recv.at[i, k, c], (near[k], z))

            def twin(k, q, c):
                src = mine(c) if k == 0 else at(q, c)
                return remote(src, at(q, c), f_send.at[i, k, c], f_recv.at[i, k, c], (sib, z))

            def second(c):
                return remote(at(source, c), at(source, c), d_send.at[i, c], d_recv.at[i, c], (other, z))

            def keep():
                return pltpu.make_async_copy(ref, out.at[me], lsem.at[i])

            def begin_():
                keep().start()
                for c in range(chunks):
                    for k in range(2):
                        first(k, c).start()
                for c in range(chunks):
                    twin(0, me, c).start()

            def forward():
                for c in range(chunks):
                    remote(mine(c), at(source, c), x_send.at[i, core, c], x_recv.at[i, core, c], (sib, z)).wait_recv()
                    second(c).start()
                    twin(1, source, c).start()
                    remote(
                        mine(c), at(other, c), x_send.at[i, 1 - core, c], x_recv.at[i, 1 - core, c], (sib, z)
                    ).wait_recv()
                    twin(2, other, c).start()

            def last():
                for c in range(chunks):
                    remote(at(across, c), at(across, c), d_send.at[i, c], d_recv.at[i, c], (other, z)).wait_recv()
                    twin(3, across, c).start()

            def finish():
                keep().wait()
                theirs = (sib, dev(core, 1 - core, 1 - core), dev(1 - core, core, 1 - core), dev(1, 1, 1 - core))
                for c in range(chunks):
                    for k in range(4):
                        remote(
                            at(theirs[k], c), at(theirs[k], c), f_send.at[i, k, c], f_recv.at[i, k, c], (sib, z)
                        ).wait_recv()

            def close():
                for c in range(chunks):
                    for k in range(2):
                        first(k, c).wait_send()
                    second(c).wait_send()
                    for k, q in enumerate((me, source, other, across)):
                        twin(k, q, c).wait_send()

            return begin_, forward, last, finish, close

        tok_begin, tok_forward, tok_last, tok_finish, tok_close = gather(0, t_ref, toks)
        cot_begin, cot_forward, cot_last, cot_finish, cot_close = gather(1, c_ref, c_out)

        loop(1, count, lambda o: pl.semaphore_signal(bar, inc=1, device_id=anyone(o), device_id_type=MESH))
        for src, dst in sections(me):
            pltpu.make_async_copy(src, dst, lsem.at[2]).start()
        keep_u = pltpu.make_async_copy(u_ref.at[me], u_out.at[me], lsem.at[3])
        keep_s = pltpu.make_async_copy(small_ref, small_out.at[flat], lsem.at[4])
        keep_u.start()
        keep_s.start()
        pl.semaphore_wait(bar, count - 1)

        loop(1, 8, send_piece)
        pltpu.make_async_copy(w_out.at[me, z], w_out.at[me, z], lsem.at[2]).wait()
        pass_on(0, 0)
        loop(1, count, lambda o: tiny(o).start())

        def first_leg(o):
            landed(o).wait_recv()
            pass_on(0, o)

        tok_begin()
        loop(1, 8, first_leg)
        loop(0, 8, lambda o: pass_on(1, o))
        tok_forward()
        cot_begin()
        loop(1, 8, lambda o: unit_piece(o).start())
        loop(0, 4, lambda o: pass_on(2, o))
        tok_last()
        tok_finish()
        keep_s.wait()
        loop(1, count, lambda o: tiny(o).wait_recv())

        lanes = lax.broadcasted_iota(jnp.int32, (1, 128), 1)
        per = 128 // own
        blocks = []
        for m in range(width // 128):
            block = small_out[m * per, 0:1, :].astype(F32)
            for i in range(1, per):
                block = jnp.where(lanes >= i * own, small_out[m * per + i, 0:1, :].astype(F32), block)
            blocks.append(block)
        gain = jnp.concatenate(blocks, axis=1)
        step = 32

        def norm_rows(o):
            def some(r, _):
                sl = pl.ds(r * step, step)
                v = toks[o, sl].astype(F32)
                n_out[o, sl] = (
                    v * lax.rsqrt(jnp.mean(v * v, axis=-1, keepdims=True) + EPSILON) * gain
                ).astype(BF16)
                return 0

            lax.fori_loop(0, rows // step, some, 0)

        def third_leg(o):
            pass_on(2, o)
            norm_rows(o - 4)
            norm_rows(o)

        loop(4, 8, third_leg)
        cot_forward()
        loop(0, 4, lambda o: pass_on(3, o))
        cot_last()
        loop(4, 8, lambda o: pass_on(3, o))
        cot_finish()
        for t in range(n_z - 1):
            loop(0, 8, functools.partial(sent, t))
        loop(1, 8, lambda o: landed(o).wait_send())
        loop(1, 8, lambda o: unit_piece(o).wait())
        loop(1, count, lambda o: tiny(o).wait_send())
        keep_u.wait()
        tok_close()
        cot_close()

    dma = pltpu.SemaphoreType.DMA
    anywhere, vmem = pl.BlockSpec(memory_space=pl.ANY), pl.BlockSpec(memory_space=pltpu.VMEM)
    plane = jax.ShapeDtypeStruct((8, rows, width), BF16)
    legs = n_z - 1
    return pl.pallas_call(
        kernel,
        out_shape=[
            jax.ShapeDtypeStruct((8, n_z, own, cols), BF16),
            jax.ShapeDtypeStruct((8, own, units), BF16),
            plane,
            plane,
            jax.ShapeDtypeStruct((count,) + small.shape, BF16),
        ],
        in_specs=[anywhere] * 5,
        out_specs=[anywhere, anywhere, vmem, anywhere, vmem],
        scratch_shapes=[
            pltpu.VMEM((8, rows, width), BF16),
            dma((5,)),
            dma((7,)),
            dma((7,)),
            dma((7,)),
            dma((7,)),
            dma((legs, 8)),
            dma((legs, 8)),
            dma((legs, 8)),
            dma((legs, 8)),
            dma((count - 1,)),
            dma((count - 1,)),
            dma((2, 2, chunks)),
            dma((2, 2, chunks)),
            dma((2, chunks)),
            dma((2, chunks)),
            dma((2, 4, chunks)),
            dma((2, 4, chunks)),
        ],
        cost_estimate=busy(150),
        compiler_params=pltpu.CompilerParams(
            collective_id=cid, has_side_effects=True, vmem_limit_bytes=58 << 20
        ),
    )(weight, ups, tokens, cotangent, small)


def relay(left, first, second, first_dims, second_dims, gain, extras, norm_back, cid):
    _, rows, depth = left.shape
    width = gain.shape[1]
    multiply = second is not None
    out_cols = 0 if not multiply else second.shape[1] if second_dims == NN else second.shape[0]
    chunks = 4
    part = rows // chunks
    tile = 512
    out_tiles = [(a, min(a + tile, out_cols)) for a in range(0, out_cols, tile)]

    def kernel(left_ref, first_ref, gain_ref, *refs):
        extra_refs, refs = refs[: len(extras)], refs[len(extras) :]
        if multiply:
            second_ref, *refs = refs
        rows_out, all_ref, *refs = refs
        if multiply:
            prod_out, *refs = refs
        if norm_back:
            gain_grad, *refs = refs
        if multiply:
            *refs, w2, stage = refs
        (L, W, plane, T, A, B, R, S, msem, fsem, lsem, sa, ra, sb, rb, x_send, x_recv, d_send, d_recv, f_send, f_recv) = refs
        me, z, core, cx, cy = _place(8)

        def dev(dx, dy, c):
            return 2 * (2 * lax.rem(cy + dy, 2) + lax.rem(cx + dx, 2)) + c

        def remote(src, dst, send, recv, device):
            return pltpu.make_async_remote_copy(src, dst, send, recv, device_id=(device, z), device_id_type=MESH)

        sib = dev(0, 0, 1 - core)
        nf, ng, across = dev(1 - core, core, core), dev(core, 1 - core, core), dev(1, 1, core)
        bar = pltpu.get_barrier_semaphore()
        for d in (sib, nf, ng):
            pl.semaphore_signal(bar, inc=1, device_id=(d, z), device_id_type=MESH)
        if multiply:
            load = pltpu.make_async_copy(second_ref, w2, lsem.at[2])
            load.start()

        load_first = pltpu.make_async_copy(first_ref, W, lsem.at[3])
        load_first.start()

        mine = (across, ng, nf, me)
        theirs = (dev(1, 1, 1 - core), dev(1 - core, core, 1 - core), dev(core, 1 - core, 1 - core), sib)

        turns = (theirs[0], mine[0], theirs[2], mine[2], theirs[1], theirs[3], mine[1], mine[3])

        def load_left(i):
            return pltpu.make_async_copy(left_ref.at[turns[i]], L.at[i], msem.at[i])

        for i in range(8):
            load_left(i).start()

        def partial(i, write):
            load_left(i).wait()

            def some(n, _):
                cols = pl.ds(pl.multiple_of(n * tile, tile), tile)
                w = W[:, cols] if first_dims == NN else W[cols, :]
                write(cols, lax.dot_general(L[i], w, first_dims, preferred_element_type=F32))
                return 0

            lax.fori_loop(0, width // tile, some, 0)

        def give(i, k):
            def write(cols, v):
                T[k, :, cols] = v.astype(BF16)

            partial(i, write)
            remote(T.at[k], A.at[k], sa.at[k], ra.at[k], sib).start()

        def got(k):
            remote(T.at[k], A.at[k], sa.at[k], ra.at[k], sib).wait_recv()

        def cut(c):
            return pl.ds(c * part, part)

        def ship(k, c, d):
            return remote(B.at[k, cut(c)], R.at[k, cut(c)], sb.at[k, c], rb.at[k, c], d)

        def send_sum(i, k):
            def write(cols, v):
                S[:, cols] = v

            partial(i, write)
            got(k)
            for c in range(chunks):
                B[k, cut(c)] = (S[cut(c)] + A[k, cut(c)].astype(F32)).astype(BF16)
                ship(k, c, nf).start()

        def keep_sum(i, k):
            got(k)

            def write(cols, v):
                S[:, cols] = v + A[k, :, cols].astype(F32)

            partial(i, write)

        pl.semaphore_wait(bar, 3)
        load_first.wait()
        give(0, 0)
        send_sum(1, 0)
        give(2, 2)
        send_sum(3, 2)
        give(4, 1)
        give(5, 3)
        keep_sum(6, 1)
        for c in range(chunks):
            ship(0, c, nf).wait_recv()
            B[1, cut(c)] = (S[cut(c)] + R[0, cut(c)].astype(F32)).astype(BF16)
            ship(1, c, ng).start()
        keep_sum(7, 3)

        source, other = nf, ng

        def at(q, c):
            return plane.at[q, cut(c)]

        def step(k, c):
            return remote(at(me, c), at(me, c), x_send.at[k, c], x_recv.at[k, c], (dev(1, 0, core), dev(0, 1, core))[k])

        def twin(k, q, c):
            return remote(at(q, c), at(q, c), f_send.at[k, c], f_recv.at[k, c], sib)

        def second_step(c):
            return remote(at(source, c), at(source, c), d_send.at[c], d_recv.at[c], other)

        gains = gain_ref[...]
        if norm_back:
            gain_grad[...] = jnp.zeros_like(gain_grad)
        for c in range(chunks):
            ship(2, c, nf).wait_recv()
            ship(1, c, ng).wait_recv()
            for h in range(2):
                sl = pl.ds(c * part + h * (part // 2), part // 2)
                total = S[sl] + R[2, sl].astype(F32) + R[1, sl].astype(F32)
                if norm_back:
                    v = extra_refs[0][sl]
                    root = lax.rsqrt(jnp.mean(v * v, axis=-1, keepdims=True) + EPSILON)
                    hat = v * root
                    scaled = total * gains
                    gain_grad[...] += jnp.sum(total * hat, axis=0, keepdims=True)
                    done = extra_refs[1][sl] + root * (scaled - hat * jnp.mean(scaled * hat, axis=-1, keepdims=True))
                    low = done
                else:
                    done = extra_refs[0][sl].astype(F32) + total
                    low = done * lax.rsqrt(jnp.mean(done * done, axis=-1, keepdims=True) + EPSILON) * gains
                rows_out[sl] = done
                plane[me, sl] = low.astype(BF16)
            for k in range(2):
                step(k, c).start()
            twin(0, me, c).start()
        if multiply:
            load.wait()

        flushes = []

        kept = []

        def product(q):
            keep = pltpu.make_async_copy(plane.at[q], all_ref.at[q], fsem.at[len(kept)])
            keep.start()
            kept.append(keep)
            if not multiply:
                return
            slot = len(flushes) % 2
            if len(flushes) > 1:
                flushes[-2].wait()
            for a, b in out_tiles:
                w = w2[:, a:b] if second_dims == NN else w2[a:b, :]
                stage[slot, :, a:b] = lax.dot_general(plane[q], w, second_dims, preferred_element_type=F32)
            flush = pltpu.make_async_copy(stage.at[slot], prod_out.at[q], lsem.at[slot])
            flush.start()
            flushes.append(flush)

        def twin_got(k):
            for c in range(chunks):
                twin(k, theirs_at[k], c).wait_recv()

        theirs_at = (sib, dev(core, 1 - core, 1 - core), dev(1 - core, core, 1 - core), dev(1, 1, 1 - core))
        product(me)
        for c in range(chunks):
            remote(at(source, c), at(source, c), x_send.at[core, c], x_recv.at[core, c], sib).wait_recv()
            second_step(c).start()
            twin(1, source, c).start()
            remote(at(other, c), at(other, c), x_send.at[1 - core, c], x_recv.at[1 - core, c], sib).wait_recv()
            twin(2, other, c).start()
            if c == 0:
                twin_got(0)
                product(sib)
        product(source)
        product(other)
        for c in range(chunks):
            remote(at(across, c), at(across, c), d_send.at[c], d_recv.at[c], sib).wait_recv()
            twin(3, across, c).start()
            if c == 0:
                twin_got(1)
                product(theirs_at[1])
            if c == 1:
                twin_got(2)
                product(theirs_at[2])
        product(across)
        twin_got(3)
        product(theirs_at[3])

        for k in range(4):
            remote(T.at[k], A.at[k], sa.at[k], ra.at[k], sib).wait_send()
        for c in range(chunks):
            for k in range(3):
                ship(k, c, nf).wait_send()
            for k in range(2):
                step(k, c).wait_send()
            second_step(c).wait_send()
            for k, q in enumerate((me, source, other, across)):
                twin(k, q, c).wait_send()
        for flush in flushes[-2:] + kept:
            flush.wait()

    dma = pltpu.SemaphoreType.DMA
    anywhere, vmem = pl.BlockSpec(memory_space=pl.ANY), pl.BlockSpec(memory_space=pltpu.VMEM)
    block = lambda n: pltpu.VMEM((n, rows, width), BF16)
    out_shape = [
        jax.ShapeDtypeStruct((rows, width), F32),
        jax.ShapeDtypeStruct((8, rows, width), BF16),
    ]
    out_specs = [vmem, anywhere]
    operands = [left, first, gain, *extras]
    in_specs = [anywhere, anywhere] + [vmem] * (1 + len(extras))
    later = []
    if multiply:
        out_shape.append(jax.ShapeDtypeStruct((8, rows, out_cols), F32))
        out_specs.append(anywhere)
        operands.append(second)
        in_specs.append(anywhere)
        later = [pltpu.VMEM(second.shape, BF16), pltpu.VMEM((2, rows, out_cols), F32)]
    if norm_back:
        out_shape.append(jax.ShapeDtypeStruct((1, width), F32))
        out_specs.append(vmem)
    return pl.pallas_call(
        kernel,
        out_shape=out_shape,
        in_specs=in_specs,
        out_specs=out_specs,
        scratch_shapes=[
            pltpu.VMEM(left.shape, BF16),
            pltpu.VMEM(first.shape, BF16),
            block(8),
            block(4),
            block(4),
            block(3),
            block(3),
            pltpu.VMEM((rows, width), F32),
            dma((8,)),
            dma((8,)),
            dma((4,)),
            dma((4,)),
            dma((4,)),
            dma((3, chunks)),
            dma((3, chunks)),
            dma((2, chunks)),
            dma((2, chunks)),
            dma((chunks,)),
            dma((chunks,)),
            dma((4, chunks)),
            dma((4, chunks)),
            *later,
        ],
        cost_estimate=busy(80),
        compiler_params=pltpu.CompilerParams(
            collective_id=cid, has_side_effects=True, vmem_limit_bytes=58 << 20
        ),
    )(*operands)


def unit_pairs(a, main):
    tail = a[:, 2 * main :]
    size = tail.shape[1]
    turned = pltpu.roll(tail, size // 2, 1)
    left = lax.broadcasted_iota(jnp.int32, tail.shape, 1) < size // 2
    return (a[:, :main], a[:, main : 2 * main]), (jnp.where(left, tail, turned), jnp.where(left, turned, tail)), left


def units_forward(x, weight, scales, units, main):
    blocks, rows, width = x.shape
    cols = weight.shape[1]

    def kernel(x_ref, w_ref, s_ref, up_ref, hidden_ref, scaled_ref):
        scale = s_ref[pl.ds(pl.program_id(0), 1), :][:, 0:1]
        for a in range(0, cols, 512):
            b = min(a + 512, cols)
            up_ref[:, a:b] = jnp.dot(x_ref[...], w_ref[:, a:b], preferred_element_type=F32)
        (g, u), (g_tail, u_tail), _ = unit_pairs(up_ref[...], main)
        hidden = g * sigmoid(g) * u
        tail = (g_tail * sigmoid(g_tail) * u_tail)[:, : units - main]
        hidden_ref[:, :main] = hidden.astype(BF16)
        hidden_ref[:, main:] = tail.astype(BF16)
        scaled_ref[:, :main] = (hidden * scale).astype(BF16)
        scaled_ref[:, main:] = (tail * scale).astype(BF16)

    row = lambda n: pl.BlockSpec((rows, n), lambda i: (i, 0))
    whole = lambda a: pl.BlockSpec(a.shape, lambda i: (0, 0))
    tokens = blocks * rows
    return pl.pallas_call(
        kernel,
        grid=(blocks,),
        in_specs=[row(width), whole(weight), whole(scales)],
        out_specs=[row(cols), row(units), row(units)],
        out_shape=[
            jax.ShapeDtypeStruct((tokens, cols), F32),
            jax.ShapeDtypeStruct((tokens, units), BF16),
            jax.ShapeDtypeStruct((tokens, units), BF16),
        ],
        cost_estimate=busy(20),
        compiler_params=pltpu.CompilerParams(vmem_limit_bytes=48 << 20),
    )(x.reshape(tokens, width), weight, scales)


def units_backward(cot, weight, upgate, scales, units, main):
    blocks, rows, width = cot.shape
    cols = upgate.shape[1]

    def kernel(c_ref, w_ref, up_ref, s_ref, low_ref):
        scale = s_ref[pl.ds(pl.program_id(0), 1), :][:, 0:1]
        pair, pair_tail, left = unit_pairs(up_ref[...], main)
        tail_rows = w_ref[main:, :]
        grad = dot(c_ref[...], w_ref[:main, :], NT) * scale
        grad_tail = dot(c_ref[...], jnp.concatenate([tail_rows, tail_rows], axis=0), NT) * scale

        def both(g, u, grad):
            s = sigmoid(g)
            return grad * u * s * (1.0 + g * (1.0 - s)), grad * g * s

        gate_grad, up_grad = both(*pair, grad)
        low_ref[:, :main] = gate_grad.astype(BF16)
        low_ref[:, main : 2 * main] = up_grad.astype(BF16)
        gate_grad, up_grad = both(*pair_tail, grad_tail)
        low_ref[:, 2 * main :] = jnp.where(left, gate_grad, up_grad).astype(BF16)

    row = lambda n: pl.BlockSpec((rows, n), lambda i: (i, 0))
    whole = lambda a: pl.BlockSpec(a.shape, lambda i: (0, 0))
    tokens = blocks * rows
    return pl.pallas_call(
        kernel,
        grid=(blocks,),
        in_specs=[row(width), whole(weight), row(cols), whole(scales)],
        out_specs=row(cols),
        out_shape=jax.ShapeDtypeStruct((tokens, cols), BF16),
        cost_estimate=busy(12),
        compiler_params=pltpu.CompilerParams(vmem_limit_bytes=48 << 20),
    )(cot.reshape(tokens, width), weight, upgate, scales)


def conclude(grad, left, weight, raw_weight, block, ups, tokens, middle, middle_grad, gain, lines, conv, bounds, cid):
    n_z = 4
    own, cols = grad.shape[2], grad.shape[3] - 128
    units = ups.shape[2]
    rows, width = tokens.shape
    count = 8 * n_z
    per = 128 * count // width
    conv_cols = conv.shape[1] // count
    chunks = 2
    part = rows // chunks
    tile = 512
    last = n_z - 1

    def kernel(
        g_ref, l_ref, w_ref, wr_ref, b_ref, u_ref, t_ref, m_ref, mg_ref, gain_ref, lines_ref, conv_ref,
        result, tg, in_out, u_out, line_sum, line_planes, conv_sum, conv_planes,
        lines_out, conv_out, W, L, own_buf, UD, T, A, B, R, S, A7, B7, R7, X7, line_buf,
        lsem, wsem, osem, mine_sem, us, ur, ds, dr, i_send, i_recv, u_send, u_recv, p_send, p_recv, c_send, c_recv,
        sa, ra, sb, rb, sa7, ra7, sb7, rb7,
    ):
        me, z, core, cx, cy = _place(8)
        flat = me * n_z + z

        def dev(dx, dy, c):
            return 2 * (2 * lax.rem(cy + dy, 2) + lax.rem(cx + dx, 2)) + c

        sib = dev(0, 0, 1 - core)
        nf, ng, across = dev(1 - core, core, core), dev(core, 1 - core, core), dev(1, 1, core)

        def partner(o):
            return dev(o // 4, lax.rem(o // 2, 2), lax.rem(core + o, 2))

        def anyone(o):
            other = lax.rem(flat + o, count)
            return (other // n_z, lax.rem(other, n_z))

        def remote(src, dst, send, recv, device):
            return pltpu.make_async_remote_copy(src, dst, send, recv, device_id=device, device_id_type=MESH)

        def loop(first, end, body):
            def step(o, _):
                body(o)
                return 0

            lax.fori_loop(first, end, step, 0)

        bar = pltpu.get_barrier_semaphore()
        loop(1, count, lambda o: pl.semaphore_signal(bar, inc=1, device_id=anyone(o), device_id_type=MESH))

        mine = (across, ng, nf, me)
        theirs = (dev(1, 1, 1 - core), dev(1 - core, core, 1 - core), dev(core, 1 - core, 1 - core), sib)
        turns = (theirs[0], theirs[2], mine[0], theirs[1], mine[2], theirs[3], mine[1], mine[3])

        def load_left(i):
            return (pltpu.make_async_copy(l_ref.at[turns[i]], L.at[i % 2], lsem.at[i % 2]),)

        def start(copies):
            for copy in copies:
                copy.start()

        def wait(copies):
            for copy in copies:
                copy.wait()

        load_weight = (
            pltpu.make_async_copy(w_ref, W.at[:, pl.ds(0, cols)], wsem.at[0]),
            pltpu.make_async_copy(wr_ref, W.at[:, pl.ds(cols, 128)], wsem.at[7]),
        )
        load_middle = pltpu.make_async_copy(m_ref, result, wsem.at[1])
        load_grad = pltpu.make_async_copy(mg_ref, tg, wsem.at[2])

        def load_own(zz):
            return pltpu.make_async_copy(g_ref.at[:, zz, :, pl.ds(0, cols)], own_buf.at[zz], osem.at[zz])

        def give7(k):
            return remote(b_ref.at[theirs[k]], A7.at[k], sa7.at[k], ra7.at[k], (sib, z))

        def mine7(k):
            return pltpu.make_async_copy(b_ref.at[mine[k]], X7 if k == 3 else B7.at[k], mine_sem.at[k])

        def start7():
            for k in (0, 2, 1, 3):
                give7(k).start()
                mine7(k).start()

        start(load_left(0))
        start(load_weight)
        for zz in (0, 3, 2, 1):
            load_own(zz).start()
        start(load_left(1))
        load_middle.start()
        load_grad.start()
        pl.semaphore_wait(bar, count - 1)

        def up_slot(s, o):
            return s * 8 + o

        def down_slot(s, o):
            return 39 - (s * 8 + o)

        def up(s, o, src):
            return remote(src, UD.at[up_slot(s, o)], us.at[s, o], ur.at[s, o], (me, z + 1))

        def down(s, o, src):
            return remote(src, UD.at[down_slot(s, o)], ds.at[s, o], dr.at[s, o], (me, z - 1))

        def start_line(s, o):
            q = partner(o)

            @pl.when(z == 0)
            def _():
                up(s, o, g_ref.at[q, last - s, :, pl.ds(0, cols)]).start()

            @pl.when(z == last)
            def _():
                down(s, o, g_ref.at[q, s, :, pl.ds(0, cols)]).start()

        start7()
        for s in range(last):
            loop(0, 8, functools.partial(start_line, s))
        for zz in range(n_z):
            load_own(zz).wait()

        def sections(q):
            for a, b in zip(bounds[:-1], bounds[1:]):
                at = pl.multiple_of(8 * a + q * (b - a), 128)
                yield pl.ds(a, b - a), in_out.at[:, pl.ds(at, b - a)]

        def deliver(o, slot):
            @pl.when(o == 0)
            def _():
                for src, dst in sections(me):
                    pltpu.make_async_copy(UD.at[slot, :, src], dst, wsem.at[3]).start()

            @pl.when(o > 0)
            def _():
                for src, dst in sections(me):
                    remote(UD.at[slot, :, src], dst, i_send.at[o - 1], i_recv.at[o - 1], (partner(o), z)).start()

        def add(slot, *others):
            total = UD[slot].astype(F32)
            for other in others:
                total = total + other.astype(F32)
            UD[slot] = total.astype(BF16)

        def up_tick(i):
            s, o = i // 8, lax.rem(i, 8)
            q, u = partner(o), up_slot(s, o)

            @pl.when((z >= 1) & (z <= last - s))
            def _():
                remote(UD.at[u], UD.at[u], us.at[s, o], ur.at[s, o], (sib, z)).wait_recv()

            @pl.when((z >= 1) & (z < last - s))
            def _():
                add(u, own_buf[last - s, q])
                up(s, o, UD.at[u]).start()

            @pl.when((z == last) & (s == 0))
            def _():
                add(u, own_buf[last, q])
                deliver(o, u)

            @pl.when((z == 1) & (s == 2))
            def _():
                add(u, UD[down_slot(1, o)], own_buf[1, q])
                deliver(o, u)

        def down_tick(i):
            s, o = i // 8, lax.rem(i, 8)
            q, d = partner(o), down_slot(s, o)

            @pl.when((z <= last - 1) & (z >= s))
            def _():
                remote(UD.at[d], UD.at[d], ds.at[s, o], dr.at[s, o], (sib, z)).wait_recv()

            @pl.when((z <= last - 1) & (z > s))
            def _():
                add(d, own_buf[s, q])
                down(s, o, UD.at[d]).start()

            @pl.when((z == 0) & (s == 0))
            def _():
                add(d, own_buf[0, q])
                deliver(o, d)

            @pl.when((z == 2) & (s == 2))
            def _():
                add(d, UD[up_slot(1, o)], own_buf[2, q])
                deliver(o, d)

        lag = 4
        low = 1 - z // 2

        def tick(i):
            at_up, at_down = i - lag * (1 - low), i - lag * low

            @pl.when((at_up >= 0) & (at_up < 24))
            def _():
                up_tick(at_up)

            @pl.when((at_down >= 0) & (at_down < 24))
            def _():
                down_tick(at_down)

        def cut(c):
            return pl.ds(c * part, part)

        def partial(i, write):
            wait(load_left(i))

            def some(n, _):
                at = pl.ds(pl.multiple_of(n * tile, tile), tile)
                write(at, lax.dot_general(L[i % 2], W[at, :], NT, preferred_element_type=F32))
                return 0

            lax.fori_loop(0, width // tile, some, 0)
            if i + 2 < 8:
                start(load_left(i + 2))

        def give(i, k, slot, before):
            if before is not None:
                remote(T.at[slot], A.at[before], sa.at[before], ra.at[before], (sib, z)).wait_send()

            def write(at, v):
                T[slot, :, at] = v.astype(BF16)

            partial(i, write)
            remote(T.at[slot], A.at[k], sa.at[k], ra.at[k], (sib, z)).start()

        def got(k):
            remote(T.at[0], A.at[k], sa.at[k], ra.at[k], (sib, z)).wait_recv()

        def ship(k, c, d):
            return remote(B.at[k, cut(c)], R.at[k, cut(c)], sb.at[k, c], rb.at[k, c], (d, z))

        def ship7(k, c, d):
            return remote(B7.at[k, cut(c)], R7.at[k, cut(c)], sb7.at[k, c], rb7.at[k, c], (d, z))

        def send_sum(i, k):
            got(k)

            def write(at, v):
                B[k, :, at] = (v + A[k, :, at].astype(F32)).astype(BF16)

            partial(i, write)
            for c in range(chunks):
                ship(k, c, nf).start()

        def keep_sum(i, k):
            got(k)

            def write(at, v):
                S[:, at] = v + A[k, :, at].astype(F32)

            partial(i, write)

        def second_hop():
            for c in range(chunks):
                ship(0, c, nf).wait_recv()
                B[1, cut(c)] = (S[cut(c)] + R[0, cut(c)].astype(F32)).astype(BF16)
                ship(1, c, ng).start()

        def send7(k):
            mine7(k).wait()
            give7(k).wait_recv()
            for c in range(chunks):
                B7[k, cut(c)] = (B7[k, cut(c)].astype(F32) + A7[k, cut(c)].astype(F32)).astype(BF16)
                ship7(k, c, nf).start()

        def second_hop7():
            mine7(1).wait()
            give7(1).wait_recv()
            for c in range(chunks):
                ship7(0, c, nf).wait_recv()
                sl = cut(c)
                B7[1, sl] = (B7[1, sl].astype(F32) + A7[1, sl].astype(F32) + R7[0, sl].astype(F32)).astype(BF16)
                ship7(1, c, ng).start()

        small = 32

        def finish_rows():
            load_grad.wait()
            line_buf[...] = lines_ref[...]
            line_buf[0:1] = jnp.zeros((1, width), F32)
            gains = gain_ref[...]
            for c in range(chunks):
                ship(2, c, nf).wait_recv()
                ship(1, c, ng).wait_recv()

                def some(r, _):
                    sl = pl.ds(pl.multiple_of(c * part + r * small, small), small)
                    total = S[sl] + R[2, sl].astype(F32) + R[1, sl].astype(F32)
                    v = t_ref[sl].astype(F32)
                    root = lax.rsqrt(jnp.mean(v * v, axis=-1, keepdims=True) + EPSILON)
                    hat = v * root
                    scaled = total * gains
                    line_buf[0:1] += jnp.sum(total * hat, axis=0, keepdims=True)
                    tg[sl] += root * (scaled - hat * jnp.mean(scaled * hat, axis=-1, keepdims=True))
                    return 0

                lax.fori_loop(0, part // small, some, 0)

        def finish7():
            load_middle.wait()
            mine7(3).wait()
            give7(3).wait_recv()
            for c in range(chunks):
                ship7(2, c, nf).wait_recv()
                ship7(1, c, ng).wait_recv()

                def some(r, _):
                    sl = pl.ds(pl.multiple_of(c * part + r * small, small), small)
                    result[sl] += (
                        X7[sl].astype(F32) + A7[3, sl].astype(F32) + R7[2, sl].astype(F32) + R7[1, sl].astype(F32)
                    )
                    return 0

                lax.fori_loop(0, part // small, some, 0)

        def line_part(d):
            return line_buf.at[:, pl.ds(pl.multiple_of((d // per) * 128, 128), 128)]

        def conv_part(d):
            return conv_ref.at[:, pl.ds(pl.multiple_of(d * conv_cols, conv_cols), conv_cols)]

        def packet(o):
            d = lax.rem(flat + o, count)
            return remote(line_part(d), lines_out.at[flat], p_send.at[o - 1], p_recv.at[o - 1], anyone(o))

        def conv_packet(o):
            d = lax.rem(flat + o, count)
            return remote(conv_part(d), conv_out.at[flat], c_send.at[o - 1], c_recv.at[o - 1], anyone(o))

        keep_line = pltpu.make_async_copy(line_part(flat), lines_out.at[flat], wsem.at[4])
        keep_conv = pltpu.make_async_copy(conv_part(flat), conv_out.at[flat], wsem.at[5])
        keep_up = pltpu.make_async_copy(u_ref.at[me], u_out.at[me], wsem.at[6])

        def unit_piece(o):
            q = partner(o)
            return remote(u_ref.at[q], u_out.at[me], u_send.at[o - 1], u_recv.at[o - 1], (q, z))

        def send_packets():
            keep_line.start()
            loop(1, count, lambda o: packet(o).start())

        def others():
            keep_conv.start()
            keep_up.start()
            loop(1, count, lambda o: conv_packet(o).start())

        def first_give():
            wait(load_weight)
            give(0, 0, 0, None)
            give(1, 2, 1, None)

        work = (
            lambda: (send7(0), send7(2)),
            first_give,
            lambda: (send_sum(2, 0), give(3, 1, 0, 0)),
            lambda: (send_sum(4, 2), give(5, 3, 1, 2)),
            lambda: (second_hop7(), keep_sum(6, 1)),
            others,
            lambda: (second_hop(), keep_sum(7, 3)),
            lambda: (finish7(), loop(1, 8, lambda o: unit_piece(o).start())),
            lambda: None,
            lambda: (finish_rows(), send_packets()),
            lambda: None,
            lambda: None,
            lambda: None,
            lambda: None,
        )
        for g, item in enumerate(work):
            item()
            loop(2 * g, 2 * g + 2, tick)

        def line_sent(s, o):
            @pl.when(z < last - s)
            def _():
                up(s, o, UD.at[up_slot(s, o)]).wait_send()

            @pl.when(z > s)
            def _():
                down(s, o, UD.at[down_slot(s, o)]).wait_send()

        for s in range(last):
            loop(0, 8, functools.partial(line_sent, s))
        for k, slot in ((1, 0), (3, 1)):
            remote(T.at[slot], A.at[k], sa.at[k], ra.at[k], (sib, z)).wait_send()
        for k in range(4):
            give7(k).wait_send()
        for c in range(chunks):
            for k in range(3):
                ship(k, c, nf).wait_send()
                ship7(k, c, nf).wait_send()
        piece = UD.at[0]

        def arrived(o):
            remote(piece, piece, i_send.at[o - 1], i_recv.at[o - 1], (sib, z)).wait()

        pltpu.make_async_copy(piece, piece, wsem.at[3]).wait()
        loop(1, 8, arrived)
        loop(1, 8, lambda o: unit_piece(o).wait())
        loop(1, count, lambda o: packet(o).wait())
        loop(1, count, lambda o: conv_packet(o).wait())
        keep_line.wait()
        keep_conv.wait()
        keep_up.wait()
        all_lines, all_conv = lines_out[0], conv_out[0]
        for d in range(1, count):
            all_lines, all_conv = all_lines + lines_out[d], all_conv + conv_out[d]
        line_sum[...] = all_lines
        conv_sum[...] = all_conv
        for d in range(8):
            line_planes[d : d + 1] = sum(lines_out[d * n_z + i, 4:5] for i in range(n_z))
            conv_planes[d : d + 1] = sum(conv_out[d * n_z + i, 4:5] for i in range(n_z))

    dma = pltpu.SemaphoreType.DMA
    anywhere, vmem = pl.BlockSpec(memory_space=pl.ANY), pl.BlockSpec(memory_space=pltpu.VMEM)
    blocks = lambda n: pltpu.VMEM((n, rows, width), BF16)
    f32_rows = jax.ShapeDtypeStruct((rows, width), F32)
    return pl.pallas_call(
        kernel,
        out_shape=[
            f32_rows,
            f32_rows,
            jax.ShapeDtypeStruct((own, 8 * bounds[-1]), BF16),
            jax.ShapeDtypeStruct((8, own, units), BF16),
            jax.ShapeDtypeStruct((8, 128), F32),
            jax.ShapeDtypeStruct((8, 128), F32),
            jax.ShapeDtypeStruct((8, conv_cols), F32),
            jax.ShapeDtypeStruct((8, conv_cols), F32),
        ],
        in_specs=[anywhere] * 6 + [vmem, anywhere, anywhere, vmem, vmem, anywhere],
        out_specs=[vmem, vmem, anywhere, anywhere] + [vmem] * 4,
        scratch_shapes=[
            pltpu.VMEM((count, 8, 128), F32),
            pltpu.VMEM((count, 8, conv_cols), F32),
            pltpu.VMEM((width, cols + 128), BF16),
            pltpu.VMEM((2, rows, cols + 128), BF16),
            pltpu.VMEM((n_z, 8, own, cols), BF16),
            pltpu.VMEM((40, own, cols), BF16),
            blocks(2),
            blocks(4),
            blocks(3),
            blocks(3),
            pltpu.VMEM((rows, width), F32),
            blocks(4),
            blocks(3),
            blocks(3),
            pltpu.VMEM((rows, width), BF16),
            pltpu.VMEM((8, width), F32),
            dma((2,)),
            dma((8,)),
            dma((n_z,)),
            dma((4,)),
            dma((3, 8)),
            dma((3, 8)),
            dma((3, 8)),
            dma((3, 8)),
            dma((7,)),
            dma((7,)),
            dma((7,)),
            dma((7,)),
            dma((count - 1,)),
            dma((count - 1,)),
            dma((count - 1,)),
            dma((count - 1,)),
            dma((4,)),
            dma((4,)),
            dma((3, chunks)),
            dma((3, chunks)),
            dma((4,)),
            dma((4,)),
            dma((3, chunks)),
            dma((3, chunks)),
        ],
        cost_estimate=busy(120),
        compiler_params=pltpu.CompilerParams(
            collective_id=cid, has_side_effects=True, vmem_limit_bytes=60 << 20
        ),
    )(grad, left, weight, raw_weight, block, ups, tokens, middle, middle_grad, gain, lines, conv)


def gather_small(x, n_dp, n_z, cid):
    rows, cols = x.shape
    count = n_dp * n_z

    def kernel(x_ref, o_ref, lsem, ssem, rsem):
        flat = lax.axis_index("dp") * n_z + lax.axis_index("fsdp")
        bar = pltpu.get_barrier_semaphore()

        def device(o):
            other = lax.rem(flat + o, count)
            return (other // n_z, lax.rem(other, n_z))

        def copy(o):
            return pltpu.make_async_remote_copy(
                x_ref, o_ref.at[flat], ssem.at[o - 1], rsem.at[o - 1], device_id=device(o), device_id_type=MESH
            )

        def greet(o, _):
            pl.semaphore_signal(bar, inc=1, device_id=device(o), device_id_type=MESH)
            return 0

        def send(o, _):
            copy(o).start()
            return 0

        def wait(o, _):
            copy(o).wait()
            return 0

        lax.fori_loop(1, count, greet, 0)
        local = pltpu.make_async_copy(x_ref, o_ref.at[flat], lsem)
        local.start()
        pl.semaphore_wait(bar, count - 1)
        lax.fori_loop(1, count, send, 0)
        lax.fori_loop(1, count, wait, 0)
        local.wait()

    dma = pltpu.SemaphoreType.DMA
    return pl.pallas_call(
        kernel,
        out_shape=jax.ShapeDtypeStruct((count, rows, cols), x.dtype),
        in_specs=[pl.BlockSpec(memory_space=pl.ANY)],
        out_specs=pl.BlockSpec(memory_space=pl.ANY),
        scratch_shapes=[dma, dma((count - 1,)), dma((count - 1,))],
        cost_estimate=busy(15),
        compiler_params=pltpu.CompilerParams(collective_id=cid, has_side_effects=True),
    )(x)


def scatter_small(x, n_dp, n_z, cid):
    count, rows, cols = x.shape

    def kernel(x_ref, o_ref, lsem, ssem, rsem):
        flat = lax.axis_index("dp") * n_z + lax.axis_index("fsdp")
        bar = pltpu.get_barrier_semaphore()

        def device(o):
            other = lax.rem(flat + o, count)
            return (other // n_z, lax.rem(other, n_z))

        def copy(o):
            return pltpu.make_async_remote_copy(
                x_ref.at[lax.rem(flat + o, count)], o_ref.at[flat], ssem.at[o - 1], rsem.at[o - 1], device_id=device(o), device_id_type=MESH
            )

        def greet(o, _):
            pl.semaphore_signal(bar, inc=1, device_id=device(o), device_id_type=MESH)
            return 0

        def send(o, _):
            copy(o).start()
            return 0

        def wait(o, _):
            copy(o).wait()
            return 0

        lax.fori_loop(1, count, greet, 0)
        local = pltpu.make_async_copy(x_ref.at[flat], o_ref.at[flat], lsem)
        local.start()
        pl.semaphore_wait(bar, count - 1)
        lax.fori_loop(1, count, send, 0)
        lax.fori_loop(1, count, wait, 0)
        local.wait()

    dma = pltpu.SemaphoreType.DMA
    return pl.pallas_call(
        kernel,
        out_shape=jax.ShapeDtypeStruct((count, rows, cols), x.dtype),
        in_specs=[pl.BlockSpec(memory_space=pl.ANY)],
        out_specs=pl.BlockSpec(memory_space=pl.ANY),
        scratch_shapes=[dma, dma((count - 1,)), dma((count - 1,))],
        cost_estimate=busy(15),
        compiler_params=pltpu.CompilerParams(collective_id=cid, has_side_effects=True),
    )(x)


def pack(parts, unit):
    flat = jnp.concatenate([part.reshape(-1) for part in parts])
    size = flat.shape[0]
    full = -(-size // (128 * unit)) * 128 * unit
    return jnp.pad(flat, (0, full - size)).reshape(-1, 128)


def dot(a, b, dims=NN, out=F32):
    return lax.dot_general(a, b, dims, preferred_element_type=F32).astype(out)


def local(
    n_dp,
    n_z,
    tokens,
    cotangent,
    group_ids,
    norm_first,
    input_weight,
    decay_weight,
    conv_weight,
    decay_scale,
    decay_bias,
    output_gain,
    output_weight,
    norm_second,
    upgate_weight,
    down_weight,
):
    count = n_dp * n_z
    rows, width = tokens.shape
    all_heads = decay_scale.shape[0]
    heads = all_heads // n_dp
    taps = conv_weight.shape[0]
    own_conv = conv_weight.shape[1]
    own_d = norm_first.shape[0]
    units = upgate_weight.shape[1] // (2 * n_dp)
    key, value = heads * DK, heads * DV
    cols = 2 * key + 2 * value
    square = n_dp == 8 and n_z == 4
    here = lax.axis_index("dp")
    flat = here * n_z + lax.axis_index("fsdp")

    def spread(x, cid):
        if square:
            return ag_square(x, cid).reshape(n_dp * rows, width)
        return lax.all_gather(x, "dp", axis=0, tiled=True)

    def total(x, cid):
        if square:
            return rs_square(x.reshape(n_dp, rows, width), cid)
        return lax.psum_scatter(x, "dp", scatter_dimension=0, tiled=True).astype(F32)

    def by_dp(a, parts):
        return a.reshape(a.shape[0], n_dp, parts)

    main = units // 128 * 128
    bounds = (0, key, 2 * key, 2 * key + value, 2 * key + 2 * value)
    gates = by_dp(upgate_weight[:, : n_dp * units], units)
    ups = by_dp(upgate_weight[:, n_dp * units :], units)
    up_mine = jnp.concatenate(
        [gates[:, :, :main], ups[:, :, :main], gates[:, :, main:], ups[:, :, main:]], axis=2
    ).transpose(1, 0, 2)
    def whole_rows(a):
        a = lax.all_gather(a[:, None], "fsdp", axis=1, tiled=True)
        return a.reshape(width, a.shape[-1])

    conv_size = taps * own_conv
    inputs = tokens.astype(F32)
    first_root = lax.rsqrt(jnp.mean(inputs * inputs, axis=-1, keepdims=True) + EPSILON)
    if square:
        small = jnp.concatenate(
            [norm_first] * (128 // own_d)
            + [norm_second] * (128 // own_d)
            + [jnp.broadcast_to(group_ids.astype(BF16), (128,)), jnp.zeros((640,), BF16), conv_weight.reshape(-1)]
            + [decay_weight.reshape(-1)]
        ).reshape(32, 128)
        in_full, up_plane, normed_all, cot_all, small = begin(
            input_weight, up_mine, tokens, cotangent, small, bounds, n_z, 1
        )
        in_full = in_full.reshape(width, cols)
        normed_all = normed_all.reshape(n_dp * rows, width)
        cot_all = cot_all.reshape(n_dp * rows, width)
        conv_full = small[:, 8:16].reshape(count, taps, own_conv)
        decay_full = small[:, 16:].reshape(width, 2 * all_heads)
        first_full = small[:, 0, :own_d]
        second_full = small[:, 1, :own_d]
        every_id = small[:, 2, 0]
        output_weight, down_weight, up_plane = lax.optimization_barrier(
            (output_weight, down_weight, up_plane, small)
        )[:3]
    else:
        in_mine = [
            by_dp(input_weight[:, n_dp * a : n_dp * b], b - a).transpose(1, 0, 2)
            for a, b in zip(bounds[:-1], bounds[1:])
        ]
        in_mine = jnp.concatenate(in_mine, axis=2)
        decay_full = lax.all_gather(decay_weight, ("dp", "fsdp"), axis=0, tiled=True)
        in_full = whole_rows(lax.all_to_all(in_mine, "dp", 0, 0, tiled=True))
        up_plane = lax.all_to_all(up_mine, "dp", 0, 0, tiled=True)
        small = gather_small(
            pack((conv_weight, norm_first, norm_second, group_ids.astype(BF16)), 16), n_dp, n_z, 1
        ).reshape(count, -1)
        conv_full = small[:, :conv_size].reshape(count, taps, own_conv)
        first_full = small[:, conv_size : conv_size + own_d]
        second_full = small[:, conv_size + own_d : conv_size + 2 * own_d]
        every_id = small[:, conv_size + 2 * own_d]
    out_full = lax.all_gather(output_weight, "fsdp", axis=0, tiled=True)
    up_full = whole_rows(up_plane)
    down_full = lax.all_gather(down_weight, "fsdp", axis=0, tiled=True)
    conv_full = conv_full.transpose(1, 0, 2).reshape(taps, -1)
    first_full = first_full.reshape(1, width).astype(F32)
    second_full = second_full.reshape(1, width).astype(F32)
    every_id = every_id.astype(jnp.int32)
    scales = 1.0 / jnp.sum((every_id[:, None] == every_id[None, :]).astype(F32), axis=0).reshape(n_dp, n_z)
    scales = lax.dynamic_index_in_dim(scales, lax.axis_index("fsdp"), axis=1, keepdims=False)
    seed = cotangent.astype(F32) * lax.dynamic_index_in_dim(scales, here, axis=0, keepdims=False)
    lanes_of_scales = jnp.broadcast_to(scales[:, None], (n_dp, 128))
    scales = jnp.broadcast_to(scales[:, None, None], (n_dp, rows, 1)).reshape(n_dp * rows, 1)
    if not square:
        normed_all = spread((inputs * first_root * first_full).astype(BF16), 2)
        cot_all = spread(cotangent, 3)

    def conv_columns(start, size):
        return lax.dynamic_slice_in_dim(conv_full, start + here * size, size, axis=1)

    conv_mine = jnp.concatenate(
        [conv_columns(0, key), conv_columns(n_dp * key, key), conv_columns(2 * n_dp * key, value)], axis=1
    ).astype(F32)
    decay_mine = jnp.pad(
        jnp.stack(
            [
                lax.dynamic_slice_in_dim(decay_scale, here * heads, heads),
                lax.dynamic_slice_in_dim(decay_bias, here * heads, heads),
            ]
        ),
        ((0, 0), (0, 128 - heads)),
    )
    gain = output_gain[None, :]

    raw_weight = jnp.pad(
        jnp.concatenate(
            [lax.dynamic_slice_in_dim(decay_full, i * all_heads + here * heads, heads, axis=1) for i in range(2)], axis=1
        ),
        ((0, 0), (0, 128 - 2 * heads)),
    )
    projected = dot(normed_all, in_full)
    raw = dot(normed_all, raw_weight)
    mixed, inverse, solved, core, before_silu = mixer_forward(projected, raw, conv_mine, decay_mine, gain, heads, rows)
    if square:
        middle, second_all = relay(
            mixed.reshape(n_dp, rows, value), out_full, None, NN, NN, second_full, (tokens,), False, 4
        )
        upgate, hidden, hidden_seed = units_forward(second_all, up_full, lanes_of_scales, units, main)
        second_all = second_all.reshape(n_dp * rows, width)
    else:
        middle = inputs + total(dot(mixed, out_full, out=BF16), 4)
        second_root = lax.rsqrt(jnp.mean(middle * middle, axis=-1, keepdims=True) + EPSILON)
        second_all = spread((middle * second_root * second_full).astype(BF16), 5)
        upgate = dot(second_all, up_full)

        def halves_of(a):
            return (a[:, :main], a[:, main : 2 * main]), (a[:, 2 * main : main + units], a[:, main + units :])

        acts = [(g, u, jax.nn.sigmoid(g)) for g, u in halves_of(upgate)]
        hidden = jnp.concatenate([g * s * u for g, u, s in acts], axis=1)
        hidden_seed = (hidden * scales).astype(BF16)
        hidden = hidden.astype(BF16)

    down_grad = dot(hidden_seed, cot_all, TN, out=BF16)
    down_grad, cot_all = lax.optimization_barrier((down_grad, cot_all))
    if square:
        upgate_low = units_backward(
            cot_all.reshape(n_dp, rows, width), down_full, upgate, lanes_of_scales, units, main
        )
    else:
        hidden_grad = dot(cot_all, down_full, NT) * scales
        parts = list(zip(acts, (hidden_grad[:, :main], hidden_grad[:, main:])))
        upgate_low = jnp.concatenate(
            [x for (g, u, s), grad in parts for x in (grad * u * s * (1.0 + g * (1.0 - s)), grad * g * s)], axis=1
        ).astype(BF16)
    upgate_grad = dot(second_all, upgate_low, TN, out=BF16)
    upgate_low, upgate_grad = lax.optimization_barrier((upgate_low, upgate_grad))

    def norm_back(v, root, gain_row, grad):
        hat = v * root
        scaled = grad * gain_row
        gain_grad = jnp.sum(grad * hat, axis=0)
        return root * (scaled - hat * jnp.mean(scaled * hat, axis=-1, keepdims=True)), gain_grad

    def owned_rows(a):
        return lax.psum_scatter(a, "fsdp", scatter_dimension=0, tiled=True)

    def owned_parts(a):
        return lax.psum_scatter(a, "fsdp", scatter_dimension=0, tiled=True)

    def by_plane(a):
        return a.reshape(n_dp, n_z, own_d, a.shape[-1]).transpose(1, 0, 2, 3).reshape(width, -1)

    down_total = owned_rows(down_grad)
    block_part = dot(hidden, down_full, out=BF16)
    upgate_low, upgate_grad, down_total, block_part, seed = lax.optimization_barrier(
        (upgate_low, by_plane(upgate_grad), down_total, block_part, seed)
    )
    upgate_sum = owned_parts(upgate_grad)
    if square:
        middle_grad, middle_all, mixed_grad, second_grad = relay(
            upgate_low.reshape(n_dp, rows, 2 * units), up_full, out_full, NT, NT, second_full, (middle, seed), True, 6
        )
        middle_all = middle_all.reshape(n_dp * rows, width)
        mixed_grad = mixed_grad.reshape(n_dp * rows, value)
    else:
        normed_two_grad = total(dot(upgate_low, up_full, NT, out=BF16), 6)
        middle_part, second_grad = norm_back(middle, second_root, second_full, normed_two_grad)
        middle_grad = seed + middle_part
        middle_all = spread(middle_grad.astype(BF16), 8)
        mixed_grad = dot(middle_all, out_full, NT)
    output_grad = dot(mixed, middle_all, TN, out=BF16)
    mixed_grad, output_grad, upgate_sum = lax.optimization_barrier((mixed_grad, output_grad, upgate_sum))
    output_total = owned_rows(output_grad)
    projected_low, conv_grad, gain_grad, decay_grad = mixer_backward(
        projected, raw, conv_mine, decay_mine, gain, inverse, solved, core, before_silu, mixed_grad, heads, rows
    )
    projected_low, output_total = lax.optimization_barrier((projected_low, output_total))
    def upgate_rows(a):
        return jnp.concatenate(
            [
                jnp.concatenate([x, y], axis=2).transpose(1, 0, 2).reshape(own_d, -1)
                for x, y in (
                    (a[:, :, :main], a[:, :, 2 * main : main + units]),
                    (a[:, :, main : 2 * main], a[:, :, main + units :]),
                )
            ],
            axis=1,
        ).astype(F32)

    in_grad = dot(normed_all, projected_low, TN, out=BF16)
    raw_grad = in_grad[:, cols : cols + 2 * heads].astype(F32)
    down_total = down_total.astype(F32)
    output_total = output_total.astype(F32)
    if square:
        lines = jnp.concatenate(
            [
                jnp.zeros((1, width), F32),
                second_grad.reshape(1, width),
                jnp.tile(gain_grad[:, :128], (1, width // 128)),
                jnp.tile(gain_grad[:, 128:], (1, width // 128)),
                jnp.tile(jnp.pad(decay_grad[:, :heads].reshape(1, -1), ((0, 0), (0, 128 - 2 * heads))), (1, width // 128)),
                jnp.zeros((3, width), F32),
            ],
            axis=0,
        )
        conv_lines = jnp.zeros((8, n_dp * (2 * key + value)), F32)
        for at, a, b in (
            (here * key, 0, key),
            (n_dp * key + here * key, key, 2 * key),
            (2 * n_dp * key + here * value, 2 * key, 2 * key + value),
        ):
            conv_lines = lax.dynamic_update_slice(conv_lines, conv_grad[:, a:b], (0, at))
        conv_lines = lax.dynamic_update_slice(conv_lines, raw_grad.reshape(1, -1), (taps, 0))
        result, tokens_grad, input_total, up_total, summed, planes, conv_total, raw_planes = conclude(
            in_grad.reshape(n_dp, n_z, own_d, cols + 128),
            projected_low.reshape(n_dp, rows, cols + 128),
            in_full,
            raw_weight,
            block_part.reshape(n_dp, rows, width),
            upgate_sum.reshape(n_dp, own_d, 2 * units),
            tokens,
            middle,
            middle_grad,
            first_full,
            lines,
            conv_lines,
            bounds,
            9,
        )
        input_total = input_total.astype(F32)
        decay_total = raw_planes.reshape(n_dp, own_d, 2, heads).transpose(1, 2, 0, 3).reshape(own_d, 2 * all_heads)
        upgate_total = upgate_rows(up_total)
        per = 128 // own_d
        place = lax.rem(flat, per) * own_d
        first_total = lax.dynamic_slice_in_dim(summed[0], place, own_d)
        second_total = lax.dynamic_slice_in_dim(summed[1], place, own_d)
        gain_total = summed[2:4].reshape(-1)
        scale_total = planes[:, :heads].reshape(-1)
        bias_total = planes[:, heads : 2 * heads].reshape(-1)
        conv_total = conv_total[:taps]
    else:
        projected_low, in_grad = lax.optimization_barrier((projected_low, in_grad))
        back_one = (
            dot(projected_low[:, :cols], in_full, NT) + dot(projected_low[:, cols:], raw_weight, NT)
        ).astype(BF16)
        in_sum = owned_parts(by_plane(in_grad[:, :cols]))
        normed_one_grad = total(back_one, 9)
        result = middle + total(block_part, 7)
        input_part, first_grad = norm_back(inputs, first_root, first_full, normed_one_grad)
        tokens_grad = middle_grad + input_part

        up_total = lax.all_to_all(upgate_sum.reshape(n_dp, own_d, -1), "dp", 0, 0, tiled=True)
        upgate_total = upgate_rows(up_total)
        in_total = lax.all_to_all(in_sum.reshape(n_dp, own_d, -1), "dp", 0, 0, tiled=True)
        raw_rows = jnp.zeros((width, 2, all_heads), F32)
        raw_rows = lax.dynamic_update_slice(raw_rows, raw_grad.reshape(width, 2, heads), (0, 0, here * heads))
        decay_total = lax.psum_scatter(raw_rows.reshape(width, -1), ("dp", "fsdp"), scatter_dimension=0, tiled=True)
        in_total = in_total.transpose(1, 0, 2).astype(F32)
        input_total = jnp.concatenate(
            [in_total[:, :, a:b].reshape(own_d, -1) for a, b in zip(bounds[:-1], bounds[1:])], axis=1
        )

        share = key // own_conv, value // own_conv
        owner = jnp.concatenate(
            [
                here * share[0] + jnp.arange(share[0]),
                (n_dp + here) * share[0] + jnp.arange(share[0]),
                2 * n_dp * share[0] + here * share[1] + jnp.arange(share[1]),
            ]
        )
        blocks = conv_grad.reshape(taps, -1, own_conv).transpose(1, 0, 2).reshape(-1, taps * own_conv)
        for_owner = owner[None, :] == jnp.arange(count)[:, None]
        everyone = jnp.concatenate([gain_grad.reshape(-1), decay_grad[:, :heads].reshape(-1)])
        packets = jnp.concatenate(
            [
                first_grad.reshape(count, own_d),
                second_grad.reshape(count, own_d),
                jnp.sum(jnp.where(for_owner[:, :, None], blocks[None], 0.0), axis=1),
                jnp.broadcast_to(everyone[None], (count, everyone.size)),
            ],
            axis=1,
        )
        size = packets.shape[1]
        lines = -(-size // 1024) * 8
        packets = jnp.pad(packets, ((0, 0), (0, lines * 128 - size))).reshape(count, lines, 128)
        shared = scatter_small(packets, n_dp, n_z, 10).reshape(count, -1)
        summed = jnp.sum(shared, axis=0)
        first_total = summed[:own_d]
        second_total = summed[own_d : 2 * own_d]
        start = 2 * own_d + taps * own_conv
        conv_total = summed[2 * own_d : start].reshape(taps, own_conv)
        gain_total = summed[start : start + gain_grad.size]
        start += gain_grad.size
        scale_bias = jnp.sum(shared[:, start : start + 2 * heads].reshape(n_dp, n_z, 2, heads), axis=1)
        scale_total = scale_bias[:, 0].reshape(-1)
        bias_total = scale_bias[:, 1].reshape(-1)
    return (
        result,
        tokens_grad,
        first_total,
        input_total,
        decay_total,
        conv_total,
        scale_total,
        bias_total,
        gain_total,
        output_total,
        second_total,
        upgate_total,
        down_total,
    )


def solution(mesh):
    both = ("dp", "fsdp")
    rows, vector = P(both, None), P(both)
    return jax.shard_map(
        functools.partial(local, mesh.shape["dp"], mesh.shape["fsdp"]),
        mesh=mesh,
        in_specs=(
            rows, rows, vector, vector, rows, rows, P(None, both), P(), P(), P(), rows, vector, rows, rows,
        ),
        out_specs=(
            rows, rows, vector, rows, rows, P(None, both), P(), P(), P(), rows, vector, rows, rows,
        ),
        check_vma=False,
    )
```

```python
import functools

import jax
import jax.numpy as jnp
from jax import lax
from jax.experimental import pallas as pl
from jax.experimental.pallas import tpu as pltpu
from jax.sharding import PartitionSpec as P

MESH = pl.DeviceIdType.MESH
F32 = jnp.float32
BF16 = jnp.bfloat16
EPSILON = 1e-06
DK = 128
DV = 256
BASE = 8
NN = (((1,), (0,)), ((), ()))
NT = (((1,), (1,)), ((), ()))
TN = (((0,), (0,)), ((), ()))


def dot1(a, b, dims=NN):
    return lax.dot_general(a.astype(BF16), b.astype(BF16), dims, preferred_element_type=F32)


def halves(a):
    if a.dtype == BF16:
        return (a,)
    high = a.astype(BF16)
    return (high, (a - high.astype(F32)).astype(BF16))


def dot3(a, b, dims=NN):
    a, b = halves(a), halves(b)
    total = lax.dot_general(a[0], b[0], dims, preferred_element_type=F32)
    if len(a) > 1:
        total = total + lax.dot_general(a[1], b[0], dims, preferred_element_type=F32)
    if len(b) > 1:
        total = total + lax.dot_general(a[0], b[1], dims, preferred_element_type=F32)
    return total


def sum_rows(mask, b):
    mask = jnp.where(mask, 1.0, 0.0).astype(BF16)
    high = b.astype(BF16)
    rest = b - high.astype(F32)
    middle = rest.astype(BF16)
    low = (rest - middle.astype(F32)).astype(BF16)
    return dot1(mask, high) + (dot1(mask, middle) + dot1(mask, low))


def shift_down(v, n):
    turned = pltpu.roll(v, n, 0)
    places = lax.broadcasted_iota(jnp.int32, (8, 1), 0)
    return jnp.concatenate([jnp.where(places >= n, turned[:8], 0.0), turned[8:]], axis=0)


def shift_up(v, n):
    length = v.shape[0]
    turned = pltpu.roll(v, length - n, 0)
    places = lax.broadcasted_iota(jnp.int32, (8, 1), 0)
    return jnp.concatenate([turned[:-8], jnp.where(places < 8 - n, turned[-8:], 0.0)], axis=0)


def conv(c, taps):
    count = taps.shape[0]
    total = c * taps[count - 1 : count]
    for j in range(count - 1):
        total = total + shift_down(c, count - 1 - j) * taps[j : j + 1]
    return total


def sigmoid(v):
    return 1.0 / (1.0 + jnp.exp(-v))


def gate_of(v):
    return 0.5 * jnp.tanh(0.5 * v) + 0.5


def softplus(v):
    return jnp.maximum(v, 0.0) + jnp.log1p(jnp.exp(-jnp.abs(v)))


def unit_inverses(lowers, row_ids, col_ids):
    length = lowers[0].shape[0]
    size = BASE
    same = row_ids // size == col_ids // size
    pick = jnp.where(col_ids[:, :128] == lax.rem(row_ids[:, :128], size), 1.0, 0.0).astype(BF16)
    lanes = lax.broadcasted_iota(jnp.int32, (length // size, size, 128), 2)
    places = lax.broadcasted_iota(jnp.int32, (length // size, size, 128), 1)
    compact = [dot3(jnp.where(same, lower, 0.0), pick).reshape(length // size, size, 128) for lower in lowers]
    solved = [jnp.where(lanes == places, 1.0, 0.0) for _ in lowers]
    for j in range(size - 1):
        solved = [x - a[:, :, j : j + 1] * x[:, j : j + 1, :] for a, x in zip(compact, solved)]
    inverses = [jnp.where(same, dot3(x.reshape(length, 128), pick, NT), 0.0) for x in solved]
    while size < length:
        wide = 2 * size
        off = (row_ids // wide == col_ids // wide) & (row_ids // size != col_ids // size)
        inner = [dot3(jnp.where(off, lower, 0.0), inverse) for lower, inverse in zip(lowers, inverses)]
        inverses = [inverse - dot3(inverse, x) for inverse, x in zip(inverses, inner)]
        size = wide
    return inverses


def common(raw, decay, heads, length):
    rows = lax.broadcasted_iota(jnp.int32, (length, 1), 0)
    row_ids = lax.broadcasted_iota(jnp.int32, (length, length), 0)
    col_ids = lax.broadcasted_iota(jnp.int32, (length, length), 1)
    lanes = lax.broadcasted_iota(jnp.int32, raw.shape, 1)
    shifted = raw + decay[1:2]
    rate = jnp.where(lanes < heads, -jnp.exp(decay[0:1]) * softplus(shifted), 0.0)
    beta = sigmoid(raw)
    cumulated = sum_rows(row_ids >= col_ids, rate)
    return rows, row_ids, col_ids, lanes, shifted, rate, beta, cumulated, cumulated.T


def head_parts(h, heads):
    key = slice(h * DK, (h + 1) * DK)
    keyk = slice((heads + h) * DK, (heads + h + 1) * DK)
    val = slice(heads * DV + h * DV, heads * DV + (h + 1) * DV)
    gat = slice(2 * heads * DV + h * DV, 2 * heads * DV + (h + 1) * DV)
    return key, keyk, val, gat


def mixer_forward_kernel(heads, proj_ref, raw_ref, taps_ref, decay_ref, gain_ref, mixed_ref, inv_ref, solved_ref, core_ref, conv_ref):
    length = proj_ref.shape[0]
    decay = decay_ref[...]
    gain = gain_ref[...]
    raw = raw_ref[...]
    rows, row_ids, col_ids, lanes, shifted, rate, beta, cumulated, cum_t = common(raw, decay, heads, length)
    def active(cols):
        y = conv(proj_ref[:, cols], taps_ref[:, cols])
        conv_ref[:, cols] = y
        return y * gate_of(y)

    parts = [head_parts(h, heads) for h in range(heads)]
    queries, keys, values, growths, betas, lowers = [], [], [], [], [], []
    for h, (qs, ks, vs, gs) in enumerate(parts):
        k = active(ks)
        k = (k * lax.rsqrt(jnp.sum(k * k, axis=-1, keepdims=True) + EPSILON)).astype(BF16)
        beta_h = beta[:, heads + h : heads + h + 1]
        gap = cumulated[:, h : h + 1] - cum_t[h : h + 1, :]
        growth = jnp.where(row_ids >= col_ids, jnp.exp(jnp.where(row_ids >= col_ids, gap, 0.0)), 0.0)
        keys.append(k)
        growths.append(growth)
        betas.append(beta_h)
        lowers.append(jnp.where(row_ids > col_ids, growth * dot1(k, k, NT) * beta_h, 0.0))
    inverses = unit_inverses(lowers, row_ids, col_ids)
    for h, (qs, ks, vs, gs) in enumerate(parts):
        q = active(qs)
        q = (q * lax.rsqrt(jnp.sum(q * q, axis=-1, keepdims=True) + EPSILON) * DK ** (-0.5)).astype(BF16)
        v = active(vs).astype(BF16)
        inv_ref[h] = inverses[h]
        solved = dot3(inverses[h], betas[h] * v.astype(F32))
        core = dot3(growths[h] * dot1(q, keys[h], NT), solved)
        solved_ref[:, h * DV : (h + 1) * DV] = solved
        core_ref[:, h * DV : (h + 1) * DV] = core
        gate = proj_ref[:, gs]
        normed = core * lax.rsqrt(jnp.mean(core * core, axis=-1, keepdims=True) + EPSILON) * gain
        mixed_ref[:, h * DV : (h + 1) * DV] = (normed * (gate * gate_of(gate))).astype(BF16)


def mixer_forward(proj, raw, taps, decay, gain, heads, length):
    tokens, width = proj.shape
    seqs = tokens // length
    hv = heads * DV
    row = lambda cols: pl.BlockSpec((length, cols), lambda s: (s, 0))
    whole = lambda a: pl.BlockSpec(a.shape, lambda s: (0,) * a.ndim)
    return pl.pallas_call(
        functools.partial(mixer_forward_kernel, heads),
        grid=(seqs,),
        in_specs=[row(width), row(128), whole(taps), whole(decay), whole(gain)],
        out_specs=[row(hv), pl.BlockSpec((None, heads, length, length), lambda s: (s, 0, 0, 0)), row(hv), row(hv), row(taps.shape[1])],
        out_shape=[
            jax.ShapeDtypeStruct((tokens, hv), BF16),
            jax.ShapeDtypeStruct((seqs, heads, length, length), F32),
            jax.ShapeDtypeStruct((tokens, hv), F32),
            jax.ShapeDtypeStruct((tokens, hv), F32),
            jax.ShapeDtypeStruct((tokens, taps.shape[1]), F32),
        ],
        cost_estimate=busy(55), compiler_params=pltpu.CompilerParams(vmem_limit_bytes=48 << 20),
    )(proj, raw, taps, decay, gain)


def mixer_backward_kernel(
    heads, proj_ref, raw_ref, taps_ref, decay_ref, gain_ref, inv_ref, solved_ref, core_ref, pre_ref, grad_ref,
    low_ref, conv_ref, gain_grad_ref, decay_grad_ref,
):
    length = proj_ref.shape[0]
    count = taps_ref.shape[0]
    decay = decay_ref[...]
    gain = gain_ref[...]
    raw = raw_ref[...]
    rows, row_ids, col_ids, lanes, shifted, rate, beta, cumulated, cum_t = common(raw, decay, heads, length)
    within = row_ids >= col_ids
    strict = row_ids > col_ids

    @pl.when(pl.program_id(0) == 0)
    def _():
        conv_ref[...] = jnp.zeros_like(conv_ref)
        gain_grad_ref[...] = jnp.zeros_like(gain_grad_ref)
        decay_grad_ref[...] = jnp.zeros_like(decay_grad_ref)

    cum_grad = jnp.zeros(raw.shape, F32)
    beta_grad = jnp.zeros(raw.shape, F32)
    for h in range(heads):
        qs, ks, vs, gs = head_parts(h, heads)
        hs = slice(h * DV, (h + 1) * DV)

        def active(cols):
            y = pre_ref[:, cols]
            s = gate_of(y)
            return y * s, s * (1.0 + y * (1.0 - s))

        def conv_back(cols, grad):
            c = proj_ref[:, cols]
            total = grad * taps_ref[count - 1 : count, cols]
            conv_ref[count - 1 : count, cols] += jnp.sum(grad * c, axis=0, keepdims=True)
            for j in range(count - 1):
                n = count - 1 - j
                later = shift_up(grad, n)
                total = total + later * taps_ref[j : j + 1, cols]
                conv_ref[j : j + 1, cols] += jnp.sum(later * c, axis=0, keepdims=True)
            low_ref[:, cols] = total.astype(BF16)

        core = core_ref[:, hs]
        gate = proj_ref[:, gs]
        gate_sig = gate_of(gate)
        grad = grad_ref[:, hs]
        root = lax.rsqrt(jnp.mean(core * core, axis=-1, keepdims=True) + EPSILON)
        normed = core * root
        silu_gate = gate * gate_sig
        gain_grad_ref[...] += jnp.sum(grad * normed * silu_gate, axis=0, keepdims=True)
        low_ref[:, gs] = (grad * normed * gain * gate_sig * (1.0 + gate * (1.0 - gate_sig))).astype(BF16)
        normed_grad = grad * gain * silu_gate
        core_grad = root * (normed_grad - normed * jnp.mean(normed_grad * normed, axis=-1, keepdims=True))

        q_act, q_slope = active(qs)
        q_root = lax.rsqrt(jnp.sum(q_act * q_act, axis=-1, keepdims=True) + EPSILON)
        q_unit = q_act * q_root
        q = (q_unit * DK ** (-0.5)).astype(BF16)
        k_act, k_slope = active(ks)
        k_root = lax.rsqrt(jnp.sum(k_act * k_act, axis=-1, keepdims=True) + EPSILON)
        k_unit = k_act * k_root
        k = k_unit.astype(BF16)
        v_act, v_slope = active(vs)
        v = v_act.astype(BF16).astype(F32)
        beta_h = beta[:, heads + h : heads + h + 1]
        gap = cumulated[:, h : h + 1] - cum_t[h : h + 1, :]
        growth = jnp.where(within, jnp.exp(jnp.where(within, gap, 0.0)), 0.0)
        decayed_gram = jnp.where(strict, growth * dot1(k, k, NT), 0.0)
        weights = growth * dot1(q, k, NT)
        inverse = inv_ref[h]
        solved = solved_ref[:, hs]
        core_low = core_grad.astype(BF16)
        solved_grad = dot3(weights, core_low, TN)
        weights_grad = dot3(core_low, solved, NT)
        value_grad = dot3(inverse, solved_grad.astype(BF16), TN)
        lower_grad = jnp.where(strict, -dot3(value_grad.astype(BF16), solved, NT), 0.0)
        gap_part = lower_grad * decayed_gram
        beta_col = jnp.sum(gap_part, axis=-1, keepdims=True) + jnp.sum(value_grad * v, axis=-1, keepdims=True)
        gap_grad = gap_part * beta_h + weights_grad * weights
        cum_col = jnp.sum(gap_grad, axis=-1, keepdims=True)
        cum_row = jnp.sum(gap_grad, axis=0, keepdims=True)
        cum_col = cum_col - jnp.broadcast_to(cum_row, (8, length)).T[:, 0:1]
        gram_grad = lower_grad * growth * beta_h
        score_grad = weights_grad * growth
        k_grad = dot3(gram_grad, k) + dot3(gram_grad, k, TN) + dot3(score_grad, q, TN)
        q_grad = dot3(score_grad, k)
        cum_grad = jnp.where(lanes == h, cum_col, cum_grad)
        beta_grad = jnp.where(lanes == heads + h, beta_col, beta_grad)

        q_grad = q_grad * DK ** (-0.5)
        q_grad = q_root * (q_grad - q_unit * jnp.sum(q_grad * q_unit, axis=-1, keepdims=True))
        conv_back(qs, q_grad * q_slope)
        k_grad = k_root * (k_grad - k_unit * jnp.sum(k_grad * k_unit, axis=-1, keepdims=True))
        conv_back(ks, k_grad * k_slope)
        conv_back(vs, value_grad * beta_h * v_slope)

    rate_grad = sum_rows(col_ids >= row_ids, cum_grad)
    bias_part = rate_grad * -jnp.exp(decay[0:1]) * sigmoid(shifted)
    raw_grad = jnp.where(lanes < heads, bias_part, beta_grad * beta * (1.0 - beta))
    low_ref[:, heads * 768 :] = raw_grad.astype(BF16)
    decay_grad_ref[0:1] += jnp.sum(jnp.where(lanes < heads, rate_grad * rate, 0.0), axis=0, keepdims=True)
    decay_grad_ref[1:2] += jnp.sum(jnp.where(lanes < heads, bias_part, 0.0), axis=0, keepdims=True)


def mixer_backward(proj, raw, taps, decay, gain, inverse, solved, core, pre, grad, heads, length):
    tokens, width = proj.shape
    seqs = tokens // length
    hv = heads * DV
    row = lambda cols: pl.BlockSpec((length, cols), lambda s: (s, 0))
    whole = lambda a: pl.BlockSpec(a.shape, lambda s: (0,) * a.ndim)
    return pl.pallas_call(
        functools.partial(mixer_backward_kernel, heads),
        grid=(seqs,),
        in_specs=[row(width), row(128), whole(taps), whole(decay), whole(gain),
                  pl.BlockSpec((None, heads, length, length), lambda s: (s, 0, 0, 0)), row(hv), row(hv), row(taps.shape[1]), row(hv)],
        out_specs=[row(width + 128), whole(taps), whole(gain), whole(decay)],
        out_shape=[
            jax.ShapeDtypeStruct((tokens, width + 128), BF16),
            jax.ShapeDtypeStruct(taps.shape, F32),
            jax.ShapeDtypeStruct(gain.shape, F32),
            jax.ShapeDtypeStruct(decay.shape, F32),
        ],
        cost_estimate=busy(50), compiler_params=pltpu.CompilerParams(vmem_limit_bytes=56 << 20),
    )(proj, raw, taps, decay, gain, inverse, solved, core, pre, grad)


def busy(us):
    return pl.CostEstimate(flops=us * 1_000_000_000, bytes_accessed=0, transcendentals=0)


def _place(n_dp):
    me = lax.axis_index("dp")
    z = lax.axis_index("fsdp")
    core = lax.rem(me, 2)
    chip = me // 2
    return me, z, core, lax.rem(chip, 2), chip // 2

def ag_square(x, cid, chunks=4):
    rows, cols = x.shape
    r = rows // chunks
    def kernel(x_ref, o_ref, lsem, ssem, rsem, dssem, drsem, fs, fr):
        me, z, core, cx, cy = _place(8)
        dev = lambda dx, dy, c: 2*(2*lax.rem(cy+dy,2)+lax.rem(cx+dx,2))+c
        nx, ny, nd = dev(1,0,core), dev(0,1,core), dev(1,1,core)
        src = dev(1-core, core, core)
        tgt = dev(core, 1-core, core)
        sib = dev(0,0,1-core)
        bar = pltpu.get_barrier_semaphore()
        for d in (sib,nx,ny):
            pl.semaphore_signal(bar, inc=1, device_id=(d,z), device_id_type=MESH)
        pl.semaphore_wait(bar, 3)
        lc = pltpu.make_async_copy(x_ref, o_ref.at[me], lsem); lc.start()
        def rc(a, b, s, q, d):
            return pltpu.make_async_remote_copy(a, b, s, q, device_id=(d,z), device_id_type=MESH)
        own = []
        for c in range(chunks):
            sl = pl.ds(c*r, r)
            for i, d in ((0,nx),(1,ny)):
                cp = rc(x_ref.at[sl], o_ref.at[me,sl], ssem.at[i,c], rsem.at[i,c], d); cp.start(); own.append(cp)
        sibs=[]
        for c in range(chunks):
            sl = pl.ds(c*r, r)
            cp = rc(x_ref.at[sl], o_ref.at[me,sl], fs.at[0,c], fr.at[0,c], sib); cp.start(); sibs.append(cp)
        other = dev(core, 1-core, core)
        for c in range(chunks):
            sl = pl.ds(c*r, r)
            rc(x_ref.at[sl], o_ref.at[src,sl], ssem.at[core,c], rsem.at[core,c], sib).wait_recv()
            cp = rc(o_ref.at[src,sl], o_ref.at[src,sl], dssem.at[c], drsem.at[c], tgt); cp.start(); sibs.append((cp,))
            cp = rc(o_ref.at[src,sl], o_ref.at[src,sl], fs.at[1,c], fr.at[1,c], sib); cp.start(); sibs.append(cp)
            rc(x_ref.at[sl], o_ref.at[other,sl], ssem.at[1-core,c], rsem.at[1-core,c], sib).wait_recv()
            cp = rc(o_ref.at[other,sl], o_ref.at[other,sl], fs.at[2,c], fr.at[2,c], sib); cp.start(); sibs.append(cp)
        for c in range(chunks):
            sl = pl.ds(c*r, r)
            rc(x_ref.at[sl], o_ref.at[nd,sl], dssem.at[c], drsem.at[c], sib).wait_recv()
            cp = rc(o_ref.at[nd,sl], o_ref.at[nd,sl], fs.at[3,c], fr.at[3,c], sib); cp.start(); sibs.append(cp)
        for cp in own: cp.wait_send()
        for cp in sibs:
            if isinstance(cp, tuple): cp[0].wait_send()
            else: cp.wait()
        lc.wait()
    D=pltpu.SemaphoreType.DMA
    return pl.pallas_call(kernel, out_shape=jax.ShapeDtypeStruct((8,rows,cols),x.dtype),
        in_specs=[pl.BlockSpec(memory_space=pl.ANY)], out_specs=pl.BlockSpec(memory_space=pl.ANY),
        scratch_shapes=[D, D((2,chunks)), D((2,chunks)), D((chunks,)), D((chunks,)), D((4,chunks)), D((4,chunks))],
        cost_estimate=busy(40), compiler_params=pltpu.CompilerParams(collective_id=cid, has_side_effects=True))(x)

def rs_square(x, cid, chunks=4):
    _, rows, cols = x.shape
    r = rows // chunks
    def kernel(x_ref, o_ref, X, A, B, R, lsem, sa, ra, sb, rb):
        me, z, core, cx, cy = _place(8)
        dev = lambda dx, dy, c: 2*(2*lax.rem(cy+dy,2)+lax.rem(cx+dx,2))+c
        fdx, fdy = 1-core, core
        nf, ng = dev(fdx,fdy,core), dev(fdy,fdx,core)
        sib = dev(0,0,1-core)
        bar = pltpu.get_barrier_semaphore()
        for d in (sib,nf,ng):
            pl.semaphore_signal(bar, inc=1, device_id=(d,z), device_id_type=MESH)
        mine = [dev(1,1,core), ng, nf, me]
        s_f, s_g = dev(core,1-core,1-core), dev(1-core,core,1-core)
        theirs = [dev(1,1,1-core), s_g, s_f, sib]
        loads=[]
        for k in range(4):
            for c in range(chunks):
                sl=pl.ds(c*r,r)
                cp=pltpu.make_async_copy(x_ref.at[mine[k],sl], X.at[k,sl], lsem.at[k,c]); cp.start(); loads.append(cp)
        pl.semaphore_wait(bar, 3)
        def rc(a, b, s, q, d):
            return pltpu.make_async_remote_copy(a, b, s, q, device_id=(d,z), device_id_type=MESH)
        sends=[]; ga={}
        for k in range(4):
            for c in range(chunks):
                sl=pl.ds(c*r,r)
                cp=rc(x_ref.at[theirs[k],sl], A.at[k,sl], sa.at[k,c], ra.at[k,c], sib); cp.start(); sends.append(cp); ga[k,c]=cp
        def pair(k,c):
            sl=pl.ds(c*r,r)
            loads[k*chunks+c].wait(); ga[k,c].wait_recv()
            return X[k,sl].astype(F32)+A[k,sl].astype(F32)
        gb={}
        def ship(slot, c, d):
            sl=pl.ds(c*r,r)
            cp=rc(B.at[slot,sl], R.at[slot,sl], sb.at[slot,c], rb.at[slot,c], d); cp.start(); sends.append(cp); gb[slot,c]=cp
        for c in range(chunks):
            sl=pl.ds(c*r,r)
            B[0,sl]=pair(0,c).astype(BF16); ship(0,c,nf)
        for c in range(chunks):
            sl=pl.ds(c*r,r)
            B[2,sl]=pair(2,c).astype(BF16); ship(2,c,nf)
        for c in range(chunks):
            sl=pl.ds(c*r,r)
            v=pair(1,c)
            gb[0,c].wait_recv()
            B[1,sl]=(v+R[0,sl].astype(F32)).astype(BF16); ship(1,c,ng)
        for c in range(chunks):
            sl=pl.ds(c*r,r)
            v=pair(3,c)
            gb[2,c].wait_recv()
            o_ref[sl]=v+R[2,sl].astype(F32)
        for c in range(chunks):
            sl=pl.ds(c*r,r)
            gb[1,c].wait_recv()
            o_ref[sl]=o_ref[sl]+R[1,sl].astype(F32)
        for cp in sends: cp.wait_send()
    D=pltpu.SemaphoreType.DMA
    V=lambda n: pltpu.VMEM((n,rows,cols),x.dtype)
    return pl.pallas_call(kernel, out_shape=jax.ShapeDtypeStruct((rows,cols),F32),
        in_specs=[pl.BlockSpec(memory_space=pl.ANY)], out_specs=pl.BlockSpec(memory_space=pltpu.VMEM),
        scratch_shapes=[V(4),V(4),V(3),V(3), D((4,chunks)), D((4,chunks)), D((4,chunks)), D((3,chunks)), D((3,chunks))],
        cost_estimate=busy(40), compiler_params=pltpu.CompilerParams(collective_id=cid, has_side_effects=True, vmem_limit_bytes=40<<20))(x)

def begin(weight, ups, tokens, cotangent, small, bounds, n_z, cid):
    own = weight.shape[0]
    cols = bounds[-1]
    units = ups.shape[2]
    rows, width = tokens.shape
    count = 8 * n_z
    chunks = 2
    part = rows // chunks

    def kernel(
        w_ref, u_ref, t_ref, c_ref, small_ref, w_out, u_out, n_out, c_out, small_out,
        toks, lsem, a_send, a_recv, g_send, g_recv, up_send, up_recv, down_send, down_recv,
        small_send, small_recv, x_send, x_recv, d_send, d_recv, f_send, f_recv,
    ):
        me, z, core, cx, cy = _place(8)
        flat = me * n_z + z
        bar = pltpu.get_barrier_semaphore()

        def dev(dx, dy, c):
            return 2 * (2 * lax.rem(cy + dy, 2) + lax.rem(cx + dx, 2)) + c

        sib = dev(0, 0, 1 - core)

        def partner(o):
            return dev(o // 4, lax.rem(o // 2, 2), lax.rem(core + o, 2))

        def remote(src, dst, send, recv, device):
            return pltpu.make_async_remote_copy(src, dst, send, recv, device_id=device, device_id_type=MESH)

        def loop(first, last, body):
            def step(o, _):
                body(o)
                return 0

            lax.fori_loop(first, last, step, 0)

        def sections(q):
            for first, last in zip(bounds[:-1], bounds[1:]):
                size = last - first
                at = pl.multiple_of(8 * first + q * size, 128)
                yield w_ref.at[:, pl.ds(at, size)], w_out.at[me, z, :, pl.ds(first, size)]

        def send_piece(o):
            q = partner(o)
            for src, dst in sections(q):
                remote(src, dst, a_send.at[o - 1], a_recv.at[o - 1], (q, z)).start()

        def landed(o):
            at = w_out.at[partner(o), z]
            return remote(at, at, a_send.at[o - 1], a_recv.at[o - 1], (sib, z))

        def up(t, o):
            at = w_out.at[partner(o), z - t]
            return remote(at, at, up_send.at[t, o], up_recv.at[t, o], (me, z + 1))

        def down(t, o):
            at = w_out.at[partner(o), z + t]
            return remote(at, at, down_send.at[t, o], down_recv.at[t, o], (me, z - 1))

        def pass_on(t, o):
            if t > 0:

                @pl.when(z >= t)
                def _():
                    at = w_out.at[partner(o), z - t]
                    remote(at, at, up_send.at[t - 1, o], up_recv.at[t - 1, o], (sib, z)).wait_recv()

                @pl.when(z + t < n_z)
                def _():
                    at = w_out.at[partner(o), z + t]
                    remote(at, at, down_send.at[t - 1, o], down_recv.at[t - 1, o], (sib, z)).wait_recv()

            if t < n_z - 1:

                @pl.when((z >= t) & (z < n_z - 1))
                def _():
                    up(t, o).start()

                @pl.when((z + t < n_z) & (z > 0))
                def _():
                    down(t, o).start()

        def sent(t, o):
            @pl.when((z >= t) & (z < n_z - 1))
            def _():
                up(t, o).wait_send()

            @pl.when((z + t < n_z) & (z > 0))
            def _():
                down(t, o).wait_send()

        def unit_piece(o):
            q = partner(o)
            return remote(u_ref.at[q], u_out.at[me], g_send.at[o - 1], g_recv.at[o - 1], (q, z))

        def tiny(o):
            to = (me, lax.rem(z + o, n_z))
            return remote(small_ref, small_out.at[flat], small_send.at[o - 1], small_recv.at[o - 1], to)

        def tiny_line(o):
            at, i = small_out.at[pl.ds(me * n_z, n_z)], n_z - 2 + o
            return remote(at, at, small_send.at[i], small_recv.at[i], (partner(o), z))

        near = (dev(1, 0, core), dev(0, 1, core))
        source, other, across = dev(1 - core, core, core), dev(core, 1 - core, core), dev(1, 1, core)

        def gather(i, ref, out):
            def at(q, c):
                return out.at[q, pl.ds(c * part, part)]

            def mine(c):
                return ref.at[pl.ds(c * part, part)]

            def first(k, c):
                return remote(mine(c), at(me, c), x_send.at[i, k, c], x_recv.at[i, k, c], (near[k], z))

            def twin(k, q, c):
                src = mine(c) if k == 0 else at(q, c)
                return remote(src, at(q, c), f_send.at[i, k, c], f_recv.at[i, k, c], (sib, z))

            def second(c):
                return remote(at(source, c), at(source, c), d_send.at[i, c], d_recv.at[i, c], (other, z))

            def keep():
                return pltpu.make_async_copy(ref, out.at[me], lsem.at[i])

            def begin_():
                keep().start()
                for c in range(chunks):
                    for k in range(2):
                        first(k, c).start()
                for c in range(chunks):
                    twin(0, me, c).start()

            def forward():
                for c in range(chunks):
                    remote(mine(c), at(source, c), x_send.at[i, core, c], x_recv.at[i, core, c], (sib, z)).wait_recv()
                    second(c).start()
                    twin(1, source, c).start()
                    remote(
                        mine(c), at(other, c), x_send.at[i, 1 - core, c], x_recv.at[i, 1 - core, c], (sib, z)
                    ).wait_recv()
                    twin(2, other, c).start()

            def last():
                for c in range(chunks):
                    remote(at(across, c), at(across, c), d_send.at[i, c], d_recv.at[i, c], (other, z)).wait_recv()
                    twin(3, across, c).start()

            def finish():
                keep().wait()
                theirs = (sib, dev(core, 1 - core, 1 - core), dev(1 - core, core, 1 - core), dev(1, 1, 1 - core))
                for c in range(chunks):
                    for k in range(4):
                        remote(
                            at(theirs[k], c), at(theirs[k], c), f_send.at[i, k, c], f_recv.at[i, k, c], (sib, z)
                        ).wait_recv()

            def close():
                for c in range(chunks):
                    for k in range(2):
                        first(k, c).wait_send()
                    second(c).wait_send()
                    for k, q in enumerate((me, source, other, across)):
                        twin(k, q, c).wait_send()

            return begin_, forward, last, finish, close

        tok_begin, tok_forward, tok_last, tok_finish, tok_close = gather(0, t_ref, toks)
        cot_begin, cot_forward, cot_last, cot_finish, cot_close = gather(1, c_ref, c_out)

        def greet(device):
            pl.semaphore_signal(bar, inc=1, device_id=device, device_id_type=MESH)

        loop(1, 8, lambda o: greet((partner(o), z)))
        loop(1, n_z, lambda o: greet((me, lax.rem(z + o, n_z))))
        for src, dst in sections(me):
            pltpu.make_async_copy(src, dst, lsem.at[2]).start()
        keep_u = pltpu.make_async_copy(u_ref.at[me], u_out.at[me], lsem.at[3])
        keep_s = pltpu.make_async_copy(small_ref, small_out.at[flat], lsem.at[4])
        keep_u.start()
        keep_s.start()
        pl.semaphore_wait(bar, 7 + n_z - 1)

        loop(1, 8, send_piece)
        pltpu.make_async_copy(w_out.at[me, z], w_out.at[me, z], lsem.at[2]).wait()
        pass_on(0, 0)
        loop(1, n_z, lambda o: tiny(o).start())

        def first_leg(o):
            landed(o).wait_recv()
            pass_on(0, o)

        tok_begin()
        loop(1, 8, first_leg)
        loop(0, 8, lambda o: pass_on(1, o))
        keep_s.wait()
        loop(1, n_z, lambda o: tiny(o).wait_recv())
        loop(1, 8, lambda o: tiny_line(o).start())
        tok_forward()
        cot_begin()
        loop(1, 8, lambda o: unit_piece(o).start())
        loop(0, 4, lambda o: pass_on(2, o))
        tok_last()
        tok_finish()
        loop(1, 8, lambda o: tiny_line(o).wait_recv())

        lanes = lax.broadcasted_iota(jnp.int32, (1, 128), 1)
        per = 128 // own
        blocks = []
        for m in range(width // 128):
            block = small_out[m * per, 0:1, :].astype(F32)
            for i in range(1, per):
                block = jnp.where(lanes >= i * own, small_out[m * per + i, 0:1, :].astype(F32), block)
            blocks.append(block)
        gain = jnp.concatenate(blocks, axis=1)
        step = 32

        def norm_rows(o):
            def some(r, _):
                sl = pl.ds(r * step, step)
                v = toks[o, sl].astype(F32)
                n_out[o, sl] = (
                    v * lax.rsqrt(jnp.mean(v * v, axis=-1, keepdims=True) + EPSILON) * gain
                ).astype(BF16)
                return 0

            lax.fori_loop(0, rows // step, some, 0)

        def third_leg(o):
            pass_on(2, o)
            norm_rows(o - 4)
            norm_rows(o)

        loop(4, 8, third_leg)
        cot_forward()
        loop(0, 4, lambda o: pass_on(3, o))
        cot_last()
        loop(4, 8, lambda o: pass_on(3, o))
        cot_finish()
        for t in range(n_z - 1):
            loop(0, 8, functools.partial(sent, t))
        loop(1, 8, lambda o: landed(o).wait_send())
        loop(1, 8, lambda o: unit_piece(o).wait())
        loop(1, n_z, lambda o: tiny(o).wait_send())
        loop(1, 8, lambda o: tiny_line(o).wait_send())
        keep_u.wait()
        tok_close()
        cot_close()

    dma = pltpu.SemaphoreType.DMA
    anywhere, vmem = pl.BlockSpec(memory_space=pl.ANY), pl.BlockSpec(memory_space=pltpu.VMEM)
    plane = jax.ShapeDtypeStruct((8, rows, width), BF16)
    legs = n_z - 1
    return pl.pallas_call(
        kernel,
        out_shape=[
            jax.ShapeDtypeStruct((8, n_z, own, cols), BF16),
            jax.ShapeDtypeStruct((8, own, units), BF16),
            plane,
            plane,
            jax.ShapeDtypeStruct((count,) + small.shape, BF16),
        ],
        in_specs=[anywhere] * 5,
        out_specs=[anywhere, anywhere, vmem, anywhere, vmem],
        scratch_shapes=[
            pltpu.VMEM((8, rows, width), BF16),
            dma((5,)),
            dma((7,)),
            dma((7,)),
            dma((7,)),
            dma((7,)),
            dma((legs, 8)),
            dma((legs, 8)),
            dma((legs, 8)),
            dma((legs, 8)),
            dma((n_z + 6,)),
            dma((n_z + 6,)),
            dma((2, 2, chunks)),
            dma((2, 2, chunks)),
            dma((2, chunks)),
            dma((2, chunks)),
            dma((2, 4, chunks)),
            dma((2, 4, chunks)),
        ],
        cost_estimate=busy(150),
        compiler_params=pltpu.CompilerParams(
            collective_id=cid, has_side_effects=True, vmem_limit_bytes=58 << 20
        ),
    )(weight, ups, tokens, cotangent, small)


def relay(left, first, second, first_dims, second_dims, gain, extras, norm_back, cid):
    _, rows, depth = left.shape
    width = gain.shape[1]
    multiply = second is not None
    out_cols = 0 if not multiply else second.shape[1] if second_dims == NN else second.shape[0]
    chunks = 4
    part = rows // chunks
    tile = 512
    out_tiles = [(a, min(a + tile, out_cols)) for a in range(0, out_cols, tile)]

    def kernel(left_ref, first_ref, gain_ref, *refs):
        extra_refs, refs = refs[: len(extras)], refs[len(extras) :]
        if multiply:
            second_ref, *refs = refs
        rows_out, all_ref, *refs = refs
        if multiply:
            prod_out, *refs = refs
        if norm_back:
            gain_grad, *refs = refs
        if multiply:
            *refs, w2, stage = refs
        (L, W, plane, T, A, B, R, S, msem, fsem, lsem, sa, ra, sb, rb, x_send, x_recv, d_send, d_recv, f_send, f_recv) = refs
        me, z, core, cx, cy = _place(8)

        def dev(dx, dy, c):
            return 2 * (2 * lax.rem(cy + dy, 2) + lax.rem(cx + dx, 2)) + c

        def remote(src, dst, send, recv, device):
            return pltpu.make_async_remote_copy(src, dst, send, recv, device_id=(device, z), device_id_type=MESH)

        sib = dev(0, 0, 1 - core)
        nf, ng, across = dev(1 - core, core, core), dev(core, 1 - core, core), dev(1, 1, core)
        bar = pltpu.get_barrier_semaphore()
        for d in (sib, nf, ng):
            pl.semaphore_signal(bar, inc=1, device_id=(d, z), device_id_type=MESH)
        if multiply:
            load = pltpu.make_async_copy(second_ref, w2, lsem.at[2])
            load.start()

        load_first = pltpu.make_async_copy(first_ref, W, lsem.at[3])
        load_first.start()

        mine = (across, ng, nf, me)
        theirs = (dev(1, 1, 1 - core), dev(1 - core, core, 1 - core), dev(core, 1 - core, 1 - core), sib)

        turns = (theirs[0], mine[0], theirs[2], mine[2], theirs[1], theirs[3], mine[1], mine[3])

        def load_left(i):
            return pltpu.make_async_copy(left_ref.at[turns[i]], L.at[i], msem.at[i])

        for i in range(8):
            load_left(i).start()

        def partial(i, write):
            load_left(i).wait()

            def some(n, _):
                cols = pl.ds(pl.multiple_of(n * tile, tile), tile)
                w = W[:, cols] if first_dims == NN else W[cols, :]
                write(cols, lax.dot_general(L[i], w, first_dims, preferred_element_type=F32))
                return 0

            lax.fori_loop(0, width // tile, some, 0)

        def give(i, k):
            def write(cols, v):
                T[k, :, cols] = v.astype(BF16)

            partial(i, write)
            remote(T.at[k], A.at[k], sa.at[k], ra.at[k], sib).start()

        def got(k):
            remote(T.at[k], A.at[k], sa.at[k], ra.at[k], sib).wait_recv()

        def cut(c):
            return pl.ds(c * part, part)

        def ship(k, c, d):
            return remote(B.at[k, cut(c)], R.at[k, cut(c)], sb.at[k, c], rb.at[k, c], d)

        def send_sum(i, k):
            def write(cols, v):
                S[:, cols] = v

            partial(i, write)
            got(k)
            for c in range(chunks):
                B[k, cut(c)] = (S[cut(c)] + A[k, cut(c)].astype(F32)).astype(BF16)
                ship(k, c, nf).start()

        def keep_sum(i, k):
            got(k)

            def write(cols, v):
                S[:, cols] = v + A[k, :, cols].astype(F32)

            partial(i, write)

        pl.semaphore_wait(bar, 3)
        load_first.wait()
        give(0, 0)
        send_sum(1, 0)
        give(2, 2)
        send_sum(3, 2)
        give(4, 1)
        give(5, 3)
        keep_sum(6, 1)
        for c in range(chunks):
            ship(0, c, nf).wait_recv()
            B[1, cut(c)] = (S[cut(c)] + R[0, cut(c)].astype(F32)).astype(BF16)
            ship(1, c, ng).start()
        keep_sum(7, 3)

        source, other = nf, ng

        def at(q, c):
            return plane.at[q, cut(c)]

        def step(k, c):
            return remote(at(me, c), at(me, c), x_send.at[k, c], x_recv.at[k, c], (dev(1, 0, core), dev(0, 1, core))[k])

        def twin(k, q, c):
            return remote(at(q, c), at(q, c), f_send.at[k, c], f_recv.at[k, c], sib)

        def second_step(c):
            return remote(at(source, c), at(source, c), d_send.at[c], d_recv.at[c], other)

        gains = gain_ref[...]
        if norm_back:
            gain_grad[...] = jnp.zeros_like(gain_grad)
        for c in range(chunks):
            ship(2, c, nf).wait_recv()
            ship(1, c, ng).wait_recv()
            for h in range(2):
                sl = pl.ds(c * part + h * (part // 2), part // 2)
                total = S[sl] + R[2, sl].astype(F32) + R[1, sl].astype(F32)
                if norm_back:
                    v = extra_refs[0][sl]
                    root = lax.rsqrt(jnp.mean(v * v, axis=-1, keepdims=True) + EPSILON)
                    hat = v * root
                    scaled = total * gains
                    gain_grad[...] += jnp.sum(total * hat, axis=0, keepdims=True)
                    done = extra_refs[1][sl] + root * (scaled - hat * jnp.mean(scaled * hat, axis=-1, keepdims=True))
                    low = done
                else:
                    done = extra_refs[0][sl].astype(F32) + total
                    low = done * lax.rsqrt(jnp.mean(done * done, axis=-1, keepdims=True) + EPSILON) * gains
                rows_out[sl] = done
                plane[me, sl] = low.astype(BF16)
            for k in range(2):
                step(k, c).start()
            twin(0, me, c).start()
        if multiply:
            load.wait()

        flushes = []

        kept = []

        def product(q):
            keep = pltpu.make_async_copy(plane.at[q], all_ref.at[q], fsem.at[len(kept)])
            keep.start()
            kept.append(keep)
            if not multiply:
                return
            slot = len(flushes) % 2
            if len(flushes) > 1:
                flushes[-2].wait()
            for a, b in out_tiles:
                w = w2[:, a:b] if second_dims == NN else w2[a:b, :]
                stage[slot, :, a:b] = lax.dot_general(plane[q], w, second_dims, preferred_element_type=F32)
            flush = pltpu.make_async_copy(stage.at[slot], prod_out.at[q], lsem.at[slot])
            flush.start()
            flushes.append(flush)

        def twin_got(k):
            for c in range(chunks):
                twin(k, theirs_at[k], c).wait_recv()

        theirs_at = (sib, dev(core, 1 - core, 1 - core), dev(1 - core, core, 1 - core), dev(1, 1, 1 - core))
        product(me)
        for c in range(chunks):
            remote(at(source, c), at(source, c), x_send.at[core, c], x_recv.at[core, c], sib).wait_recv()
            second_step(c).start()
            twin(1, source, c).start()
            remote(at(other, c), at(other, c), x_send.at[1 - core, c], x_recv.at[1 - core, c], sib).wait_recv()
            twin(2, other, c).start()
            if c == 0:
                twin_got(0)
                product(sib)
        product(source)
        product(other)
        for c in range(chunks):
            remote(at(across, c), at(across, c), d_send.at[c], d_recv.at[c], sib).wait_recv()
            twin(3, across, c).start()
            if c == 0:
                twin_got(1)
                product(theirs_at[1])
            if c == 1:
                twin_got(2)
                product(theirs_at[2])
        product(across)
        twin_got(3)
        product(theirs_at[3])

        for k in range(4):
            remote(T.at[k], A.at[k], sa.at[k], ra.at[k], sib).wait_send()
        for c in range(chunks):
            for k in range(3):
                ship(k, c, nf).wait_send()
            for k in range(2):
                step(k, c).wait_send()
            second_step(c).wait_send()
            for k, q in enumerate((me, source, other, across)):
                twin(k, q, c).wait_send()
        for flush in flushes[-2:] + kept:
            flush.wait()

    dma = pltpu.SemaphoreType.DMA
    anywhere, vmem = pl.BlockSpec(memory_space=pl.ANY), pl.BlockSpec(memory_space=pltpu.VMEM)
    block = lambda n: pltpu.VMEM((n, rows, width), BF16)
    out_shape = [
        jax.ShapeDtypeStruct((rows, width), F32),
        jax.ShapeDtypeStruct((8, rows, width), BF16),
    ]
    out_specs = [vmem, anywhere]
    operands = [left, first, gain, *extras]
    in_specs = [anywhere, anywhere] + [vmem] * (1 + len(extras))
    later = []
    if multiply:
        out_shape.append(jax.ShapeDtypeStruct((8, rows, out_cols), F32))
        out_specs.append(anywhere)
        operands.append(second)
        in_specs.append(anywhere)
        later = [pltpu.VMEM(second.shape, BF16), pltpu.VMEM((2, rows, out_cols), F32)]
    if norm_back:
        out_shape.append(jax.ShapeDtypeStruct((1, width), F32))
        out_specs.append(vmem)
    return pl.pallas_call(
        kernel,
        out_shape=out_shape,
        in_specs=in_specs,
        out_specs=out_specs,
        scratch_shapes=[
            pltpu.VMEM(left.shape, BF16),
            pltpu.VMEM(first.shape, BF16),
            block(8),
            block(4),
            block(4),
            block(3),
            block(3),
            pltpu.VMEM((rows, width), F32),
            dma((8,)),
            dma((8,)),
            dma((4,)),
            dma((4,)),
            dma((4,)),
            dma((3, chunks)),
            dma((3, chunks)),
            dma((2, chunks)),
            dma((2, chunks)),
            dma((chunks,)),
            dma((chunks,)),
            dma((4, chunks)),
            dma((4, chunks)),
            *later,
        ],
        cost_estimate=busy(80),
        compiler_params=pltpu.CompilerParams(
            collective_id=cid, has_side_effects=True, vmem_limit_bytes=58 << 20
        ),
    )(*operands)


def unit_pairs(a, main):
    tail = a[:, 2 * main :]
    size = tail.shape[1]
    turned = pltpu.roll(tail, size // 2, 1)
    left = lax.broadcasted_iota(jnp.int32, tail.shape, 1) < size // 2
    return (a[:, :main], a[:, main : 2 * main]), (jnp.where(left, tail, turned), jnp.where(left, turned, tail)), left


def units_forward(x, weight, scales, units, main):
    blocks, rows, width = x.shape
    cols = weight.shape[1]

    def kernel(x_ref, w_ref, s_ref, up_ref, hidden_ref, scaled_ref):
        scale = s_ref[pl.ds(pl.program_id(0), 1), :][:, 0:1]
        for a in range(0, cols, 512):
            b = min(a + 512, cols)
            up_ref[:, a:b] = jnp.dot(x_ref[...], w_ref[:, a:b], preferred_element_type=F32)
        (g, u), (g_tail, u_tail), _ = unit_pairs(up_ref[...], main)
        hidden = g * sigmoid(g) * u
        tail = (g_tail * sigmoid(g_tail) * u_tail)[:, : units - main]
        hidden_ref[:, :main] = hidden.astype(BF16)
        hidden_ref[:, main:] = tail.astype(BF16)
        scaled_ref[:, :main] = (hidden * scale).astype(BF16)
        scaled_ref[:, main:] = (tail * scale).astype(BF16)

    row = lambda n: pl.BlockSpec((rows, n), lambda i: (i, 0))
    whole = lambda a: pl.BlockSpec(a.shape, lambda i: (0, 0))
    tokens = blocks * rows
    return pl.pallas_call(
        kernel,
        grid=(blocks,),
        in_specs=[row(width), whole(weight), whole(scales)],
        out_specs=[row(cols), row(units), row(units)],
        out_shape=[
            jax.ShapeDtypeStruct((tokens, cols), F32),
            jax.ShapeDtypeStruct((tokens, units), BF16),
            jax.ShapeDtypeStruct((tokens, units), BF16),
        ],
        cost_estimate=busy(20),
        compiler_params=pltpu.CompilerParams(vmem_limit_bytes=48 << 20),
    )(x.reshape(tokens, width), weight, scales)


def units_backward(cot, weight, upgate, scales, units, main):
    blocks, rows, width = cot.shape
    cols = upgate.shape[1]

    def kernel(c_ref, w_ref, up_ref, s_ref, low_ref):
        scale = s_ref[pl.ds(pl.program_id(0), 1), :][:, 0:1]
        pair, pair_tail, left = unit_pairs(up_ref[...], main)
        tail_rows = w_ref[main:, :]
        grad = dot(c_ref[...], w_ref[:main, :], NT) * scale
        grad_tail = dot(c_ref[...], jnp.concatenate([tail_rows, tail_rows], axis=0), NT) * scale

        def both(g, u, grad):
            s = sigmoid(g)
            return grad * u * s * (1.0 + g * (1.0 - s)), grad * g * s

        gate_grad, up_grad = both(*pair, grad)
        low_ref[:, :main] = gate_grad.astype(BF16)
        low_ref[:, main : 2 * main] = up_grad.astype(BF16)
        gate_grad, up_grad = both(*pair_tail, grad_tail)
        low_ref[:, 2 * main :] = jnp.where(left, gate_grad, up_grad).astype(BF16)

    row = lambda n: pl.BlockSpec((rows, n), lambda i: (i, 0))
    whole = lambda a: pl.BlockSpec(a.shape, lambda i: (0, 0))
    tokens = blocks * rows
    return pl.pallas_call(
        kernel,
        grid=(blocks,),
        in_specs=[row(width), whole(weight), row(cols), whole(scales)],
        out_specs=row(cols),
        out_shape=jax.ShapeDtypeStruct((tokens, cols), BF16),
        cost_estimate=busy(12),
        compiler_params=pltpu.CompilerParams(vmem_limit_bytes=48 << 20),
    )(cot.reshape(tokens, width), weight, upgate, scales)


def conclude(grad, left, weight, raw_weight, block, ups, tokens, middle, middle_grad, gain, lines, conv, bounds, cid):
    n_z = 4
    own, cols = grad.shape[2], grad.shape[3] - 128
    units = ups.shape[2]
    rows, width = tokens.shape
    count = 8 * n_z
    per = 128 * count // width
    conv_cols = conv.shape[1] // count
    chunks = 2
    part = rows // chunks
    tile = 512
    last = n_z - 1

    def kernel(
        g_ref, l_ref, w_ref, wr_ref, b_ref, u_ref, t_ref, m_ref, mg_ref, gain_ref, lines_ref, conv_ref,
        result, tg, in_out, u_out, line_sum, line_planes, conv_sum, conv_planes,
        lines_out, conv_out, W, L, own_buf, UD, T, A, B, R, S, A7, B7, R7, X7, line_buf,
        lsem, wsem, osem, mine_sem, us, ur, ds, dr, i_send, i_recv, u_send, u_recv, p_send, p_recv, c_send, c_recv,
        sa, ra, sb, rb, sa7, ra7, sb7, rb7,
    ):
        me, z, core, cx, cy = _place(8)
        flat = me * n_z + z

        def dev(dx, dy, c):
            return 2 * (2 * lax.rem(cy + dy, 2) + lax.rem(cx + dx, 2)) + c

        sib = dev(0, 0, 1 - core)
        nf, ng, across = dev(1 - core, core, core), dev(core, 1 - core, core), dev(1, 1, core)

        def partner(o):
            return dev(o // 4, lax.rem(o // 2, 2), lax.rem(core + o, 2))

        def anyone(o):
            other = lax.rem(flat + o, count)
            return (other // n_z, lax.rem(other, n_z))

        def remote(src, dst, send, recv, device):
            return pltpu.make_async_remote_copy(src, dst, send, recv, device_id=device, device_id_type=MESH)

        def loop(first, end, body):
            def step(o, _):
                body(o)
                return 0

            lax.fori_loop(first, end, step, 0)

        bar = pltpu.get_barrier_semaphore()
        loop(1, count, lambda o: pl.semaphore_signal(bar, inc=1, device_id=anyone(o), device_id_type=MESH))

        mine = (across, ng, nf, me)
        theirs = (dev(1, 1, 1 - core), dev(1 - core, core, 1 - core), dev(core, 1 - core, 1 - core), sib)
        turns = (theirs[0], theirs[2], mine[0], theirs[1], mine[2], theirs[3], mine[1], mine[3])

        def load_left(i):
            return (pltpu.make_async_copy(l_ref.at[turns[i]], L.at[i % 2], lsem.at[i % 2]),)

        def start(copies):
            for copy in copies:
                copy.start()

        def wait(copies):
            for copy in copies:
                copy.wait()

        load_weight = (
            pltpu.make_async_copy(w_ref, W.at[:, pl.ds(0, cols)], wsem.at[0]),
            pltpu.make_async_copy(wr_ref, W.at[:, pl.ds(cols, 128)], wsem.at[7]),
        )
        load_middle = pltpu.make_async_copy(m_ref, result, wsem.at[1])
        load_grad = pltpu.make_async_copy(mg_ref, tg, wsem.at[2])

        def load_own(zz):
            return pltpu.make_async_copy(g_ref.at[:, zz, :, pl.ds(0, cols)], own_buf.at[zz], osem.at[zz])

        def give7(k):
            return remote(b_ref.at[theirs[k]], A7.at[k], sa7.at[k], ra7.at[k], (sib, z))

        def mine7(k):
            return pltpu.make_async_copy(b_ref.at[mine[k]], X7 if k == 3 else B7.at[k], mine_sem.at[k])

        def start7():
            for k in (0, 2, 1, 3):
                give7(k).start()
                mine7(k).start()

        start(load_left(0))
        start(load_weight)
        for zz in (0, 3, 2, 1):
            load_own(zz).start()
        start(load_left(1))
        load_middle.start()
        load_grad.start()
        pl.semaphore_wait(bar, count - 1)

        def up_slot(s, o):
            return s * 8 + o

        def down_slot(s, o):
            return 39 - (s * 8 + o)

        def up(s, o, src):
            return remote(src, UD.at[up_slot(s, o)], us.at[s, o], ur.at[s, o], (me, z + 1))

        def down(s, o, src):
            return remote(src, UD.at[down_slot(s, o)], ds.at[s, o], dr.at[s, o], (me, z - 1))

        def start_line(s, o):
            q = partner(o)

            @pl.when(z == 0)
            def _():
                up(s, o, g_ref.at[q, last - s, :, pl.ds(0, cols)]).start()

            @pl.when(z == last)
            def _():
                down(s, o, g_ref.at[q, s, :, pl.ds(0, cols)]).start()

        start7()
        for s in range(last):
            loop(0, 8, functools.partial(start_line, s))
        for zz in range(n_z):
            load_own(zz).wait()

        def sections(q):
            for a, b in zip(bounds[:-1], bounds[1:]):
                at = pl.multiple_of(8 * a + q * (b - a), 128)
                yield pl.ds(a, b - a), in_out.at[:, pl.ds(at, b - a)]

        def deliver(o, slot):
            @pl.when(o == 0)
            def _():
                for src, dst in sections(me):
                    pltpu.make_async_copy(UD.at[slot, :, src], dst, wsem.at[3]).start()

            @pl.when(o > 0)
            def _():
                for src, dst in sections(me):
                    remote(UD.at[slot, :, src], dst, i_send.at[o - 1], i_recv.at[o - 1], (partner(o), z)).start()

        def add(slot, *others):
            total = UD[slot].astype(F32)
            for other in others:
                total = total + other.astype(F32)
            UD[slot] = total.astype(BF16)

        def up_tick(i):
            s, o = i // 8, lax.rem(i, 8)
            q, u = partner(o), up_slot(s, o)

            @pl.when((z >= 1) & (z <= last - s))
            def _():
                remote(UD.at[u], UD.at[u], us.at[s, o], ur.at[s, o], (sib, z)).wait_recv()

            @pl.when((z >= 1) & (z < last - s))
            def _():
                add(u, own_buf[last - s, q])
                up(s, o, UD.at[u]).start()

            @pl.when((z == last) & (s == 0))
            def _():
                add(u, own_buf[last, q])
                deliver(o, u)

            @pl.when((z == 1) & (s == 2))
            def _():
                add(u, UD[down_slot(1, o)], own_buf[1, q])
                deliver(o, u)

        def down_tick(i):
            s, o = i // 8, lax.rem(i, 8)
            q, d = partner(o), down_slot(s, o)

            @pl.when((z <= last - 1) & (z >= s))
            def _():
                remote(UD.at[d], UD.at[d], ds.at[s, o], dr.at[s, o], (sib, z)).wait_recv()

            @pl.when((z <= last - 1) & (z > s))
            def _():
                add(d, own_buf[s, q])
                down(s, o, UD.at[d]).start()

            @pl.when((z == 0) & (s == 0))
            def _():
                add(d, own_buf[0, q])
                deliver(o, d)

            @pl.when((z == 2) & (s == 2))
            def _():
                add(d, UD[up_slot(1, o)], own_buf[2, q])
                deliver(o, d)

        lag = 4
        low = 1 - z // 2

        def tick(i):
            at_up, at_down = i - lag * (1 - low), i - lag * low

            @pl.when((at_up >= 0) & (at_up < 24))
            def _():
                up_tick(at_up)

            @pl.when((at_down >= 0) & (at_down < 24))
            def _():
                down_tick(at_down)

        def cut(c):
            return pl.ds(c * part, part)

        def partial(i, write):
            wait(load_left(i))

            def some(n, _):
                at = pl.ds(pl.multiple_of(n * tile, tile), tile)
                write(at, lax.dot_general(L[i % 2], W[at, :], NT, preferred_element_type=F32))
                return 0

            lax.fori_loop(0, width // tile, some, 0)
            if i + 2 < 8:
                start(load_left(i + 2))

        def give(i, k, slot, before):
            if before is not None:
                remote(T.at[slot], A.at[before], sa.at[before], ra.at[before], (sib, z)).wait_send()

            def write(at, v):
                T[slot, :, at] = v.astype(BF16)

            partial(i, write)
            remote(T.at[slot], A.at[k], sa.at[k], ra.at[k], (sib, z)).start()

        def got(k):
            remote(T.at[0], A.at[k], sa.at[k], ra.at[k], (sib, z)).wait_recv()

        def ship(k, c, d):
            return remote(B.at[k, cut(c)], R.at[k, cut(c)], sb.at[k, c], rb.at[k, c], (d, z))

        def ship7(k, c, d):
            return remote(B7.at[k, cut(c)], R7.at[k, cut(c)], sb7.at[k, c], rb7.at[k, c], (d, z))

        def send_sum(i, k):
            got(k)

            def write(at, v):
                B[k, :, at] = (v + A[k, :, at].astype(F32)).astype(BF16)

            partial(i, write)
            for c in range(chunks):
                ship(k, c, nf).start()

        def keep_sum(i, k):
            got(k)

            def write(at, v):
                S[:, at] = v + A[k, :, at].astype(F32)

            partial(i, write)

        def second_hop():
            for c in range(chunks):
                ship(0, c, nf).wait_recv()
                B[1, cut(c)] = (S[cut(c)] + R[0, cut(c)].astype(F32)).astype(BF16)
                ship(1, c, ng).start()

        def send7(k):
            mine7(k).wait()
            give7(k).wait_recv()
            for c in range(chunks):
                B7[k, cut(c)] = (B7[k, cut(c)].astype(F32) + A7[k, cut(c)].astype(F32)).astype(BF16)
                ship7(k, c, nf).start()

        def second_hop7():
            mine7(1).wait()
            give7(1).wait_recv()
            for c in range(chunks):
                ship7(0, c, nf).wait_recv()
                sl = cut(c)
                B7[1, sl] = (B7[1, sl].astype(F32) + A7[1, sl].astype(F32) + R7[0, sl].astype(F32)).astype(BF16)
                ship7(1, c, ng).start()

        small = 32

        def finish_rows():
            load_grad.wait()
            line_buf[...] = lines_ref[...]
            line_buf[0:1] = jnp.zeros((1, width), F32)
            gains = gain_ref[...]
            for c in range(chunks):
                ship(2, c, nf).wait_recv()
                ship(1, c, ng).wait_recv()

                def some(r, _):
                    sl = pl.ds(pl.multiple_of(c * part + r * small, small), small)
                    total = S[sl] + R[2, sl].astype(F32) + R[1, sl].astype(F32)
                    v = t_ref[sl].astype(F32)
                    root = lax.rsqrt(jnp.mean(v * v, axis=-1, keepdims=True) + EPSILON)
                    hat = v * root
                    scaled = total * gains
                    line_buf[0:1] += jnp.sum(total * hat, axis=0, keepdims=True)
                    tg[sl] += root * (scaled - hat * jnp.mean(scaled * hat, axis=-1, keepdims=True))
                    return 0

                lax.fori_loop(0, part // small, some, 0)

        def finish7():
            load_middle.wait()
            mine7(3).wait()
            give7(3).wait_recv()
            for c in range(chunks):
                ship7(2, c, nf).wait_recv()
                ship7(1, c, ng).wait_recv()

                def some(r, _):
                    sl = pl.ds(pl.multiple_of(c * part + r * small, small), small)
                    result[sl] += (
                        X7[sl].astype(F32) + A7[3, sl].astype(F32) + R7[2, sl].astype(F32) + R7[1, sl].astype(F32)
                    )
                    return 0

                lax.fori_loop(0, part // small, some, 0)

        def line_part(d):
            return line_buf.at[:, pl.ds(pl.multiple_of((d // per) * 128, 128), 128)]

        def conv_part(d):
            return conv_ref.at[:, pl.ds(pl.multiple_of(d * conv_cols, conv_cols), conv_cols)]

        def packet(o):
            d = lax.rem(flat + o, count)
            return remote(line_part(d), lines_out.at[flat], p_send.at[o - 1], p_recv.at[o - 1], anyone(o))

        def conv_packet(o):
            d = lax.rem(flat + o, count)
            return remote(conv_part(d), conv_out.at[flat], c_send.at[o - 1], c_recv.at[o - 1], anyone(o))

        keep_line = pltpu.make_async_copy(line_part(flat), lines_out.at[flat], wsem.at[4])
        keep_conv = pltpu.make_async_copy(conv_part(flat), conv_out.at[flat], wsem.at[5])
        keep_up = pltpu.make_async_copy(u_ref.at[me], u_out.at[me], wsem.at[6])

        def unit_piece(o):
            q = partner(o)
            return remote(u_ref.at[q], u_out.at[me], u_send.at[o - 1], u_recv.at[o - 1], (q, z))

        def send_packets():
            keep_line.start()
            loop(1, count, lambda o: packet(o).start())

        def others():
            keep_conv.start()
            keep_up.start()
            loop(1, count, lambda o: conv_packet(o).start())

        def first_give():
            wait(load_weight)
            give(0, 0, 0, None)
            give(1, 2, 1, None)

        work = (
            lambda: (send7(0), send7(2)),
            first_give,
            lambda: (send_sum(2, 0), give(3, 1, 0, 0)),
            lambda: (send_sum(4, 2), give(5, 3, 1, 2)),
            lambda: (second_hop7(), keep_sum(6, 1)),
            others,
            lambda: (second_hop(), keep_sum(7, 3)),
            lambda: (finish7(), loop(1, 8, lambda o: unit_piece(o).start())),
            lambda: None,
            lambda: (finish_rows(), send_packets()),
            lambda: None,
            lambda: None,
            lambda: None,
            lambda: None,
        )
        for g, item in enumerate(work):
            item()
            loop(2 * g, 2 * g + 2, tick)

        def line_sent(s, o):
            @pl.when(z < last - s)
            def _():
                up(s, o, UD.at[up_slot(s, o)]).wait_send()

            @pl.when(z > s)
            def _():
                down(s, o, UD.at[down_slot(s, o)]).wait_send()

        for s in range(last):
            loop(0, 8, functools.partial(line_sent, s))
        for k, slot in ((1, 0), (3, 1)):
            remote(T.at[slot], A.at[k], sa.at[k], ra.at[k], (sib, z)).wait_send()
        for k in range(4):
            give7(k).wait_send()
        for c in range(chunks):
            for k in range(3):
                ship(k, c, nf).wait_send()
                ship7(k, c, nf).wait_send()
        piece = UD.at[0]

        def arrived(o):
            remote(piece, piece, i_send.at[o - 1], i_recv.at[o - 1], (sib, z)).wait()

        pltpu.make_async_copy(piece, piece, wsem.at[3]).wait()
        loop(1, 8, arrived)
        loop(1, 8, lambda o: unit_piece(o).wait())
        loop(1, count, lambda o: packet(o).wait())
        loop(1, count, lambda o: conv_packet(o).wait())
        keep_line.wait()
        keep_conv.wait()
        keep_up.wait()
        all_lines, all_conv = lines_out[0], conv_out[0]
        for d in range(1, count):
            all_lines, all_conv = all_lines + lines_out[d], all_conv + conv_out[d]
        line_sum[...] = all_lines
        conv_sum[...] = all_conv
        for d in range(8):
            line_planes[d : d + 1] = sum(lines_out[d * n_z + i, 4:5] for i in range(n_z))
            conv_planes[d : d + 1] = sum(conv_out[d * n_z + i, 4:5] for i in range(n_z))

    dma = pltpu.SemaphoreType.DMA
    anywhere, vmem = pl.BlockSpec(memory_space=pl.ANY), pl.BlockSpec(memory_space=pltpu.VMEM)
    blocks = lambda n: pltpu.VMEM((n, rows, width), BF16)
    f32_rows = jax.ShapeDtypeStruct((rows, width), F32)
    return pl.pallas_call(
        kernel,
        out_shape=[
            f32_rows,
            f32_rows,
            jax.ShapeDtypeStruct((own, 8 * bounds[-1]), BF16),
            jax.ShapeDtypeStruct((8, own, units), BF16),
            jax.ShapeDtypeStruct((8, 128), F32),
            jax.ShapeDtypeStruct((8, 128), F32),
            jax.ShapeDtypeStruct((8, conv_cols), F32),
            jax.ShapeDtypeStruct((8, conv_cols), F32),
        ],
        in_specs=[anywhere] * 6 + [vmem, anywhere, anywhere, vmem, vmem, anywhere],
        out_specs=[vmem, vmem, anywhere, anywhere] + [vmem] * 4,
        scratch_shapes=[
            pltpu.VMEM((count, 8, 128), F32),
            pltpu.VMEM((count, 8, conv_cols), F32),
            pltpu.VMEM((width, cols + 128), BF16),
            pltpu.VMEM((2, rows, cols + 128), BF16),
            pltpu.VMEM((n_z, 8, own, cols), BF16),
            pltpu.VMEM((40, own, cols), BF16),
            blocks(2),
            blocks(4),
            blocks(3),
            blocks(3),
            pltpu.VMEM((rows, width), F32),
            blocks(4),
            blocks(3),
            blocks(3),
            pltpu.VMEM((rows, width), BF16),
            pltpu.VMEM((8, width), F32),
            dma((2,)),
            dma((8,)),
            dma((n_z,)),
            dma((4,)),
            dma((3, 8)),
            dma((3, 8)),
            dma((3, 8)),
            dma((3, 8)),
            dma((7,)),
            dma((7,)),
            dma((7,)),
            dma((7,)),
            dma((count - 1,)),
            dma((count - 1,)),
            dma((count - 1,)),
            dma((count - 1,)),
            dma((4,)),
            dma((4,)),
            dma((3, chunks)),
            dma((3, chunks)),
            dma((4,)),
            dma((4,)),
            dma((3, chunks)),
            dma((3, chunks)),
        ],
        cost_estimate=busy(120),
        compiler_params=pltpu.CompilerParams(
            collective_id=cid, has_side_effects=True, vmem_limit_bytes=60 << 20
        ),
    )(grad, left, weight, raw_weight, block, ups, tokens, middle, middle_grad, gain, lines, conv)


def gather_small(x, n_dp, n_z, cid):
    rows, cols = x.shape
    count = n_dp * n_z

    def kernel(x_ref, o_ref, lsem, ssem, rsem):
        flat = lax.axis_index("dp") * n_z + lax.axis_index("fsdp")
        bar = pltpu.get_barrier_semaphore()

        def device(o):
            other = lax.rem(flat + o, count)
            return (other // n_z, lax.rem(other, n_z))

        def copy(o):
            return pltpu.make_async_remote_copy(
                x_ref, o_ref.at[flat], ssem.at[o - 1], rsem.at[o - 1], device_id=device(o), device_id_type=MESH
            )

        def greet(o, _):
            pl.semaphore_signal(bar, inc=1, device_id=device(o), device_id_type=MESH)
            return 0

        def send(o, _):
            copy(o).start()
            return 0

        def wait(o, _):
            copy(o).wait()
            return 0

        lax.fori_loop(1, count, greet, 0)
        local = pltpu.make_async_copy(x_ref, o_ref.at[flat], lsem)
        local.start()
        pl.semaphore_wait(bar, count - 1)
        lax.fori_loop(1, count, send, 0)
        lax.fori_loop(1, count, wait, 0)
        local.wait()

    dma = pltpu.SemaphoreType.DMA
    return pl.pallas_call(
        kernel,
        out_shape=jax.ShapeDtypeStruct((count, rows, cols), x.dtype),
        in_specs=[pl.BlockSpec(memory_space=pl.ANY)],
        out_specs=pl.BlockSpec(memory_space=pl.ANY),
        scratch_shapes=[dma, dma((count - 1,)), dma((count - 1,))],
        cost_estimate=busy(15),
        compiler_params=pltpu.CompilerParams(collective_id=cid, has_side_effects=True),
    )(x)


def scatter_small(x, n_dp, n_z, cid):
    count, rows, cols = x.shape

    def kernel(x_ref, o_ref, lsem, ssem, rsem):
        flat = lax.axis_index("dp") * n_z + lax.axis_index("fsdp")
        bar = pltpu.get_barrier_semaphore()

        def device(o):
            other = lax.rem(flat + o, count)
            return (other // n_z, lax.rem(other, n_z))

        def copy(o):
            return pltpu.make_async_remote_copy(
                x_ref.at[lax.rem(flat + o, count)], o_ref.at[flat], ssem.at[o - 1], rsem.at[o - 1], device_id=device(o), device_id_type=MESH
            )

        def greet(o, _):
            pl.semaphore_signal(bar, inc=1, device_id=device(o), device_id_type=MESH)
            return 0

        def send(o, _):
            copy(o).start()
            return 0

        def wait(o, _):
            copy(o).wait()
            return 0

        lax.fori_loop(1, count, greet, 0)
        local = pltpu.make_async_copy(x_ref.at[flat], o_ref.at[flat], lsem)
        local.start()
        pl.semaphore_wait(bar, count - 1)
        lax.fori_loop(1, count, send, 0)
        lax.fori_loop(1, count, wait, 0)
        local.wait()

    dma = pltpu.SemaphoreType.DMA
    return pl.pallas_call(
        kernel,
        out_shape=jax.ShapeDtypeStruct((count, rows, cols), x.dtype),
        in_specs=[pl.BlockSpec(memory_space=pl.ANY)],
        out_specs=pl.BlockSpec(memory_space=pl.ANY),
        scratch_shapes=[dma, dma((count - 1,)), dma((count - 1,))],
        cost_estimate=busy(15),
        compiler_params=pltpu.CompilerParams(collective_id=cid, has_side_effects=True),
    )(x)


def pack(parts, unit):
    flat = jnp.concatenate([part.reshape(-1) for part in parts])
    size = flat.shape[0]
    full = -(-size // (128 * unit)) * 128 * unit
    return jnp.pad(flat, (0, full - size)).reshape(-1, 128)


def dot(a, b, dims=NN, out=F32):
    return lax.dot_general(a, b, dims, preferred_element_type=F32).astype(out)


def local(
    n_dp,
    n_z,
    tokens,
    cotangent,
    group_ids,
    norm_first,
    input_weight,
    decay_weight,
    conv_weight,
    decay_scale,
    decay_bias,
    output_gain,
    output_weight,
    norm_second,
    upgate_weight,
    down_weight,
):
    count = n_dp * n_z
    rows, width = tokens.shape
    all_heads = decay_scale.shape[0]
    heads = all_heads // n_dp
    taps = conv_weight.shape[0]
    own_conv = conv_weight.shape[1]
    own_d = norm_first.shape[0]
    units = upgate_weight.shape[1] // (2 * n_dp)
    key, value = heads * DK, heads * DV
    cols = 2 * key + 2 * value
    square = n_dp == 8 and n_z == 4
    here = lax.axis_index("dp")
    flat = here * n_z + lax.axis_index("fsdp")

    def spread(x, cid):
        if square:
            return ag_square(x, cid).reshape(n_dp * rows, width)
        return lax.all_gather(x, "dp", axis=0, tiled=True)

    def total(x, cid):
        if square:
            return rs_square(x.reshape(n_dp, rows, width), cid)
        return lax.psum_scatter(x, "dp", scatter_dimension=0, tiled=True).astype(F32)

    def by_dp(a, parts):
        return a.reshape(a.shape[0], n_dp, parts)

    main = units // 128 * 128
    bounds = (0, key, 2 * key, 2 * key + value, 2 * key + 2 * value)
    gates = by_dp(upgate_weight[:, : n_dp * units], units)
    ups = by_dp(upgate_weight[:, n_dp * units :], units)
    up_mine = jnp.concatenate(
        [gates[:, :, :main], ups[:, :, :main], gates[:, :, main:], ups[:, :, main:]], axis=2
    ).transpose(1, 0, 2)
    def whole_rows(a):
        a = lax.all_gather(a[:, None], "fsdp", axis=1, tiled=True)
        return a.reshape(width, a.shape[-1])

    conv_size = taps * own_conv
    inputs = tokens.astype(F32)
    first_root = lax.rsqrt(jnp.mean(inputs * inputs, axis=-1, keepdims=True) + EPSILON)
    if square:
        small = jnp.concatenate(
            [norm_first] * (128 // own_d)
            + [norm_second] * (128 // own_d)
            + [jnp.broadcast_to(group_ids.astype(BF16), (128,)), jnp.zeros((640,), BF16), conv_weight.reshape(-1)]
            + [decay_weight.reshape(-1)]
        ).reshape(32, 128)
        in_full, up_plane, normed_all, cot_all, small = begin(
            input_weight, up_mine, tokens, cotangent, small, bounds, n_z, 1
        )
        in_full = in_full.reshape(width, cols)
        normed_all = normed_all.reshape(n_dp * rows, width)
        cot_all = cot_all.reshape(n_dp * rows, width)
        conv_full = small[:, 8:16].reshape(count, taps, own_conv)
        decay_full = small[:, 16:].reshape(width, 2 * all_heads)
        first_full = small[:, 0, :own_d]
        second_full = small[:, 1, :own_d]
        every_id = small[:, 2, 0]
        output_weight, down_weight, up_plane = lax.optimization_barrier(
            (output_weight, down_weight, up_plane, small)
        )[:3]
    else:
        in_mine = [
            by_dp(input_weight[:, n_dp * a : n_dp * b], b - a).transpose(1, 0, 2)
            for a, b in zip(bounds[:-1], bounds[1:])
        ]
        in_mine = jnp.concatenate(in_mine, axis=2)
        decay_full = lax.all_gather(decay_weight, ("dp", "fsdp"), axis=0, tiled=True)
        in_full = whole_rows(lax.all_to_all(in_mine, "dp", 0, 0, tiled=True))
        up_plane = lax.all_to_all(up_mine, "dp", 0, 0, tiled=True)
        small = gather_small(
            pack((conv_weight, norm_first, norm_second, group_ids.astype(BF16)), 16), n_dp, n_z, 1
        ).reshape(count, -1)
        conv_full = small[:, :conv_size].reshape(count, taps, own_conv)
        first_full = small[:, conv_size : conv_size + own_d]
        second_full = small[:, conv_size + own_d : conv_size + 2 * own_d]
        every_id = small[:, conv_size + 2 * own_d]
    out_full = lax.all_gather(output_weight, "fsdp", axis=0, tiled=True)
    up_full = whole_rows(up_plane)
    down_full = lax.all_gather(down_weight, "fsdp", axis=0, tiled=True)
    conv_full = conv_full.transpose(1, 0, 2).reshape(taps, -1)
    first_full = first_full.reshape(1, width).astype(F32)
    second_full = second_full.reshape(1, width).astype(F32)
    every_id = every_id.astype(jnp.int32)
    scales = 1.0 / jnp.sum((every_id[:, None] == every_id[None, :]).astype(F32), axis=0).reshape(n_dp, n_z)
    scales = lax.dynamic_index_in_dim(scales, lax.axis_index("fsdp"), axis=1, keepdims=False)
    seed = cotangent.astype(F32) * lax.dynamic_index_in_dim(scales, here, axis=0, keepdims=False)
    lanes_of_scales = jnp.broadcast_to(scales[:, None], (n_dp, 128))
    scales = jnp.broadcast_to(scales[:, None, None], (n_dp, rows, 1)).reshape(n_dp * rows, 1)
    if not square:
        normed_all = spread((inputs * first_root * first_full).astype(BF16), 2)
        cot_all = spread(cotangent, 3)

    def conv_columns(start, size):
        return lax.dynamic_slice_in_dim(conv_full, start + here * size, size, axis=1)

    conv_mine = jnp.concatenate(
        [conv_columns(0, key), conv_columns(n_dp * key, key), conv_columns(2 * n_dp * key, value)], axis=1
    ).astype(F32)
    decay_mine = jnp.pad(
        jnp.stack(
            [
                lax.dynamic_slice_in_dim(decay_scale, here * heads, heads),
                lax.dynamic_slice_in_dim(decay_bias, here * heads, heads),
            ]
        ),
        ((0, 0), (0, 128 - heads)),
    )
    gain = output_gain[None, :]

    raw_weight = jnp.pad(
        jnp.concatenate(
            [lax.dynamic_slice_in_dim(decay_full, i * all_heads + here * heads, heads, axis=1) for i in range(2)], axis=1
        ),
        ((0, 0), (0, 128 - 2 * heads)),
    )
    projected = dot(normed_all, in_full)
    raw = dot(normed_all, raw_weight)
    mixed, inverse, solved, core, before_silu = mixer_forward(projected, raw, conv_mine, decay_mine, gain, heads, rows)
    if square:
        middle, second_all = relay(
            mixed.reshape(n_dp, rows, value), out_full, None, NN, NN, second_full, (tokens,), False, 4
        )
        upgate, hidden, hidden_seed = units_forward(second_all, up_full, lanes_of_scales, units, main)
        second_all = second_all.reshape(n_dp * rows, width)
    else:
        middle = inputs + total(dot(mixed, out_full, out=BF16), 4)
        second_root = lax.rsqrt(jnp.mean(middle * middle, axis=-1, keepdims=True) + EPSILON)
        second_all = spread((middle * second_root * second_full).astype(BF16), 5)
        upgate = dot(second_all, up_full)

        def halves_of(a):
            return (a[:, :main], a[:, main : 2 * main]), (a[:, 2 * main : main + units], a[:, main + units :])

        acts = [(g, u, jax.nn.sigmoid(g)) for g, u in halves_of(upgate)]
        hidden = jnp.concatenate([g * s * u for g, u, s in acts], axis=1)
        hidden_seed = (hidden * scales).astype(BF16)
        hidden = hidden.astype(BF16)

    down_grad = dot(hidden_seed, cot_all, TN, out=BF16)
    down_grad, cot_all = lax.optimization_barrier((down_grad, cot_all))
    if square:
        upgate_low = units_backward(
            cot_all.reshape(n_dp, rows, width), down_full, upgate, lanes_of_scales, units, main
        )
    else:
        hidden_grad = dot(cot_all, down_full, NT) * scales
        parts = list(zip(acts, (hidden_grad[:, :main], hidden_grad[:, main:])))
        upgate_low = jnp.concatenate(
            [x for (g, u, s), grad in parts for x in (grad * u * s * (1.0 + g * (1.0 - s)), grad * g * s)], axis=1
        ).astype(BF16)
    upgate_grad = dot(second_all, upgate_low, TN, out=BF16)
    upgate_low, upgate_grad = lax.optimization_barrier((upgate_low, upgate_grad))

    def norm_back(v, root, gain_row, grad):
        hat = v * root
        scaled = grad * gain_row
        gain_grad = jnp.sum(grad * hat, axis=0)
        return root * (scaled - hat * jnp.mean(scaled * hat, axis=-1, keepdims=True)), gain_grad

    def owned_rows(a):
        return lax.psum_scatter(a, "fsdp", scatter_dimension=0, tiled=True)

    def owned_parts(a):
        return lax.psum_scatter(a, "fsdp", scatter_dimension=0, tiled=True)

    def by_plane(a):
        return a.reshape(n_dp, n_z, own_d, a.shape[-1]).transpose(1, 0, 2, 3).reshape(width, -1)

    down_total = owned_rows(down_grad)
    block_part = dot(hidden, down_full, out=BF16)
    upgate_low, upgate_grad, down_total, block_part, seed = lax.optimization_barrier(
        (upgate_low, by_plane(upgate_grad), down_total, block_part, seed)
    )
    upgate_sum = owned_parts(upgate_grad)
    if square:
        middle_grad, middle_all, mixed_grad, second_grad = relay(
            upgate_low.reshape(n_dp, rows, 2 * units), up_full, out_full, NT, NT, second_full, (middle, seed), True, 6
        )
        middle_all = middle_all.reshape(n_dp * rows, width)
        mixed_grad = mixed_grad.reshape(n_dp * rows, value)
    else:
        normed_two_grad = total(dot(upgate_low, up_full, NT, out=BF16), 6)
        middle_part, second_grad = norm_back(middle, second_root, second_full, normed_two_grad)
        middle_grad = seed + middle_part
        middle_all = spread(middle_grad.astype(BF16), 8)
        mixed_grad = dot(middle_all, out_full, NT)
    output_grad = dot(mixed, middle_all, TN, out=BF16)
    mixed_grad, output_grad, upgate_sum, down_total = lax.optimization_barrier(
        (mixed_grad, output_grad, upgate_sum, down_total.astype(F32))
    )
    output_total = owned_rows(output_grad)
    projected_low, conv_grad, gain_grad, decay_grad = mixer_backward(
        projected, raw, conv_mine, decay_mine, gain, inverse, solved, core, before_silu, mixed_grad, heads, rows
    )
    projected_low, output_total = lax.optimization_barrier((projected_low, output_total))
    def upgate_rows(a):
        return jnp.concatenate(
            [
                jnp.concatenate([x, y], axis=2).transpose(1, 0, 2).reshape(own_d, -1)
                for x, y in (
                    (a[:, :, :main], a[:, :, 2 * main : main + units]),
                    (a[:, :, main : 2 * main], a[:, :, main + units :]),
                )
            ],
            axis=1,
        ).astype(F32)

    in_grad = dot(normed_all, projected_low, TN, out=BF16)
    raw_grad = in_grad[:, cols : cols + 2 * heads].astype(F32)
    output_total = output_total.astype(F32)
    if square:
        lines = jnp.concatenate(
            [
                jnp.zeros((1, width), F32),
                second_grad.reshape(1, width),
                jnp.tile(gain_grad[:, :128], (1, width // 128)),
                jnp.tile(gain_grad[:, 128:], (1, width // 128)),
                jnp.tile(jnp.pad(decay_grad[:, :heads].reshape(1, -1), ((0, 0), (0, 128 - 2 * heads))), (1, width // 128)),
                jnp.zeros((3, width), F32),
            ],
            axis=0,
        )
        mine = jnp.arange(n_dp)[None, :, None] == here
        conv_lines = jnp.concatenate(
            [
                jnp.where(mine, conv_grad[:, None, a:b], 0.0).reshape(taps, -1)
                for a, b in ((0, key), (key, 2 * key), (2 * key, 2 * key + value))
            ],
            axis=1,
        )
        conv_lines = jnp.concatenate(
            [conv_lines, raw_grad.reshape(1, -1), jnp.zeros((7 - taps, conv_lines.shape[1]), F32)], axis=0
        )
        result, tokens_grad, input_total, up_total, summed, planes, conv_total, raw_planes = conclude(
            in_grad.reshape(n_dp, n_z, own_d, cols + 128),
            projected_low.reshape(n_dp, rows, cols + 128),
            in_full,
            raw_weight,
            block_part.reshape(n_dp, rows, width),
            upgate_sum.reshape(n_dp, own_d, 2 * units),
            tokens,
            middle,
            middle_grad,
            first_full,
            lines,
            conv_lines,
            bounds,
            9,
        )
        input_total = input_total.astype(F32)
        decay_total = raw_planes.reshape(n_dp, own_d, 2, heads).transpose(1, 2, 0, 3).reshape(own_d, 2 * all_heads)
        upgate_total = upgate_rows(up_total)
        per = 128 // own_d
        place = lax.rem(flat, per) * own_d
        first_total = lax.dynamic_slice_in_dim(summed[0], place, own_d)
        second_total = lax.dynamic_slice_in_dim(summed[1], place, own_d)
        gain_total = summed[2:4].reshape(-1)
        scale_total = planes[:, :heads].reshape(-1)
        bias_total = planes[:, heads : 2 * heads].reshape(-1)
        conv_total = conv_total[:taps]
    else:
        projected_low, in_grad = lax.optimization_barrier((projected_low, in_grad))
        back_one = (
            dot(projected_low[:, :cols], in_full, NT) + dot(projected_low[:, cols:], raw_weight, NT)
        ).astype(BF16)
        in_sum = owned_parts(by_plane(in_grad[:, :cols]))
        normed_one_grad = total(back_one, 9)
        result = middle + total(block_part, 7)
        input_part, first_grad = norm_back(inputs, first_root, first_full, normed_one_grad)
        tokens_grad = middle_grad + input_part

        up_total = lax.all_to_all(upgate_sum.reshape(n_dp, own_d, -1), "dp", 0, 0, tiled=True)
        upgate_total = upgate_rows(up_total)
        in_total = lax.all_to_all(in_sum.reshape(n_dp, own_d, -1), "dp", 0, 0, tiled=True)
        raw_rows = jnp.zeros((width, 2, all_heads), F32)
        raw_rows = lax.dynamic_update_slice(raw_rows, raw_grad.reshape(width, 2, heads), (0, 0, here * heads))
        decay_total = lax.psum_scatter(raw_rows.reshape(width, -1), ("dp", "fsdp"), scatter_dimension=0, tiled=True)
        in_total = in_total.transpose(1, 0, 2).astype(F32)
        input_total = jnp.concatenate(
            [in_total[:, :, a:b].reshape(own_d, -1) for a, b in zip(bounds[:-1], bounds[1:])], axis=1
        )

        share = key // own_conv, value // own_conv
        owner = jnp.concatenate(
            [
                here * share[0] + jnp.arange(share[0]),
                (n_dp + here) * share[0] + jnp.arange(share[0]),
                2 * n_dp * share[0] + here * share[1] + jnp.arange(share[1]),
            ]
        )
        blocks = conv_grad.reshape(taps, -1, own_conv).transpose(1, 0, 2).reshape(-1, taps * own_conv)
        for_owner = owner[None, :] == jnp.arange(count)[:, None]
        everyone = jnp.concatenate([gain_grad.reshape(-1), decay_grad[:, :heads].reshape(-1)])
        packets = jnp.concatenate(
            [
                first_grad.reshape(count, own_d),
                second_grad.reshape(count, own_d),
                jnp.sum(jnp.where(for_owner[:, :, None], blocks[None], 0.0), axis=1),
                jnp.broadcast_to(everyone[None], (count, everyone.size)),
            ],
            axis=1,
        )
        size = packets.shape[1]
        lines = -(-size // 1024) * 8
        packets = jnp.pad(packets, ((0, 0), (0, lines * 128 - size))).reshape(count, lines, 128)
        shared = scatter_small(packets, n_dp, n_z, 10).reshape(count, -1)
        summed = jnp.sum(shared, axis=0)
        first_total = summed[:own_d]
        second_total = summed[own_d : 2 * own_d]
        start = 2 * own_d + taps * own_conv
        conv_total = summed[2 * own_d : start].reshape(taps, own_conv)
        gain_total = summed[start : start + gain_grad.size]
        start += gain_grad.size
        scale_bias = jnp.sum(shared[:, start : start + 2 * heads].reshape(n_dp, n_z, 2, heads), axis=1)
        scale_total = scale_bias[:, 0].reshape(-1)
        bias_total = scale_bias[:, 1].reshape(-1)
    return (
        result,
        tokens_grad,
        first_total,
        input_total,
        decay_total,
        conv_total,
        scale_total,
        bias_total,
        gain_total,
        output_total,
        second_total,
        upgate_total,
        down_total,
    )


def solution(mesh):
    both = ("dp", "fsdp")
    rows, vector = P(both, None), P(both)
    return jax.shard_map(
        functools.partial(local, mesh.shape["dp"], mesh.shape["fsdp"]),
        mesh=mesh,
        in_specs=(
            rows, rows, vector, vector, rows, rows, P(None, both), P(), P(), P(), rows, vector, rows, rows,
        ),
        out_specs=(
            rows, rows, vector, rows, rows, P(None, both), P(), P(), P(), rows, vector, rows, rows,
        ),
        check_vma=False,
    )
```
